128 devices in a mesh: wide: 16 (over x, z), narrow: 8 (over y, core).
Axes of the slice: x: 4, y: 4, z: 4, core: 2. Of those that a mesh axis runs over, the one named last changes fastest.
Arguments:
- tokens: bfloat16 [16384, 2048], P(('wide', 'narrow')), may hold values from -6 to 6
- lengths: int32 [16, 2], P('wide'), may hold values from 1 to 960, 1024 in all within a row
- picks: int32 [16384, 2], P(('wide', 'narrow')), may hold values from 0 to 3
- cotangent: bfloat16 [16384, 2048], P(('wide', 'narrow'))
- block_master: float32 [2048, 24576], P(('wide', 'narrow'))
- block_first: float32 [2048, 24576], P(('wide', 'narrow')), may hold values from -0.00024414062 to 0.00024414062
- block_second: float32 [2048, 24576], P(('wide', 'narrow')), may hold values from 5.111863e-10 to 8.257626e-09
- gains: float32 [2, 2048], replicated
- gains_first: float32 [2, 2048], replicated, may hold values from -0.00048828125 to 0.00048828125
- gains_second: float32 [2, 2048], replicated, may hold values from 4.915253e-09 to 1.9661012e-08
- router_in: float32 [2048, 256], replicated, may hold values from -0.125 to 0.125
- router_in_first: float32 [2048, 256], replicated, may hold values from -0.00024414062 to 0.00024414062
- router_in_second: float32 [2048, 256], replicated, may hold values from 5.111863e-10 to 8.257626e-09
- router_out: float32 [256, 8], replicated, may hold values from -0.27 to 0.27
- router_out_first: float32 [256, 8], replicated, may hold values from -0.00024414062 to 0.00024414062
- router_out_second: float32 [256, 8], replicated, may hold values from 5.111863e-10 to 8.257626e-09
Outputs:
- output: bfloat16 [16384, 2048], P(('wide', 'narrow'))
- input_grad: float32 [16384, 2048], P(('wide', 'narrow'))
- counts: float32 [2, 4], replicated
- grad_norm: float32 [], replicated
- new_block: float32 [2048, 24576], P(('wide', 'narrow'))
- new_block_first: float32 [2048, 24576], P(('wide', 'narrow'))
- new_block_second: float32 [2048, 24576], P(('wide', 'narrow'))
- block_copy: bfloat16 [2048, 24576], P(('wide', 'narrow'))
- new_gains: float32 [2, 2048], replicated
- new_gains_first: float32 [2, 2048], replicated
- new_gains_second: float32 [2, 2048], replicated
- new_router_in: float32 [2048, 256], replicated
- new_router_in_first: float32 [2048, 256], replicated
- new_router_in_second: float32 [2048, 256], replicated
- new_router_out: float32 [256, 8], replicated
- new_router_out_first: float32 [256, 8], replicated
- new_router_out_second: float32 [256, 8], replicated
The draws below stay inside these ranges and needn't reach their ends.
Inputs may be any that keep to these rules, and one draw needn't show every extreme that they name: `lengths`: each row sums to 1024.
All inputs are finite; a program needn't handle non-finite values.
Results may differ from the reference program's by a relative error of at most 0.023.
Values may be sent and summed in bfloat16 or wider, within the bound.
A program may use at most 640 MiB of HBM per device.

```python
import math
import jax
import jax.numpy as jnp
import numpy as np
from jax import lax

D = 2048
HEADS = 16
HEAD_DIM = 128
FF = 8192
RH = 256
LEVELS = 4
SEGS = 2
STEP = 10
TOK_DEV = 128
GROUP = 1024
TOKENS = 16384
WTOT = 24576
PARAMS = 50862080
N_WIDE = 16
N_NARROW = 8


def draw_picks(key, part):
    key = jax.random.fold_in(key, 11)
    token_index = jnp.arange(TOKENS, dtype=jnp.int32)
    ceiling = 2 + 3 * token_index // TOKENS
    raw_levels = jax.random.randint(key, (TOKENS, 2), 0, 12, dtype=jnp.int32)
    chosen = raw_levels % ceiling[:, None]
    chosen = chosen.at[0].set(0)
    return chosen.at[TOKENS - 1].set(LEVELS - 1).astype(jnp.int32)


def draw_cotangent(key, part):
    key = jax.random.fold_in(key, 12)
    column = jnp.arange(D, dtype=jnp.float32) / D
    base = jax.random.normal(key, (TOKENS, D), jnp.float32)
    ramp = 0.5 + column
    return (base * ramp[None, :]).astype(jnp.bfloat16)


def draw_gains(key, part):
    key = jax.random.fold_in(key, 13)
    column = jnp.arange(D, dtype=jnp.float32) / D
    noise = jax.random.uniform(key, (2, D), jnp.float32, 0.8, 1.2)
    ramp = 0.6 + 1.2 * column
    return noise * ramp[None, :]


def draw_block_master(key, part):
    key = jax.random.fold_in(key, 14)
    column = jnp.arange(WTOT, dtype=jnp.int32)
    base_scale = D ** (-0.5)
    out_scale = (GROUP / 8.0) ** 0.5 * D ** (-0.5)
    down_scale = 2.0 * FF ** (-0.5)
    scales = jnp.where(column < 3 * D, base_scale, jnp.where(column < 4 * D, out_scale, jnp.where(column < 4 * D + FF, base_scale, down_scale)))
    base = jax.random.normal(key, (D, WTOT), jnp.float32)
    return base * scales[None, :].astype(jnp.float32)


def level_of(rng, extent, cuts, least, top_value):
    level = 1.0
    for dim, shards_of in cuts:
        heights = jax.random.uniform(jax.random.fold_in(jax.random.fold_in(rng, 6), dim), (shards_of,), jnp.float32, least / len(cuts), top_value / len(cuts))
        level = level * jnp.repeat(jnp.exp(heights), extent[dim] // shards_of).reshape((-1,) + (1,) * (len(extent) - 1 - dim))
    return level


def length_profile(count, total, limit, skew):
    portions = [(1 << 20) // math.isqrt(grade ** skew) + 1 for grade in range(2, count + 1)]
    rest, given = total - limit - (count - 1), [1] * (count - 1)
    while rest > 0:
        movable = [i for i in range(count - 1) if given[i] < limit]
        pool, remaining = sum([portions[i] for i in movable]), rest
        for i in movable:
            addition = min(limit - given[i], max(1, remaining * portions[i] // pool), rest)
            given[i] = given[i] + addition
            rest = rest - addition
    return np.array([limit] + given)


def ragged(rng, amount, total, reach, slope):
    if amount == 2:
        one = jax.random.randint(rng, (), max(1, total - reach), min(reach, total - 1) + 1)
        return jnp.stack([one, total - one])
    sizes = jnp.asarray(length_profile(amount, total, reach, slope), jnp.int32)
    couples = (amount - 1) // 2
    giver, taker = sizes[1:1 + 2 * couples:2], sizes[2:2 + 2 * couples:2]
    margin = jnp.minimum(giver - 1, reach - taker)
    passed = jax.random.randint(jax.random.fold_in(rng, 1), (couples,), 0, 1 << 20) % (margin + 1)
    sizes = sizes.at[1:1 + 2 * couples:2].set(giver - passed).at[2:2 + 2 * couples:2].set(taker + passed)
    return sizes[jax.random.permutation(jax.random.fold_in(rng, 2), amount)]


def bell_draw(rng, extent, deviation, most, shards=(), held_as=jnp.bfloat16):
    result = deviation * jax.random.normal(rng, extent, jnp.float32)
    if shards:
        result = result * level_of(rng, extent, shards, -0.22, 0.18)
    return jnp.clip(result, -most, most).astype(held_as)


def setup_inputs(seed: int = 0) -> dict:
    arg_keys = jax.random.split(jax.random.key(seed), 17)
    return {
        "tokens": bell_draw(arg_keys[0], (TOKENS, D), 1.0, 6.0, ((0, 128),)),
        "lengths": jax.vmap(lambda own: ragged(own, SEGS, TOK_DEV * N_NARROW, TOK_DEV * N_NARROW - TOK_DEV // 2, 2))(jax.random.split(arg_keys[1], N_WIDE)).reshape((N_WIDE, SEGS)).astype(jnp.int32),
        "picks": draw_picks(jax.random.fold_in(arg_keys[16], 71), 0),
        "cotangent": draw_cotangent(jax.random.fold_in(arg_keys[16], 71), 0),
        "block_master": draw_block_master(jax.random.fold_in(arg_keys[16], 71), 0),
        "block_first": bell_draw(arg_keys[5], (D, WTOT), (0.11 / PARAMS ** 0.5), 0.00024414062, ((0, 128),), jnp.float32),
        "block_second": jnp.clip(jnp.exp(math.log(8.257625694341186e-09) - 2.7821582 * jax.random.uniform(arg_keys[6], (D, WTOT), jnp.float32) ** level_of(arg_keys[6], (D, WTOT), ((0, 128),), -0.2, 0.2)), 5.111863154994012e-10, 8.257625694341186e-09),
        "gains": draw_gains(jax.random.fold_in(arg_keys[16], 71), 0),
        "gains_first": bell_draw(arg_keys[8], (2, D), (0.25 / PARAMS ** 0.5), 0.00048828125, (), jnp.float32),
        "gains_second": jnp.clip(jnp.exp(jax.random.uniform(arg_keys[9], (2, D), jnp.float32, math.log(4.915253093429328e-09), math.log(1.9661012373717313e-08))), 4.915253093429328e-09, 1.9661012373717313e-08),
        "router_in": bell_draw(arg_keys[10], (D, RH), D ** -0.5, 0.125, (), jnp.float32),
        "router_in_first": bell_draw(arg_keys[11], (D, RH), (0.11 / PARAMS ** 0.5), 0.00024414062, (), jnp.float32),
        "router_in_second": jnp.clip(jnp.exp(jax.random.uniform(arg_keys[12], (D, RH), jnp.float32, math.log(5.111863154994012e-10), math.log(8.257625694341186e-09))), 5.111863154994012e-10, 8.257625694341186e-09),
        "router_out": bell_draw(arg_keys[13], (RH, 2 * LEVELS), 0.045, 0.27, (), jnp.float32),
        "router_out_first": bell_draw(arg_keys[14], (RH, 2 * LEVELS), (0.11 / PARAMS ** 0.5), 0.00024414062, (), jnp.float32),
        "router_out_second": jnp.clip(jnp.exp(jax.random.uniform(arg_keys[15], (RH, 2 * LEVELS), jnp.float32, math.log(5.111863154994012e-10), math.log(8.257625694341186e-09))), 5.111863154994012e-10, 8.257625694341186e-09),
    }


HIGHEST = lax.Precision.HIGHEST
NORM_EPS = 1e-05
CLIP_NORM = 1.0

@jax.custom_vjp
def low(v):
    return lax.optimization_barrier(v.astype(jnp.bfloat16)).astype(jnp.float32)

@jax.custom_vjp
def low_back(v):
    return v

def low_keep(v):
    return (low(v), None)

def low_pass(kept, grad):
    return (grad,)

def back_keep(v):
    return (v, None)

def back_low(kept, grad):
    return (low(grad),)
low.defvjp(low_keep, low_pass)
low_back.defvjp(back_keep, back_low)

def layer_norm(values, gain_row):
    average = lax.optimization_barrier(jnp.mean(values, axis=-1, keepdims=True))
    centered = values - average
    spread = lax.optimization_barrier(jnp.mean(centered * centered, axis=-1, keepdims=True))
    return centered * lax.rsqrt(spread + NORM_EPS) * gain_row

def rotate(values, position):
    halfway = values.shape[-1] // 2
    frequency = 10000.0 ** (-jnp.arange(halfway, dtype=jnp.float32) / halfway)
    angles = position.astype(jnp.float32)[:, None] * frequency[None, :]
    cosine = jnp.cos(angles)[:, None, :]
    sine_part = jnp.sin(angles)[:, None, :]
    first_part = values[..., :halfway]
    second_part = values[..., halfway:]
    return jnp.concatenate([first_part * cosine - second_part * sine_part, first_part * sine_part + second_part * cosine], axis=-1)

def segment_info(seg_lengths, token_index):
    seg_ends = jnp.cumsum(seg_lengths).astype(jnp.int32)
    segment = lax.optimization_barrier(jnp.sum((token_index[:, None] >= seg_ends[None, :]).astype(jnp.int32), axis=1))
    starts = seg_ends - seg_lengths
    owners = segment[:, None] == jnp.arange(seg_lengths.shape[0], dtype=jnp.int32)[None, :]
    start_of = lax.optimization_barrier(jnp.sum(jnp.where(owners, starts[None, :], 0), axis=1)).astype(jnp.int32)
    return (segment, token_index - start_of)

def router_gates(normed, first_layer, second_layer, picks):
    hidden = jax.nn.gelu(jnp.dot(normed, first_layer, precision=HIGHEST))
    logits = jnp.dot(hidden, second_layer, precision=HIGHEST)
    levels = jnp.arange(LEVELS, dtype=jnp.int32)
    chosen_attn = (picks[:, 0:1] == levels[None, :]).astype(jnp.float32)
    chosen_ffn = (picks[:, 1:2] == levels[None, :]).astype(jnp.float32)
    gate_attn = float(LEVELS) * lax.optimization_barrier(jnp.sum(jax.nn.softmax(logits[:, :LEVELS], axis=-1) * chosen_attn, axis=-1))
    gate_ffn = float(LEVELS) * lax.optimization_barrier(jnp.sum(jax.nn.softmax(logits[:, LEVELS:], axis=-1) * chosen_ffn, axis=-1))
    return (gate_attn, gate_ffn)

def group_attention(pieces):
    query, keys, values_in, segment = pieces
    group_index = jnp.arange(query.shape[0], dtype=jnp.int32)
    scores = jnp.einsum('qhd,khd->hqk', query, keys, precision=HIGHEST) * HEAD_DIM ** (-0.5)
    scores = low_back(scores)
    allowed = (segment[:, None] == segment[None, :]) & (group_index[None, :] <= group_index[:, None])
    scores = jnp.where(allowed[None], scores, -1e+30)
    top_score = lax.optimization_barrier(jnp.max(scores, axis=-1, keepdims=True))
    expo = jnp.exp(scores - top_score)
    probs = expo / lax.optimization_barrier(jnp.sum(expo, axis=-1, keepdims=True))
    return jnp.einsum('hqk,khd->qhd', low(probs), values_in, precision=HIGHEST)

def adamw(weight, moment_one, moment_two, gradient, step_rate):
    moment_one = 0.9 * moment_one + 0.1 * gradient
    moment_two = 0.95 * moment_two + 0.05 * gradient * gradient
    first_hat = moment_one / (1.0 - 0.9 ** STEP)
    second_hat = moment_two / (1.0 - 0.95 ** STEP)
    updated = weight - step_rate * (first_hat / (jnp.sqrt(second_hat) + 1e-08) + 0.1 * weight)
    return (updated, moment_one, moment_two)

def reference(tokens, lengths, picks, cotangent, block_master, block_first, block_second, gains, gains_first, gains_second, router_in, router_in_first, router_in_second, router_out, router_out_first, router_out_second):
    group_index = jnp.arange(GROUP, dtype=jnp.int32)
    segments, positions = jax.vmap(lambda row: segment_info(row, group_index))(lengths)
    flat_pos = positions.reshape(TOKENS)
    weights = block_master.astype(jnp.bfloat16).astype(jnp.float32)
    inputs = tokens.astype(jnp.float32)
    head_mask = jnp.arange(HEADS, dtype=jnp.int32)[None, :] < HEADS * (picks[:, 0:1] + 1) // LEVELS
    unit_mask = (jnp.arange(FF, dtype=jnp.int32)[None, :] < FF * (picks[:, 1:2] + 1) // LEVELS).astype(jnp.float32)

    def forward(values, gain_rows, first_layer, second_layer, weight_block):
        w_qkv = weight_block[:, :3 * D]
        w_out = weight_block[:, 3 * D:4 * D]
        w_up = weight_block[:, 4 * D:4 * D + FF]
        w_down = weight_block[:, 4 * D + FF:]
        normed = low(layer_norm(values, gain_rows[0]))
        gate_attn, gate_ffn = router_gates(normed, first_layer, second_layer, picks)
        projected = low_back(jnp.dot(normed, w_qkv, precision=HIGHEST))
        query = low(rotate(projected[:, :D].reshape(TOKENS, HEADS, HEAD_DIM), flat_pos))
        keys = low(rotate(projected[:, D:2 * D].reshape(TOKENS, HEADS, HEAD_DIM), flat_pos))
        values_in = low(projected[:, 2 * D:].reshape(TOKENS, HEADS, HEAD_DIM))
        shaped = (N_WIDE, GROUP, HEADS, HEAD_DIM)
        attended = lax.map(jax.checkpoint(group_attention), (query.reshape(shaped), keys.reshape(shaped), values_in.reshape(shaped), segments))
        attended = low_back(attended.reshape(TOKENS, HEADS, HEAD_DIM))
        mixed = low(jnp.where(head_mask[:, :, None], attended, 0.0).reshape(TOKENS, D))
        attn_out = low_back(jnp.dot(mixed, w_out.T, precision=HIGHEST))
        after_attn = values + gate_attn[:, None] * attn_out
        normed_two = low(layer_norm(after_attn, gain_rows[1]))
        up_proj = low_back(jnp.dot(normed_two, w_up, precision=HIGHEST))
        positive = jnp.maximum(up_proj, 0.0)
        activity = low(positive * positive * unit_mask)
        ffn_out = low_back(jnp.dot(activity, w_down.T, precision=HIGHEST))
        return after_attn + gate_ffn[:, None] * ffn_out
    primal, pullback = jax.vjp(forward, inputs, gains, router_in, router_out, weights)
    d_inputs, gain_grad, router_in_grad, router_out_grad, block_grad = pullback(cotangent.astype(jnp.float32))
    levels = jnp.arange(LEVELS, dtype=jnp.int32)
    counts = jnp.stack([lax.optimization_barrier(jnp.sum((picks[:, 0:1] == levels[None, :]).astype(jnp.float32), axis=0)), lax.optimization_barrier(jnp.sum((picks[:, 1:2] == levels[None, :]).astype(jnp.float32), axis=0))])
    total = jnp.sum(block_grad * block_grad) + jnp.sum(gain_grad * gain_grad) + jnp.sum(router_in_grad * router_in_grad) + jnp.sum(router_out_grad * router_out_grad)
    grad_norm = jnp.sqrt(total)
    clip_factor = jnp.minimum(1.0, CLIP_NORM / grad_norm)
    new_block, new_block_first, new_block_second = adamw(block_master, block_first, block_second, block_grad * clip_factor, 0.02)
    new_gains, new_gains_first, new_gains_second = adamw(gains, gains_first, gains_second, gain_grad * clip_factor, 0.6)
    new_router_in, new_router_in_first, new_router_in_second = adamw(router_in, router_in_first, router_in_second, router_in_grad * clip_factor, 0.02)
    new_router_out, new_router_out_first, new_router_out_second = adamw(router_out, router_out_first, router_out_second, router_out_grad * clip_factor, 0.02)
    return (primal.astype(jnp.bfloat16), d_inputs, counts, grad_norm, new_block, new_block_first, new_block_second, new_block.astype(jnp.bfloat16), new_gains, new_gains_first, new_gains_second, new_router_in, new_router_in_first, new_router_in_second, new_router_out, new_router_out_first, new_router_out_second)
```

```python
import functools

import jax
import jax.numpy as jnp
from jax import lax
from jax.experimental import pallas as pl
from jax.experimental.pallas import tpu as pltpu
from jax.sharding import PartitionSpec as P

D = 2048
HEADS = 16
HEAD_DIM = 128
FF = 8192
RH = 256
LEVELS = 4
STEP = 10
TOK = 128
GROUP = 1024
SIDE = 4
WIDE = 16
NARROW = 8
ROWS = 16

NORM_EPS = 1e-05
CLIP_NORM = 1.0
CONTRACT_COLS = (((1,), (1,)), ((), ()))
CONTRACT_ROWS = (((0,), (0,)), ((), ()))
MESH = pl.DeviceIdType.MESH
BF = jnp.bfloat16
F32 = jnp.float32


def here():
    w = lax.axis_index("wide")
    n = lax.axis_index("narrow")
    return lax.div(w, SIDE), lax.rem(w, SIDE), lax.div(n, 2), lax.rem(n, 2)


def wrap(i):
    return lax.rem(i + 2 * SIDE, SIDE)


def moved(dx=0, dz=0, dy=0, dc=0):
    x, z, y, c = here()
    return (wrap(x + dx) * SIDE + wrap(z + dz), wrap(y + dy) * 2 + lax.rem(c + dc, 2))


NEAR_Y = [dict(dy=1), dict(dy=-1), dict(dc=1)]
NARROW_ALL = [dict(dy=a, dc=b) for a in range(SIDE) for b in range(2) if a or b]
NEAR_XZ = [dict(dx=1), dict(dx=-1), dict(dz=1), dict(dz=-1)]
LINES_XZ = [dict(dx=a) for a in (1, 2, 3)] + [dict(dz=a) for a in (1, 2, 3)]
WIDE_ALL = [dict(dx=a, dz=b) for a in range(SIDE) for b in range(SIDE) if a or b]


def greet(partners):
    barrier = pltpu.get_barrier_semaphore()
    for p in partners:
        pl.semaphore_signal(barrier, inc=1, device_id=moved(**p), device_id_type=MESH)
    pl.semaphore_wait(barrier, len(partners))


def span(start, size):
    if not isinstance(start, int):
        start = pl.multiple_of(start, ROWS)
    return pl.ds(start, size)


class Net:
    def __init__(self, send, recv, local):
        self.send, self.recv, self.local = send, recv, local
        self.used, self.used_local = 0, 0
        self.sent, self.kept = [], []

    def put(self, src, dst, target):
        i = self.used
        self.used += 1
        copy = pltpu.make_async_remote_copy(
            src_ref=src,
            dst_ref=dst,
            send_sem=self.send.at[i],
            recv_sem=self.recv.at[i],
            device_id=target,
            device_id_type=MESH,
        )
        copy.start()
        self.sent.append(copy)
        return copy

    def keep(self, src, dst):
        i = self.used_local
        self.used_local += 1
        copy = pltpu.make_async_copy(src, dst, self.local.at[i])
        copy.start()
        return copy

    def finish(self):
        for copy in self.sent:
            copy.wait_send()


def take_turns(*parts):
    live = list(parts)
    while live:
        still = []
        for part in live:
            try:
                next(part)
                still.append(part)
            except StopIteration:
                pass
        live = still


def comm_call(body, ins, outs, scratch, cid, copies, locals_, name, flops=0):
    n_in, n_out, n_scr = len(ins), len(outs), len(scratch)

    def kernel(*refs):
        in_refs = refs[:n_in]
        out_refs = refs[n_in : n_in + n_out]
        scr = refs[n_in + n_out : n_in + n_out + n_scr]
        send, recv, local = refs[n_in + n_out + n_scr :]
        net = Net(send, recv, local)
        body(net, in_refs, out_refs, scr)
        net.finish()
        assert net.used <= copies and net.used_local <= locals_, (net.used, net.used_local)

    return pl.pallas_call(
        kernel,
        out_shape=outs,
        in_specs=[pl.BlockSpec(memory_space=pl.ANY)] * n_in,
        out_specs=[pl.BlockSpec(memory_space=pl.ANY)] * n_out,
        scratch_shapes=list(scratch)
        + [
            pltpu.SemaphoreType.DMA((copies,)),
            pltpu.SemaphoreType.DMA((copies,)),
            pltpu.SemaphoreType.DMA((max(locals_, 1),)),
        ],
        compiler_params=pltpu.CompilerParams(
            collective_id=cid, has_side_effects=True, vmem_limit_bytes=56 * 2**20
        ),
        name=name,
    )(*ins)


def gather_narrow(net, own, out):
    x, z, y, c = here()
    rows = own.shape[0]
    half = rows // 2

    def block(dy, lo=0, size=rows):
        return out.at[span((wrap(y + dy) * 2 + c) * rows + lo, size)]

    mine = net.keep(own, block(0))
    up = net.put(own, block(0), moved(dy=1))
    down = net.put(own, block(0), moved(dy=-1))
    across = [net.put(own, block(0), moved(dc=1))]
    yield
    up.wait_recv()
    on = net.put(block(-1, 0, half), block(-1, 0, half), moved(dy=1))
    across.append(net.put(block(-1), block(-1), moved(dc=1)))
    yield
    down.wait_recv()
    back = net.put(block(1, half, half), block(1, half, half), moved(dy=-1))
    across.append(net.put(block(1), block(1), moved(dc=1)))
    yield
    on.wait_recv()
    across.append(net.put(block(2, 0, half), block(2, 0, half), moved(dc=1)))
    yield
    back.wait_recv()
    across.append(net.put(block(2, half, half), block(2, half, half), moved(dc=1)))
    yield
    mine.wait()
    for copy in across:
        copy.wait_recv()


GATHER_COPIES = 10


def gather_call(own, cid, name):
    rows, cols = own.shape

    def body(net, ins, outs, scr):
        greet(NEAR_Y)
        take_turns(gather_narrow(net, ins[0], outs[0]))

    return comm_call(
        body,
        [own],
        [jax.ShapeDtypeStruct((NARROW * rows, cols), own.dtype)],
        [],
        cid,
        GATHER_COPIES,
        1,
        name,
    )[0]


def reduce_scratch(rows, cols):
    return [
        pltpu.VMEM((SIDE, rows, cols), BF),
        pltpu.VMEM((SIDE, rows, cols), BF),
        pltpu.VMEM((2, rows // 2, cols), BF),
        pltpu.VMEM((2, rows, cols), BF),
        pltpu.VMEM((3, rows, cols), BF),
        pltpu.VMEM((rows, cols), F32),
    ]


REDUCE_COPIES = 10
REDUCE_LOCALS = 5


def reduce_narrow(net, part, out, scr):
    own, other, through, landed, ready, total = scr
    x, z, y, c = here()
    rows, cols = out.shape
    half = rows // 2

    def block(dy, core):
        return part.at[span((wrap(y + dy) * 2 + core) * rows, rows)]

    order = (2, 1, 3, 0)
    local, cross = {}, {}
    for dy in order:
        cross[dy] = net.put(block(dy, 1 - c), other.at[dy], moved(dc=1))
        local[dy] = net.keep(block(dy, c), own.at[dy])

    def pair(dy, lo, size):
        s = span(lo, size)
        return own[dy, s, :].astype(F32) + other[dy, s, :].astype(F32)

    yield
    local[2].wait()
    cross[2].wait_recv()
    ready[0] = pair(2, 0, rows).astype(BF)
    first, last = span(0, half), span(half, half)
    via_up = net.put(ready.at[0, first], through.at[0], moved(dy=1))
    via_down = net.put(ready.at[0, last], through.at[1], moved(dy=-1))
    yield
    local[1].wait()
    cross[1].wait_recv()
    ready[1, last, :] = pair(1, half, half).astype(BF)
    up_late = net.put(ready.at[1, last], landed.at[0, last], moved(dy=1))
    local[3].wait()
    cross[3].wait_recv()
    ready[2, first, :] = pair(3, 0, half).astype(BF)
    down_first = net.put(ready.at[2, first], landed.at[1, first], moved(dy=-1))
    yield
    via_up.wait_recv()
    ready[1, first, :] = (pair(1, 0, half) + through[0].astype(F32)).astype(BF)
    up_first = net.put(ready.at[1, first], landed.at[0, first], moved(dy=1))
    via_down.wait_recv()
    ready[2, last, :] = (pair(3, half, half) + through[1].astype(F32)).astype(BF)
    down_late = net.put(ready.at[2, last], landed.at[1, last], moved(dy=-1))
    yield
    local[0].wait()
    cross[0].wait_recv()
    total[...] = pair(0, 0, rows)
    yield
    for copy in (up_late, down_first, up_first, down_late):
        copy.wait_recv()
    total[...] += landed[0].astype(F32) + landed[1].astype(F32)
    done = net.keep(total, out)
    yield
    done.wait()


def reduce_call(parts, cid, name):
    n = len(parts)
    shapes = [(p.shape[0] // NARROW, p.shape[1]) for p in parts]
    scratch = [s for shape in shapes for s in reduce_scratch(*shape)]

    def body(net, ins, outs, scr):
        greet(NEAR_Y)
        take_turns(
            *[reduce_narrow(net, ins[i], outs[i], scr[6 * i : 6 * i + 6]) for i in range(n)]
        )

    return comm_call(
        body,
        list(parts),
        [jax.ShapeDtypeStruct(s, F32) for s in shapes],
        scratch,
        cid,
        REDUCE_COPIES * n,
        REDUCE_LOCALS * n,
        name,
    )


def spread_narrow(net, src, slab):
    w = lax.axis_index("wide")
    n = lax.axis_index("narrow")
    base = w * TOK + n * ROWS
    mine = net.keep(src.at[n], slab.at[span(base, ROWS)])
    copies = []
    for p in NARROW_ALL:
        target = moved(**p)
        copies.append(net.put(src.at[target[1]], slab.at[span(base, ROWS)], target))
    yield
    mine.wait()
    for copy in copies:
        copy.wait_recv()


SPREAD_COPIES = 7


def gather_wide(net, slab, lead):
    x, z, y, c = here()
    rows = TOK // 2
    half = rows // 2
    low = 0 if lead == "x" else rows

    def block(a, b, lo=0, size=rows):
        px, pz = (a, b) if lead == "x" else (b, a)
        return slab.at[span((wrap(x + px) * SIDE + wrap(z + pz)) * TOK + low + lo, size)]

    def lead_to(d):
        return moved(dx=d) if lead == "x" else moved(dz=d)

    def then_to(d):
        return moved(dz=d) if lead == "x" else moved(dx=d)

    def both(src, to):
        return net.put(src, src, to(1)), net.put(src, src, to(-1))

    fore, aft = both(block(0, 0), lead_to)
    second = {0: both(block(0, 0), then_to)}
    yield
    fore.wait_recv()
    on = net.put(block(-1, 0, 0, half), block(-1, 0, 0, half), lead_to(1))
    second[-1] = both(block(-1, 0), then_to)
    aft.wait_recv()
    back = net.put(block(1, 0, half, half), block(1, 0, half, half), lead_to(-1))
    second[1] = both(block(1, 0), then_to)
    yield
    last = []

    def relay(a):
        f, b = second[a]
        f.wait_recv()
        last.append(net.put(block(a, -1, 0, half), block(a, -1, 0, half), then_to(1)))
        b.wait_recv()
        last.append(net.put(block(a, 1, half, half), block(a, 1, half, half), then_to(-1)))

    relay(0)
    yield
    on.wait_recv()
    back.wait_recv()
    second[2] = both(block(2, 0), then_to)
    yield
    relay(-1)
    relay(1)
    yield
    relay(2)
    yield
    for copy in last:
        copy.wait_recv()


WIDE_COPIES = 20


def chain(*parts):
    for part in parts:
        yield from part


def first_gather(owns, sources, cid):
    k, m = len(owns), len(sources)

    def body(net, ins, outs, scr):
        greet(NARROW_ALL + NEAR_XZ)

        def weights(i):
            yield from spread_narrow(net, ins[k + i], outs[k + i])
            a = gather_wide(net, outs[k + i], "x")
            b = gather_wide(net, outs[k + i], "z")
            live = [a, b]
            while live:
                for g in list(live):
                    try:
                        next(g)
                    except StopIteration:
                        live.remove(g)
                yield

        take_turns(
            weights(0),
            gather_narrow(net, ins[0], outs[0]),
            *[weights(i) for i in range(1, m)],
            *[gather_narrow(net, ins[i], outs[i]) for i in range(1, k)],
        )

    shapes = [jax.ShapeDtypeStruct((NARROW * o.shape[0], o.shape[1]), o.dtype) for o in owns] + [
        jax.ShapeDtypeStruct((D, s.shape[2]), s.dtype) for s in sources
    ]
    return comm_call(
        body,
        list(owns) + list(sources),
        shapes,
        [],
        cid,
        k * GATHER_COPIES + m * (SPREAD_COPIES + 2 * WIDE_COPIES),
        k + m,
        "first_gather",
    )


def grad_scratch(cols):
    part = TOK // 2
    return [
        pltpu.VMEM((2, SIDE, part, cols), BF),
        pltpu.VMEM((2, 3, SIDE, part, cols), BF),
        pltpu.VMEM((2, SIDE, part, cols), BF),
        pltpu.VMEM((2, 3, part, cols), BF),
        pltpu.VMEM((TOK, cols), BF),
    ]


GRAD_COPIES = 2 * 6 + 7
GRAD_LOCALS = 3


def reduce_wide(net, grad, out, scr, lead):
    own, landed, sums, late, total = scr
    x, z, y, c = here()
    part = TOK // 2
    half = 0 if lead == "x" else 1
    low = half * part
    blocks = grad.reshape(SIDE, SIDE, TOK, grad.shape[1])

    def line(d):
        if lead == "x":
            return blocks.at[wrap(x + d), :, span(low, part), :]
        return blocks.at[:, wrap(z + d), span(low, part), :]

    def lead_to(d):
        return moved(dx=d) if lead == "x" else moved(dz=d)

    def then_to(d):
        return moved(dz=d) if lead == "x" else moved(dx=d)

    mine = net.keep(line(0), own.at[half])
    copies = [net.put(line(d), landed.at[half, d - 1], lead_to(d)) for d in (2, 1, 3)]
    yield
    mine.wait()
    for copy in copies:
        copy.wait_recv()

    @pl.loop(0, SIDE)
    def _(i):
        s = own[half, i].astype(F32)
        for d in range(3):
            s = s + landed[half, d, i].astype(F32)
        sums[half, i] = s.astype(BF)

    me = z if lead == "x" else x
    copies = [net.put(sums.at[half, wrap(me + d)], late.at[half, d - 1], then_to(d)) for d in (2, 1, 3)]
    yield
    for copy in copies:
        copy.wait_recv()
    s = sums[half, me].astype(F32)
    for d in range(3):
        s = s + late[half, d].astype(F32)
    total[span(low, part), :] = s.astype(BF)


def return_narrow(net, total, out):
    n = lax.axis_index("narrow")

    def rows(i):
        return total.at[span(i * ROWS, ROWS)]

    mine = net.keep(rows(n), out.at[n])
    copies = []
    for p in NARROW_ALL:
        target = moved(**p)
        copies.append(net.put(rows(target[1]), out.at[n], target))
    yield
    mine.wait()
    for copy in copies:
        copy.wait_recv()


def reduce_grads(grads, small, cid):
    m = len(grads)
    scratch = [s for g in grads for s in grad_scratch(g.shape[1])]
    scratch += [pltpu.VMEM((WIDE, ROWS, RH), BF), pltpu.VMEM((ROWS, RH), F32)]

    def body(net, ins, outs, scr):
        greet(NARROW_ALL + WIDE_ALL)
        w = lax.axis_index("wide")

        def one(i):
            s = scr[5 * i : 5 * i + 5]
            a = reduce_wide(net, ins[i], outs[i], s, "x")
            b = reduce_wide(net, ins[i], outs[i], s, "z")
            live = [a, b]
            while live:
                for g in list(live):
                    try:
                        next(g)
                    except StopIteration:
                        live.remove(g)
                if live:
                    yield
            yield from return_narrow(net, s[4], outs[i])

        def little():
            landed, total = scr[5 * m :]

            def rows(i):
                return ins[m].at[span(i * ROWS, ROWS)]

            mine = net.keep(rows(w), landed.at[w])
            copies = []
            for p in WIDE_ALL:
                target = moved(**p)
                copies.append(net.put(rows(target[0]), landed.at[w], target))
            yield
            yield
            mine.wait()
            for copy in copies:
                copy.wait_recv()
            s = landed[0].astype(F32)
            for i in range(1, WIDE):
                s = s + landed[i].astype(F32)
            total[...] = s
            done = net.keep(total, outs[m])
            yield
            done.wait()

        take_turns(*[one(i) for i in range(m)], little())

    shapes = [jax.ShapeDtypeStruct((NARROW, ROWS, g.shape[1]), BF) for g in grads]
    shapes.append(jax.ShapeDtypeStruct((ROWS, RH), F32))
    return comm_call(
        body,
        list(grads) + [small],
        shapes,
        scratch,
        cid,
        m * GRAD_COPIES + 15,
        m * GRAD_LOCALS + 2,
        "reduce_grads",
    )


def last_sums(vector, shard, cid):
    rows = vector.shape[0]

    def body(net, ins, outs, scr):
        vec, own = ins
        vec_out, full = outs
        first, mid, second, total = scr
        w = lax.axis_index("wide")
        n = lax.axis_index("narrow")
        greet(NARROW_ALL + WIDE_ALL)

        def sums():
            mine = net.keep(vec, first.at[n])
            copies = [net.put(vec, first.at[n], moved(**p)) for p in NARROW_ALL]
            yield
            mine.wait()
            for copy in copies:
                copy.wait_recv()
            s = first[0]
            for i in range(1, NARROW):
                s = s + first[i]
            mid[...] = s
            mine = net.keep(mid, second.at[w])
            copies = [net.put(mid, second.at[w], moved(**p)) for p in WIDE_ALL]
            yield
            mine.wait()
            for copy in copies:
                copy.wait_recv()
            s = second[0]
            for i in range(1, WIDE):
                s = s + second[i]
            total[...] = s
            done = net.keep(total, vec_out)
            yield
            done.wait()

        def table():
            spot = full.at[span(n * GROUP // 4 + w * ROWS, ROWS)]
            mine = net.keep(own, spot)
            copies = [net.put(own, spot, moved(**p)) for p in WIDE_ALL]
            yield
            mine.wait()
            for copy in copies:
                copy.wait_recv()
            x, z, y, c = here()

            def block(dy):
                return full.at[span((wrap(y + dy) * 2 + c) * RH, RH)]

            along = [net.put(block(0), block(0), moved(dy=d)) for d in (1, 3, 2)]
            across = [net.put(block(0), block(0), moved(dc=1))]
            yield
            for copy, d in zip(along, (1, 3, 2)):
                copy.wait_recv()
                across.append(net.put(block(-d), block(-d), moved(dc=1)))
            yield
            for copy in across:
                copy.wait_recv()

        take_turns(sums(), table())

    return comm_call(
        body,
        [vector, shard],
        [jax.ShapeDtypeStruct((rows, 128), F32), jax.ShapeDtypeStruct((D, RH), F32)],
        [
            pltpu.VMEM((NARROW, rows, 128), F32),
            pltpu.VMEM((rows, 128), F32),
            pltpu.VMEM((WIDE, rows, 128), F32),
            pltpu.VMEM((rows, 128), F32),
        ],
        cid,
        7 + 15 + 15 + 7,
        4,
        "last_sums",
    )


def layer_norm(values, gain_row):
    average = jnp.mean(values, axis=-1, keepdims=True)
    centered = values - average
    spread = jnp.mean(centered * centered, axis=-1, keepdims=True)
    return centered * lax.rsqrt(spread + NORM_EPS) * gain_row


def rotate(values, position):
    halfway = values.shape[-1] // 2
    frequency = 10000.0 ** (-jnp.arange(halfway, dtype=jnp.float32) / halfway)
    angles = position.astype(jnp.float32)[:, None] * frequency[None, :]
    cosine = jnp.cos(angles)[:, None, :]
    sine_part = jnp.sin(angles)[:, None, :]
    first_part = values[..., :halfway]
    second_part = values[..., halfway:]
    return jnp.concatenate(
        [
            first_part * cosine - second_part * sine_part,
            first_part * sine_part + second_part * cosine,
        ],
        axis=-1,
    )


def segment_info(seg_lengths, token_index):
    seg_ends = jnp.cumsum(seg_lengths)
    segment = jnp.sum((token_index[:, None] >= seg_ends[None, :]).astype(jnp.int32), axis=1)
    starts = seg_ends - seg_lengths
    owners = segment[:, None] == jnp.arange(seg_lengths.shape[0], dtype=jnp.int32)[None, :]
    start_of = jnp.sum(jnp.where(owners, starts[None, :], 0), axis=1)
    return (segment, token_index - start_of)


def router_gates(normed, first_layer, second_layer, picks):
    hidden = jax.nn.gelu(jnp.dot(normed, first_layer))
    logits = jnp.dot(hidden, second_layer)
    levels = jnp.arange(LEVELS, dtype=jnp.int32)
    chosen_attn = (picks[:, 0:1] == levels[None, :]).astype(jnp.float32)
    chosen_ffn = (picks[:, 1:2] == levels[None, :]).astype(jnp.float32)
    gate_attn = float(LEVELS) * jnp.sum(
        jax.nn.softmax(logits[:, :LEVELS], axis=-1) * chosen_attn, axis=-1
    )
    gate_ffn = float(LEVELS) * jnp.sum(
        jax.nn.softmax(logits[:, LEVELS:], axis=-1) * chosen_ffn, axis=-1
    )
    return (gate_attn, gate_ffn)


def adamw(weight, moment_one, moment_two, gradient, step_rate):
    moment_one = 0.9 * moment_one + 0.1 * gradient
    moment_two = 0.95 * moment_two + 0.05 * gradient * gradient
    first_hat = moment_one / (1.0 - 0.9**STEP)
    second_hat = moment_two / (1.0 - 0.95**STEP)
    updated = weight - step_rate * (first_hat / (jnp.sqrt(second_hat) + 1e-08) + 0.1 * weight)
    return (updated, moment_one, moment_two)


def cut(rows, start, width, pieces):
    part = rows[:, start : start + width].reshape(rows.shape[0], pieces, width // pieces)
    return part.transpose(1, 0, 2)


def joined(part):
    return part.transpose(1, 0, 2).reshape(ROWS, -1)


def on_device(
    tokens,
    lengths,
    picks,
    cotangent,
    block_master,
    block_first,
    block_second,
    gains,
    gains_first,
    gains_second,
    router_in,
    router_in_first,
    router_in_second,
    router_out,
    router_out_first,
    router_out_second,
):
    score_scale = HEAD_DIM ** (-0.5)
    rank_number = lax.axis_index("narrow")
    own_heads = HEADS // NARROW
    head_part = D // NARROW
    unit_part = FF // NARROW

    low = block_master.astype(BF)
    source_a = jnp.concatenate([cut(low, i * D, D, NARROW) for i in range(4)], axis=2)
    source_b = jnp.concatenate([cut(low, 4 * D + i * FF, FF, NARROW) for i in range(2)], axis=2)
    inputs = tokens.astype(F32)
    norm_one, norm_one_back = jax.vjp(layer_norm, inputs, gains[0])
    normed_own = norm_one.astype(BF)
    (gate_attn, gate_ffn), router_back = jax.vjp(
        lambda normed, first_layer, second_layer: router_gates(
            normed, first_layer, second_layer, picks
        ),
        normed_own.astype(F32),
        router_in,
        router_out,
    )
    upstream = cotangent.astype(F32)
    d_ffn_own = (upstream * gate_ffn[:, None]).astype(BF)
    marks = jnp.where(jnp.arange(128)[None, :] < 64, picks[:, 0:1], picks[:, 1:2]).astype(BF)

    normed_low, d_ffn_low, group_marks, slab_a, slab_b = first_gather(
        [normed_own, d_ffn_own, marks], [source_a, source_b], 0
    )
    w_qkv, w_out = slab_a[:, : 3 * head_part], slab_a[:, 3 * head_part :]
    w_up, w_down = slab_b[:, :unit_part], slab_b[:, unit_part:]
    picks_attn = group_marks[:, 0:1].astype(jnp.int32)
    picks_ffn = group_marks[:, 64:65].astype(jnp.int32)

    key_index = jnp.arange(GROUP, dtype=jnp.int32)
    key_segment, key_position = segment_info(lengths[0], key_index)
    allowed = (key_segment[:, None] == key_segment[None, :]) & (
        key_index[None, :] <= key_index[:, None]
    )
    projected = jnp.dot(normed_low, w_qkv, preferred_element_type=F32)
    query_raw = projected[:, :head_part].reshape(GROUP, own_heads, HEAD_DIM)
    key_raw = projected[:, head_part : 2 * head_part].reshape(GROUP, own_heads, HEAD_DIM)
    rotated, rotate_back = jax.vjp(lambda values: rotate(values, key_position), query_raw)
    query_low = rotated.astype(BF)
    key_low = rotate(key_raw, key_position).astype(BF)
    value_low = projected[:, 2 * head_part :].reshape(GROUP, own_heads, HEAD_DIM).astype(BF)
    scores = (
        jnp.einsum("qhd,khd->hqk", query_low, key_low, preferred_element_type=F32) * score_scale
    )
    scores = jnp.where(allowed[None], scores, -1e30)
    top_score = jnp.max(scores, axis=-1, keepdims=True)
    expo = jnp.exp(scores - top_score)
    probs = expo / jnp.sum(expo, axis=-1, keepdims=True)
    probs_low = probs.astype(BF)
    attended = jnp.einsum("hqk,khd->qhd", probs_low, value_low, preferred_element_type=F32)
    head_number = rank_number * own_heads + jnp.arange(own_heads, dtype=jnp.int32)
    head_mask = (head_number[None, :] < HEADS * (picks_attn + 1) // LEVELS).astype(F32)
    mixed_low = (attended * head_mask[:, :, None]).reshape(GROUP, head_part).astype(BF)
    attn_part = lax.dot_general(mixed_low, w_out, CONTRACT_COLS, preferred_element_type=F32)
    (attn_out,) = reduce_call([attn_part.astype(BF)], 1, "sum_attention")

    after_attn = inputs + gate_attn[:, None] * attn_out
    norm_two, norm_two_back = jax.vjp(layer_norm, after_attn, gains[1])
    normed_two_low = gather_call(norm_two.astype(BF), 2, "gather_normed")

    up_proj = jnp.dot(normed_two_low, w_up, preferred_element_type=F32)
    unit_number = rank_number * unit_part + jnp.arange(unit_part, dtype=jnp.int32)
    unit_mask = (unit_number[None, :] < FF * (picks_ffn + 1) // LEVELS).astype(F32)
    positive = jnp.maximum(up_proj, 0.0)
    activity_low = (positive * positive * unit_mask).astype(BF)
    ffn_part = lax.dot_general(activity_low, w_down, CONTRACT_COLS, preferred_element_type=F32)
    d_activity = jnp.dot(d_ffn_low, w_down, preferred_element_type=F32)
    d_up_low = (d_activity * unit_mask * 2.0 * positive).astype(BF)
    d_norm_part = lax.dot_general(d_up_low, w_up, CONTRACT_COLS, preferred_element_type=F32)
    grad_down = lax.dot_general(
        d_ffn_low, activity_low, CONTRACT_ROWS, preferred_element_type=F32
    ).astype(BF)
    grad_up = lax.dot_general(
        normed_two_low, d_up_low, CONTRACT_ROWS, preferred_element_type=F32
    ).astype(BF)
    d_norm_two, ffn_out = reduce_call(
        [d_norm_part.astype(BF), ffn_part.astype(BF)], 3, "sum_ffn"
    )

    result = (after_attn + gate_ffn[:, None] * ffn_out).astype(BF)
    d_gate_ffn = jnp.sum(upstream * ffn_out, axis=1)
    d_after, d_gain_two = norm_two_back(d_norm_two)
    d_after = d_after + upstream
    d_gate_attn = jnp.sum(d_after * attn_out, axis=1)
    d_attn_low = gather_call((d_after * gate_attn[:, None]).astype(BF), 4, "gather_dattn")

    grad_out = lax.dot_general(
        d_attn_low, mixed_low, CONTRACT_ROWS, preferred_element_type=F32
    ).astype(BF)
    d_mixed = jnp.dot(d_attn_low, w_out, preferred_element_type=F32)
    d_attended = (d_mixed.reshape(GROUP, own_heads, HEAD_DIM) * head_mask[:, :, None]).astype(BF)
    d_probs = jnp.einsum("qhd,khd->hqk", d_attended, value_low, preferred_element_type=F32)
    centre = jnp.sum(probs * d_probs, axis=-1, keepdims=True)
    d_scores = (probs * (d_probs - centre)).astype(BF)
    d_query = (
        jnp.einsum("hqk,khd->qhd", d_scores, key_low, preferred_element_type=F32) * score_scale
    )
    d_key = (
        jnp.einsum("hqk,qhd->khd", d_scores, query_low, preferred_element_type=F32) * score_scale
    )
    d_value = jnp.einsum("hqk,qhd->khd", probs_low, d_attended, preferred_element_type=F32)
    d_query_raw = rotate_back(d_query)[0].reshape(GROUP, head_part)
    d_key_raw = rotate_back(d_key)[0].reshape(GROUP, head_part)
    d_proj_low = jnp.concatenate(
        [d_query_raw, d_key_raw, d_value.reshape(GROUP, head_part)], axis=1
    ).astype(BF)
    grad_qkv = lax.dot_general(
        normed_low, d_proj_low, CONTRACT_ROWS, preferred_element_type=F32
    ).astype(BF)
    d_normed_part = lax.dot_general(d_proj_low, w_qkv, CONTRACT_COLS, preferred_element_type=F32)
    d_normed_router, grad_router_in, grad_router_out = router_back((d_gate_attn, d_gate_ffn))
    d_normed, router_in_part = reduce_call(
        [d_normed_part.astype(BF), grad_router_in.astype(BF)], 5, "sum_dnormed"
    )
    d_inputs, d_gain_one = norm_one_back(d_normed + d_normed_router)
    d_inputs = d_inputs + d_after

    sum_qkv, sum_out, sum_up, sum_down, router_in_shard = reduce_grads(
        [grad_qkv, grad_out, grad_up, grad_down], router_in_part.astype(BF), 6
    )
    block_grad = jnp.concatenate(
        [joined(sum_qkv[:, :, i * head_part : (i + 1) * head_part]) for i in range(3)]
        + [joined(sum_out), joined(sum_up), joined(sum_down)],
        axis=1,
    ).astype(F32)

    levels = jnp.arange(LEVELS, dtype=jnp.int32)
    counts_local = jnp.concatenate(
        [
            jnp.sum((picks[:, 0:1] == levels[None, :]).astype(F32), axis=0),
            jnp.sum((picks[:, 1:2] == levels[None, :]).astype(F32), axis=0),
        ]
    )
    local_squares = jnp.sum(block_grad * block_grad) + jnp.sum(router_in_shard * router_in_shard)
    pieces = [
        d_gain_one,
        d_gain_two,
        grad_router_out.ravel(),
        counts_local,
        local_squares[None],
    ]
    size = sum(p.shape[0] for p in pieces)
    padded = -(-size // 1024) * 1024
    vector = jnp.concatenate(pieces + [jnp.zeros((padded - size,), F32)]).reshape(-1, 128)
    vector, router_in_grad = last_sums(vector, router_in_shard, 7)
    flat = vector.ravel()
    gain_grad = flat[: 2 * D].reshape(2, D)
    router_out_grad = flat[2 * D : 2 * D + RH * 8].reshape(RH, 8)
    at = 2 * D + RH * 8
    counts = flat[at : at + 8].reshape(2, LEVELS)
    squares = flat[at + 8]

    total = squares + jnp.sum(gain_grad * gain_grad) + jnp.sum(router_out_grad * router_out_grad)
    grad_norm = jnp.sqrt(total)
    clip_factor = jnp.minimum(1.0, CLIP_NORM / grad_norm)
    new_block, new_block_first, new_block_second = adamw(
        block_master, block_first, block_second, block_grad * clip_factor, 0.02
    )
    new_gains, new_gains_first, new_gains_second = adamw(
        gains, gains_first, gains_second, gain_grad * clip_factor, 0.6
    )
    new_router_in, new_router_in_first, new_router_in_second = adamw(
        router_in, router_in_first, router_in_second, router_in_grad * clip_factor, 0.02
    )
    new_router_out, new_router_out_first, new_router_out_second = adamw(
        router_out, router_out_first, router_out_second, router_out_grad * clip_factor, 0.02
    )
    return (
        result,
        d_inputs,
        counts,
        grad_norm,
        new_block,
        new_block_first,
        new_block_second,
        new_block.astype(BF),
        new_gains,
        new_gains_first,
        new_gains_second,
        new_router_in,
        new_router_in_first,
        new_router_in_second,
        new_router_out,
        new_router_out_first,
        new_router_out_second,
    )


def solution(mesh):
    both = P(("wide", "narrow"), None)
    return jax.shard_map(
        on_device,
        mesh=mesh,
        in_specs=(both, P("wide", None)) + (both,) * 5 + (P(),) * 9,
        out_specs=(both, both, P(), P()) + (both,) * 4 + (P(),) * 9,
        check_vma=False,
    )
```

```python
import functools

import jax
import jax.numpy as jnp
from jax import lax
from jax.experimental import pallas as pl
from jax.experimental.pallas import tpu as pltpu
from jax.sharding import PartitionSpec as P

D = 2048
HEADS = 16
HEAD_DIM = 128
FF = 8192
RH = 256
LEVELS = 4
STEP = 10
TOK = 128
GROUP = 1024
SIDE = 4
WIDE = 16
NARROW = 8
ROWS = 16

NORM_EPS = 1e-05
CLIP_NORM = 1.0
CONTRACT_COLS = (((1,), (1,)), ((), ()))
CONTRACT_ROWS = (((0,), (0,)), ((), ()))
MESH = pl.DeviceIdType.MESH
BF = jnp.bfloat16
F32 = jnp.float32


def here():
    w = lax.axis_index("wide")
    n = lax.axis_index("narrow")
    return lax.div(w, SIDE), lax.rem(w, SIDE), lax.div(n, 2), lax.rem(n, 2)


def wrap(i):
    return lax.rem(i + 2 * SIDE, SIDE)


def moved(dx=0, dz=0, dy=0, dc=0):
    x, z, y, c = here()
    return (wrap(x + dx) * SIDE + wrap(z + dz), wrap(y + dy) * 2 + lax.rem(c + dc, 2))


NEAR_Y = [dict(dy=1), dict(dy=-1), dict(dc=1)]
NARROW_ALL = [dict(dy=a, dc=b) for a in range(SIDE) for b in range(2) if a or b]
NEAR_XZ = [dict(dx=1), dict(dx=-1), dict(dz=1), dict(dz=-1)]
LINES_XZ = [dict(dx=a) for a in (1, 2, 3)] + [dict(dz=a) for a in (1, 2, 3)]
WIDE_ALL = [dict(dx=a, dz=b) for a in range(SIDE) for b in range(SIDE) if a or b]


def greet(partners):
    barrier = pltpu.get_barrier_semaphore()
    for p in partners:
        pl.semaphore_signal(barrier, inc=1, device_id=moved(**p), device_id_type=MESH)
    pl.semaphore_wait(barrier, len(partners))


def span(start, size):
    if not isinstance(start, int):
        start = pl.multiple_of(start, ROWS)
    return pl.ds(start, size)


def lanes(start, size):
    if not isinstance(start, int):
        start = pl.multiple_of(start, 128)
    return pl.ds(start, size)


def step(*parts):
    for part in parts:
        next(part, None)


class Net:
    def __init__(self, send, recv, local):
        self.send, self.recv, self.local = send, recv, local
        self.used, self.used_local = 0, 0
        self.sent, self.kept = [], []

    def put(self, src, dst, target):
        i = self.used
        self.used += 1
        copy = pltpu.make_async_remote_copy(
            src_ref=src,
            dst_ref=dst,
            send_sem=self.send.at[i],
            recv_sem=self.recv.at[i],
            device_id=target,
            device_id_type=MESH,
        )
        copy.start()
        self.sent.append(copy)
        return copy

    def keep(self, src, dst):
        i = self.used_local
        self.used_local += 1
        copy = pltpu.make_async_copy(src, dst, self.local.at[i])
        copy.start()
        return copy

    def finish(self):
        for copy in self.sent:
            copy.wait_send()


def take_turns(*parts):
    live = list(parts)
    while live:
        still = []
        for part in live:
            try:
                next(part)
                still.append(part)
            except StopIteration:
                pass
        live = still


def comm_call(body, ins, outs, scratch, cid, copies, locals_, name, flops=0):
    n_in, n_out, n_scr = len(ins), len(outs), len(scratch)

    def kernel(*refs):
        in_refs = refs[:n_in]
        out_refs = refs[n_in : n_in + n_out]
        scr = refs[n_in + n_out : n_in + n_out + n_scr]
        send, recv, local = refs[n_in + n_out + n_scr :]
        net = Net(send, recv, local)
        body(net, in_refs, out_refs, scr)
        net.finish()
        assert net.used <= copies and net.used_local <= locals_, (net.used, net.used_local)

    return pl.pallas_call(
        kernel,
        out_shape=outs,
        in_specs=[pl.BlockSpec(memory_space=pl.ANY)] * n_in,
        out_specs=[pl.BlockSpec(memory_space=pl.ANY)] * n_out,
        scratch_shapes=list(scratch)
        + [
            pltpu.SemaphoreType.DMA((copies,)),
            pltpu.SemaphoreType.DMA((copies,)),
            pltpu.SemaphoreType.DMA((max(locals_, 1),)),
        ],
        compiler_params=pltpu.CompilerParams(
            collective_id=cid, has_side_effects=True, vmem_limit_bytes=56 * 2**20
        ),
        name=name,
    )(*ins)


def gather_narrow(net, own, out):
    x, z, y, c = here()
    rows = own.shape[0]
    half = rows // 2

    def block(dy, lo=0, size=rows):
        return out.at[span((wrap(y + dy) * 2 + c) * rows + lo, size)]

    up = net.put(own, block(0), moved(dy=1))
    down = net.put(own, block(0), moved(dy=-1))
    across = [net.put(own, block(0), moved(dc=1))]
    mine = net.keep(own, block(0))
    yield None
    mine.wait()
    across[0].wait_recv()
    yield 0
    up.wait_recv()
    on = net.put(block(-1, 0, half), block(-1, 0, half), moved(dy=1))
    across.append(net.put(block(-1), block(-1), moved(dc=1)))
    yield None
    down.wait_recv()
    back = net.put(block(1, half, half), block(1, half, half), moved(dy=-1))
    across.append(net.put(block(1), block(1), moved(dc=1)))
    across[1].wait_recv()
    yield 3
    across[2].wait_recv()
    yield 1
    on.wait_recv()
    across.append(net.put(block(2, 0, half), block(2, 0, half), moved(dc=1)))
    back.wait_recv()
    across.append(net.put(block(2, half, half), block(2, half, half), moved(dc=1)))
    across[3].wait_recv()
    across[4].wait_recv()
    yield 2


GATHER_COPIES = 10


def gather_call(own, cid, name):
    rows, cols = own.shape

    def body(net, ins, outs, scr):
        greet(NEAR_Y)
        take_turns(gather_narrow(net, ins[0], outs[0]))

    return comm_call(
        body,
        [own],
        [jax.ShapeDtypeStruct((NARROW * rows, cols), own.dtype)],
        [],
        cid,
        GATHER_COPIES,
        1,
        name,
    )[0]


def reduce_scratch(rows, cols):
    return [
        pltpu.VMEM((SIDE, rows, cols), BF),
        pltpu.VMEM((SIDE, rows, cols), BF),
        pltpu.VMEM((2, rows // 2, cols), BF),
        pltpu.VMEM((2, rows, cols), BF),
        pltpu.VMEM((3, rows, cols), BF),
        pltpu.VMEM((rows, cols), F32),
    ]


REDUCE_COPIES = 10
REDUCE_LOCALS = 5


def reduce_narrow(net, part, out, scr):
    own, other, through, landed, ready, total = scr
    x, z, y, c = here()
    rows, cols = out.shape
    half = rows // 2

    def block(dy, core):
        return part.at[span((wrap(y + dy) * 2 + core) * rows, rows)]

    order = (2, 1, 3, 0)
    local, cross = {}, {}
    for dy in order:
        cross[dy] = net.put(block(dy, 1 - c), other.at[dy], moved(dc=1))
        local[dy] = net.keep(block(dy, c), own.at[dy])

    def pair(dy, lo, size):
        s = span(lo, size)
        return own[dy, s, :].astype(F32) + other[dy, s, :].astype(F32)

    yield
    local[2].wait()
    cross[2].wait_recv()
    ready[0] = pair(2, 0, rows).astype(BF)
    first, last = span(0, half), span(half, half)
    via_up = net.put(ready.at[0, first], through.at[0], moved(dy=1))
    via_down = net.put(ready.at[0, last], through.at[1], moved(dy=-1))
    yield
    local[1].wait()
    cross[1].wait_recv()
    ready[1, last, :] = pair(1, half, half).astype(BF)
    up_late = net.put(ready.at[1, last], landed.at[0, last], moved(dy=1))
    local[3].wait()
    cross[3].wait_recv()
    ready[2, first, :] = pair(3, 0, half).astype(BF)
    down_first = net.put(ready.at[2, first], landed.at[1, first], moved(dy=-1))
    yield
    via_up.wait_recv()
    ready[1, first, :] = (pair(1, 0, half) + through[0].astype(F32)).astype(BF)
    up_first = net.put(ready.at[1, first], landed.at[0, first], moved(dy=1))
    via_down.wait_recv()
    ready[2, last, :] = (pair(3, half, half) + through[1].astype(F32)).astype(BF)
    down_late = net.put(ready.at[2, last], landed.at[1, last], moved(dy=-1))
    yield
    local[0].wait()
    cross[0].wait_recv()
    total[...] = pair(0, 0, rows)
    yield
    for copy in (up_late, down_first, up_first, down_late):
        copy.wait_recv()
    total[...] += landed[0].astype(F32) + landed[1].astype(F32)
    done = net.keep(total, out)
    yield
    done.wait()


def pairs_scratch(rows, cols):
    return [
        pltpu.VMEM((SIDE, 2 * rows, cols), BF),
        pltpu.VMEM((SIDE, rows, cols), BF),
        pltpu.VMEM((2, rows // 2, cols), BF),
        pltpu.VMEM((2, rows, cols), BF),
        pltpu.VMEM((3, rows, cols), BF),
        pltpu.VMEM((rows, cols), F32),
    ]


PAIR_ORDER = (2, 1, 3, 0)


def reduce_pairs(net, out, scr):
    parts, other, through, landed, ready, total = scr
    x, z, y, c = here()
    rows = total.shape[0]
    half = rows // 2
    first, last = pl.ds(0, half), pl.ds(half, half)

    def cross(dy):
        return net.put(parts.at[dy, span((1 - c) * rows, rows)], other.at[dy], moved(dc=1))

    def pair(dy, lo, size):
        mine = parts[dy, span(c * rows + lo, size), :].astype(F32)
        return mine + other[dy, pl.ds(lo, size), :].astype(F32)

    cross_two = cross(2)
    yield
    cross_one = cross(1)
    cross_two.wait_recv()
    ready[0] = pair(2, 0, rows).astype(BF)
    via_up = net.put(ready.at[0, first], through.at[0], moved(dy=1))
    via_down = net.put(ready.at[0, last], through.at[1], moved(dy=-1))
    yield
    cross_three = cross(3)
    cross_one.wait_recv()
    ready[1, last, :] = pair(1, half, half).astype(BF)
    up_late = net.put(ready.at[1, last], landed.at[0, last], moved(dy=1))
    yield
    cross_own = cross(0)
    cross_three.wait_recv()
    ready[2, first, :] = pair(3, 0, half).astype(BF)
    down_first = net.put(ready.at[2, first], landed.at[1, first], moved(dy=-1))
    yield
    via_up.wait_recv()
    ready[1, first, :] = (pair(1, 0, half) + through[0].astype(F32)).astype(BF)
    up_first = net.put(ready.at[1, first], landed.at[0, first], moved(dy=1))
    via_down.wait_recv()
    ready[2, last, :] = (pair(3, half, half) + through[1].astype(F32)).astype(BF)
    down_late = net.put(ready.at[2, last], landed.at[1, last], moved(dy=-1))
    yield
    cross_own.wait_recv()
    total[...] = pair(0, 0, rows)
    yield
    for copy in (up_late, down_first, up_first, down_late):
        copy.wait_recv()
    total[...] += landed[0].astype(F32) + landed[1].astype(F32)
    done = net.keep(total, out)
    yield
    done.wait()


def reduce_call(parts, cid, name):
    n = len(parts)
    shapes = [(p.shape[0] // NARROW, p.shape[1]) for p in parts]
    scratch = [s for shape in shapes for s in reduce_scratch(*shape)]

    def body(net, ins, outs, scr):
        greet(NEAR_Y)
        take_turns(
            *[reduce_narrow(net, ins[i], outs[i], scr[6 * i : 6 * i + 6]) for i in range(n)]
        )

    return comm_call(
        body,
        list(parts),
        [jax.ShapeDtypeStruct(s, F32) for s in shapes],
        scratch,
        cid,
        REDUCE_COPIES * n,
        REDUCE_LOCALS * n,
        name,
    )


def spread_narrow(net, src, slab):
    w = lax.axis_index("wide")
    n = lax.axis_index("narrow")
    base = n * ROWS if slab.shape[0] == TOK else w * TOK + n * ROWS
    mine = net.keep(src.at[n], slab.at[span(base, ROWS)])
    copies = []
    for p in NARROW_ALL:
        target = moved(**p)
        copies.append(net.put(src.at[target[1]], slab.at[span(base, ROWS)], target))
    yield
    mine.wait()
    for copy in copies:
        copy.wait_recv()


SPREAD_COPIES = 7


def gather_wide(net, slab, lead, stage=None):
    x, z, y, c = here()
    rows = TOK // 2
    half = rows // 2
    low = 0 if lead == "x" else rows

    def block(a, b, lo=0, size=rows):
        px, pz = (a, b) if lead == "x" else (b, a)
        return slab.at[span((wrap(x + px) * SIDE + wrap(z + pz)) * TOK + low + lo, size)]

    def lead_to(d):
        return moved(dx=d) if lead == "x" else moved(dz=d)

    def then_to(d):
        return moved(dz=d) if lead == "x" else moved(dx=d)

    def both(src, to, dst=None):
        dst = src if dst is None else dst
        return net.put(src, dst, to(1)), net.put(src, dst, to(-1))

    mine = block(0, 0) if stage is None else stage.at[pl.ds(low, rows)]
    fore, aft = both(mine, lead_to, block(0, 0))
    second = {0: both(mine, then_to, block(0, 0))}
    yield
    fore.wait_recv()
    on = net.put(block(-1, 0, 0, half), block(-1, 0, 0, half), lead_to(1))
    second[-1] = both(block(-1, 0), then_to)
    aft.wait_recv()
    back = net.put(block(1, 0, half, half), block(1, 0, half, half), lead_to(-1))
    second[1] = both(block(1, 0), then_to)
    yield
    last = []

    def relay(a):
        f, b = second[a]
        f.wait_recv()
        last.append(net.put(block(a, -1, 0, half), block(a, -1, 0, half), then_to(1)))
        b.wait_recv()
        last.append(net.put(block(a, 1, half, half), block(a, 1, half, half), then_to(-1)))

    kept = None if stage is None else net.keep(mine, block(0, 0))
    relay(0)
    yield
    on.wait_recv()
    back.wait_recv()
    second[2] = both(block(2, 0), then_to)
    yield
    relay(-1)
    relay(1)
    yield
    relay(2)
    yield
    if kept is not None:
        kept.wait()
    for copy in last:
        copy.wait_recv()


WIDE_COPIES = 20


def chain(*parts):
    for part in parts:
        yield from part


def first_gather(owns, sources, cid):
    k, m = len(owns), len(sources)

    def body(net, ins, outs, scr):
        greet(NARROW_ALL + NEAR_XZ)

        def weights(i):
            yield from spread_narrow(net, ins[k + i], outs[k + i])
            if i:
                return
            a = gather_wide(net, outs[k + i], "x")
            b = gather_wide(net, outs[k + i], "z")
            live = [a, b]
            while live:
                for g in list(live):
                    try:
                        next(g)
                    except StopIteration:
                        live.remove(g)
                yield

        take_turns(
            weights(0),
            gather_narrow(net, ins[0], outs[0]),
            *[weights(i) for i in range(1, m)],
            *[gather_narrow(net, ins[i], outs[i]) for i in range(1, k)],
        )

    shapes = [jax.ShapeDtypeStruct((NARROW * o.shape[0], o.shape[1]), o.dtype) for o in owns] + [
        jax.ShapeDtypeStruct((TOK if i else D, s.shape[2]), s.dtype)
        for i, s in enumerate(sources)
    ]
    return comm_call(
        body,
        list(owns) + list(sources),
        shapes,
        [],
        cid,
        k * GATHER_COPIES + m * (SPREAD_COPIES + 2 * WIDE_COPIES),
        k + m,
        "first_gather",
    )


def turn(values, cosine, sine):
    return values * cosine + pltpu.roll(values, HEAD_DIM // 2, 1) * sine


def allowed_keys(first_row, rows, first_length):
    query = first_row + lax.broadcasted_iota(jnp.int32, (rows, 1), 0)
    key = lax.broadcasted_iota(jnp.int32, (rows, GROUP), 1)
    start = jnp.where(query >= first_length, first_length, 0)
    return (key <= query) & (key >= start)


def branch_mask(marks, lane):
    n = lax.axis_index("narrow").astype(F32)
    return (n < 2.0 * (marks[:, lane : lane + 1].astype(F32) + 1.0)).astype(F32)


def attention_forward(normed, slab, turns, first_length, marks, d_ffn_own, stage, cid):
    pair_rows = 2 * TOK
    head_part = D // NARROW

    def body(net, ins, outs, scr):
        normed, slab, turns, first_length, marks, d_ffn_own, stage = ins
        attn_sum, q_out, k_out, v_out, p_out, a_out, d_ffn, slab_b = outs
        xv, wv, tv, lv, mv, qv, kv, vv, pv, av = scr[:10]
        x, z, y, c = here()
        loads = [net.keep(a, b) for a, b in zip(ins[:5], scr[:5])]
        greet(NEAR_Y + NEAR_XZ)
        moves = [
            gather_wide(net, slab_b, "x", stage),
            gather_wide(net, slab_b, "z", stage),
            gather_narrow(net, d_ffn_own, d_ffn),
        ]
        step(*moves)
        for load in loads:
            load.wait()

        @pl.loop(0, SIDE)
        def _(i):
            r = span(i * pair_rows, pair_rows)
            proj = jnp.dot(xv[r, :], wv[:, : 3 * head_part], preferred_element_type=F32)
            cosine, sine = tv[0, r, :], tv[1, r, :]
            for h in range(2):
                at = pl.ds(h * HEAD_DIM, HEAD_DIM)
                a = h * HEAD_DIM
                qv[r, at] = turn(proj[:, a : a + HEAD_DIM], cosine, sine).astype(BF)
                a += head_part
                kv[r, at] = turn(proj[:, a : a + HEAD_DIM], cosine, sine).astype(BF)
            vv[r, :] = proj[:, 2 * head_part :].astype(BF)

        stores = [net.keep(qv, q_out), net.keep(kv, k_out), net.keep(vv, v_out)]
        total = reduce_pairs(net, attn_sum, scr[10:])
        length = lv[0:1, 0:1]
        for dy in PAIR_ORDER:
            first = wrap(y + dy) * pair_rows
            r = span(first, pair_rows)
            allowed = allowed_keys(first, pair_rows, length)
            heads = []
            for h in range(2):
                at = pl.ds(h * HEAD_DIM, HEAD_DIM)
                scores = lax.dot_general(
                    qv[r, at], kv[:, at], CONTRACT_COLS, preferred_element_type=F32
                )
                scores = jnp.where(allowed, scores * HEAD_DIM ** (-0.5), -1e30)
                expo = jnp.exp(scores - jnp.max(scores, axis=-1, keepdims=True))
                probs = expo * (1.0 / jnp.sum(expo, axis=-1, keepdims=True))
                pv[h, r, :] = probs.astype(BF)
                heads.append(jnp.dot(pv[h, r, :], vv[:, at], preferred_element_type=F32))
            mask = branch_mask(mv[r, :], 0)
            av[r, :] = (jnp.concatenate(heads, axis=1) * mask).astype(BF)
            scr[10][dy] = lax.dot_general(
                av[r, :], wv[:, 3 * head_part :], CONTRACT_COLS, preferred_element_type=F32
            ).astype(BF)
            step(total, *moves)
        stores += [net.keep(pv, p_out), net.keep(av, a_out)]
        take_turns(total, *moves)
        for store in stores:
            store.wait()

    low = jax.ShapeDtypeStruct((GROUP, head_part), BF)
    return comm_call(
        body,
        [normed, slab, turns, first_length, marks, d_ffn_own, stage],
        [
            jax.ShapeDtypeStruct((TOK, D), F32),
            low,
            low,
            low,
            jax.ShapeDtypeStruct((2, GROUP, GROUP), BF),
            low,
            jax.ShapeDtypeStruct((GROUP, D), BF),
            jax.ShapeDtypeStruct((D, stage.shape[1]), BF),
        ],
        [
            pltpu.VMEM((GROUP, D), BF),
            pltpu.VMEM(slab.shape, BF),
            pltpu.VMEM(turns.shape, F32),
            pltpu.VMEM(first_length.shape, jnp.int32),
            pltpu.VMEM(marks.shape, BF),
            pltpu.VMEM((GROUP, head_part), BF),
            pltpu.VMEM((GROUP, head_part), BF),
            pltpu.VMEM((GROUP, head_part), BF),
            pltpu.VMEM((2, GROUP, GROUP), BF),
            pltpu.VMEM((GROUP, head_part), BF),
        ]
        + pairs_scratch(TOK, D),
        cid,
        REDUCE_COPIES + 2 * WIDE_COPIES + GATHER_COPIES,
        5 + 5 + 4,
        "attention_forward",
    )


def feed_forward(normed_own, d_ffn, slab, marks, cid):
    pair_rows = 2 * TOK
    units = FF // NARROW
    strip = 256

    def body(net, ins, outs, scr):
        own, d_ffn, slab, marks = ins
        norm_sum, ffn_part, g_up, g_down = outs
        xv, dv, w_up, w_down, mv, act, du, da, gu, gd, yv = scr[:11]
        x, z, y, c = here()
        loads = [
            net.keep(d_ffn, dv),
            net.keep(slab.at[:, pl.ds(units, units)], w_down),
            net.keep(slab.at[:, pl.ds(0, units)], w_up),
            net.keep(marks, mv),
        ]
        greet(NEAR_Y)
        gather = gather_narrow(net, own, xv)
        next(gather)
        loads[0].wait()
        loads[1].wait()

        @pl.loop(0, SIDE)
        def _(i):
            r = span(i * pair_rows, pair_rows)
            da[r, :] = jnp.dot(dv[r, :], w_down[...], preferred_element_type=F32)

        loads[2].wait()
        loads[3].wait()
        for dy in gather:
            if dy is not None:
                r = span(wrap(y + dy) * pair_rows, pair_rows)
                up = jnp.dot(xv[r, :], w_up[...], preferred_element_type=F32)
                positive = jnp.maximum(up, 0.0)
                masked = positive * branch_mask(mv[r, :], 64)
                act[r, :] = (positive * masked).astype(BF)
                du[r, :] = (da[r, :] * (2.0 * masked)).astype(BF)

        total = reduce_pairs(net, norm_sum, scr[11:])
        for dy in PAIR_ORDER:
            r = span(wrap(y + dy) * pair_rows, pair_rows)
            scr[11][dy] = lax.dot_general(
                du[r, :], w_up[...], CONTRACT_COLS, preferred_element_type=F32
            ).astype(BF)
            next(total)

        def gradient(left, right, to, start, stop):
            @pl.loop(start, stop)
            def _(i):
                at = lanes(i * strip, strip)
                to[span(i * strip, strip), :] = lax.dot_general(
                    left[:, at], right[...], CONTRACT_ROWS, preferred_element_type=F32
                ).astype(BF)

        gradient(dv, act, gd, 0, 4)
        next(total)
        gradient(dv, act, gd, 4, 8)
        stores = [net.keep(gd, g_down)]
        step(total)
        gradient(xv, du, gu, 0, 8)
        stores.append(net.keep(gu, g_up))
        step(total)

        @pl.loop(0, SIDE)
        def _(i):
            r = span(i * pair_rows, pair_rows)
            yv[r, :] = lax.dot_general(
                act[r, :], w_down[...], CONTRACT_COLS, preferred_element_type=F32
            ).astype(BF)

        stores.append(net.keep(yv, ffn_part))
        take_turns(total)
        for store in stores:
            store.wait()

    wide = pltpu.VMEM((GROUP, D), BF)
    tall = pltpu.VMEM((D, units), BF)
    square = pltpu.VMEM((GROUP, units), BF)
    return comm_call(
        body,
        [normed_own, d_ffn, slab, marks],
        [
            jax.ShapeDtypeStruct((TOK, D), F32),
            jax.ShapeDtypeStruct((GROUP, D), BF),
            jax.ShapeDtypeStruct((D, units), BF),
            jax.ShapeDtypeStruct((D, units), BF),
        ],
        [wide, wide, tall, tall, pltpu.VMEM(marks.shape, BF), square, square]
        + [pltpu.VMEM((GROUP, units), F32), tall, tall, wide]
        + pairs_scratch(TOK, D),
        cid,
        GATHER_COPIES + REDUCE_COPIES,
        4 + 1 + 1 + 3,
        "feed_forward",
    )


def gather_and_reduce(own, part, cid):
    def body(net, ins, outs, scr):
        greet(NEAR_Y)
        take_turns(gather_narrow(net, ins[0], outs[0]), reduce_narrow(net, ins[1], outs[1], scr))

    return comm_call(
        body,
        [own, part],
        [jax.ShapeDtypeStruct((GROUP, D), BF), jax.ShapeDtypeStruct((TOK, D), F32)],
        reduce_scratch(TOK, D),
        cid,
        GATHER_COPIES + REDUCE_COPIES,
        1 + REDUCE_LOCALS,
        "gather_and_reduce",
    )


def grad_scratch(cols):
    part = TOK // 2
    return [
        pltpu.VMEM((2, SIDE, part, cols), BF),
        pltpu.VMEM((2, 3, SIDE, part, cols), BF),
        pltpu.VMEM((2, SIDE, part, cols), BF),
        pltpu.VMEM((2, 3, part, cols), BF),
        pltpu.VMEM((TOK, cols), BF),
    ]


GRAD_COPIES = 2 * 6 + 7
GRAD_LOCALS = 3


def reduce_wide(net, grad, out, scr, lead):
    own, landed, sums, late, total = scr
    x, z, y, c = here()
    part = TOK // 2
    half = 0 if lead == "x" else 1
    low = half * part
    blocks = grad.reshape(SIDE, SIDE, TOK, grad.shape[1])

    def line(d):
        if lead == "x":
            return blocks.at[wrap(x + d), :, span(low, part), :]
        return blocks.at[:, wrap(z + d), span(low, part), :]

    def lead_to(d):
        return moved(dx=d) if lead == "x" else moved(dz=d)

    def then_to(d):
        return moved(dz=d) if lead == "x" else moved(dx=d)

    mine = net.keep(line(0), own.at[half])
    copies = [net.put(line(d), landed.at[half, d - 1], lead_to(d)) for d in (2, 1, 3)]
    yield
    mine.wait()
    for copy in copies:
        copy.wait_recv()

    @pl.loop(0, SIDE)
    def _(i):
        s = own[half, i].astype(F32)
        for d in range(3):
            s = s + landed[half, d, i].astype(F32)
        sums[half, i] = s.astype(BF)

    me = z if lead == "x" else x
    copies = [net.put(sums.at[half, wrap(me + d)], late.at[half, d - 1], then_to(d)) for d in (2, 1, 3)]
    yield
    for copy in copies:
        copy.wait_recv()
    s = sums[half, me].astype(F32)
    for d in range(3):
        s = s + late[half, d].astype(F32)
    total[span(low, part), :] = s.astype(BF)


def return_narrow(net, total, out):
    n = lax.axis_index("narrow")

    def rows(i):
        return total.at[span(i * ROWS, ROWS)]

    mine = net.keep(rows(n), out.at[n])
    copies = []
    for p in NARROW_ALL:
        target = moved(**p)
        copies.append(net.put(rows(target[1]), out.at[n], target))
    yield
    mine.wait()
    for copy in copies:
        copy.wait_recv()


def reduce_grads(grads, small, cid):
    m = len(grads)
    scratch = [s for g in grads for s in grad_scratch(g.shape[1])]
    scratch += [pltpu.VMEM((WIDE, ROWS, RH), BF), pltpu.VMEM((ROWS, RH), F32)]

    def body(net, ins, outs, scr):
        greet(NARROW_ALL + WIDE_ALL)
        w = lax.axis_index("wide")

        def one(i):
            s = scr[5 * i : 5 * i + 5]
            a = reduce_wide(net, ins[i], outs[i], s, "x")
            b = reduce_wide(net, ins[i], outs[i], s, "z")
            live = [a, b]
            while live:
                for g in list(live):
                    try:
                        next(g)
                    except StopIteration:
                        live.remove(g)
                if live:
                    yield
            yield from return_narrow(net, s[4], outs[i])

        def little():
            landed, total = scr[5 * m :]

            def rows(i):
                return ins[m].at[span(i * ROWS, ROWS)]

            mine = net.keep(rows(w), landed.at[w])
            copies = []
            for p in WIDE_ALL:
                target = moved(**p)
                copies.append(net.put(rows(target[0]), landed.at[w], target))
            yield
            yield
            mine.wait()
            for copy in copies:
                copy.wait_recv()
            s = landed[0].astype(F32)
            for i in range(1, WIDE):
                s = s + landed[i].astype(F32)
            total[...] = s
            done = net.keep(total, outs[m])
            yield
            done.wait()

        take_turns(*[one(i) for i in range(m)], little())

    shapes = [jax.ShapeDtypeStruct((NARROW, ROWS, g.shape[1]), BF) for g in grads]
    shapes.append(jax.ShapeDtypeStruct((ROWS, RH), F32))
    return comm_call(
        body,
        list(grads) + [small],
        shapes,
        scratch,
        cid,
        m * GRAD_COPIES + 15,
        m * GRAD_LOCALS + 2,
        "reduce_grads",
    )


def last_sums(vector, shard, cid):
    rows = vector.shape[0]

    def body(net, ins, outs, scr):
        vec, own = ins
        vec_out, full = outs
        first, mid, second, total = scr
        w = lax.axis_index("wide")
        n = lax.axis_index("narrow")
        greet(NARROW_ALL + WIDE_ALL)

        def sums():
            mine = net.keep(vec, first.at[n])
            copies = [net.put(vec, first.at[n], moved(**p)) for p in NARROW_ALL]
            yield
            mine.wait()
            for copy in copies:
                copy.wait_recv()
            s = first[0]
            for i in range(1, NARROW):
                s = s + first[i]
            mid[...] = s
            mine = net.keep(mid, second.at[w])
            copies = [net.put(mid, second.at[w], moved(**p)) for p in WIDE_ALL]
            yield
            mine.wait()
            for copy in copies:
                copy.wait_recv()
            s = second[0]
            for i in range(1, WIDE):
                s = s + second[i]
            total[...] = s
            done = net.keep(total, vec_out)
            yield
            done.wait()

        def table():
            spot = full.at[span(n * GROUP // 4 + w * ROWS, ROWS)]
            mine = net.keep(own, spot)
            copies = [net.put(own, spot, moved(**p)) for p in WIDE_ALL]
            yield
            mine.wait()
            for copy in copies:
                copy.wait_recv()
            x, z, y, c = here()

            def block(dy):
                return full.at[span((wrap(y + dy) * 2 + c) * RH, RH)]

            along = [net.put(block(0), block(0), moved(dy=d)) for d in (1, 3, 2)]
            across = [net.put(block(0), block(0), moved(dc=1))]
            yield
            for copy, d in zip(along, (1, 3, 2)):
                copy.wait_recv()
                across.append(net.put(block(-d), block(-d), moved(dc=1)))
            yield
            for copy in across:
                copy.wait_recv()

        take_turns(sums(), table())

    return comm_call(
        body,
        [vector, shard],
        [jax.ShapeDtypeStruct((rows, 128), F32), jax.ShapeDtypeStruct((D, RH), F32)],
        [
            pltpu.VMEM((NARROW, rows, 128), F32),
            pltpu.VMEM((rows, 128), F32),
            pltpu.VMEM((WIDE, rows, 128), F32),
            pltpu.VMEM((rows, 128), F32),
        ],
        cid,
        7 + 15 + 15 + 7,
        4,
        "last_sums",
    )


def layer_norm(values, gain_row):
    average = jnp.mean(values, axis=-1, keepdims=True)
    centered = values - average
    spread = jnp.mean(centered * centered, axis=-1, keepdims=True)
    return centered * lax.rsqrt(spread + NORM_EPS) * gain_row


def rotate(values, position):
    halfway = values.shape[-1] // 2
    frequency = 10000.0 ** (-jnp.arange(halfway, dtype=jnp.float32) / halfway)
    angles = position.astype(jnp.float32)[:, None] * frequency[None, :]
    cosine = jnp.cos(angles)[:, None, :]
    sine_part = jnp.sin(angles)[:, None, :]
    first_part = values[..., :halfway]
    second_part = values[..., halfway:]
    return jnp.concatenate(
        [
            first_part * cosine - second_part * sine_part,
            first_part * sine_part + second_part * cosine,
        ],
        axis=-1,
    )


def segment_info(seg_lengths, token_index):
    seg_ends = jnp.cumsum(seg_lengths)
    segment = jnp.sum((token_index[:, None] >= seg_ends[None, :]).astype(jnp.int32), axis=1)
    starts = seg_ends - seg_lengths
    owners = segment[:, None] == jnp.arange(seg_lengths.shape[0], dtype=jnp.int32)[None, :]
    start_of = jnp.sum(jnp.where(owners, starts[None, :], 0), axis=1)
    return (segment, token_index - start_of)


def router_gates(normed, first_layer, second_layer, picks):
    hidden = jax.nn.gelu(jnp.dot(normed, first_layer))
    logits = jnp.dot(hidden, second_layer)
    levels = jnp.arange(LEVELS, dtype=jnp.int32)
    chosen_attn = (picks[:, 0:1] == levels[None, :]).astype(jnp.float32)
    chosen_ffn = (picks[:, 1:2] == levels[None, :]).astype(jnp.float32)
    gate_attn = float(LEVELS) * jnp.sum(
        jax.nn.softmax(logits[:, :LEVELS], axis=-1) * chosen_attn, axis=-1
    )
    gate_ffn = float(LEVELS) * jnp.sum(
        jax.nn.softmax(logits[:, LEVELS:], axis=-1) * chosen_ffn, axis=-1
    )
    return (gate_attn, gate_ffn)


def adamw(weight, moment_one, moment_two, gradient, step_rate):
    moment_one = 0.9 * moment_one + 0.1 * gradient
    moment_two = 0.95 * moment_two + 0.05 * gradient * gradient
    first_hat = moment_one / (1.0 - 0.9**STEP)
    second_hat = moment_two / (1.0 - 0.95**STEP)
    updated = weight - step_rate * (first_hat / (jnp.sqrt(second_hat) + 1e-08) + 0.1 * weight)
    return (updated, moment_one, moment_two)


def cut(rows, start, width, pieces):
    part = rows[:, start : start + width].reshape(rows.shape[0], pieces, width // pieces)
    return part.transpose(1, 0, 2)


def joined(part):
    return part.transpose(1, 0, 2).reshape(ROWS, -1)


def on_device(
    tokens,
    lengths,
    picks,
    cotangent,
    block_master,
    block_first,
    block_second,
    gains,
    gains_first,
    gains_second,
    router_in,
    router_in_first,
    router_in_second,
    router_out,
    router_out_first,
    router_out_second,
):
    score_scale = HEAD_DIM ** (-0.5)
    rank_number = lax.axis_index("narrow")
    own_heads = HEADS // NARROW
    head_part = D // NARROW

    low = block_master.astype(BF)
    source_a = jnp.concatenate([cut(low, i * D, D, NARROW) for i in range(4)], axis=2)
    source_b = jnp.concatenate([cut(low, 4 * D + i * FF, FF, NARROW) for i in range(2)], axis=2)
    inputs = tokens.astype(F32)
    norm_one, norm_one_back = jax.vjp(layer_norm, inputs, gains[0])
    normed_own = norm_one.astype(BF)
    (gate_attn, gate_ffn), router_back = jax.vjp(
        lambda normed, first_layer, second_layer: router_gates(
            normed, first_layer, second_layer, picks
        ),
        normed_own.astype(F32),
        router_in,
        router_out,
    )
    upstream = cotangent.astype(F32)
    d_ffn_own = (upstream * gate_ffn[:, None]).astype(BF)
    marks = jnp.where(jnp.arange(128)[None, :] < 64, picks[:, 0:1], picks[:, 1:2]).astype(BF)

    normed_low, group_marks, slab_a, stage_b = first_gather(
        [normed_own, marks], [source_a, source_b], 0
    )
    w_qkv, w_out = slab_a[:, : 3 * head_part], slab_a[:, 3 * head_part :]
    picks_attn = group_marks[:, 0:1].astype(jnp.int32)

    key_index = jnp.arange(GROUP, dtype=jnp.int32)
    _, key_position = segment_info(lengths[0], key_index)
    half_dim = HEAD_DIM // 2
    frequency = 10000.0 ** (-jnp.arange(half_dim, dtype=F32) / half_dim)
    angles = key_position.astype(F32)[:, None] * frequency[None, :]
    cosine, sine = jnp.cos(angles), jnp.sin(angles)
    turns = jnp.stack(
        [
            jnp.concatenate([cosine, cosine], axis=1),
            jnp.concatenate([-sine, sine], axis=1),
        ]
    )
    first_length = jnp.broadcast_to(lengths[:, 0:1], (8, 128))
    attn_out, query_flat, key_flat, value_flat, probs_low, mixed_low, d_ffn_low, slab_b = (
        attention_forward(
            normed_low, slab_a, turns, first_length, group_marks, d_ffn_own, stage_b, 1
        )
    )
    query_low = query_flat.reshape(GROUP, own_heads, HEAD_DIM)
    key_low = key_flat.reshape(GROUP, own_heads, HEAD_DIM)
    value_low = value_flat.reshape(GROUP, own_heads, HEAD_DIM)
    probs = probs_low.astype(F32)
    head_number = rank_number * own_heads + jnp.arange(own_heads, dtype=jnp.int32)
    head_mask = (head_number[None, :] < HEADS * (picks_attn + 1) // LEVELS).astype(F32)

    after_attn = inputs + gate_attn[:, None] * attn_out
    norm_two, norm_two_back = jax.vjp(layer_norm, after_attn, gains[1])

    d_norm_two, ffn_part, grad_up, grad_down = feed_forward(
        norm_two.astype(BF), d_ffn_low, slab_b, group_marks, 2
    )
    d_after, d_gain_two = norm_two_back(d_norm_two)
    d_after = d_after + upstream
    d_gate_attn = jnp.sum(d_after * attn_out, axis=1)
    d_attn_low, ffn_out = gather_and_reduce(
        (d_after * gate_attn[:, None]).astype(BF), ffn_part, 3
    )

    result = (after_attn + gate_ffn[:, None] * ffn_out).astype(BF)
    d_gate_ffn = jnp.sum(upstream * ffn_out, axis=1)
    _, rotate_back = jax.vjp(
        lambda values: rotate(values, key_position), jnp.zeros((GROUP, own_heads, HEAD_DIM), F32)
    )

    grad_out = lax.dot_general(
        d_attn_low, mixed_low, CONTRACT_ROWS, preferred_element_type=F32
    ).astype(BF)
    d_mixed = jnp.dot(d_attn_low, w_out, preferred_element_type=F32)
    d_attended = (d_mixed.reshape(GROUP, own_heads, HEAD_DIM) * head_mask[:, :, None]).astype(BF)
    d_probs = jnp.einsum("qhd,khd->hqk", d_attended, value_low, preferred_element_type=F32)
    centre = jnp.sum(probs * d_probs, axis=-1, keepdims=True)
    d_scores = (probs * (d_probs - centre)).astype(BF)
    d_query = (
        jnp.einsum("hqk,khd->qhd", d_scores, key_low, preferred_element_type=F32) * score_scale
    )
    d_key = (
        jnp.einsum("hqk,qhd->khd", d_scores, query_low, preferred_element_type=F32) * score_scale
    )
    d_value = jnp.einsum("hqk,qhd->khd", probs_low, d_attended, preferred_element_type=F32)
    d_query_raw = rotate_back(d_query)[0].reshape(GROUP, head_part)
    d_key_raw = rotate_back(d_key)[0].reshape(GROUP, head_part)
    d_proj_low = jnp.concatenate(
        [d_query_raw, d_key_raw, d_value.reshape(GROUP, head_part)], axis=1
    ).astype(BF)
    grad_qkv = lax.dot_general(
        normed_low, d_proj_low, CONTRACT_ROWS, preferred_element_type=F32
    ).astype(BF)
    d_normed_part = lax.dot_general(d_proj_low, w_qkv, CONTRACT_COLS, preferred_element_type=F32)
    d_normed_router, grad_router_in, grad_router_out = router_back((d_gate_attn, d_gate_ffn))
    d_normed, router_in_part = reduce_call(
        [d_normed_part.astype(BF), grad_router_in.astype(BF)], 5, "sum_dnormed"
    )
    d_inputs, d_gain_one = norm_one_back(d_normed + d_normed_router)
    d_inputs = d_inputs + d_after

    sum_qkv, sum_out, sum_up, sum_down, router_in_shard = reduce_grads(
        [grad_qkv, grad_out, grad_up, grad_down], router_in_part.astype(BF), 6
    )
    block_grad = jnp.concatenate(
        [joined(sum_qkv[:, :, i * head_part : (i + 1) * head_part]) for i in range(3)]
        + [joined(sum_out), joined(sum_up), joined(sum_down)],
        axis=1,
    ).astype(F32)

    levels = jnp.arange(LEVELS, dtype=jnp.int32)
    counts_local = jnp.concatenate(
        [
            jnp.sum((picks[:, 0:1] == levels[None, :]).astype(F32), axis=0),
            jnp.sum((picks[:, 1:2] == levels[None, :]).astype(F32), axis=0),
        ]
    )
    local_squares = jnp.sum(block_grad * block_grad) + jnp.sum(router_in_shard * router_in_shard)
    pieces = [
        d_gain_one,
        d_gain_two,
        grad_router_out.ravel(),
        counts_local,
        local_squares[None],
    ]
    size = sum(p.shape[0] for p in pieces)
    padded = -(-size // 1024) * 1024
    vector = jnp.concatenate(pieces + [jnp.zeros((padded - size,), F32)]).reshape(-1, 128)
    vector, router_in_grad = last_sums(vector, router_in_shard, 7)
    flat = vector.ravel()
    gain_grad = flat[: 2 * D].reshape(2, D)
    router_out_grad = flat[2 * D : 2 * D + RH * 8].reshape(RH, 8)
    at = 2 * D + RH * 8
    counts = flat[at : at + 8].reshape(2, LEVELS)
    squares = flat[at + 8]

    total = squares + jnp.sum(gain_grad * gain_grad) + jnp.sum(router_out_grad * router_out_grad)
    grad_norm = jnp.sqrt(total)
    clip_factor = jnp.minimum(1.0, CLIP_NORM / grad_norm)
    new_block, new_block_first, new_block_second = adamw(
        block_master, block_first, block_second, block_grad * clip_factor, 0.02
    )
    new_gains, new_gains_first, new_gains_second = adamw(
        gains, gains_first, gains_second, gain_grad * clip_factor, 0.6
    )
    new_router_in, new_router_in_first, new_router_in_second = adamw(
        router_in, router_in_first, router_in_second, router_in_grad * clip_factor, 0.02
    )
    new_router_out, new_router_out_first, new_router_out_second = adamw(
        router_out, router_out_first, router_out_second, router_out_grad * clip_factor, 0.02
    )
    return (
        result,
        d_inputs,
        counts,
        grad_norm,
        new_block,
        new_block_first,
        new_block_second,
        new_block.astype(BF),
        new_gains,
        new_gains_first,
        new_gains_second,
        new_router_in,
        new_router_in_first,
        new_router_in_second,
        new_router_out,
        new_router_out_first,
        new_router_out_second,
    )


def solution(mesh):
    both = P(("wide", "narrow"), None)
    return jax.shard_map(
        on_device,
        mesh=mesh,
        in_specs=(both, P("wide", None)) + (both,) * 5 + (P(),) * 9,
        out_specs=(both, both, P(), P()) + (both,) * 4 + (P(),) * 9,
        check_vma=False,
    )
```

```python
import functools

import jax
import jax.numpy as jnp
from jax import lax
from jax.experimental import pallas as pl
from jax.experimental.pallas import tpu as pltpu
from jax.sharding import PartitionSpec as P

D = 2048
HEADS = 16
HEAD_DIM = 128
FF = 8192
RH = 256
LEVELS = 4
STEP = 10
TOK = 128
GROUP = 1024
SIDE = 4
WIDE = 16
NARROW = 8
ROWS = 16

NORM_EPS = 1e-05
CLIP_NORM = 1.0
CONTRACT_COLS = (((1,), (1,)), ((), ()))
CONTRACT_ROWS = (((0,), (0,)), ((), ()))
MESH = pl.DeviceIdType.MESH
BF = jnp.bfloat16
F32 = jnp.float32


def here():
    w = lax.axis_index("wide")
    n = lax.axis_index("narrow")
    return lax.div(w, SIDE), lax.rem(w, SIDE), lax.div(n, 2), lax.rem(n, 2)


def wrap(i):
    return lax.rem(i + 2 * SIDE, SIDE)


def moved(dx=0, dz=0, dy=0, dc=0):
    x, z, y, c = here()
    return (wrap(x + dx) * SIDE + wrap(z + dz), wrap(y + dy) * 2 + lax.rem(c + dc, 2))


NEAR_Y = [dict(dy=1), dict(dy=-1), dict(dc=1)]
NARROW_ALL = [dict(dy=a, dc=b) for a in range(SIDE) for b in range(2) if a or b]
NEAR_XZ = [dict(dx=1), dict(dx=-1), dict(dz=1), dict(dz=-1)]
LINES_XZ = [dict(dx=a) for a in (1, 2, 3)] + [dict(dz=a) for a in (1, 2, 3)]
WIDE_ALL = [dict(dx=a, dz=b) for a in range(SIDE) for b in range(SIDE) if a or b]


def greet(partners):
    barrier = pltpu.get_barrier_semaphore()
    for p in partners:
        pl.semaphore_signal(barrier, inc=1, device_id=moved(**p), device_id_type=MESH)
    pl.semaphore_wait(barrier, len(partners))


def span(start, size):
    if not isinstance(start, int):
        start = pl.multiple_of(start, ROWS)
    return pl.ds(start, size)


def lanes(start, size):
    if not isinstance(start, int):
        start = pl.multiple_of(start, 128)
    return pl.ds(start, size)


def step(*parts):
    for part in parts:
        next(part, None)


class Net:
    def __init__(self, send, recv, local):
        self.send, self.recv, self.local = send, recv, local
        self.used, self.used_local = 0, 0
        self.sent = []

    def put(self, src, dst, target):
        i = self.used
        self.used += 1
        copy = pltpu.make_async_remote_copy(
            src_ref=src,
            dst_ref=dst,
            send_sem=self.send.at[i],
            recv_sem=self.recv.at[i],
            device_id=target,
            device_id_type=MESH,
        )
        copy.start()
        self.sent.append(copy)
        return copy

    def keep(self, src, dst):
        i = self.used_local
        self.used_local += 1
        copy = pltpu.make_async_copy(src, dst, self.local.at[i])
        copy.start()
        return copy

    def sent_by(self, *copies):
        for copy in copies:
            copy.wait_send()
        done = [id(copy) for copy in copies]
        self.sent = [copy for copy in self.sent if id(copy) not in done]

    def finish(self):
        for copy in self.sent:
            copy.wait_send()


def take_turns(*parts):
    live = list(parts)
    while live:
        still = []
        for part in live:
            try:
                next(part)
                still.append(part)
            except StopIteration:
                pass
        live = still


def comm_call(body, ins, outs, scratch, cid, copies, locals_, name, flops=0):
    n_in, n_out, n_scr = len(ins), len(outs), len(scratch)

    def kernel(*refs):
        in_refs = refs[:n_in]
        out_refs = refs[n_in : n_in + n_out]
        scr = refs[n_in + n_out : n_in + n_out + n_scr]
        send, recv, local = refs[n_in + n_out + n_scr :]
        net = Net(send, recv, local)
        body(net, in_refs, out_refs, scr)
        net.finish()
        assert net.used <= copies and net.used_local <= locals_, (net.used, net.used_local)

    return pl.pallas_call(
        kernel,
        out_shape=outs,
        in_specs=[pl.BlockSpec(memory_space=pl.ANY)] * n_in,
        out_specs=[pl.BlockSpec(memory_space=pl.ANY)] * n_out,
        scratch_shapes=list(scratch)
        + [
            pltpu.SemaphoreType.DMA((copies,)),
            pltpu.SemaphoreType.DMA((copies,)),
            pltpu.SemaphoreType.DMA((max(locals_, 1),)),
        ],
        compiler_params=pltpu.CompilerParams(
            collective_id=cid, has_side_effects=True, vmem_limit_bytes=62 * 2**20
        ),
        name=name,
    )(*ins)


def gather_narrow(net, own, out):
    x, z, y, c = here()
    rows = own.shape[0]
    half = rows // 2

    def block(dy, lo=0, size=rows):
        return out.at[span((wrap(y + dy) * 2 + c) * rows + lo, size)]

    up = net.put(own, block(0), moved(dy=1))
    down = net.put(own, block(0), moved(dy=-1))
    across = [net.put(own, block(0), moved(dc=1))]
    mine = net.keep(own, block(0))
    yield None
    mine.wait()
    across[0].wait_recv()
    yield 0
    up.wait_recv()
    on = net.put(block(-1, 0, half), block(-1, 0, half), moved(dy=1))
    across.append(net.put(block(-1), block(-1), moved(dc=1)))
    yield None
    down.wait_recv()
    back = net.put(block(1, half, half), block(1, half, half), moved(dy=-1))
    across.append(net.put(block(1), block(1), moved(dc=1)))
    across[1].wait_recv()
    yield 3
    across[2].wait_recv()
    yield 1
    on.wait_recv()
    across.append(net.put(block(2, 0, half), block(2, 0, half), moved(dc=1)))
    back.wait_recv()
    across.append(net.put(block(2, half, half), block(2, half, half), moved(dc=1)))
    across[3].wait_recv()
    across[4].wait_recv()
    yield 2
    net.sent_by(up, down, on, back, *across)


GATHER_COPIES = 10


def gather_call(own, cid, name):
    rows, cols = own.shape

    def body(net, ins, outs, scr):
        greet(NEAR_Y)
        take_turns(gather_narrow(net, ins[0], outs[0]))

    return comm_call(
        body,
        [own],
        [jax.ShapeDtypeStruct((NARROW * rows, cols), own.dtype)],
        [],
        cid,
        GATHER_COPIES,
        1,
        name,
    )[0]


def reduce_scratch(rows, cols):
    return [
        pltpu.VMEM((SIDE, rows, cols), BF),
        pltpu.VMEM((SIDE, rows, cols), BF),
        pltpu.VMEM((2, rows // 2, cols), BF),
        pltpu.VMEM((2, rows, cols), BF),
        pltpu.VMEM((3, rows, cols), BF),
        pltpu.VMEM((rows, cols), F32),
    ]


REDUCE_COPIES = 10
REDUCE_LOCALS = 5


def reduce_narrow(net, part, out, scr):
    own, other, through, landed, ready, total = scr
    x, z, y, c = here()
    rows, cols = out.shape
    half = rows // 2

    def block(dy, core):
        return part.at[span((wrap(y + dy) * 2 + core) * rows, rows)]

    order = (2, 1, 3, 0)
    local, cross = {}, {}
    for dy in order:
        cross[dy] = net.put(block(dy, 1 - c), other.at[dy], moved(dc=1))
        local[dy] = net.keep(block(dy, c), own.at[dy])

    def pair(dy, lo, size):
        s = span(lo, size)
        return own[dy, s, :].astype(F32) + other[dy, s, :].astype(F32)

    yield
    local[2].wait()
    cross[2].wait_recv()
    ready[0] = pair(2, 0, rows).astype(BF)
    first, last = span(0, half), span(half, half)
    via_up = net.put(ready.at[0, first], through.at[0], moved(dy=1))
    via_down = net.put(ready.at[0, last], through.at[1], moved(dy=-1))
    yield
    local[1].wait()
    cross[1].wait_recv()
    ready[1, last, :] = pair(1, half, half).astype(BF)
    up_late = net.put(ready.at[1, last], landed.at[0, last], moved(dy=1))
    local[3].wait()
    cross[3].wait_recv()
    ready[2, first, :] = pair(3, 0, half).astype(BF)
    down_first = net.put(ready.at[2, first], landed.at[1, first], moved(dy=-1))
    yield
    via_up.wait_recv()
    ready[1, first, :] = (pair(1, 0, half) + through[0].astype(F32)).astype(BF)
    up_first = net.put(ready.at[1, first], landed.at[0, first], moved(dy=1))
    via_down.wait_recv()
    ready[2, last, :] = (pair(3, half, half) + through[1].astype(F32)).astype(BF)
    down_late = net.put(ready.at[2, last], landed.at[1, last], moved(dy=-1))
    yield
    local[0].wait()
    cross[0].wait_recv()
    total[...] = pair(0, 0, rows)
    yield
    for copy in (up_late, down_first, up_first, down_late):
        copy.wait_recv()
    total[...] += landed[0].astype(F32) + landed[1].astype(F32)
    done = net.keep(total, out)
    yield
    done.wait()


def pairs_scratch(rows, cols):
    return [
        pltpu.VMEM((SIDE, 2 * rows, cols), BF),
        pltpu.VMEM((SIDE, rows, cols), BF),
        pltpu.VMEM((2, rows // 2, cols), BF),
        pltpu.VMEM((2, rows, cols), BF),
        pltpu.VMEM((3, rows, cols), BF),
        pltpu.VMEM((rows, cols), F32),
    ]


PAIR_ORDER = (2, 1, 3, 0)


def reduce_pairs(net, out, scr):
    parts, other, through, landed, ready, total = scr
    x, z, y, c = here()
    rows = total.shape[0]
    half = rows // 2
    first, last = pl.ds(0, half), pl.ds(half, half)

    def cross(dy):
        return net.put(parts.at[dy, span((1 - c) * rows, rows)], other.at[dy], moved(dc=1))

    def pair(dy, lo, size):
        mine = parts[dy, span(c * rows + lo, size), :].astype(F32)
        return mine + other[dy, pl.ds(lo, size), :].astype(F32)

    cross_two = cross(2)
    yield
    cross_one = cross(1)
    cross_two.wait_recv()
    ready[0] = pair(2, 0, rows).astype(BF)
    via_up = net.put(ready.at[0, first], through.at[0], moved(dy=1))
    via_down = net.put(ready.at[0, last], through.at[1], moved(dy=-1))
    yield
    cross_three = cross(3)
    cross_one.wait_recv()
    ready[1, last, :] = pair(1, half, half).astype(BF)
    up_late = net.put(ready.at[1, last], landed.at[0, last], moved(dy=1))
    yield
    cross_own = cross(0)
    cross_three.wait_recv()
    ready[2, first, :] = pair(3, 0, half).astype(BF)
    down_first = net.put(ready.at[2, first], landed.at[1, first], moved(dy=-1))
    yield
    via_up.wait_recv()
    ready[1, first, :] = (pair(1, 0, half) + through[0].astype(F32)).astype(BF)
    up_first = net.put(ready.at[1, first], landed.at[0, first], moved(dy=1))
    via_down.wait_recv()
    ready[2, last, :] = (pair(3, half, half) + through[1].astype(F32)).astype(BF)
    down_late = net.put(ready.at[2, last], landed.at[1, last], moved(dy=-1))
    yield
    cross_own.wait_recv()
    total[...] = pair(0, 0, rows)
    yield
    for copy in (up_late, down_first, up_first, down_late):
        copy.wait_recv()
    total[...] += landed[0].astype(F32) + landed[1].astype(F32)
    done = net.keep(total, out)
    yield
    done.wait()


def reduce_call(parts, cid, name):
    n = len(parts)
    shapes = [(p.shape[0] // NARROW, p.shape[1]) for p in parts]
    scratch = [s for shape in shapes for s in reduce_scratch(*shape)]

    def body(net, ins, outs, scr):
        greet(NEAR_Y)
        take_turns(
            *[reduce_narrow(net, ins[i], outs[i], scr[6 * i : 6 * i + 6]) for i in range(n)]
        )

    return comm_call(
        body,
        list(parts),
        [jax.ShapeDtypeStruct(s, F32) for s in shapes],
        scratch,
        cid,
        REDUCE_COPIES * n,
        REDUCE_LOCALS * n,
        name,
    )


def spread_narrow(net, src, slab):
    w = lax.axis_index("wide")
    n = lax.axis_index("narrow")
    base = n * ROWS if slab.shape[0] == TOK else w * TOK + n * ROWS
    mine = net.keep(src.at[n], slab.at[span(base, ROWS)])
    copies = []
    for p in NARROW_ALL:
        target = moved(**p)
        copies.append(net.put(src.at[target[1]], slab.at[span(base, ROWS)], target))
    yield
    mine.wait()
    for copy in copies:
        copy.wait_recv()


SPREAD_COPIES = 7


def gather_wide(net, slab, lead, stage=None):
    x, z, y, c = here()
    rows = TOK // 2
    half = rows // 2
    low = 0 if lead == "x" else rows

    def block(a, b, lo=0, size=rows):
        px, pz = (a, b) if lead == "x" else (b, a)
        return slab.at[span((wrap(x + px) * SIDE + wrap(z + pz)) * TOK + low + lo, size)]

    def lead_to(d):
        return moved(dx=d) if lead == "x" else moved(dz=d)

    def then_to(d):
        return moved(dz=d) if lead == "x" else moved(dx=d)

    def both(src, to, dst=None):
        dst = src if dst is None else dst
        return net.put(src, dst, to(1)), net.put(src, dst, to(-1))

    mine = block(0, 0) if stage is None else stage.at[pl.ds(low, rows)]
    fore, aft = both(mine, lead_to, block(0, 0))
    second = {0: both(mine, then_to, block(0, 0))}
    yield
    fore.wait_recv()
    on = net.put(block(-1, 0, 0, half), block(-1, 0, 0, half), lead_to(1))
    second[-1] = both(block(-1, 0), then_to)
    aft.wait_recv()
    back = net.put(block(1, 0, half, half), block(1, 0, half, half), lead_to(-1))
    second[1] = both(block(1, 0), then_to)
    yield
    last = []

    def relay(a):
        f, b = second[a]
        f.wait_recv()
        last.append(net.put(block(a, -1, 0, half), block(a, -1, 0, half), then_to(1)))
        b.wait_recv()
        last.append(net.put(block(a, 1, half, half), block(a, 1, half, half), then_to(-1)))

    kept = None if stage is None else net.keep(mine, block(0, 0))
    relay(0)
    yield
    on.wait_recv()
    back.wait_recv()
    second[2] = both(block(2, 0), then_to)
    yield
    relay(-1)
    relay(1)
    yield
    relay(2)
    yield
    if kept is not None:
        kept.wait()
    for copy in last:
        copy.wait_recv()


WIDE_COPIES = 20


def chain(*parts):
    for part in parts:
        yield from part


def first_gather(owns, sources, cid):
    k, m = len(owns), len(sources)

    def body(net, ins, outs, scr):
        greet(NARROW_ALL + NEAR_XZ)

        for _ in spread_narrow(net, ins[k], outs[k]):
            pass
        take_turns(
            gather_wide(net, outs[k], "x"),
            gather_wide(net, outs[k], "z"),
            *[gather_narrow(net, ins[i], outs[i]) for i in range(k)],
            *[spread_narrow(net, ins[k + i], outs[k + i]) for i in range(1, m)],
        )

    shapes = [jax.ShapeDtypeStruct((NARROW * o.shape[0], o.shape[1]), o.dtype) for o in owns] + [
        jax.ShapeDtypeStruct((TOK if i else D, s.shape[2]), s.dtype)
        for i, s in enumerate(sources)
    ]
    return comm_call(
        body,
        list(owns) + list(sources),
        shapes,
        [],
        cid,
        k * GATHER_COPIES + m * (SPREAD_COPIES + 2 * WIDE_COPIES),
        k + m,
        "first_gather",
    )


def turn(values, cosine, sine):
    return values * cosine + pltpu.roll(values, HEAD_DIM // 2, 1) * sine


def allowed_keys(first_row, rows, first_length):
    query = first_row + lax.broadcasted_iota(jnp.int32, (rows, 1), 0)
    key = lax.broadcasted_iota(jnp.int32, (rows, GROUP), 1)
    start = jnp.where(query >= first_length, first_length, 0)
    return (key <= query) & (key >= start)


def branch_mask(marks, lane):
    n = lax.axis_index("narrow").astype(F32)
    return (n < 2.0 * (marks[:, lane : lane + 1].astype(F32) + 1.0)).astype(F32)


def attention_forward(normed, slab, turns, first_length, marks, d_ffn_own, stage, cid):
    pair_rows = 2 * TOK
    head_part = D // NARROW

    def body(net, ins, outs, scr):
        normed, slab, turns, first_length, marks, d_ffn_own, stage = ins
        attn_sum, q_out, k_out, v_out, p_out, a_out, d_ffn, slab_b = outs
        xv, wv, tv, lv, mv, qv, kv, vv, pv, av = scr[:10]
        x, z, y, c = here()
        loads = [net.keep(a, b) for a, b in zip(ins[:5], scr[:5])]
        greet(NEAR_Y + NEAR_XZ)
        moves = [
            gather_wide(net, slab_b, "x", stage),
            gather_wide(net, slab_b, "z", stage),
            gather_narrow(net, d_ffn_own, d_ffn),
        ]
        step(*moves)
        for load in loads:
            load.wait()

        @pl.loop(0, SIDE)
        def _(i):
            r = span(i * pair_rows, pair_rows)
            proj = jnp.dot(xv[r, :], wv[:, : 3 * head_part], preferred_element_type=F32)
            cosine, sine = tv[0, r, :], tv[1, r, :]
            for h in range(2):
                at = pl.ds(h * HEAD_DIM, HEAD_DIM)
                a = h * HEAD_DIM
                qv[r, at] = turn(proj[:, a : a + HEAD_DIM], cosine, sine).astype(BF)
                a += head_part
                kv[r, at] = turn(proj[:, a : a + HEAD_DIM], cosine, sine).astype(BF)
            vv[r, :] = proj[:, 2 * head_part :].astype(BF)

        stores = [net.keep(qv, q_out), net.keep(kv, k_out), net.keep(vv, v_out)]
        total = reduce_pairs(net, attn_sum, scr[10:])
        length = lv[0:1, 0:1]
        for dy in PAIR_ORDER:
            first = wrap(y + dy) * pair_rows
            r = span(first, pair_rows)
            allowed = allowed_keys(first, pair_rows, length)
            heads = []
            for h in range(2):
                at = pl.ds(h * HEAD_DIM, HEAD_DIM)
                scores = lax.dot_general(
                    qv[r, at], kv[:, at], CONTRACT_COLS, preferred_element_type=F32
                )
                scores = jnp.where(allowed, scores * HEAD_DIM ** (-0.5), -1e30)
                expo = jnp.exp(scores - jnp.max(scores, axis=-1, keepdims=True))
                probs = expo * (1.0 / jnp.sum(expo, axis=-1, keepdims=True))
                low = probs.astype(BF)
                pv[wrap(y + dy), :, pl.ds(h * GROUP, GROUP)] = low
                heads.append(jnp.dot(low, vv[:, at], preferred_element_type=F32))
            mask = branch_mask(mv[r, :], 0)
            av[r, :] = (jnp.concatenate(heads, axis=1) * mask).astype(BF)
            scr[10][dy] = lax.dot_general(
                av[r, :], wv[:, 3 * head_part :], CONTRACT_COLS, preferred_element_type=F32
            ).astype(BF)
            step(total, *moves)
        stores += [net.keep(pv, p_out), net.keep(av, a_out)]
        take_turns(total, *moves)
        for store in stores:
            store.wait()

    low = jax.ShapeDtypeStruct((GROUP, head_part), BF)
    return comm_call(
        body,
        [normed, slab, turns, first_length, marks, d_ffn_own, stage],
        [
            jax.ShapeDtypeStruct((TOK, D), F32),
            low,
            low,
            low,
            jax.ShapeDtypeStruct((SIDE, pair_rows, 2 * GROUP), BF),
            low,
            jax.ShapeDtypeStruct((GROUP, D), BF),
            jax.ShapeDtypeStruct((D, stage.shape[1]), BF),
        ],
        [
            pltpu.VMEM((GROUP, D), BF),
            pltpu.VMEM(slab.shape, BF),
            pltpu.VMEM(turns.shape, F32),
            pltpu.VMEM(first_length.shape, jnp.int32),
            pltpu.VMEM(marks.shape, BF),
            pltpu.VMEM((GROUP, head_part), BF),
            pltpu.VMEM((GROUP, head_part), BF),
            pltpu.VMEM((GROUP, head_part), BF),
            pltpu.VMEM((SIDE, pair_rows, 2 * GROUP), BF),
            pltpu.VMEM((GROUP, head_part), BF),
        ]
        + pairs_scratch(TOK, D),
        cid,
        REDUCE_COPIES + 2 * WIDE_COPIES + GATHER_COPIES,
        5 + 5 + 4,
        "attention_forward",
    )


def feed_forward(normed_own, d_ffn, slab, marks, cid):
    pair_rows = 2 * TOK
    units = FF // NARROW
    strip = 256

    def body(net, ins, outs, scr):
        own, d_ffn, slab, marks = ins
        norm_sum, ffn_part, g_up, g_down = outs
        xv, dv, w_up, w_down, mv, act, du, da, gu, gd, yv = scr[:11]
        x, z, y, c = here()
        loads = [
            net.keep(d_ffn, dv),
            net.keep(slab.at[:, pl.ds(units, units)], w_down),
            net.keep(slab.at[:, pl.ds(0, units)], w_up),
            net.keep(marks, mv),
        ]
        greet(NEAR_Y)
        gather = gather_narrow(net, own, xv)
        next(gather)
        loads[0].wait()
        loads[1].wait()

        @pl.loop(0, SIDE)
        def _(i):
            r = span(i * pair_rows, pair_rows)
            da[r, :] = jnp.dot(dv[r, :], w_down[...], preferred_element_type=F32)

        loads[2].wait()
        loads[3].wait()
        for dy in gather:
            if dy is not None:
                r = span(wrap(y + dy) * pair_rows, pair_rows)
                up = jnp.dot(xv[r, :], w_up[...], preferred_element_type=F32)
                positive = jnp.maximum(up, 0.0)
                masked = positive * branch_mask(mv[r, :], 64)
                act[r, :] = (positive * masked).astype(BF)
                du[r, :] = (da[r, :] * (2.0 * masked)).astype(BF)

        total = reduce_pairs(net, norm_sum, scr[11:])
        for dy in PAIR_ORDER:
            r = span(wrap(y + dy) * pair_rows, pair_rows)
            scr[11][dy] = lax.dot_general(
                du[r, :], w_up[...], CONTRACT_COLS, preferred_element_type=F32
            ).astype(BF)
            next(total)

        def gradient(left, right, to, start, stop):
            @pl.loop(start, stop)
            def _(i):
                at = lanes(i * strip, strip)
                to[span(i * strip, strip), :] = lax.dot_general(
                    left[:, at], right[...], CONTRACT_ROWS, preferred_element_type=F32
                ).astype(BF)

        gradient(dv, act, gd, 0, 4)
        next(total)
        gradient(dv, act, gd, 4, 8)
        stores = [net.keep(gd, g_down)]
        step(total)
        gradient(xv, du, gu, 0, 8)
        stores.append(net.keep(gu, g_up))
        step(total)

        @pl.loop(0, SIDE)
        def _(i):
            r = span(i * pair_rows, pair_rows)
            yv[r, :] = lax.dot_general(
                act[r, :], w_down[...], CONTRACT_COLS, preferred_element_type=F32
            ).astype(BF)

        stores.append(net.keep(yv, ffn_part))
        take_turns(total)
        for store in stores:
            store.wait()

    wide = pltpu.VMEM((GROUP, D), BF)
    tall = pltpu.VMEM((D, units), BF)
    square = pltpu.VMEM((GROUP, units), BF)
    return comm_call(
        body,
        [normed_own, d_ffn, slab, marks],
        [
            jax.ShapeDtypeStruct((TOK, D), F32),
            jax.ShapeDtypeStruct((GROUP, D), BF),
            jax.ShapeDtypeStruct((D, units), BF),
            jax.ShapeDtypeStruct((D, units), BF),
        ],
        [wide, wide, tall, tall, pltpu.VMEM(marks.shape, BF), square, square]
        + [pltpu.VMEM((GROUP, units), F32), tall, tall, wide]
        + pairs_scratch(TOK, D),
        cid,
        GATHER_COPIES + REDUCE_COPIES,
        4 + 1 + 1 + 3,
        "feed_forward",
    )


def wide_scratch(cols):
    part, half = TOK // 2, TOK // 4
    return [
        pltpu.VMEM((2, 2, SIDE, half, cols), BF),
        pltpu.VMEM((2, 2, SIDE, part, cols), BF),
        pltpu.VMEM((2, 2, SIDE, half, cols), BF),
        pltpu.VMEM((2, SIDE, part, cols), BF),
        pltpu.VMEM((2, 2, half, cols), BF),
        pltpu.VMEM((2, 2, part, cols), BF),
        pltpu.VMEM((2, 2, half, cols), BF),
        pltpu.VMEM((TOK, cols), BF),
    ]


REDUCE_WIDE_COPIES = 24
REDUCE_WIDE_LOCALS = 6


def reduce_wide(net, grad, scr, lead):
    via, landed, ready, sums, via_two, landed_two, ready_two, total = scr
    x, z, y, c = here()
    part, half = TOK // 2, TOK // 4
    k = 0 if lead == "x" else 1
    low = k * part
    blocks = grad.reshape(SIDE, SIDE, TOK, grad.shape[1])
    first, last = pl.ds(0, half), pl.ds(half, half)

    def line(d, lo, size):
        rows = pl.ds(low + lo, size)
        if lead == "x":
            return (wrap(x + d), slice(None), rows, slice(None))
        return (slice(None), wrap(z + d), rows, slice(None))

    def lead_to(d):
        return moved(dx=d) if lead == "x" else moved(dz=d)

    def then_to(d):
        return moved(dz=d) if lead == "x" else moved(dx=d)

    via_up = net.put(blocks.at[line(2, 0, half)], via.at[k, 0], lead_to(1))
    via_down = net.put(blocks.at[line(2, half, half)], via.at[k, 1], lead_to(-1))
    up_late = net.put(blocks.at[line(1, half, half)], landed.at[k, 0, :, last], lead_to(1))
    down_first = net.put(blocks.at[line(3, 0, half)], landed.at[k, 1, :, first], lead_to(-1))
    loads = [
        net.keep(blocks.at[line(1, 0, half)], ready.at[k, 0]),
        net.keep(blocks.at[line(3, half, half)], ready.at[k, 1]),
        net.keep(blocks.at[line(0, 0, part)], sums.at[k]),
    ]
    yield
    for load in loads:
        load.wait()
    via_up.wait_recv()

    @pl.loop(0, SIDE)
    def _(i):
        ready[k, 0, i] = (ready[k, 0, i].astype(F32) + via[k, 0, i].astype(F32)).astype(BF)

    up_first = net.put(ready.at[k, 0], landed.at[k, 0, :, first], lead_to(1))
    via_down.wait_recv()

    @pl.loop(0, SIDE)
    def _(i):
        ready[k, 1, i] = (ready[k, 1, i].astype(F32) + via[k, 1, i].astype(F32)).astype(BF)

    down_late = net.put(ready.at[k, 1], landed.at[k, 1, :, last], lead_to(-1))
    yield
    for copy in (up_late, down_first, up_first, down_late):
        copy.wait_recv()

    @pl.loop(0, SIDE)
    def _(i):
        both = landed[k, 0, i].astype(F32) + landed[k, 1, i].astype(F32)
        sums[k, i] = (sums[k, i].astype(F32) + both).astype(BF)

    me = z if lead == "x" else x

    def block(d, rows):
        return sums.at[k, wrap(me + d), rows]

    via_up = net.put(block(2, first), via_two.at[k, 0], then_to(1))
    via_down = net.put(block(2, last), via_two.at[k, 1], then_to(-1))
    up_late = net.put(block(1, last), landed_two.at[k, 0, last], then_to(1))
    down_first = net.put(block(3, first), landed_two.at[k, 1, first], then_to(-1))
    yield
    via_up.wait_recv()
    ready_two[k, 0] = (block(1, first)[...].astype(F32) + via_two[k, 0].astype(F32)).astype(BF)
    up_first = net.put(ready_two.at[k, 0], landed_two.at[k, 0, first], then_to(1))
    via_down.wait_recv()
    ready_two[k, 1] = (block(3, last)[...].astype(F32) + via_two[k, 1].astype(F32)).astype(BF)
    down_late = net.put(ready_two.at[k, 1], landed_two.at[k, 1, last], then_to(-1))
    yield
    for copy in (up_late, down_first, up_first, down_late):
        copy.wait_recv()
    both = landed_two[k, 0].astype(F32) + landed_two[k, 1].astype(F32)
    total[pl.ds(low, part), :] = (sums[k, me].astype(F32) + both).astype(BF)


def return_narrow(net, total, out, pieces):
    n = lax.axis_index("narrow")
    copies, mine = [], []
    for start, width, to in pieces:
        spot = out.at[:, lanes(to + n * width, width)]
        columns = pl.ds(start, width)
        for p in NARROW_ALL:
            target = moved(**p)
            copies.append(net.put(total.at[span(target[1] * ROWS, ROWS), columns], spot, target))
        mine.append(net.keep(total.at[span(n * ROWS, ROWS), columns], spot))
    yield
    for copy in mine:
        copy.wait()
    for copy in copies:
        copy.wait_recv()


def wide_then_narrow(net, grad, out, scr, pieces):
    a, b = reduce_wide(net, grad, scr, "x"), reduce_wide(net, grad, scr, "z")
    while True:
        more = [next(a, StopIteration), next(b, StopIteration)]
        if StopIteration in more:
            break
        yield
    yield from return_narrow(net, scr[7], out, pieces)


def attention_backward(d_attn_own, ffn_part, g_up, g_down, normed, kept, cid):
    pair_rows = 2 * TOK
    head_part = D // NARROW
    units = FF // NARROW
    strip = 256
    scale = HEAD_DIM ** (-0.5)
    scratch = (
        [pltpu.VMEM(r.shape, r.dtype) for r in kept]
        + [
            pltpu.VMEM((GROUP, D), BF),
            pltpu.VMEM((GROUP, head_part), F32),
            pltpu.VMEM((GROUP, head_part), F32),
            pltpu.VMEM((GROUP, 3 * head_part), BF),
            pltpu.VMEM((D, 4 * head_part), BF),
        ]
        + pairs_scratch(TOK, D)[1:]
        + reduce_scratch(TOK, D)
        + wide_scratch(4 * head_part)
        + wide_scratch(units)
        + wide_scratch(units)
    )

    def body(net, ins, outs, scr):
        d_attn_own, ffn_part, g_up, g_down, normed = ins[:5]
        norm_sum, ffn_sum, block = outs
        wv, tv, mv, qv, kv, vv, pv, av = scr[:8]
        big, dk, dv, dproj, ga = scr[8:13]
        pairs, narrow = [pv, *scr[13:18]], scr[18:24]
        wide_a, wide_up, wide_down = scr[24:32], scr[32:40], scr[40:48]
        x, z, y, c = here()
        loads = [net.keep(a, b) for a, b in zip(ins[5:], scr[:8])]
        greet(NARROW_ALL + NEAR_XZ)
        gather = gather_narrow(net, d_attn_own, big)
        next(gather)
        down = wide_then_narrow(net, g_down, block, wide_down, [(0, units, 4 * D + FF)])
        up = wide_then_narrow(net, g_up, block, wide_up, [(0, units, 4 * D)])
        quarter = [(i * head_part, head_part, i * D) for i in range(4)]
        mixed = wide_then_narrow(net, ga, block, wide_a, quarter)
        feed = reduce_narrow(net, ffn_part, ffn_sum, narrow)
        next(down)
        dk[...] = jnp.zeros_like(dk)
        dv[...] = jnp.zeros_like(dv)
        for load in loads:
            load.wait()

        def one_pair(dy):
            r = span(wrap(y + dy) * pair_rows, pair_rows)
            mask = branch_mask(mv[r, :], 0)
            back = jnp.dot(big[r, :], wv[:, 3 * head_part :], preferred_element_type=F32)
            back = (back * mask).astype(BF)
            for h in range(2):
                at = pl.ds(h * HEAD_DIM, HEAD_DIM)
                d_out = back[:, h * HEAD_DIM : (h + 1) * HEAD_DIM]
                d_probs = lax.dot_general(
                    d_out, vv[:, at], CONTRACT_COLS, preferred_element_type=F32
                )
                probs_low = pv[wrap(y + dy), :, pl.ds(h * GROUP, GROUP)]
                probs = probs_low.astype(F32)
                weighted = probs * d_probs
                centre = jnp.sum(weighted, axis=-1, keepdims=True)
                ds = (weighted - probs * centre).astype(BF)
                dq = jnp.dot(ds, kv[:, at], preferred_element_type=F32) * scale
                dproj[r, at] = turn(dq, tv[0, r, :], -tv[1, r, :]).astype(BF)
                dk[:, at] += lax.dot_general(
                    ds, qv[r, at], CONTRACT_ROWS, preferred_element_type=F32
                )
                dv[:, at] += lax.dot_general(
                    probs_low, d_out, CONTRACT_ROWS, preferred_element_type=F32
                )

        for dy in gather:
            if dy is not None:
                one_pair(dy)
                if dy == 0:
                    step(down, up)
                if dy == 1:
                    step(down)

        @pl.loop(0, SIDE)
        def _(i):
            r = span(i * pair_rows, pair_rows)
            cosine, sine = tv[0, r, :], -tv[1, r, :]
            for h in range(2):
                at = pl.ds(h * HEAD_DIM, HEAD_DIM)
                to = pl.ds(head_part + h * HEAD_DIM, HEAD_DIM)
                dproj[r, to] = turn(dk[r, at] * scale, cosine, sine).astype(BF)
            dproj[r, pl.ds(2 * head_part, head_part)] = dv[r, :].astype(BF)

        total = reduce_pairs(net, norm_sum, pairs)
        for dy in PAIR_ORDER:
            r = span(wrap(y + dy) * pair_rows, pair_rows)
            pairs[0][dy] = lax.dot_general(
                dproj[r, :], wv[:, : 3 * head_part], CONTRACT_COLS, preferred_element_type=F32
            ).astype(BF)
            next(total)

        @pl.loop(0, D // strip)
        def _(i):
            r = span(i * strip, strip)
            ga[r, pl.ds(3 * head_part, head_part)] = lax.dot_general(
                big[:, lanes(i * strip, strip)], av[...], CONTRACT_ROWS, preferred_element_type=F32
            ).astype(BF)

        refill = net.keep(normed, big)
        step(down, up, feed)
        refill.wait()

        @pl.loop(0, D // strip)
        def _(i):
            r = span(i * strip, strip)
            ga[r, pl.ds(0, 3 * head_part)] = lax.dot_general(
                big[:, lanes(i * strip, strip)],
                dproj[...],
                CONTRACT_ROWS,
                preferred_element_type=F32,
            ).astype(BF)

        take_turns(mixed, total, down, up, feed)

    return comm_call(
        body,
        [d_attn_own, ffn_part, g_up, g_down, normed] + list(kept),
        [
            jax.ShapeDtypeStruct((TOK, D), F32),
            jax.ShapeDtypeStruct((TOK, D), F32),
            jax.ShapeDtypeStruct((ROWS, 4 * D + 2 * FF), BF),
        ],
        scratch,
        cid,
        GATHER_COPIES + 2 * REDUCE_COPIES + 3 * REDUCE_WIDE_COPIES + 6 * 7,
        8 + 1 + 1 + 1 + REDUCE_LOCALS + 3 * REDUCE_WIDE_LOCALS + 6,
        "attention_backward",
    )


def small_wide(part, cid):
    def body(net, ins, outs, scr):
        landed, total = scr
        greet(WIDE_ALL)
        w = lax.axis_index("wide")

        def rows(i):
            return ins[0].at[span(i * ROWS, ROWS)]

        mine = net.keep(rows(w), landed.at[w])
        copies = []
        for p in WIDE_ALL:
            target = moved(**p)
            copies.append(net.put(rows(target[0]), landed.at[w], target))
        mine.wait()
        for copy in copies:
            copy.wait_recv()
        s = landed[0].astype(F32)
        for i in range(1, WIDE):
            s = s + landed[i].astype(F32)
        total[...] = s
        net.keep(total, outs[0]).wait()

    return comm_call(
        body,
        [part],
        [jax.ShapeDtypeStruct((ROWS, RH), F32)],
        [pltpu.VMEM((WIDE, ROWS, RH), BF), pltpu.VMEM((ROWS, RH), F32)],
        cid,
        15,
        2,
        "small_wide",
    )[0]


def last_sums(vector, shard, cid):
    rows = vector.shape[0]

    def body(net, ins, outs, scr):
        vec, own = ins
        vec_out, full = outs
        first, mid, second, total = scr
        w = lax.axis_index("wide")
        n = lax.axis_index("narrow")
        greet(NARROW_ALL + WIDE_ALL)

        def sums():
            mine = net.keep(vec, first.at[n])
            copies = [net.put(vec, first.at[n], moved(**p)) for p in NARROW_ALL]
            yield
            mine.wait()
            for copy in copies:
                copy.wait_recv()
            s = first[0]
            for i in range(1, NARROW):
                s = s + first[i]
            mid[...] = s
            mine = net.keep(mid, second.at[w])
            copies = [net.put(mid, second.at[w], moved(**p)) for p in WIDE_ALL]
            yield
            mine.wait()
            for copy in copies:
                copy.wait_recv()
            s = second[0]
            for i in range(1, WIDE):
                s = s + second[i]
            total[...] = s
            done = net.keep(total, vec_out)
            yield
            done.wait()

        def table():
            spot = full.at[span(n * GROUP // 4 + w * ROWS, ROWS)]
            mine = net.keep(own, spot)
            copies = [net.put(own, spot, moved(**p)) for p in WIDE_ALL]
            yield
            mine.wait()
            for copy in copies:
                copy.wait_recv()
            x, z, y, c = here()

            def block(dy):
                return full.at[span((wrap(y + dy) * 2 + c) * RH, RH)]

            along = [net.put(block(0), block(0), moved(dy=d)) for d in (1, 3, 2)]
            across = [net.put(block(0), block(0), moved(dc=1))]
            yield
            for copy, d in zip(along, (1, 3, 2)):
                copy.wait_recv()
                across.append(net.put(block(-d), block(-d), moved(dc=1)))
            yield
            for copy in across:
                copy.wait_recv()

        take_turns(sums(), table())

    return comm_call(
        body,
        [vector, shard],
        [jax.ShapeDtypeStruct((rows, 128), F32), jax.ShapeDtypeStruct((D, RH), F32)],
        [
            pltpu.VMEM((NARROW, rows, 128), F32),
            pltpu.VMEM((rows, 128), F32),
            pltpu.VMEM((WIDE, rows, 128), F32),
            pltpu.VMEM((rows, 128), F32),
        ],
        cid,
        7 + 15 + 15 + 7,
        4,
        "last_sums",
    )


def layer_norm(values, gain_row):
    average = jnp.mean(values, axis=-1, keepdims=True)
    centered = values - average
    spread = jnp.mean(centered * centered, axis=-1, keepdims=True)
    return centered * lax.rsqrt(spread + NORM_EPS) * gain_row


def segment_info(seg_lengths, token_index):
    seg_ends = jnp.cumsum(seg_lengths)
    segment = jnp.sum((token_index[:, None] >= seg_ends[None, :]).astype(jnp.int32), axis=1)
    starts = seg_ends - seg_lengths
    owners = segment[:, None] == jnp.arange(seg_lengths.shape[0], dtype=jnp.int32)[None, :]
    start_of = jnp.sum(jnp.where(owners, starts[None, :], 0), axis=1)
    return (segment, token_index - start_of)


def router_gates(normed, first_layer, second_layer, picks):
    hidden = jax.nn.gelu(jnp.dot(normed, first_layer))
    logits = jnp.dot(hidden, second_layer)
    levels = jnp.arange(LEVELS, dtype=jnp.int32)
    chosen_attn = (picks[:, 0:1] == levels[None, :]).astype(jnp.float32)
    chosen_ffn = (picks[:, 1:2] == levels[None, :]).astype(jnp.float32)
    gate_attn = float(LEVELS) * jnp.sum(
        jax.nn.softmax(logits[:, :LEVELS], axis=-1) * chosen_attn, axis=-1
    )
    gate_ffn = float(LEVELS) * jnp.sum(
        jax.nn.softmax(logits[:, LEVELS:], axis=-1) * chosen_ffn, axis=-1
    )
    return (gate_attn, gate_ffn)


def adamw(weight, moment_one, moment_two, gradient, step_rate):
    moment_one = 0.9 * moment_one + 0.1 * gradient
    moment_two = 0.95 * moment_two + 0.05 * gradient * gradient
    first_hat = moment_one / (1.0 - 0.9**STEP)
    second_hat = moment_two / (1.0 - 0.95**STEP)
    updated = weight - step_rate * (first_hat / (jnp.sqrt(second_hat) + 1e-08) + 0.1 * weight)
    return (updated, moment_one, moment_two)


def cut(rows, start, width, pieces):
    part = rows[:, start : start + width].reshape(rows.shape[0], pieces, width // pieces)
    return part.transpose(1, 0, 2)


def on_device(
    tokens,
    lengths,
    picks,
    cotangent,
    block_master,
    block_first,
    block_second,
    gains,
    gains_first,
    gains_second,
    router_in,
    router_in_first,
    router_in_second,
    router_out,
    router_out_first,
    router_out_second,
):
    low = block_master.astype(BF)
    source_a = jnp.concatenate([cut(low, i * D, D, NARROW) for i in range(4)], axis=2)
    source_b = jnp.concatenate([cut(low, 4 * D + i * FF, FF, NARROW) for i in range(2)], axis=2)
    inputs = tokens.astype(F32)
    norm_one, norm_one_back = jax.vjp(layer_norm, inputs, gains[0])
    normed_own = norm_one.astype(BF)
    (gate_attn, gate_ffn), router_back = jax.vjp(
        lambda normed, first_layer, second_layer: router_gates(
            normed, first_layer, second_layer, picks
        ),
        normed_own.astype(F32),
        router_in,
        router_out,
    )
    upstream = cotangent.astype(F32)
    d_ffn_own = (upstream * gate_ffn[:, None]).astype(BF)
    marks = jnp.where(jnp.arange(128)[None, :] < 64, picks[:, 0:1], picks[:, 1:2]).astype(BF)

    normed_low, group_marks, slab_a, stage_b = first_gather(
        [normed_own, marks], [source_a, source_b], 0
    )

    key_index = jnp.arange(GROUP, dtype=jnp.int32)
    _, key_position = segment_info(lengths[0], key_index)
    half_dim = HEAD_DIM // 2
    frequency = 10000.0 ** (-jnp.arange(half_dim, dtype=F32) / half_dim)
    angles = key_position.astype(F32)[:, None] * frequency[None, :]
    cosine, sine = jnp.cos(angles), jnp.sin(angles)
    turns = jnp.stack(
        [
            jnp.concatenate([cosine, cosine], axis=1),
            jnp.concatenate([-sine, sine], axis=1),
        ]
    )
    first_length = jnp.broadcast_to(lengths[:, 0:1], (8, 128))
    attn_out, query_low, key_low, value_low, probs_low, mixed_low, d_ffn_low, slab_b = (
        attention_forward(
            normed_low, slab_a, turns, first_length, group_marks, d_ffn_own, stage_b, 1
        )
    )

    after_attn = inputs + gate_attn[:, None] * attn_out
    norm_two, norm_two_back = jax.vjp(layer_norm, after_attn, gains[1])

    d_norm_two, ffn_part, grad_up, grad_down = feed_forward(
        norm_two.astype(BF), d_ffn_low, slab_b, group_marks, 2
    )
    d_after, d_gain_two = norm_two_back(d_norm_two)
    d_after = d_after + upstream
    d_gate_attn = jnp.sum(d_after * attn_out, axis=1)
    d_normed, ffn_out, block_low = attention_backward(
        (d_after * gate_attn[:, None]).astype(BF),
        ffn_part,
        grad_up,
        grad_down,
        normed_low,
        [slab_a, turns, group_marks, query_low, key_low, value_low, probs_low, mixed_low],
        3,
    )

    result = (after_attn + gate_ffn[:, None] * ffn_out).astype(BF)
    d_gate_ffn = jnp.sum(upstream * ffn_out, axis=1)
    d_normed_router, grad_router_in, grad_router_out = router_back((d_gate_attn, d_gate_ffn))
    (router_in_part,) = reduce_call([grad_router_in.astype(BF)], 5, "sum_router")
    router_in_shard = small_wide(router_in_part.astype(BF), 6)
    d_inputs, d_gain_one = norm_one_back(d_normed + d_normed_router)
    d_inputs = d_inputs + d_after
    block_grad = block_low.astype(F32)

    levels = jnp.arange(LEVELS, dtype=jnp.int32)
    counts_local = jnp.concatenate(
        [
            jnp.sum((picks[:, 0:1] == levels[None, :]).astype(F32), axis=0),
            jnp.sum((picks[:, 1:2] == levels[None, :]).astype(F32), axis=0),
        ]
    )
    local_squares = jnp.sum(block_grad * block_grad) + jnp.sum(router_in_shard * router_in_shard)
    pieces = [
        d_gain_one,
        d_gain_two,
        grad_router_out.ravel(),
        counts_local,
        local_squares[None],
    ]
    size = sum(p.shape[0] for p in pieces)
    padded = -(-size // 1024) * 1024
    vector = jnp.concatenate(pieces + [jnp.zeros((padded - size,), F32)]).reshape(-1, 128)
    vector, router_in_grad = last_sums(vector, router_in_shard, 7)
    flat = vector.ravel()
    gain_grad = flat[: 2 * D].reshape(2, D)
    router_out_grad = flat[2 * D : 2 * D + RH * 8].reshape(RH, 8)
    at = 2 * D + RH * 8
    counts = flat[at : at + 8].reshape(2, LEVELS)
    squares = flat[at + 8]

    total = squares + jnp.sum(gain_grad * gain_grad) + jnp.sum(router_out_grad * router_out_grad)
    grad_norm = jnp.sqrt(total)
    clip_factor = jnp.minimum(1.0, CLIP_NORM / grad_norm)
    new_block, new_block_first, new_block_second = adamw(
        block_master, block_first, block_second, block_grad * clip_factor, 0.02
    )
    new_gains, new_gains_first, new_gains_second = adamw(
        gains, gains_first, gains_second, gain_grad * clip_factor, 0.6
    )
    new_router_in, new_router_in_first, new_router_in_second = adamw(
        router_in, router_in_first, router_in_second, router_in_grad * clip_factor, 0.02
    )
    new_router_out, new_router_out_first, new_router_out_second = adamw(
        router_out, router_out_first, router_out_second, router_out_grad * clip_factor, 0.02
    )
    return (
        result,
        d_inputs,
        counts,
        grad_norm,
        new_block,
        new_block_first,
        new_block_second,
        new_block.astype(BF),
        new_gains,
        new_gains_first,
        new_gains_second,
        new_router_in,
        new_router_in_first,
        new_router_in_second,
        new_router_out,
        new_router_out_first,
        new_router_out_second,
    )


def solution(mesh):
    both = P(("wide", "narrow"), None)
    return jax.shard_map(
        on_device,
        mesh=mesh,
        in_specs=(both, P("wide", None)) + (both,) * 5 + (P(),) * 9,
        out_specs=(both, both, P(), P()) + (both,) * 4 + (P(),) * 9,
        check_vma=False,
    )
```

```python
import functools

import jax
import jax.numpy as jnp
from jax import lax
from jax.experimental import pallas as pl
from jax.experimental.pallas import tpu as pltpu
from jax.sharding import PartitionSpec as P

D = 2048
HEADS = 16
HEAD_DIM = 128
FF = 8192
RH = 256
LEVELS = 4
STEP = 10
TOK = 128
GROUP = 1024
SIDE = 4
WIDE = 16
NARROW = 8
ROWS = 16

NORM_EPS = 1e-05
CLIP_NORM = 1.0
CONTRACT_COLS = (((1,), (1,)), ((), ()))
CONTRACT_ROWS = (((0,), (0,)), ((), ()))
MESH = pl.DeviceIdType.MESH
BF = jnp.bfloat16
F32 = jnp.float32


FORWARD_PLAN = (
    "sa", "gm", "sb", "sa", "wa", "gx", "wa", "gx", "gm", "gm", "wa", "wa", "sb", "gm", "gx",
    "wa", "gg", "gm", "wa", "wb", "gx", "gx", "gx", "gm", "wa", "Q", "wb", "gg", "T2", "T1",
    "gg", "wb", "total", "gg", "T3", "total", "wb", "T0", "gg", "total", "wb", "gx", "total",
    "gm", "total", "wb", "total", "wb", "gg", "total", "wa", "gg",
)
FEED_PLAN = (
    "gather", "gather", "DA", "U0", "gather", "gather", "U3", "gather", "U1", "gather", "U2",
    "N2", "GD", "total", "N1", "wide", "N3", "total", "N0", "DS", "total", "YF", "total",
    "wide", "GU", "total", "gather", "DT", "total", "wide", "total",
)
BACKWARD_PLAN = (
    "gather", "up", "gates", "gather", "up", "LD", "gather", "down", "feed", "feed", "P0",
    "gather", "P3", "gates", "P1", "feed", "up", "gather", "down", "gather", "P2", "feed", "up",
    "RT", "gates", "GO", "GQ", "up", "gather", "gates", "mixed", "down", "N2", "feed", "N0",
    "total", "N3", "down", "N1", "feed", "up", "up", "mixed", "gates", "total", "total",
    "total", "gates", "total", "down", "mixed", "mixed", "mixed", "gates", "total", "gates",
    "total", "mixed",
)


def here():
    w = lax.axis_index("wide")
    n = lax.axis_index("narrow")
    return lax.div(w, SIDE), lax.rem(w, SIDE), lax.div(n, 2), lax.rem(n, 2)


def wrap(i):
    return lax.rem(i + 2 * SIDE, SIDE)


def moved(dx=0, dz=0, dy=0, dc=0):
    x, z, y, c = here()
    return (wrap(x + dx) * SIDE + wrap(z + dz), wrap(y + dy) * 2 + lax.rem(c + dc, 2))


NEAR_Y = [dict(dy=1), dict(dy=-1), dict(dc=1)]
NARROW_ALL = [dict(dy=a, dc=b) for a in range(SIDE) for b in range(2) if a or b]
NEAR_XZ = [dict(dx=1), dict(dx=-1), dict(dz=1), dict(dz=-1)]
LINES_XZ = [dict(dx=a) for a in (1, 2, 3)] + [dict(dz=a) for a in (1, 2, 3)]
WIDE_ALL = [dict(dx=a, dz=b) for a in range(SIDE) for b in range(SIDE) if a or b]


def greet(partners):
    barrier = pltpu.get_barrier_semaphore()
    for p in partners:
        pl.semaphore_signal(barrier, inc=1, device_id=moved(**p), device_id_type=MESH)
    pl.semaphore_wait(barrier, len(partners))


def span(start, size):
    if not isinstance(start, int):
        start = pl.multiple_of(start, ROWS)
    return pl.ds(start, size)


def lanes(start, size):
    if not isinstance(start, int):
        start = pl.multiple_of(start, 128)
    return pl.ds(start, size)


def step(*parts):
    for part in parts:
        next(part, None)


class Net:
    def __init__(self, send, recv, local):
        self.send, self.recv, self.local = send, recv, local
        self.used, self.used_local = 0, 0
        self.sent = []

    def put(self, src, dst, target):
        i = self.used
        self.used += 1
        copy = pltpu.make_async_remote_copy(
            src_ref=src,
            dst_ref=dst,
            send_sem=self.send.at[i],
            recv_sem=self.recv.at[i],
            device_id=target,
            device_id_type=MESH,
        )
        copy.start()
        self.sent.append(copy)
        return copy

    def keep(self, src, dst):
        i = self.used_local
        self.used_local += 1
        copy = pltpu.make_async_copy(src, dst, self.local.at[i])
        copy.start()
        return copy

    def sent_by(self, *copies):
        for copy in copies:
            copy.wait_send()
        done = [id(copy) for copy in copies]
        self.sent = [copy for copy in self.sent if id(copy) not in done]

    def finish(self):
        for copy in self.sent:
            copy.wait_send()


def take_turns(*parts):
    live = list(parts)
    while live:
        still = []
        for part in live:
            try:
                next(part)
                still.append(part)
            except StopIteration:
                pass
        live = still


def follow(plan, works, moves):
    for name in plan:
        if name in works:
            works[name]()
        else:
            next(moves[name], None)
    take_turns(*moves.values())


def comm_call(body, ins, outs, scratch, cid, copies, locals_, name, flops=0):
    n_in, n_out, n_scr = len(ins), len(outs), len(scratch)

    def kernel(*refs):
        in_refs = refs[:n_in]
        out_refs = refs[n_in : n_in + n_out]
        scr = refs[n_in + n_out : n_in + n_out + n_scr]
        send, recv, local = refs[n_in + n_out + n_scr :]
        net = Net(send, recv, local)
        body(net, in_refs, out_refs, scr)
        net.finish()
        assert net.used <= copies and net.used_local <= locals_, (net.used, net.used_local)

    return pl.pallas_call(
        kernel,
        out_shape=outs,
        in_specs=[pl.BlockSpec(memory_space=pl.ANY)] * n_in,
        out_specs=[pl.BlockSpec(memory_space=pl.ANY)] * n_out,
        scratch_shapes=list(scratch)
        + [
            pltpu.SemaphoreType.DMA((copies,)),
            pltpu.SemaphoreType.DMA((copies,)),
            pltpu.SemaphoreType.DMA((max(locals_, 1),)),
        ],
        compiler_params=pltpu.CompilerParams(
            collective_id=cid, has_side_effects=True, vmem_limit_bytes=63 * 2**20
        ),
        name=name,
    )(*ins)


def gather_narrow(net, own, out):
    x, z, y, c = here()
    rows = own.shape[0]
    half = rows // 2

    def block(dy, lo=0, size=rows):
        return out.at[span((wrap(y + dy) * 2 + c) * rows + lo, size)]

    first, last = own.at[pl.ds(0, half)], own.at[pl.ds(half, half)]
    up = net.put(first, block(0, 0, half), moved(dy=1))
    down = net.put(last, block(0, half, half), moved(dy=-1))
    up_late = net.put(last, block(0, half, half), moved(dy=1))
    down_late = net.put(first, block(0, 0, half), moved(dy=-1))
    across = [net.put(own, block(0), moved(dc=1))]
    mine = net.keep(own, block(0))
    yield
    mine.wait()
    across[0].wait_recv()
    yield
    up.wait_recv()
    on = net.put(block(-1, 0, half), block(-1, 0, half), moved(dy=1))
    down.wait_recv()
    back = net.put(block(1, half, half), block(1, half, half), moved(dy=-1))
    yield
    up_late.wait_recv()
    across.append(net.put(block(-1), block(-1), moved(dc=1)))
    down_late.wait_recv()
    across.append(net.put(block(1), block(1), moved(dc=1)))
    across[1].wait_recv()
    across[2].wait_recv()
    yield
    on.wait_recv()
    across.append(net.put(block(2, 0, half), block(2, 0, half), moved(dc=1)))
    back.wait_recv()
    across.append(net.put(block(2, half, half), block(2, half, half), moved(dc=1)))
    yield
    across[3].wait_recv()
    across[4].wait_recv()
    yield
    net.sent_by(up, down, up_late, down_late, on, back, *across)


GATHER_COPIES = 12


def gather_small(net, own, out):
    c = here()[3]
    y = here()[2]
    rows = own.shape[0]

    def block(dy):
        return out.at[span((wrap(y + dy) * 2 + c) * rows, rows)]

    along = [net.put(own, block(0), moved(dy=d)) for d in (2, 1, 3)]
    across = [net.put(own, block(0), moved(dc=1))]
    mine = net.keep(own, block(0))
    yield
    for copy, d in zip(along, (2, 1, 3)):
        copy.wait_recv()
        across.append(net.put(block(-d), block(-d), moved(dc=1)))
    yield
    mine.wait()
    for copy in across:
        copy.wait_recv()


GATHER_SMALL_COPIES = 7


def gather_call(own, cid, name):
    rows, cols = own.shape

    def body(net, ins, outs, scr):
        greet(NEAR_Y)
        take_turns(gather_narrow(net, ins[0], outs[0]))

    return comm_call(
        body,
        [own],
        [jax.ShapeDtypeStruct((NARROW * rows, cols), own.dtype)],
        [],
        cid,
        GATHER_COPIES,
        1,
        name,
    )[0]


def reduce_scratch(rows, cols):
    return [
        pltpu.VMEM((SIDE, rows, cols), BF),
        pltpu.VMEM((SIDE, rows, cols), BF),
        pltpu.VMEM((2, rows // 2, cols), BF),
        pltpu.VMEM((2, rows, cols), BF),
        pltpu.VMEM((3, rows, cols), BF),
        pltpu.VMEM((rows, cols), F32),
    ]


REDUCE_COPIES = 10
REDUCE_LOCALS = 5


def reduce_narrow(net, part, out, scr):
    own, other, through, landed, ready, total = scr
    x, z, y, c = here()
    rows, cols = out.shape
    half = rows // 2

    def block(dy, core):
        return part.at[span((wrap(y + dy) * 2 + core) * rows, rows)]

    order = (2, 1, 3, 0)
    local, cross = {}, {}
    for dy in order:
        cross[dy] = net.put(block(dy, 1 - c), other.at[dy], moved(dc=1))
        local[dy] = net.keep(block(dy, c), own.at[dy])

    def pair(dy, lo, size):
        s = span(lo, size)
        return own[dy, s, :].astype(F32) + other[dy, s, :].astype(F32)

    yield
    local[2].wait()
    cross[2].wait_recv()
    ready[0] = pair(2, 0, rows).astype(BF)
    first, last = span(0, half), span(half, half)
    via_up = net.put(ready.at[0, first], through.at[0], moved(dy=1))
    via_down = net.put(ready.at[0, last], through.at[1], moved(dy=-1))
    yield
    local[1].wait()
    cross[1].wait_recv()
    ready[1, last, :] = pair(1, half, half).astype(BF)
    up_late = net.put(ready.at[1, last], landed.at[0, last], moved(dy=1))
    local[3].wait()
    cross[3].wait_recv()
    ready[2, first, :] = pair(3, 0, half).astype(BF)
    down_first = net.put(ready.at[2, first], landed.at[1, first], moved(dy=-1))
    yield
    via_up.wait_recv()
    ready[1, first, :] = (pair(1, 0, half) + through[0].astype(F32)).astype(BF)
    up_first = net.put(ready.at[1, first], landed.at[0, first], moved(dy=1))
    via_down.wait_recv()
    ready[2, last, :] = (pair(3, half, half) + through[1].astype(F32)).astype(BF)
    down_late = net.put(ready.at[2, last], landed.at[1, last], moved(dy=-1))
    yield
    local[0].wait()
    cross[0].wait_recv()
    total[...] = pair(0, 0, rows)
    yield
    for copy in (up_late, down_first, up_first, down_late):
        copy.wait_recv()
    total[...] += landed[0].astype(F32) + landed[1].astype(F32)
    done = net.keep(total, out)
    yield
    done.wait()


def pairs_scratch(rows, cols):
    return [
        pltpu.VMEM((SIDE * 2 * rows, cols), BF),
        pltpu.VMEM((SIDE, rows, cols), BF),
        pltpu.VMEM((2, rows // 2, cols), BF),
        pltpu.VMEM((2, rows, cols), BF),
        pltpu.VMEM((3, rows, cols), BF),
        pltpu.VMEM((rows, cols), F32),
    ]


PAIR_ORDER = (2, 1, 3, 0)


class Pairs:
    def __init__(self, net, out, scr):
        self.net, self.out, self.scr = net, out, scr
        self.crossed = {}

    def store(self, dy, value):
        rows = value.shape[0]
        self.scr[0][pl.ds(dy * rows, rows), :] = value.astype(BF)

    def cross(self, dy):
        parts, other = self.scr[:2]
        c = here()[3]
        rows = other.shape[1]
        self.crossed[dy] = self.net.put(
            parts.at[span((2 * dy + 1 - c) * rows, rows)], other.at[dy], moved(dc=1)
        )

    def steps(self):
        net = self.net
        parts, other, through, landed, ready, total = self.scr
        c = here()[3]
        rows = total.shape[0]
        half = rows // 2
        first, last = pl.ds(0, half), pl.ds(half, half)

        def pair(dy, lo, size):
            mine = parts[span((2 * dy + c) * rows + lo, size), :].astype(F32)
            return mine + other[dy, pl.ds(lo, size), :].astype(F32)

        self.crossed[2].wait_recv()
        ready[0] = pair(2, 0, rows).astype(BF)
        via_up = net.put(ready.at[0, first], through.at[0], moved(dy=1))
        via_down = net.put(ready.at[0, last], through.at[1], moved(dy=-1))
        yield
        self.crossed[1].wait_recv()
        ready[1, last, :] = pair(1, half, half).astype(BF)
        up_late = net.put(ready.at[1, last], landed.at[0, last], moved(dy=1))
        yield
        self.crossed[3].wait_recv()
        ready[2, first, :] = pair(3, 0, half).astype(BF)
        down_first = net.put(ready.at[2, first], landed.at[1, first], moved(dy=-1))
        yield
        via_up.wait_recv()
        ready[1, first, :] = (pair(1, 0, half) + through[0].astype(F32)).astype(BF)
        up_first = net.put(ready.at[1, first], landed.at[0, first], moved(dy=1))
        via_down.wait_recv()
        ready[2, last, :] = (pair(3, half, half) + through[1].astype(F32)).astype(BF)
        down_late = net.put(ready.at[2, last], landed.at[1, last], moved(dy=-1))
        yield
        self.crossed[0].wait_recv()
        total[...] = pair(0, 0, rows)
        yield
        for copy in (up_late, down_first, up_first, down_late):
            copy.wait_recv()
        total[...] += landed[0].astype(F32) + landed[1].astype(F32)
        done = net.keep(total, self.out)
        yield
        done.wait()


def spread_narrow(net, src, slab):
    w = lax.axis_index("wide")
    n = lax.axis_index("narrow")
    base = n * ROWS if slab.shape[0] == TOK else w * TOK + n * ROWS
    mine = net.keep(src.at[n], slab.at[span(base, ROWS)])
    copies = []
    for p in NARROW_ALL:
        target = moved(**p)
        copies.append(net.put(src.at[target[1]], slab.at[span(base, ROWS)], target))
    yield
    mine.wait()
    for copy in copies:
        copy.wait_recv()


SPREAD_COPIES = 7


def gather_wide(net, slab, lead, stage=None):
    x, z, y, c = here()
    rows = TOK // 2
    half = rows // 2
    low = 0 if lead == "x" else rows

    def block(a, b, lo=0, size=rows):
        px, pz = (a, b) if lead == "x" else (b, a)
        return slab.at[span((wrap(x + px) * SIDE + wrap(z + pz)) * TOK + low + lo, size)]

    def lead_to(d):
        return moved(dx=d) if lead == "x" else moved(dz=d)

    def then_to(d):
        return moved(dz=d) if lead == "x" else moved(dx=d)

    def both(src, to, dst=None):
        dst = src if dst is None else dst
        return net.put(src, dst, to(1)), net.put(src, dst, to(-1))

    mine = block(0, 0) if stage is None else stage.at[pl.ds(low, rows)]
    fore, aft = both(mine, lead_to, block(0, 0))
    second = {0: both(mine, then_to, block(0, 0))}
    yield
    fore.wait_recv()
    on = net.put(block(-1, 0, 0, half), block(-1, 0, 0, half), lead_to(1))
    second[-1] = both(block(-1, 0), then_to)
    aft.wait_recv()
    back = net.put(block(1, 0, half, half), block(1, 0, half, half), lead_to(-1))
    second[1] = both(block(1, 0), then_to)
    yield
    last = []

    def relay(a):
        f, b = second[a]
        f.wait_recv()
        last.append(net.put(block(a, -1, 0, half), block(a, -1, 0, half), then_to(1)))
        b.wait_recv()
        last.append(net.put(block(a, 1, half, half), block(a, 1, half, half), then_to(-1)))

    kept = None if stage is None else net.keep(mine, block(0, 0))
    relay(0)
    yield
    on.wait_recv()
    back.wait_recv()
    second[2] = both(block(2, 0), then_to)
    yield
    relay(-1)
    relay(1)
    yield
    relay(2)
    yield
    if kept is not None:
        kept.wait()
    for copy in last:
        copy.wait_recv()


WIDE_COPIES = 20


def turn(values, cosine, sine):
    return values * cosine + pltpu.roll(values, HEAD_DIM // 2, 1) * sine


def allowed_keys(first_row, rows, first_length):
    query = first_row + lax.broadcasted_iota(jnp.int32, (rows, 1), 0)
    key = lax.broadcasted_iota(jnp.int32, (rows, GROUP), 1)
    start = jnp.where(query >= first_length, first_length, 0)
    return (key <= query) & (key >= start)


PICK_ATTN, PICK_FFN, GATE_FFN = 0, 32, 64


def branch_mask(marks, lane):
    n = lax.axis_index("narrow").astype(F32)
    return (n < 2.0 * (marks[:, lane : lane + 1] + 1.0)).astype(F32)


def attention_forward(normed_own, source_a, source_b, turns, first_length, marks, upstream, cid):
    pair_rows = 2 * TOK
    head_part = D // NARROW

    def body(net, ins, outs, scr):
        normed_own, source_a, source_b, turns, first_length, marks, upstream = ins
        attn_sum, q_out, k_out, v_out, p_out, a_out, g_out, slab_a, slab_b, normed, marks_out = outs
        xv, wv, tv, lv, mv, qv, kv, vv, pv, av = scr[:10]
        stage = scr[-1]
        x, z, y, c = here()
        loads = [net.keep(turns, tv), net.keep(first_length, lv)]
        greet(NARROW_ALL + NEAR_XZ)
        sums = Pairs(net, attn_sum, scr[10:16])
        stores = []
        moves = dict(
            sa=spread_narrow(net, source_a, wv),
            sb=spread_narrow(net, source_b, stage),
            gx=gather_narrow(net, normed_own, xv),
            gm=gather_narrow(net, marks, mv),
            gg=gather_narrow(net, upstream, g_out),
            wa=side_by_side(*[gather_wide(net, wv, lead) for lead in "xz"]),
            wb=side_by_side(*[gather_wide(net, slab_b, lead, stage) for lead in "xz"]),
            total=sums.steps(),
        )

        def project():
            stores.extend([net.keep(xv, normed), net.keep(wv, slab_a)])
            for load in loads:
                load.wait()

            @pl.loop(0, SIDE)
            def _(i):
                r = span(i * pair_rows, pair_rows)
                proj = jnp.dot(xv[r, :], wv[:, : 3 * head_part], preferred_element_type=F32)
                cosine, sine = tv[0, r, :], tv[1, r, :]
                for h in range(2):
                    at = pl.ds(h * HEAD_DIM, HEAD_DIM)
                    a = h * HEAD_DIM
                    qv[r, at] = turn(proj[:, a : a + HEAD_DIM], cosine, sine).astype(BF)
                    a += head_part
                    kv[r, at] = turn(proj[:, a : a + HEAD_DIM], cosine, sine).astype(BF)
                vv[r, :] = proj[:, 2 * head_part :].astype(BF)

            stores.extend([net.keep(qv, q_out), net.keep(kv, k_out), net.keep(vv, v_out)])

        def attend(dy):
            first = wrap(y + dy) * pair_rows
            r = span(first, pair_rows)
            allowed = allowed_keys(first, pair_rows, lv[0:1, 0:1])
            heads = []
            for h in range(2):
                at = pl.ds(h * HEAD_DIM, HEAD_DIM)
                scores = lax.dot_general(
                    qv[r, at], kv[:, at], CONTRACT_COLS, preferred_element_type=F32
                )
                scores = jnp.where(allowed, scores * HEAD_DIM ** (-0.5), -1e30)
                expo = jnp.exp(scores - jnp.max(scores, axis=-1, keepdims=True))
                probs = expo * (1.0 / jnp.sum(expo, axis=-1, keepdims=True))
                low = probs.astype(BF)
                pv[r, pl.ds(h * GROUP, GROUP)] = low
                heads.append(jnp.dot(low, vv[:, at], preferred_element_type=F32))
            mask = branch_mask(mv[r, :], PICK_ATTN)
            av[r, :] = (jnp.concatenate(heads, axis=1) * mask).astype(BF)
            back = lax.dot_general(
                av[r, :], wv[:, 3 * head_part :], CONTRACT_COLS, preferred_element_type=F32
            )
            sums.store(dy, back)
            sums.cross(dy)

        works = dict(Q=project)
        for dy in PAIR_ORDER:
            works[f"T{dy}"] = functools.partial(attend, dy)
        follow(FORWARD_PLAN, works, moves)
        stores += [net.keep(pv, p_out), net.keep(av, a_out), net.keep(mv, marks_out)]
        for store in stores:
            store.wait()

    low = jax.ShapeDtypeStruct((GROUP, head_part), BF)
    return comm_call(
        body,
        [normed_own, source_a, source_b, turns, first_length, marks, upstream],
        [
            jax.ShapeDtypeStruct((TOK, D), F32),
            low,
            low,
            low,
            jax.ShapeDtypeStruct((GROUP, 2 * GROUP), BF),
            low,
            jax.ShapeDtypeStruct((GROUP, D), BF),
            jax.ShapeDtypeStruct((D, source_a.shape[2]), BF),
            jax.ShapeDtypeStruct((D, source_b.shape[2]), BF),
            jax.ShapeDtypeStruct((GROUP, D), BF),
            jax.ShapeDtypeStruct((GROUP, 128), F32),
        ],
        [
            pltpu.VMEM((GROUP, D), BF),
            pltpu.VMEM((D, source_a.shape[2]), BF),
            pltpu.VMEM(turns.shape, F32),
            pltpu.VMEM(first_length.shape, jnp.int32),
            pltpu.VMEM((GROUP, 128), F32),
            pltpu.VMEM((GROUP, head_part), BF),
            pltpu.VMEM((GROUP, head_part), BF),
            pltpu.VMEM((GROUP, head_part), BF),
            pltpu.VMEM((GROUP, 2 * GROUP), BF),
            pltpu.VMEM((GROUP, head_part), BF),
        ]
        + pairs_scratch(TOK, D)
        + [pltpu.VMEM((TOK, source_b.shape[2]), BF)],
        cid,
        REDUCE_COPIES + 4 * WIDE_COPIES + 3 * GATHER_COPIES + 2 * SPREAD_COPIES,
        2 + 2 + 3 + 2 + 2 + 3 + 1 + 2 + 1,
        "attention_forward",
    )


def first_scratch(cols):
    part, half = TOK // 2, TOK // 4
    return [
        pltpu.VMEM((2, 2, SIDE, half, cols), BF),
        pltpu.VMEM((2, 2, SIDE, part, cols), BF),
        pltpu.VMEM((2, 2, SIDE, half, cols), BF),
        pltpu.VMEM((2, SIDE, part, cols), BF),
    ]


def second_scratch(cols):
    part, half = TOK // 2, TOK // 4
    return [
        pltpu.VMEM((2, 2, half, cols), BF),
        pltpu.VMEM((2, 2, part, cols), BF),
        pltpu.VMEM((2, 2, half, cols), BF),
        pltpu.VMEM((TOK, cols), BF),
    ]


FIRST_COPIES = 12
SECOND_COPIES = 12
FIRST_LOCALS = 6


def lead_moves(lead):
    def lead_to(d):
        return moved(dx=d) if lead == "x" else moved(dz=d)

    def then_to(d):
        return moved(dz=d) if lead == "x" else moved(dx=d)

    return lead_to, then_to


def reduce_first(net, grad, scr, lead):
    via, landed, ready, sums = scr
    x, z, y, c = here()
    part, half = TOK // 2, TOK // 4
    k = 0 if lead == "x" else 1
    low = k * part
    blocks = grad.reshape(SIDE, SIDE, TOK, grad.shape[1])
    first, last = pl.ds(0, half), pl.ds(half, half)
    lead_to, _ = lead_moves(lead)

    def line(d, lo, size):
        rows = pl.ds(low + lo, size)
        if lead == "x":
            return (wrap(x + d), slice(None), rows, slice(None))
        return (slice(None), wrap(z + d), rows, slice(None))

    via_up = net.put(blocks.at[line(2, 0, half)], via.at[k, 0], lead_to(1))
    via_down = net.put(blocks.at[line(2, half, half)], via.at[k, 1], lead_to(-1))
    up_late = net.put(blocks.at[line(1, half, half)], landed.at[k, 0, :, last], lead_to(1))
    down_first = net.put(blocks.at[line(3, 0, half)], landed.at[k, 1, :, first], lead_to(-1))
    loads = [
        net.keep(blocks.at[line(1, 0, half)], ready.at[k, 0]),
        net.keep(blocks.at[line(3, half, half)], ready.at[k, 1]),
        net.keep(blocks.at[line(0, 0, part)], sums.at[k]),
    ]
    yield
    for load in loads:
        load.wait()
    via_up.wait_recv()

    @pl.loop(0, SIDE)
    def _(i):
        ready[k, 0, i] = (ready[k, 0, i].astype(F32) + via[k, 0, i].astype(F32)).astype(BF)

    up_first = net.put(ready.at[k, 0], landed.at[k, 0, :, first], lead_to(1))
    via_down.wait_recv()

    @pl.loop(0, SIDE)
    def _(i):
        ready[k, 1, i] = (ready[k, 1, i].astype(F32) + via[k, 1, i].astype(F32)).astype(BF)

    down_late = net.put(ready.at[k, 1], landed.at[k, 1, :, last], lead_to(-1))
    yield
    for copy in (up_late, down_first, up_first, down_late):
        copy.wait_recv()

    @pl.loop(0, SIDE)
    def _(i):
        both = landed[k, 0, i].astype(F32) + landed[k, 1, i].astype(F32)
        sums[k, i] = (sums[k, i].astype(F32) + both).astype(BF)


def reduce_second(net, sums, scr, lead):
    via, landed, ready, total = scr
    x, z, y, c = here()
    part, half = TOK // 2, TOK // 4
    k = 0 if lead == "x" else 1
    first, last = pl.ds(0, half), pl.ds(half, half)
    _, then_to = lead_moves(lead)
    me = z if lead == "x" else x

    def block(d, rows):
        return sums.at[k, wrap(me + d), rows]

    via_up = net.put(block(2, first), via.at[k, 0], then_to(1))
    via_down = net.put(block(2, last), via.at[k, 1], then_to(-1))
    up_late = net.put(block(1, last), landed.at[k, 0, last], then_to(1))
    down_first = net.put(block(3, first), landed.at[k, 1, first], then_to(-1))
    yield
    via_up.wait_recv()
    ready[k, 0] = (block(1, first)[...].astype(F32) + via[k, 0].astype(F32)).astype(BF)
    up_first = net.put(ready.at[k, 0], landed.at[k, 0, first], then_to(1))
    via_down.wait_recv()
    ready[k, 1] = (block(3, last)[...].astype(F32) + via[k, 1].astype(F32)).astype(BF)
    down_late = net.put(ready.at[k, 1], landed.at[k, 1, last], then_to(-1))
    yield
    for copy in (up_late, down_first, up_first, down_late):
        copy.wait_recv()
    both = landed[k, 0].astype(F32) + landed[k, 1].astype(F32)
    total[pl.ds(k * part, part), :] = (sums[k, me].astype(F32) + both).astype(BF)


def side_by_side(*parts):
    while True:
        if StopIteration in [next(part, StopIteration) for part in parts]:
            break
        yield


def return_narrow(net, total, out, pieces):
    n = lax.axis_index("narrow")
    copies, mine = [], []
    for start, width, to in pieces:
        spot = out.at[:, lanes(to + n * width, width)]
        columns = pl.ds(start, width)
        for p in NARROW_ALL:
            target = moved(**p)
            copies.append(net.put(total.at[span(target[1] * ROWS, ROWS), columns], spot, target))
        mine.append(net.keep(total.at[span(n * ROWS, ROWS), columns], spot))
    yield
    for copy in mine:
        copy.wait()
    for copy in copies:
        copy.wait_recv()


def second_then_narrow(net, sums, out, scr, pieces):
    yield from side_by_side(*[reduce_second(net, sums, scr, lead) for lead in "xz"])
    yield from return_narrow(net, scr[3], out, pieces)


def wide_then_narrow(net, grad, out, scr, pieces):
    yield from side_by_side(*[reduce_first(net, grad, scr[:4], lead) for lead in "xz"])
    yield from second_then_narrow(net, scr[3], out, scr[4:], pieces)


def feed_forward(normed_own, upstream, slab, marks, cid):
    pair_rows = 2 * TOK
    units = FF // NARROW
    strip = 256

    def body(net, ins, outs, scr):
        own, upstream, slab, marks = ins
        norm_sum, ffn_part, g_up, down_sums, gate_out = outs
        xv, dv, w_up, w_down, mv, act, du, da, gu, gd, yv = scr[:11]
        gated, dots, dots_in, dots_sum = scr[17:21]
        n = lax.axis_index("narrow")
        x, z, y, c = here()
        loads = [
            net.keep(upstream, dv),
            net.keep(slab.at[:, pl.ds(units, units)], w_down),
            net.keep(slab.at[:, pl.ds(0, units)], w_up),
            net.keep(marks, mv),
        ]
        greet(NARROW_ALL + NEAR_XZ)
        sums = Pairs(net, norm_sum, scr[11:17])
        ones = jnp.ones((8, units), BF)
        stores, dot_copies = [], []

        def gradient(left, right, to):
            @pl.loop(0, D // strip)
            def _(i):
                at = lanes(i * strip, strip)
                to[span(i * strip, strip), :] = lax.dot_general(
                    left[:, at], right[...], CONTRACT_ROWS, preferred_element_type=F32
                ).astype(BF)

        def down_back():
            loads[0].wait()
            loads[1].wait()

            @pl.loop(0, SIDE)
            def _(i):
                r = span(i * pair_rows, pair_rows)
                da[r, :] = jnp.dot(dv[r, :], w_down[...], preferred_element_type=F32)

            loads[2].wait()
            loads[3].wait()

        def units_of(dy):
            r = span(wrap(y + dy) * pair_rows, pair_rows)
            up = jnp.dot(xv[r, :], w_up[...], preferred_element_type=F32)
            positive = jnp.maximum(up, 0.0)
            masked = positive * branch_mask(mv[r, :], PICK_FFN)
            gate = mv[r, GATE_FFN : GATE_FFN + 1]
            active = positive * masked
            act[r, :] = active.astype(BF)
            gated[r, :] = (active * gate).astype(BF)
            back = da[r, :]
            du[r, :] = (back * (2.0 * gate * masked)).astype(BF)
            dot = lax.dot_general(
                ones, (back * active).astype(BF), CONTRACT_COLS, preferred_element_type=F32
            )
            for core in range(2):
                dots[wrap(y + dy) * 2 + core] = dot[:, core * TOK : (core + 1) * TOK]

        def norm_back(dy):
            r = span(wrap(y + dy) * pair_rows, pair_rows)
            back = lax.dot_general(
                du[r, :], w_up[...], CONTRACT_COLS, preferred_element_type=F32
            )
            sums.store(dy, back)
            sums.cross(dy)

        def send_dots():
            for p in NARROW_ALL:
                target = moved(**p)
                dot_copies.append(net.put(dots.at[target[1]], dots_in.at[n], target))
            dots_in[n] = dots[n]

        def up_gradient():
            gradient(xv, du, gu)
            stores.append(net.keep(gu, g_up))

        def output():
            @pl.loop(0, SIDE)
            def _(i):
                r = span(i * pair_rows, pair_rows)
                yv[r, :] = lax.dot_general(
                    act[r, :], w_down[...], CONTRACT_COLS, preferred_element_type=F32
                ).astype(BF)

            stores.append(net.keep(yv, ffn_part))

        def take_dots():
            for copy in dot_copies:
                copy.wait_recv()
            s = dots_in[0]
            for i in range(1, NARROW):
                s = s + dots_in[i]
            dots_sum[...] = s
            stores.append(net.keep(dots_sum, gate_out))

        works = dict(
            DA=down_back,
            GD=functools.partial(gradient, dv, gated, gd),
            GU=up_gradient,
            YF=output,
            DS=send_dots,
            DT=take_dots,
        )
        for dy in PAIR_ORDER:
            works[f"U{dy}"] = functools.partial(units_of, dy)
            works[f"N{dy}"] = functools.partial(norm_back, dy)
        moves = dict(
            gather=gather_narrow(net, own, xv),
            total=sums.steps(),
            wide=side_by_side(*[reduce_first(net, gd, scr[21:], lead) for lead in "xz"]),
        )
        follow(FEED_PLAN, works, moves)
        stores.append(net.keep(scr[24], down_sums))
        for store in stores:
            store.wait()

    wide = pltpu.VMEM((GROUP, D), BF)
    tall = pltpu.VMEM((D, units), BF)
    square = pltpu.VMEM((GROUP, units), BF)
    return comm_call(
        body,
        [normed_own, upstream, slab, marks],
        [
            jax.ShapeDtypeStruct((TOK, D), F32),
            jax.ShapeDtypeStruct((GROUP, D), BF),
            jax.ShapeDtypeStruct((D, units), BF),
            jax.ShapeDtypeStruct((2, SIDE, TOK // 2, units), BF),
            jax.ShapeDtypeStruct((8, TOK), F32),
        ],
        [wide, wide, tall, tall, pltpu.VMEM(marks.shape, F32), square, square]
        + [pltpu.VMEM((GROUP, units), F32), tall, tall, wide]
        + pairs_scratch(TOK, D)
        + [square]
        + [pltpu.VMEM((NARROW, 8, TOK), F32)] * 2
        + [pltpu.VMEM((8, TOK), F32)]
        + first_scratch(units),
        cid,
        GATHER_COPIES + REDUCE_COPIES + 7 + FIRST_COPIES,
        4 + 1 + 1 + 4 + FIRST_LOCALS,
        "feed_forward",
    )


def attention_backward(d_attn_own, ffn_part, g_up, down_sums, normed, hidden_own, kept, cid):
    table_rows = D // NARROW
    pair_rows = 2 * TOK
    head_part = D // NARROW
    units = FF // NARROW
    strip = 256
    scale = HEAD_DIM ** (-0.5)
    scratch = (
        [pltpu.VMEM(r.shape, r.dtype) for r in kept]
        + [
            pltpu.VMEM((GROUP, D), BF),
            pltpu.VMEM((GROUP, head_part), F32),
            pltpu.VMEM((GROUP, head_part), F32),
            pltpu.VMEM((GROUP, 3 * head_part), BF),
            pltpu.VMEM((D, 4 * head_part), BF),
        ]
        + pairs_scratch(TOK, D)[1:]
        + reduce_scratch(TOK, D)
        + first_scratch(4 * head_part)
        + second_scratch(4 * head_part)
        + first_scratch(units)
        + second_scratch(units)
        + [pltpu.VMEM(down_sums.shape, BF)]
        + second_scratch(units)
        + [
            pltpu.VMEM((GROUP, table_rows), BF),
            pltpu.VMEM((GROUP, RH), BF),
            pltpu.VMEM((table_rows, RH), BF),
            pltpu.VMEM((WIDE, ROWS, RH), BF),
            pltpu.VMEM((ROWS, RH), BF),
            pltpu.VMEM((table_rows, RH), BF),
        ]
    )

    def body(net, ins, outs, scr):
        d_attn_own, ffn_part, g_up, down_sums, normed, hidden_own = ins[:6]
        norm_sum, ffn_sum, block, table = outs
        wv, tv, mv, qv, kv, vv, pv, av = scr[:8]
        big, dk, dv, dproj, ga = scr[8:13]
        pairs, narrow = [big, *scr[13:18]], scr[18:24]
        wide_a, wide_up, wide_down = scr[24:32], scr[32:40], scr[40:45]
        columns, hidden, part, landed, shard, mine = scr[45:51]
        n = lax.axis_index("narrow")
        x, z, y, c = here()
        first_load = net.keep(down_sums, wide_down[0])
        loads = [net.keep(a, b) for a, b in zip(ins[6:], scr[:8])]
        loads.append(net.keep(normed.at[:, lanes(n * table_rows, table_rows)], columns))
        greet(NARROW_ALL + WIDE_ALL)
        sums = Pairs(net, norm_sum, pairs)
        quarter = [(i * head_part, head_part, i * D) for i in range(4)]

        def router():
            yield from gather_small(net, hidden_own, hidden)
            w = lax.axis_index("wide")
            part[...] = lax.dot_general(
                columns[...], hidden[...], CONTRACT_ROWS, preferred_element_type=F32
            ).astype(BF)
            copies = []
            for p in WIDE_ALL:
                target = moved(**p)
                rows = part.at[span(target[0] * ROWS, ROWS)]
                copies.append(net.put(rows, landed.at[w], target))
            kept = net.keep(part.at[span(w * ROWS, ROWS)], landed.at[w])
            yield
            kept.wait()
            for copy in copies:
                copy.wait_recv()
            s = landed[0].astype(F32)
            for i in range(1, WIDE):
                s = s + landed[i].astype(F32)
            shard[...] = s.astype(BF)
            spot = mine.at[span(w * ROWS, ROWS)]
            copies = [net.put(shard, spot, moved(**p)) for p in WIDE_ALL]
            kept = net.keep(shard, spot)
            yield
            kept.wait()
            for copy in copies:
                copy.wait_recv()
            yield from gather_small(net, mine, table)

        moves = dict(
            gather=gather_narrow(net, d_attn_own, big),
            down=second_then_narrow(
                net, wide_down[0], block, wide_down[1:], [(0, units, 4 * D + FF)]
            ),
            up=wide_then_narrow(net, g_up, block, wide_up, [(0, units, 4 * D)]),
            mixed=wide_then_narrow(net, ga, block, wide_a, quarter),
            feed=reduce_narrow(net, ffn_part, ffn_sum, narrow),
            gates=router(),
            total=sums.steps(),
        )

        def wait_loads():
            first_load.wait()
            for load in loads:
                load.wait()
            dk[...] = jnp.zeros_like(dk)
            dv[...] = jnp.zeros_like(dv)

        def one_pair(dy):
            r = span(wrap(y + dy) * pair_rows, pair_rows)
            mask = branch_mask(mv[r, :], PICK_ATTN)
            back = jnp.dot(big[r, :], wv[:, 3 * head_part :], preferred_element_type=F32)
            back = (back * mask).astype(BF)
            for h in range(2):
                at = pl.ds(h * HEAD_DIM, HEAD_DIM)
                d_out = back[:, h * HEAD_DIM : (h + 1) * HEAD_DIM]
                d_probs = lax.dot_general(
                    d_out, vv[:, at], CONTRACT_COLS, preferred_element_type=F32
                )
                probs_low = pv[r, pl.ds(h * GROUP, GROUP)]
                probs = probs_low.astype(F32)
                weighted = probs * d_probs
                centre = jnp.sum(weighted, axis=-1, keepdims=True)
                ds = (weighted - probs * centre).astype(BF)
                dq = jnp.dot(ds, kv[:, at], preferred_element_type=F32) * scale
                dproj[r, at] = turn(dq, tv[0, r, :], -tv[1, r, :]).astype(BF)
                dk[:, at] += lax.dot_general(
                    ds, qv[r, at], CONTRACT_ROWS, preferred_element_type=F32
                )
                dv[:, at] += lax.dot_general(
                    probs_low, d_out, CONTRACT_ROWS, preferred_element_type=F32
                )

        refill = []

        def turn_back():
            refill.append(net.keep(normed, pv))

            @pl.loop(0, SIDE)
            def _(i):
                r = span(i * pair_rows, pair_rows)
                cosine, sine = tv[0, r, :], -tv[1, r, :]
                for h in range(2):
                    at = pl.ds(h * HEAD_DIM, HEAD_DIM)
                    to = pl.ds(head_part + h * HEAD_DIM, HEAD_DIM)
                    dproj[r, to] = turn(dk[r, at] * scale, cosine, sine).astype(BF)
                dproj[r, pl.ds(2 * head_part, head_part)] = dv[r, :].astype(BF)

        def gradient(left, right, start, width):
            @pl.loop(0, D // strip)
            def _(i):
                ga[span(i * strip, strip), pl.ds(start, width)] = lax.dot_general(
                    left[:, lanes(i * strip, strip)],
                    right[...],
                    CONTRACT_ROWS,
                    preferred_element_type=F32,
                ).astype(BF)

        def mixed_gradient():
            refill[0].wait()
            gradient(pv, dproj, 0, 3 * head_part)

        def norm_back(dy):
            r = span(wrap(y + dy) * pair_rows, pair_rows)
            back = lax.dot_general(
                dproj[r, :], wv[:, : 3 * head_part], CONTRACT_COLS, preferred_element_type=F32
            )
            sums.store(dy, back)
            sums.cross(dy)

        works = dict(
            LD=wait_loads,
            RT=turn_back,
            GO=functools.partial(gradient, big, av, 3 * head_part, head_part),
            GQ=mixed_gradient,
        )
        for dy in PAIR_ORDER:
            works[f"P{dy}"] = functools.partial(one_pair, dy)
            works[f"N{dy}"] = functools.partial(norm_back, dy)
        follow(BACKWARD_PLAN, works, moves)

    return comm_call(
        body,
        [d_attn_own, ffn_part, g_up, down_sums, normed, hidden_own] + list(kept),
        [
            jax.ShapeDtypeStruct((TOK, D), F32),
            jax.ShapeDtypeStruct((TOK, D), F32),
            jax.ShapeDtypeStruct((ROWS, 4 * D + 2 * FF), BF),
            jax.ShapeDtypeStruct((D, RH), BF),
        ],
        scratch,
        cid,
        GATHER_COPIES
        + 2 * REDUCE_COPIES
        + 2 * FIRST_COPIES
        + 3 * SECOND_COPIES
        + 6 * 7
        + 2 * (15 + GATHER_SMALL_COPIES),
        10 + 1 + 1 + 1 + REDUCE_LOCALS + 2 * FIRST_LOCALS + 6 + 4,
        "attention_backward",
    )


VECTOR_ROWS = 64
GAIN_ROWS = 2 * D // 128
SMALL_ROWS = GAIN_ROWS + RH * 2 * LEVELS // 128
SQUARE_ROWS = 8


def last_sums(vector, block, table, cid):
    def squares_of(ref, rows, cols):
        s = jnp.zeros((SQUARE_ROWS, 128), F32)
        for i in range(ref.shape[0] // rows):
            for j in range(ref.shape[1] // cols):
                piece = ref[i * rows : (i + 1) * rows, j * cols : (j + 1) * cols].astype(F32)
                piece = piece * piece
                for a in range(rows // SQUARE_ROWS):
                    for b in range(cols // 128):
                        s = s + piece[a * 8 : a * 8 + 8, b * 128 : b * 128 + 128]
        return s

    def body(net, ins, outs, scr):
        vec, block, table = ins
        vec_out, norm_out = outs
        own, first, second, total, held, full, norm = scr
        w = lax.axis_index("wide")
        n = lax.axis_index("narrow")
        loads = [net.keep(block, held), net.keep(vec, own), net.keep(table, full)]
        greet(NARROW_ALL + WIDE_ALL)
        loads[0].wait()
        squares = squares_of(held, ROWS, 2048)
        loads[1].wait()
        own[pl.ds(VECTOR_ROWS - SQUARE_ROWS, SQUARE_ROWS), :] = squares
        copies = [net.put(own, first.at[n], moved(**p)) for p in NARROW_ALL]
        mine = net.keep(own, first.at[n])
        loads[2].wait()
        squares = squares_of(full, 128, RH)
        mine.wait()
        for copy in copies:
            copy.wait_recv()
        s = first[0]
        for i in range(1, NARROW):
            s = s + first[i]
        total[0] = s
        copies = [net.put(total.at[0], second.at[w], moved(**p)) for p in WIDE_ALL]
        mine = net.keep(total.at[0], second.at[w])
        mine.wait()
        for copy in copies:
            copy.wait_recv()
        s = second[0]
        for i in range(1, WIDE):
            s = s + second[i]
        total[1] = s
        stores = [net.keep(total.at[1], vec_out)]
        small = s[:SMALL_ROWS]
        sum_all = jnp.sum(small * small) + jnp.sum(s[VECTOR_ROWS - SQUARE_ROWS :] + squares)
        norm[...] = jnp.sqrt(jnp.full((8, 128), sum_all, F32))
        stores.append(net.keep(norm, norm_out))
        for store in stores:
            store.wait()

    rows = VECTOR_ROWS
    return comm_call(
        body,
        [vector, block, table],
        [jax.ShapeDtypeStruct((rows, 128), F32), jax.ShapeDtypeStruct((8, 128), F32)],
        [
            pltpu.VMEM((rows, 128), F32),
            pltpu.VMEM((NARROW, rows, 128), F32),
            pltpu.VMEM((WIDE, rows, 128), F32),
            pltpu.VMEM((2, rows, 128), F32),
            pltpu.VMEM(block.shape, BF),
            pltpu.VMEM(table.shape, BF),
            pltpu.VMEM((8, 128), F32),
        ],
        cid,
        7 + 15,
        7,
        "last_sums",
    )


def adamw_step(master, moment_one, moment_two, grad, norm, tile):
    one_scale = 0.02 / (1.0 - 0.9**STEP)
    two_scale = 1.0 / (1.0 - 0.95**STEP)

    def kernel(w, m, v, g, n, new_w, new_m, new_v, *copy):
        clip = jnp.minimum(1.0, CLIP_NORM / n[0:1, 0:1])
        gradient = g[...].astype(F32) * clip
        one = 0.9 * m[...] + 0.1 * gradient
        two = 0.95 * v[...] + 0.05 * (gradient * gradient)
        new_m[...] = one
        new_v[...] = two
        root = jnp.sqrt(two * two_scale) + 1e-08
        updated = w[...] * (1.0 - 0.02 * 0.1) - (one * one_scale) / root
        new_w[...] = updated
        for ref in copy:
            ref[...] = updated.astype(BF)

    rows, cols = master.shape
    across = cols // tile[1]
    part = pl.BlockSpec(tile, lambda i: (i // across, i % across))
    shape = jax.ShapeDtypeStruct(master.shape, F32)
    low = jax.ShapeDtypeStruct(master.shape, BF)
    outs = [shape, shape, shape] + ([low] if rows == ROWS else [])
    return pl.pallas_call(
        kernel,
        grid=(rows * cols // (tile[0] * tile[1]),),
        out_shape=outs,
        in_specs=[part] * 4 + [pl.BlockSpec((8, 128), lambda i: (0, 0))],
        out_specs=[part] * len(outs),
        name="adamw_step",
    )(master, moment_one, moment_two, grad, norm)


def layer_norm(values, gain_row):
    average = jnp.mean(values, axis=-1, keepdims=True)
    centered = values - average
    spread = jnp.mean(centered * centered, axis=-1, keepdims=True)
    return centered * lax.rsqrt(spread + NORM_EPS) * gain_row


def segment_info(seg_lengths, token_index):
    seg_ends = jnp.cumsum(seg_lengths)
    segment = jnp.sum((token_index[:, None] >= seg_ends[None, :]).astype(jnp.int32), axis=1)
    starts = seg_ends - seg_lengths
    owners = segment[:, None] == jnp.arange(seg_lengths.shape[0], dtype=jnp.int32)[None, :]
    start_of = jnp.sum(jnp.where(owners, starts[None, :], 0), axis=1)
    return (segment, token_index - start_of)


def router_gates(logits, picks):
    levels = jnp.arange(LEVELS, dtype=jnp.int32)
    chosen_attn = (picks[:, 0:1] == levels[None, :]).astype(jnp.float32)
    chosen_ffn = (picks[:, 1:2] == levels[None, :]).astype(jnp.float32)
    gate_attn = float(LEVELS) * jnp.sum(
        jax.nn.softmax(logits[:, :LEVELS], axis=-1) * chosen_attn, axis=-1
    )
    gate_ffn = float(LEVELS) * jnp.sum(
        jax.nn.softmax(logits[:, LEVELS:], axis=-1) * chosen_ffn, axis=-1
    )
    return (gate_attn, gate_ffn)


def adamw(weight, moment_one, moment_two, gradient, step_rate):
    moment_one = 0.9 * moment_one + 0.1 * gradient
    moment_two = 0.95 * moment_two + 0.05 * gradient * gradient
    first_hat = moment_one / (1.0 - 0.9**STEP)
    second_hat = moment_two / (1.0 - 0.95**STEP)
    updated = weight - step_rate * (first_hat / (jnp.sqrt(second_hat) + 1e-08) + 0.1 * weight)
    return (updated, moment_one, moment_two)


def cut(rows, start, width, pieces):
    part = rows[:, start : start + width].reshape(rows.shape[0], pieces, width // pieces)
    return part.transpose(1, 0, 2)


def on_device(
    tokens,
    lengths,
    picks,
    cotangent,
    block_master,
    block_first,
    block_second,
    gains,
    gains_first,
    gains_second,
    router_in,
    router_in_first,
    router_in_second,
    router_out,
    router_out_first,
    router_out_second,
):
    low = block_master.astype(BF)
    source_a = jnp.concatenate([cut(low, i * D, D, NARROW) for i in range(4)], axis=2)
    source_b = jnp.concatenate([cut(low, 4 * D + i * FF, FF, NARROW) for i in range(2)], axis=2)
    inputs = tokens.astype(F32)
    norm_one, norm_one_back = jax.vjp(layer_norm, inputs, gains[0])
    normed_own = norm_one.astype(BF)
    hidden, hidden_back = jax.vjp(jax.nn.gelu, jnp.dot(normed_own.astype(F32), router_in))
    (gate_attn, gate_ffn), gates_back = jax.vjp(
        lambda logits: router_gates(logits, picks), jnp.dot(hidden, router_out)
    )
    upstream = cotangent.astype(F32)
    lane = jnp.arange(128)[None, :]
    marks = jnp.where(
        lane < PICK_FFN,
        picks[:, 0:1].astype(F32),
        jnp.where(lane < GATE_FFN, picks[:, 1:2].astype(F32), gate_ffn[:, None]),
    )

    key_index = jnp.arange(GROUP, dtype=jnp.int32)
    _, key_position = segment_info(lengths[0], key_index)
    half_dim = HEAD_DIM // 2
    frequency = 10000.0 ** (-jnp.arange(half_dim, dtype=F32) / half_dim)
    angles = key_position.astype(F32)[:, None] * frequency[None, :]
    cosine, sine = jnp.cos(angles), jnp.sin(angles)
    turns = jnp.stack(
        [
            jnp.concatenate([cosine, cosine], axis=1),
            jnp.concatenate([-sine, sine], axis=1),
        ]
    )
    first_length = jnp.broadcast_to(lengths[:, 0:1], (8, 128))
    (
        attn_out,
        query_low,
        key_low,
        value_low,
        probs_low,
        mixed_low,
        group_upstream,
        slab_a,
        slab_b,
        normed_low,
        group_marks,
    ) = attention_forward(
        normed_own, source_a, source_b, turns, first_length, marks, cotangent, 1
    )

    after_attn = inputs + gate_attn[:, None] * attn_out
    norm_two, norm_two_back = jax.vjp(layer_norm, after_attn, gains[1])

    d_norm_two, ffn_part, grad_up, down_sums, gate_rows = feed_forward(
        norm_two.astype(BF), group_upstream, slab_b, group_marks, 2
    )
    d_gate_ffn = gate_rows[0]
    d_after, d_gain_two = norm_two_back(d_norm_two)
    d_after = d_after + upstream
    d_gate_attn = jnp.sum(d_after * attn_out, axis=1)
    (d_logits,) = gates_back((d_gate_attn, d_gate_ffn))
    (d_hidden,) = hidden_back(lax.dot_general(d_logits, router_out, CONTRACT_COLS))
    d_normed, ffn_out, block_low, router_in_grad = attention_backward(
        (d_after * gate_attn[:, None]).astype(BF),
        ffn_part,
        grad_up,
        down_sums,
        normed_low,
        d_hidden.astype(BF),
        [slab_a, turns, group_marks, query_low, key_low, value_low, probs_low, mixed_low],
        3,
    )

    result = (after_attn + gate_ffn[:, None] * ffn_out).astype(BF)
    grad_router_out = lax.dot_general(hidden, d_logits, CONTRACT_ROWS)
    d_normed_router = lax.dot_general(d_hidden, router_in, CONTRACT_COLS)
    d_inputs, d_gain_one = norm_one_back(d_normed + d_normed_router)
    d_inputs = d_inputs + d_after

    levels = jnp.arange(LEVELS, dtype=jnp.int32)
    counts_local = [
        jnp.sum((picks[:, b : b + 1] == levels[None, :]).astype(F32), axis=0) for b in range(2)
    ]
    rest = jnp.zeros(((VECTOR_ROWS - SMALL_ROWS) * 128 - 2 * LEVELS,), F32)
    vector = jnp.concatenate(
        [d_gain_one, d_gain_two, grad_router_out.ravel(), *counts_local, rest]
    ).reshape(VECTOR_ROWS, 128)
    vector, norm = last_sums(vector, block_low, router_in_grad, 7)
    gain_grad = vector[:GAIN_ROWS].reshape(2, D)
    router_out_grad = vector[GAIN_ROWS:SMALL_ROWS].reshape(RH, 2 * LEVELS)
    counts = vector[SMALL_ROWS, : 2 * LEVELS].reshape(2, LEVELS)
    grad_norm = norm[0, 0]
    clip_factor = jnp.minimum(1.0, CLIP_NORM / grad_norm)
    new_block, new_block_first, new_block_second, block_copy = adamw_step(
        block_master, block_first, block_second, block_low, norm, (ROWS, 4096)
    )
    new_gains, new_gains_first, new_gains_second = adamw(
        gains, gains_first, gains_second, gain_grad * clip_factor, 0.6
    )
    new_router_in, new_router_in_first, new_router_in_second = adamw_step(
        router_in, router_in_first, router_in_second, router_in_grad, norm, (256, RH)
    )
    new_router_out, new_router_out_first, new_router_out_second = adamw(
        router_out, router_out_first, router_out_second, router_out_grad * clip_factor, 0.02
    )
    return (
        result,
        d_inputs,
        counts,
        grad_norm,
        new_block,
        new_block_first,
        new_block_second,
        block_copy,
        new_gains,
        new_gains_first,
        new_gains_second,
        new_router_in,
        new_router_in_first,
        new_router_in_second,
        new_router_out,
        new_router_out_first,
        new_router_out_second,
    )


def solution(mesh):
    both = P(("wide", "narrow"), None)
    return jax.shard_map(
        on_device,
        mesh=mesh,
        in_specs=(both, P("wide", None)) + (both,) * 5 + (P(),) * 9,
        out_specs=(both, both, P(), P()) + (both,) * 4 + (P(),) * 9,
        check_vma=False,
    )
```

```python
import functools

import jax
import jax.numpy as jnp
import numpy as np
from jax import lax
from jax.experimental import pallas as pl
from jax.experimental.pallas import tpu as pltpu
from jax.sharding import PartitionSpec as P

D = 2048
HEADS = 16
HEAD_DIM = 128
FF = 8192
RH = 256
LEVELS = 4
STEP = 10
TOK = 128
GROUP = 1024
SIDE = 4
WIDE = 16
NARROW = 8
ROWS = 16

NORM_EPS = 1e-05
CLIP_NORM = 1.0
CONTRACT_COLS = (((1,), (1,)), ((), ()))
CONTRACT_ROWS = (((0,), (0,)), ((), ()))
MESH = pl.DeviceIdType.MESH
BF = jnp.bfloat16
F32 = jnp.float32


FORWARD_PLAN = (
    "sa", "L1", "su", "RF", "gm", "sd", "gm", "sa", "wa", "gm", "gx", "wa", "su", "gx", "wa",
    "gm", "gm", "wa", "gx", "wa", "sd", "gg", "sl", "wa", "wu", "gx", "wd", "gx", "gm", "gx",
    "wu", "wa", "TB", "gg", "Q", "wd", "gm", "gg", "T2", "T1", "wd", "total", "T3", "T0",
    "total", "wd", "total", "wd", "gx", "gg", "sl", "gg", "wd", "wu", "total", "wu", "wu", "wd",
    "gg", "DA", "wu", "gg", "total", "total", "LN", "wu", "total", "wu", "gg",
)
FEED_PLAN = (
    "gather", "wu", "wu", "gather", "wu", "wu", "LD", "wu", "gather", "wu", "gather", "wu",
    "U3", "N3", "U0", "gather", "U1", "N1", "gather", "U2", "N2", "total", "total", "GE",
    "more", "total", "DS", "gather", "N0", "GD", "wide", "Y1", "Y2", "Y3", "total", "wide",
    "more", "total", "GU", "Y0", "total", "LB", "wide", "wide", "more", "total",
)
BACKWARD_PLAN = (
    "gather", "gates", "up", "feed", "gather", "gather", "feed", "LD", "P0", "down", "gather",
    "gates", "P3", "up", "gates", "gather", "P1", "gather", "feed", "P2", "down", "RT", "feed",
    "GO", "gather", "up", "gates", "down", "GQ", "mixed", "N2", "N0", "feed", "gates", "feed",
    "up", "N3", "total", "N1", "total", "mixed", "total", "down", "total", "mixed", "up",
    "gates", "mixed", "mixed", "gates", "total", "gates", "up", "total", "LB", "down", "mixed",
    "up", "total",
)


def here():
    w = lax.axis_index("wide")
    n = lax.axis_index("narrow")
    return lax.div(w, SIDE), lax.rem(w, SIDE), lax.div(n, 2), lax.rem(n, 2)


def wrap(i):
    return lax.rem(i + 2 * SIDE, SIDE)


def moved(dx=0, dz=0, dy=0, dc=0):
    x, z, y, c = here()
    return (wrap(x + dx) * SIDE + wrap(z + dz), wrap(y + dy) * 2 + lax.rem(c + dc, 2))


NEAR_Y = [dict(dy=1), dict(dy=-1), dict(dc=1)]
NARROW_ALL = [dict(dy=a, dc=b) for a in range(SIDE) for b in range(2) if a or b]
NEAR_XZ = [dict(dx=1), dict(dx=-1), dict(dz=1), dict(dz=-1)]
LINES_XZ = [dict(dx=a) for a in (1, 2, 3)] + [dict(dz=a) for a in (1, 2, 3)]
WIDE_ALL = [dict(dx=a, dz=b) for a in range(SIDE) for b in range(SIDE) if a or b]


def greet(partners):
    barrier = pltpu.get_barrier_semaphore()
    for p in partners:
        pl.semaphore_signal(barrier, inc=1, device_id=moved(**p), device_id_type=MESH)
    pl.semaphore_wait(barrier, len(partners))


def span(start, size):
    if not isinstance(start, int):
        start = pl.multiple_of(start, ROWS)
    return pl.ds(start, size)


def lanes(start, size):
    if not isinstance(start, int):
        start = pl.multiple_of(start, 128)
    return pl.ds(start, size)


def step(*parts):
    for part in parts:
        next(part, None)


class Net:
    def __init__(self, send, recv, local):
        self.send, self.recv, self.local = send, recv, local
        self.used, self.used_local = 0, 0
        self.sent = []

    def put(self, src, dst, target):
        i = self.used
        self.used += 1
        copy = pltpu.make_async_remote_copy(
            src_ref=src,
            dst_ref=dst,
            send_sem=self.send.at[i],
            recv_sem=self.recv.at[i],
            device_id=target,
            device_id_type=MESH,
        )
        copy.start()
        self.sent.append(copy)
        return copy

    def keep(self, src, dst):
        i = self.used_local
        self.used_local += 1
        copy = pltpu.make_async_copy(src, dst, self.local.at[i])
        copy.start()
        return copy

    def sent_by(self, *copies):
        for copy in copies:
            copy.wait_send()
        done = [id(copy) for copy in copies]
        self.sent = [copy for copy in self.sent if id(copy) not in done]

    def finish(self):
        for copy in self.sent:
            copy.wait_send()


def take_turns(*parts):
    live = list(parts)
    while live:
        still = []
        for part in live:
            try:
                next(part)
                still.append(part)
            except StopIteration:
                pass
        live = still


def follow(plan, works, moves):
    for name in plan:
        if name in works:
            works[name]()
        else:
            next(moves[name], None)
    take_turns(*moves.values())


def comm_call(body, ins, outs, scratch, cid, copies, locals_, name, vmem=63, cost=None):
    n_in, n_out, n_scr = len(ins), len(outs), len(scratch)

    def kernel(*refs):
        in_refs = refs[:n_in]
        out_refs = refs[n_in : n_in + n_out]
        scr = refs[n_in + n_out : n_in + n_out + n_scr]
        send, recv, local = refs[n_in + n_out + n_scr :]
        net = Net(send, recv, local)
        body(net, in_refs, out_refs, scr)
        net.finish()
        assert net.used <= copies and net.used_local <= locals_, (net.used, net.used_local)

    return pl.pallas_call(
        kernel,
        out_shape=outs,
        in_specs=[pl.BlockSpec(memory_space=pl.ANY)] * n_in,
        out_specs=[pl.BlockSpec(memory_space=pl.ANY)] * n_out,
        scratch_shapes=list(scratch)
        + [
            pltpu.SemaphoreType.DMA((copies,)),
            pltpu.SemaphoreType.DMA((copies,)),
            pltpu.SemaphoreType.DMA((max(locals_, 1),)),
        ],
        compiler_params=pltpu.CompilerParams(
            collective_id=cid, has_side_effects=True, vmem_limit_bytes=vmem * 2**20
        ),
        name=name,
        cost_estimate=cost,
    )(*ins)


def gather_narrow(net, own, out):
    x, z, y, c = here()
    rows = own.shape[0]
    half = rows // 2

    def block(dy, lo=0, size=rows):
        return out.at[span((wrap(y + dy) * 2 + c) * rows + lo, size)]

    first, last = own.at[pl.ds(0, half)], own.at[pl.ds(half, half)]
    up = net.put(first, block(0, 0, half), moved(dy=1))
    down = net.put(last, block(0, half, half), moved(dy=-1))
    up_late = net.put(last, block(0, half, half), moved(dy=1))
    down_late = net.put(first, block(0, 0, half), moved(dy=-1))
    across = [net.put(own, block(0), moved(dc=1))]
    mine = net.keep(own, block(0))
    yield
    mine.wait()
    across[0].wait_recv()
    yield
    up.wait_recv()
    on = net.put(block(-1, 0, half), block(-1, 0, half), moved(dy=1))
    down.wait_recv()
    back = net.put(block(1, half, half), block(1, half, half), moved(dy=-1))
    yield
    up_late.wait_recv()
    across.append(net.put(block(-1), block(-1), moved(dc=1)))
    down_late.wait_recv()
    across.append(net.put(block(1), block(1), moved(dc=1)))
    across[1].wait_recv()
    across[2].wait_recv()
    yield
    on.wait_recv()
    across.append(net.put(block(2, 0, half), block(2, 0, half), moved(dc=1)))
    back.wait_recv()
    across.append(net.put(block(2, half, half), block(2, half, half), moved(dc=1)))
    yield
    across[3].wait_recv()
    across[4].wait_recv()
    yield
    net.sent_by(up, down, up_late, down_late, on, back, *across)


GATHER_COPIES = 12


def gather_small(net, own, out):
    c = here()[3]
    y = here()[2]
    rows = own.shape[0]

    def block(dy):
        return out.at[span((wrap(y + dy) * 2 + c) * rows, rows)]

    along = [net.put(own, block(0), moved(dy=d)) for d in (2, 1, 3)]
    across = [net.put(own, block(0), moved(dc=1))]
    mine = net.keep(own, block(0))
    yield
    for copy, d in zip(along, (2, 1, 3)):
        copy.wait_recv()
        across.append(net.put(block(-d), block(-d), moved(dc=1)))
    yield
    mine.wait()
    for copy in across:
        copy.wait_recv()


GATHER_SMALL_COPIES = 7


def gather_call(own, cid, name):
    rows, cols = own.shape

    def body(net, ins, outs, scr):
        greet(NEAR_Y)
        take_turns(gather_narrow(net, ins[0], outs[0]))

    return comm_call(
        body,
        [own],
        [jax.ShapeDtypeStruct((NARROW * rows, cols), own.dtype)],
        [],
        cid,
        GATHER_COPIES,
        1,
        name,
    )[0]


def reduce_scratch(rows, cols):
    return [
        pltpu.VMEM((SIDE, rows, cols), BF),
        pltpu.VMEM((SIDE, rows, cols), BF),
        pltpu.VMEM((2, rows // 2, cols), BF),
        pltpu.VMEM((2, rows, cols), BF),
        pltpu.VMEM((3, rows, cols), BF),
        pltpu.VMEM((rows, cols), F32),
    ]


REDUCE_COPIES = 10
REDUCE_LOCALS = 5


def reduce_narrow(net, part, scr):
    own, other, through, landed, ready, total = scr
    x, z, y, c = here()
    rows, cols = total.shape
    half = rows // 2

    def block(dy, core):
        return part.at[span((wrap(y + dy) * 2 + core) * rows, rows)]

    order = (2, 1, 3, 0)
    local, cross = {}, {}
    for dy in order:
        cross[dy] = net.put(block(dy, 1 - c), other.at[dy], moved(dc=1))
        local[dy] = net.keep(block(dy, c), own.at[dy])

    def pair(dy, lo, size):
        s = span(lo, size)
        return own[dy, s, :].astype(F32) + other[dy, s, :].astype(F32)

    yield
    local[2].wait()
    cross[2].wait_recv()
    ready[0] = pair(2, 0, rows).astype(BF)
    first, last = span(0, half), span(half, half)
    via_up = net.put(ready.at[0, first], through.at[0], moved(dy=1))
    via_down = net.put(ready.at[0, last], through.at[1], moved(dy=-1))
    yield
    local[1].wait()
    cross[1].wait_recv()
    ready[1, last, :] = pair(1, half, half).astype(BF)
    up_late = net.put(ready.at[1, last], landed.at[0, last], moved(dy=1))
    local[3].wait()
    cross[3].wait_recv()
    ready[2, first, :] = pair(3, 0, half).astype(BF)
    down_first = net.put(ready.at[2, first], landed.at[1, first], moved(dy=-1))
    yield
    via_up.wait_recv()
    ready[1, first, :] = (pair(1, 0, half) + through[0].astype(F32)).astype(BF)
    up_first = net.put(ready.at[1, first], landed.at[0, first], moved(dy=1))
    via_down.wait_recv()
    ready[2, last, :] = (pair(3, half, half) + through[1].astype(F32)).astype(BF)
    down_late = net.put(ready.at[2, last], landed.at[1, last], moved(dy=-1))
    yield
    local[0].wait()
    cross[0].wait_recv()
    total[...] = pair(0, 0, rows)
    yield
    for copy in (up_late, down_first, up_first, down_late):
        copy.wait_recv()
    total[...] += landed[0].astype(F32) + landed[1].astype(F32)


def pairs_scratch(rows, cols):
    return [
        pltpu.VMEM((SIDE * 2 * rows, cols), BF),
        pltpu.VMEM((SIDE, rows, cols), BF),
        pltpu.VMEM((2, rows // 2, cols), BF),
        pltpu.VMEM((2, rows, cols), BF),
        pltpu.VMEM((3, rows, cols), BF),
        pltpu.VMEM((rows, cols), F32),
    ]


PAIR_ORDER = (2, 1, 3, 0)


class Pairs:
    def __init__(self, net, out, scr, far_first=True):
        self.net, self.out, self.scr, self.far_first = net, out, scr, far_first
        self.crossed = {}

    def store(self, dy, value):
        rows = value.shape[0]
        self.scr[0][pl.ds(dy * rows, rows), :] = value.astype(BF)

    def cross(self, dy):
        parts, other = self.scr[:2]
        c = here()[3]
        rows = other.shape[1]
        self.crossed[dy] = self.net.put(
            parts.at[span((2 * dy + 1 - c) * rows, rows)], other.at[dy], moved(dc=1)
        )

    def steps(self):
        net = self.net
        parts, other, through, landed, ready, total = self.scr
        c = here()[3]
        rows = total.shape[0]
        half = rows // 2
        first, last = pl.ds(0, half), pl.ds(half, half)

        def pair(dy, lo, size):
            mine = parts[span((2 * dy + c) * rows + lo, size), :].astype(F32)
            return mine + other[dy, pl.ds(lo, size), :].astype(F32)

        def far():
            self.crossed[2].wait_recv()
            ready[0] = pair(2, 0, rows).astype(BF)
            via_up = net.put(ready.at[0, first], through.at[0], moved(dy=1))
            via_down = net.put(ready.at[0, last], through.at[1], moved(dy=-1))
            return via_up, via_down

        if self.far_first:
            via_up, via_down = far()
            yield
        self.crossed[1].wait_recv()
        ready[1, last, :] = pair(1, half, half).astype(BF)
        up_late = net.put(ready.at[1, last], landed.at[0, last], moved(dy=1))
        yield
        self.crossed[3].wait_recv()
        ready[2, first, :] = pair(3, 0, half).astype(BF)
        down_first = net.put(ready.at[2, first], landed.at[1, first], moved(dy=-1))
        yield
        if not self.far_first:
            via_up, via_down = far()
            yield
        via_up.wait_recv()
        ready[1, first, :] = (pair(1, 0, half) + through[0].astype(F32)).astype(BF)
        up_first = net.put(ready.at[1, first], landed.at[0, first], moved(dy=1))
        via_down.wait_recv()
        ready[2, last, :] = (pair(3, half, half) + through[1].astype(F32)).astype(BF)
        down_late = net.put(ready.at[2, last], landed.at[1, last], moved(dy=-1))
        yield
        self.crossed[0].wait_recv()
        total[...] = pair(0, 0, rows)
        yield
        for copy in (up_late, down_first, up_first, down_late):
            copy.wait_recv()
        total[...] += landed[0].astype(F32) + landed[1].astype(F32)
        if self.out is not None:
            done = net.keep(total, self.out)
            yield
            done.wait()


def spread_narrow(net, src, slab):
    w = lax.axis_index("wide")
    n = lax.axis_index("narrow")
    base = n * ROWS if slab.shape[0] == TOK else w * TOK + n * ROWS
    mine = net.keep(src.at[n], slab.at[span(base, ROWS)])
    copies = []
    for p in NARROW_ALL:
        target = moved(**p)
        copies.append(net.put(src.at[target[1]], slab.at[span(base, ROWS)], target))
    yield
    mine.wait()
    for copy in copies:
        copy.wait_recv()


SPREAD_COPIES = 7


def gather_wide(net, slab, lead, stage=None):
    x, z, y, c = here()
    rows = TOK // 2
    half = rows // 2
    low = 0 if lead == "x" else rows

    def block(a, b, lo=0, size=rows):
        px, pz = (a, b) if lead == "x" else (b, a)
        return slab.at[span((wrap(x + px) * SIDE + wrap(z + pz)) * TOK + low + lo, size)]

    def lead_to(d):
        return moved(dx=d) if lead == "x" else moved(dz=d)

    def then_to(d):
        return moved(dz=d) if lead == "x" else moved(dx=d)

    def both(src, to, dst=None):
        dst = src if dst is None else dst
        return net.put(src, dst, to(1)), net.put(src, dst, to(-1))

    mine = block(0, 0) if stage is None else stage.at[pl.ds(low, rows)]
    fore, aft = both(mine, lead_to, block(0, 0))
    second = {0: both(mine, then_to, block(0, 0))}
    yield
    fore.wait_recv()
    on = net.put(block(-1, 0, 0, half), block(-1, 0, 0, half), lead_to(1))
    second[-1] = both(block(-1, 0), then_to)
    aft.wait_recv()
    back = net.put(block(1, 0, half, half), block(1, 0, half, half), lead_to(-1))
    second[1] = both(block(1, 0), then_to)
    yield
    last = []

    def relay(a):
        f, b = second[a]
        f.wait_recv()
        last.append(net.put(block(a, -1, 0, half), block(a, -1, 0, half), then_to(1)))
        b.wait_recv()
        last.append(net.put(block(a, 1, half, half), block(a, 1, half, half), then_to(-1)))

    kept = None if stage is None else net.keep(mine, block(0, 0))
    relay(0)
    yield
    on.wait_recv()
    back.wait_recv()
    second[2] = both(block(2, 0), then_to)
    yield
    relay(-1)
    relay(1)
    yield
    relay(2)
    yield
    if kept is not None:
        kept.wait()
    for copy in last:
        copy.wait_recv()


WIDE_COPIES = 20


def mean_of(values):
    return jnp.sum(values, axis=-1, keepdims=True) * (1.0 / D)


def normal(values):
    centered = values - mean_of(values)
    inverse = lax.rsqrt(mean_of(centered * centered) + NORM_EPS)
    return centered * inverse, inverse


def normal_back(hat, inverse, d_hat):
    return inverse * (d_hat - mean_of(d_hat) - hat * mean_of(d_hat * hat))


def turn(values, cosine, sine):
    return values * cosine + pltpu.roll(values, HEAD_DIM // 2, 1) * sine


def allowed_keys(first_row, rows, first_length):
    query = first_row + lax.broadcasted_iota(jnp.int32, (rows, 1), 0)
    key = lax.broadcasted_iota(jnp.int32, (rows, GROUP), 1)
    start = jnp.where(query >= first_length, first_length, 0)
    return (key <= query) & (key >= start)


PICK_ATTN, PICK_FFN, GATE_FFN = 0, 32, 64
LATER_UNITS = 512


def branch_mask(marks, lane):
    n = lax.axis_index("narrow").astype(F32)
    return (n < 2.0 * (marks[:, lane : lane + 1] + 1.0)).astype(F32)


def half_turns(first_length, frequency, tv):
    rows = 64
    half = GROUP // 2
    left = lax.broadcasted_iota(jnp.int32, (rows, 128), 1) < HEAD_DIM // 2
    row = lax.broadcasted_iota(jnp.int32, (rows, 128), 0)

    @pl.loop(0, half // rows)
    def _(i):
        token = row + i * rows + jnp.where(left, 0, half)
        position = token - jnp.where(token >= first_length, first_length, 0)
        angles = position.astype(F32) * frequency
        cosine, sine = jnp.cos(angles), jnp.sin(angles)
        cosine_other = pltpu.roll(cosine, HEAD_DIM // 2, 1)
        sine_other = pltpu.roll(sine, HEAD_DIM // 2, 1)
        low, high = span(i * rows, rows), span(half + i * rows, rows)
        tv[0, low, :] = jnp.where(left, cosine, cosine_other)
        tv[0, high, :] = jnp.where(left, cosine_other, cosine)
        tv[1, low, :] = jnp.where(left, -sine, sine_other)
        tv[1, high, :] = jnp.where(left, -sine_other, sine)


GELU_SCALE = (2.0 / 3.141592653589793) ** 0.5
GELU_CUBE = 0.044715


def route(normed, first_layer, second_layer, picks):
    before = jnp.dot(normed, first_layer, preferred_element_type=F32)
    square = before * before
    bent = jnp.tanh(GELU_SCALE * before * (1.0 + GELU_CUBE * square))
    hidden = 0.5 * before * (1.0 + bent)
    slope = 0.5 * (1.0 + bent) + 0.5 * before * (1.0 - bent * bent) * GELU_SCALE * (
        1.0 + 3.0 * GELU_CUBE * square
    )
    logits = jnp.dot(hidden.astype(BF), second_layer, preferred_element_type=F32)
    lane = lax.broadcasted_iota(jnp.int32, logits.shape, 1)
    gates, logit_slopes, slopes = [], [], []
    for branch in range(2):
        start = branch * LEVELS
        inside = (lane >= start) & (lane < start + LEVELS)
        shown = jnp.where(inside, logits, -1e30)
        expo = jnp.exp(shown - jnp.max(shown, axis=-1, keepdims=True))
        expo = jnp.where(inside, expo, 0.0)
        probs = expo / jnp.sum(expo, axis=-1, keepdims=True)
        chosen = jnp.where(lane == picks[:, branch : branch + 1] + start, 1.0, 0.0)
        gate = float(LEVELS) * jnp.sum(probs * chosen, axis=-1, keepdims=True)
        logit_slope = gate * (chosen - probs)
        gates.append(gate)
        logit_slopes.append(logit_slope)
        slopes.append(
            slope
            * lax.dot_general(
                logit_slope.astype(BF), second_layer, CONTRACT_COLS, preferred_element_type=F32
            )
        )
    return hidden, gates, logit_slopes, slopes


def attention_forward(
    tokens, picks, first_length, frequency, gains, router_in, router_out, sources, upstream, cid
):
    pair_rows = 2 * TOK
    head_part = D // NARROW
    units = FF // NARROW
    low = jax.ShapeDtypeStruct((GROUP, head_part), BF)
    results = dict(
        attn_sum=jax.ShapeDtypeStruct((TOK, D), F32),
        q=low,
        k=low,
        v=low,
        p=jax.ShapeDtypeStruct((GROUP, 2 * GROUP), BF),
        a=low,
        g=jax.ShapeDtypeStruct((GROUP, D), BF),
        slab_a=jax.ShapeDtypeStruct((D, 4 * head_part), BF),
        slab_up=jax.ShapeDtypeStruct((D, units - LATER_UNITS), BF),
        stage_up=jax.ShapeDtypeStruct((TOK, LATER_UNITS), BF),
        slab_down=jax.ShapeDtypeStruct((D, units), BF),
        normed=jax.ShapeDtypeStruct((GROUP, D), BF),
        marks=jax.ShapeDtypeStruct((GROUP, 128), F32),
        after=jax.ShapeDtypeStruct((TOK, D), F32),
        second=jax.ShapeDtypeStruct((TOK, D), BF),
        d_act=jax.ShapeDtypeStruct((GROUP, units), F32),
        turns=jax.ShapeDtypeStruct((2, GROUP, HEAD_DIM), F32),
        router_low=jax.ShapeDtypeStruct((D, RH), BF),
        hidden=jax.ShapeDtypeStruct((TOK, RH), F32),
        gate=jax.ShapeDtypeStruct((TOK, 128), F32),
        logit_slopes=jax.ShapeDtypeStruct((2, TOK, 128), F32),
        slopes=jax.ShapeDtypeStruct((2, TOK, RH), F32),
    )
    held = tuple(k for k in results if k not in ("attn_sum", "slab_up", "stage_up"))
    own_inputs = (tokens, picks, first_length, frequency, gains, router_in, router_out)

    def body(net, ins, outs, scr):
        out = dict(zip(results, outs))
        to = dict(zip(held, scr))
        scr = scr[len(held) :]
        xv, wv, tv, mv = to["normed"], to["slab_a"], to["turns"], to["marks"]
        qv, kv, vv, pv, av = (to[k] for k in "qkvpa")
        held_in, scr = scr[:7], scr[7:]
        own_tokens, own_picks, lv, fv, own_gains, rv, ov = held_in
        stage_up, stage_down, normed_own, marks_own = scr[:4]
        pairs = scr[4:]
        source_a, source_up, source_later, source_down, upstream = ins[7:]
        x, z, y, c = here()
        loads = [net.keep(a, b) for a, b in zip(ins[:7], held_in)]
        greet(NARROW_ALL + NEAR_XZ)
        sums = Pairs(net, out["attn_sum"], pairs)
        stores = []

        def store(*names):
            stores.extend([net.keep(to[name], out[name]) for name in names])

        moves = dict(
            sa=spread_narrow(net, source_a, wv),
            su=spread_narrow(net, source_up, stage_up),
            sl=spread_narrow(net, source_later, out["stage_up"]),
            sd=spread_narrow(net, source_down, stage_down),
            gx=gather_narrow(net, normed_own, xv),
            gm=gather_narrow(net, marks_own, mv),
            gg=gather_narrow(net, upstream, to["g"]),
            wa=side_by_side(*[gather_wide(net, wv, k) for k in "xz"]),
            wu=side_by_side(*[gather_wide(net, out["slab_up"], k, stage_up) for k in "xz"]),
            wd=side_by_side(*[gather_wide(net, to["slab_down"], k, stage_down) for k in "xz"]),
            total=sums.steps(),
        )

        def first_norm():
            for load in loads:
                load.wait()
            hat, _ = normal(own_tokens[...].astype(F32))
            normed_own[...] = (hat * own_gains[0:1, :]).astype(BF)

        def route_own():
            to["router_low"][...] = rv[...].astype(BF)
            hidden, gates, logit_slopes, slopes = route(
                normed_own[...], to["router_low"][...], ov[...], own_picks[...]
            )
            to["hidden"][...] = hidden
            to["gate"][...] = jnp.broadcast_to(gates[0], (TOK, 128))
            for branch in range(2):
                to["logit_slopes"][branch] = logit_slopes[branch]
                to["slopes"][branch] = slopes[branch]
            lane = lax.broadcasted_iota(jnp.int32, (TOK, 128), 1)
            level = own_picks[...].astype(F32)
            other = jnp.where(lane < GATE_FFN, level[:, 1:2], gates[1])
            marks_own[...] = jnp.where(lane < PICK_FFN, level[:, 0:1], other)
            store("router_low", "hidden", "gate", "logit_slopes", "slopes")

        def tables():
            half_turns(lv[0:1, 0:1], fv[0:1, :], tv)
            store("turns")

        def down_back():
            store("g", "slab_down")

            @pl.loop(0, SIDE)
            def _(i):
                r = span(i * pair_rows, pair_rows)
                to["d_act"][r, :] = jnp.dot(
                    to["g"][r, :], to["slab_down"][...], preferred_element_type=F32
                )

            store("d_act")

        def project():
            store("normed", "slab_a")

            @pl.loop(0, SIDE)
            def _(i):
                r = span(i * pair_rows, pair_rows)
                proj = jnp.dot(xv[r, :], wv[:, : 3 * head_part], preferred_element_type=F32)
                cosine, sine = tv[0, r, :], tv[1, r, :]
                for h in range(2):
                    at = pl.ds(h * HEAD_DIM, HEAD_DIM)
                    a = h * HEAD_DIM
                    qv[r, at] = turn(proj[:, a : a + HEAD_DIM], cosine, sine).astype(BF)
                    a += head_part
                    kv[r, at] = turn(proj[:, a : a + HEAD_DIM], cosine, sine).astype(BF)
                vv[r, :] = proj[:, 2 * head_part :].astype(BF)

            store("q", "k", "v")

        def attend(dy):
            first = wrap(y + dy) * pair_rows
            r = span(first, pair_rows)
            allowed = allowed_keys(first, pair_rows, lv[0:1, 0:1])
            heads = []
            for h in range(2):
                at = pl.ds(h * HEAD_DIM, HEAD_DIM)
                scores = lax.dot_general(
                    qv[r, at], kv[:, at], CONTRACT_COLS, preferred_element_type=F32
                )
                scores = jnp.where(allowed, scores * HEAD_DIM ** (-0.5), -1e30)
                expo = jnp.exp(scores - jnp.max(scores, axis=-1, keepdims=True))
                probs = expo * (1.0 / jnp.sum(expo, axis=-1, keepdims=True))
                low = probs.astype(BF)
                pv[r, pl.ds(h * GROUP, GROUP)] = low
                heads.append(jnp.dot(low, vv[:, at], preferred_element_type=F32))
            mask = branch_mask(mv[r, :], PICK_ATTN)
            av[r, :] = (jnp.concatenate(heads, axis=1) * mask).astype(BF)
            back = lax.dot_general(
                av[r, :], wv[:, 3 * head_part :], CONTRACT_COLS, preferred_element_type=F32
            )
            sums.store(dy, back)
            sums.cross(dy)

        def second_norm():
            values = own_tokens[...].astype(F32) + to["gate"][:, :1] * sums.scr[5][...]
            to["after"][...] = values
            to["second"][...] = (normal(values)[0] * own_gains[1:2, :]).astype(BF)
            store("after", "second")

        works = dict(
            L1=first_norm, RF=route_own, TB=tables, Q=project, LN=second_norm, DA=down_back
        )
        for dy in PAIR_ORDER:
            works[f"T{dy}"] = functools.partial(attend, dy)
        follow(FORWARD_PLAN, works, moves)
        store("p", "a", "marks")
        for done in stores:
            done.wait()

    got = comm_call(
        body,
        list(own_inputs) + list(sources) + [upstream],
        list(results.values()),
        [pltpu.VMEM(results[k].shape, results[k].dtype) for k in held]
        + [pltpu.VMEM(r.shape, r.dtype) for r in own_inputs]
        + [
            pltpu.VMEM((TOK, units - LATER_UNITS), BF),
            pltpu.VMEM((TOK, units), BF),
            pltpu.VMEM((TOK, D), BF),
            pltpu.VMEM((TOK, 128), F32),
        ]
        + pairs_scratch(TOK, D),
        cid,
        REDUCE_COPIES + 6 * WIDE_COPIES + 3 * GATHER_COPIES + 4 * SPREAD_COPIES,
        7 + 4 + 3 + 4 + 1 + len(held),
        "attention_forward",
    )
    return dict(zip(results, got))


def first_scratch(cols):
    part, half = TOK // 2, TOK // 4
    return [
        pltpu.VMEM((2, 2, SIDE, half, cols), BF),
        pltpu.VMEM((2, 2, SIDE, part, cols), BF),
        pltpu.VMEM((2, 2, SIDE, half, cols), BF),
        pltpu.VMEM((2, SIDE, part, cols), BF),
    ]


def second_scratch(cols):
    part, half = TOK // 2, TOK // 4
    return [
        pltpu.VMEM((2, 2, half, cols), BF),
        pltpu.VMEM((2, 2, part, cols), BF),
        pltpu.VMEM((2, 2, half, cols), BF),
        pltpu.VMEM((TOK, cols), BF),
    ]


FIRST_COPIES = 12
SECOND_COPIES = 12
FIRST_LOCALS = 6


def lead_moves(lead):
    def lead_to(d):
        return moved(dx=d) if lead == "x" else moved(dz=d)

    def then_to(d):
        return moved(dz=d) if lead == "x" else moved(dx=d)

    return lead_to, then_to


def reduce_first(net, grad, scr, lead):
    via, landed, ready, sums = scr
    x, z, y, c = here()
    part, half = TOK // 2, TOK // 4
    k = 0 if lead == "x" else 1
    low = k * part
    blocks = grad.reshape(SIDE, SIDE, TOK, grad.shape[1])
    first, last = pl.ds(0, half), pl.ds(half, half)
    lead_to, _ = lead_moves(lead)

    def line(d, lo, size):
        rows = pl.ds(low + lo, size)
        if lead == "x":
            return (wrap(x + d), slice(None), rows, slice(None))
        return (slice(None), wrap(z + d), rows, slice(None))

    via_up = net.put(blocks.at[line(2, 0, half)], via.at[k, 0], lead_to(1))
    via_down = net.put(blocks.at[line(2, half, half)], via.at[k, 1], lead_to(-1))
    up_late = net.put(blocks.at[line(1, half, half)], landed.at[k, 0, :, last], lead_to(1))
    down_first = net.put(blocks.at[line(3, 0, half)], landed.at[k, 1, :, first], lead_to(-1))
    loads = [
        net.keep(blocks.at[line(1, 0, half)], ready.at[k, 0]),
        net.keep(blocks.at[line(3, half, half)], ready.at[k, 1]),
        net.keep(blocks.at[line(0, 0, part)], sums.at[k]),
    ]
    yield
    for load in loads:
        load.wait()
    via_up.wait_recv()

    @pl.loop(0, SIDE)
    def _(i):
        ready[k, 0, i] = (ready[k, 0, i].astype(F32) + via[k, 0, i].astype(F32)).astype(BF)

    up_first = net.put(ready.at[k, 0], landed.at[k, 0, :, first], lead_to(1))
    via_down.wait_recv()

    @pl.loop(0, SIDE)
    def _(i):
        ready[k, 1, i] = (ready[k, 1, i].astype(F32) + via[k, 1, i].astype(F32)).astype(BF)

    down_late = net.put(ready.at[k, 1], landed.at[k, 1, :, last], lead_to(-1))
    yield
    for copy in (up_late, down_first, up_first, down_late):
        copy.wait_recv()

    @pl.loop(0, SIDE)
    def _(i):
        both = landed[k, 0, i].astype(F32) + landed[k, 1, i].astype(F32)
        sums[k, i] = (sums[k, i].astype(F32) + both).astype(BF)


def reduce_second(net, sums, scr, lead):
    via, landed, ready, total = scr
    x, z, y, c = here()
    part, half = TOK // 2, TOK // 4
    k = 0 if lead == "x" else 1
    first, last = pl.ds(0, half), pl.ds(half, half)
    _, then_to = lead_moves(lead)
    me = z if lead == "x" else x

    def block(d, rows):
        return sums.at[k, wrap(me + d), rows]

    via_up = net.put(block(2, first), via.at[k, 0], then_to(1))
    via_down = net.put(block(2, last), via.at[k, 1], then_to(-1))
    up_late = net.put(block(1, last), landed.at[k, 0, last], then_to(1))
    down_first = net.put(block(3, first), landed.at[k, 1, first], then_to(-1))
    yield
    via_up.wait_recv()
    ready[k, 0] = (block(1, first)[...].astype(F32) + via[k, 0].astype(F32)).astype(BF)
    up_first = net.put(ready.at[k, 0], landed.at[k, 0, first], then_to(1))
    via_down.wait_recv()
    ready[k, 1] = (block(3, last)[...].astype(F32) + via[k, 1].astype(F32)).astype(BF)
    down_late = net.put(ready.at[k, 1], landed.at[k, 1, last], then_to(-1))
    yield
    for copy in (up_late, down_first, up_first, down_late):
        copy.wait_recv()
    both = landed[k, 0].astype(F32) + landed[k, 1].astype(F32)
    total[pl.ds(k * part, part), :] = (sums[k, me].astype(F32) + both).astype(BF)


def side_by_side(*parts):
    while True:
        if StopIteration in [next(part, StopIteration) for part in parts]:
            break
        yield


def return_narrow(net, total, out, pieces):
    n = lax.axis_index("narrow")
    copies, mine = [], []
    for start, width, to in pieces:
        spot = out.at[:, lanes(to + n * width, width)]
        columns = pl.ds(start, width)
        for p in NARROW_ALL:
            target = moved(**p)
            copies.append(net.put(total.at[span(target[1] * ROWS, ROWS), columns], spot, target))
        mine.append(net.keep(total.at[span(n * ROWS, ROWS), columns], spot))
    yield
    for copy in mine:
        copy.wait()
    for copy in copies:
        copy.wait_recv()


def second_then_narrow(net, sums, out, scr, pieces):
    yield from side_by_side(*[reduce_second(net, sums, scr, lead) for lead in "xz"])
    yield from return_narrow(net, scr[3], out, pieces)


def wide_then_narrow(net, grad, out, scr, pieces):
    yield from side_by_side(*[reduce_first(net, grad, scr[:4], lead) for lead in "xz"])
    yield from second_then_narrow(net, scr[3], out, scr[4:], pieces)


def feed_forward(normed_own, upstream, w_up, stage_up, w_down, d_act, marks, own, cid):
    pair_rows = 2 * TOK
    units = FF // NARROW
    strip = 256

    def body(net, ins, outs, scr):
        own, upstream, up_in, stage_in, down_in, da_in, marks = ins[:7]
        kept_up = up_in.shape[1]
        rest = pl.ds(kept_up, units - kept_up)
        ffn_part, g_up, down_sums, after_out, attn_out, hidden_out, gain_out, router_out = outs
        xv, dv, w_up, w_down, mv, act, du, da, gu, yv = scr[:10]
        gated, dots, dots_in = scr[16:19]
        held, d_attn, d_hidden, d_gain, d_router = scr[19:26], *scr[26:30]
        gds, firsts = scr[30:32], (scr[32:36], scr[36:40])
        stage = scr[40]
        n = lax.axis_index("narrow")
        x, z, y, c = here()
        loads = [
            net.keep(a, b)
            for a, b in (
                (stage_in, stage),
                (marks, mv),
                (up_in, w_up.at[:, pl.ds(0, kept_up)]),
                (da_in, da),
                (upstream, dv),
                (down_in, w_down),
            )
        ]
        own_loads = [net.keep(a, b) for a, b in zip(ins[7:], held)]
        greet(NARROW_ALL + NEAR_XZ)
        loads.pop(0).wait()
        sums = Pairs(net, None, scr[10:16], far_first=False)
        ones = jnp.ones((8, units), BF)
        stores, dot_copies = [], []

        def gradient(left, right, to):
            @pl.loop(0, D // strip)
            def _(i):
                at = lanes(i * strip, strip)
                to[span(i * strip, strip), :] = lax.dot_general(
                    left[:, at], right[...], CONTRACT_ROWS, preferred_element_type=F32
                ).astype(BF)

        def wait_loads():
            for load in loads:
                load.wait()

        def half_gradient(i):
            columns = pl.ds(i * units // 2, units // 2)
            gradient(dv, gated.at[:, columns], gds[i])

        def units_of(dy):
            r = span(wrap(y + dy) * pair_rows, pair_rows)
            up = jnp.dot(xv[r, :], w_up[...], preferred_element_type=F32)
            positive = jnp.maximum(up, 0.0)
            masked = positive * branch_mask(mv[r, :], PICK_FFN)
            gate = mv[r, GATE_FFN : GATE_FFN + 1]
            active = positive * masked
            act[r, :] = active.astype(BF)
            gated[r, :] = (active * gate).astype(BF)
            back = da[r, :]
            du[r, :] = (back * (2.0 * gate * masked)).astype(BF)
            dot = lax.dot_general(
                ones, (back * active).astype(BF), CONTRACT_COLS, preferred_element_type=F32
            )
            for core in range(2):
                dots[wrap(y + dy) * 2 + core] = dot[:, core * TOK : (core + 1) * TOK]

        def norm_back(dy):
            r = span(wrap(y + dy) * pair_rows, pair_rows)
            back = lax.dot_general(
                du[r, :], w_up[...], CONTRACT_COLS, preferred_element_type=F32
            )
            sums.store(dy, back)
            sums.cross(dy)

        def send_dots():
            for p in NARROW_ALL:
                target = moved(**p)
                dot_copies.append(net.put(dots.at[target[1]], dots_in.at[n], target))
            dots_in[n] = dots[n]

        def up_gradient():
            gradient(xv, du, gu)
            stores.append(net.keep(gu, g_up))

        def output(dy):
            r = span(wrap(y + dy) * pair_rows, pair_rows)
            yv[r, :] = lax.dot_general(
                act[r, :], w_down[...], CONTRACT_COLS, preferred_element_type=F32
            ).astype(BF)
            stores.append(net.keep(yv.at[r], ffn_part.at[r]))

        def second_norm_back():
            for load in own_loads:
                load.wait()
            for copy in dot_copies:
                copy.wait_recv()
            s = dots_in[0]
            for i in range(1, NARROW):
                s = s + dots_in[i]
            row = lax.broadcasted_iota(jnp.int32, (TOK, TOK), 0)
            lane = lax.broadcasted_iota(jnp.int32, (TOK, TOK), 1)
            ffn = jnp.sum(jnp.where(row == lane, s[0:1, :], 0.0), axis=-1, keepdims=True)
            after, attn, gate, gains, slopes, logit_slopes, hidden = held
            total = sums.scr[5]
            hat, inverse = normal(after[...])
            d_gain[...] = jnp.sum(total[...] * hat, axis=0, keepdims=True)
            back = normal_back(hat, inverse, total[...] * gains[1:2, :])
            back = back + dv[span(n * TOK, TOK), :].astype(F32)
            total[...] = back
            d_attn[...] = (back * gate[:, :1]).astype(BF)
            attn_gate = jnp.sum(back * attn[...], axis=-1, keepdims=True)
            d_hidden[...] = (attn_gate * slopes[0] + ffn * slopes[1]).astype(BF)
            d_logits = attn_gate * logit_slopes[0] + ffn * logit_slopes[1]
            d_router[...] = lax.dot_general(
                hidden[...].astype(BF),
                d_logits.astype(BF),
                CONTRACT_ROWS,
                preferred_element_type=F32,
            )
            pairs = zip(
                (total, d_attn, d_hidden, d_gain, d_router),
                (after_out, attn_out, hidden_out, gain_out, router_out),
            )
            stores.extend([net.keep(a, b) for a, b in pairs])

        works = dict(
            LD=wait_loads,
            GD=functools.partial(half_gradient, 0),
            GE=functools.partial(half_gradient, 1),
            GU=up_gradient,
            DS=send_dots,
            LB=second_norm_back,
        )
        for dy in PAIR_ORDER:
            works[f"U{dy}"] = functools.partial(units_of, dy)
            works[f"Y{dy}"] = functools.partial(output, dy)
            works[f"N{dy}"] = functools.partial(norm_back, dy)
        moves = dict(
            gather=gather_narrow(net, own, xv),
            total=sums.steps(),
            wide=side_by_side(*[reduce_first(net, gds[0], firsts[0], lead) for lead in "xz"]),
            more=side_by_side(*[reduce_first(net, gds[1], firsts[1], lead) for lead in "xz"]),
            wu=side_by_side(*[gather_wide(net, w_up.at[:, rest], k, stage) for k in "xz"]),
        )
        follow(FEED_PLAN, works, moves)
        for i in range(2):
            columns = pl.ds(i * units // 2, units // 2)
            stores.append(net.keep(firsts[i][3], down_sums.at[:, :, :, columns]))
        for store in stores:
            store.wait()

    wide = pltpu.VMEM((GROUP, D), BF)
    tall = pltpu.VMEM((D, units), BF)
    square = pltpu.VMEM((GROUP, units), BF)
    return comm_call(
        body,
        [normed_own, upstream, w_up, stage_up, w_down, d_act, marks] + list(own),
        [
            jax.ShapeDtypeStruct((GROUP, D), BF),
            jax.ShapeDtypeStruct((D, units), BF),
            jax.ShapeDtypeStruct((2, SIDE, TOK // 2, units), BF),
            jax.ShapeDtypeStruct((TOK, D), F32),
            jax.ShapeDtypeStruct((TOK, D), BF),
            jax.ShapeDtypeStruct((TOK, RH), BF),
            jax.ShapeDtypeStruct((1, D), F32),
            jax.ShapeDtypeStruct((RH, 128), F32),
        ],
        [wide, wide, tall, tall, pltpu.VMEM(marks.shape, F32), square, square]
        + [pltpu.VMEM((GROUP, units), F32), tall, wide]
        + pairs_scratch(TOK, D)
        + [square]
        + [pltpu.VMEM((NARROW, 8, TOK), F32)] * 2
        + [pltpu.VMEM(r.shape, r.dtype) for r in own]
        + [
            pltpu.VMEM((TOK, D), BF),
            pltpu.VMEM((TOK, RH), BF),
            pltpu.VMEM((1, D), F32),
            pltpu.VMEM((RH, 128), F32),
        ]
        + [pltpu.VMEM((D, units // 2), BF)] * 2
        + first_scratch(units // 2) * 2
        + [pltpu.VMEM(stage_up.shape, BF)],
        cid,
        GATHER_COPIES + REDUCE_COPIES + 7 + 2 * FIRST_COPIES + 2 * WIDE_COPIES,
        14 + 1 + 1 + 12 + 2 * FIRST_LOCALS + 2,
        "feed_forward",
    )


VECTOR_ROWS = 64
GAIN_ROWS = 2 * D // 128
SMALL_ROWS = GAIN_ROWS + RH * 2 * LEVELS // 128
SQUARE_ROWS = 8


def squares_of(ref, rows, cols):
    s = jnp.zeros((SQUARE_ROWS, 128), F32)
    for i in range(ref.shape[0] // rows):
        for j in range(ref.shape[1] // cols):
            piece = ref[i * rows : (i + 1) * rows, j * cols : (j + 1) * cols].astype(F32)
            piece = piece * piece
            for a in range(rows // SQUARE_ROWS):
                for b in range(cols // 128):
                    s = s + piece[a * 8 : a * 8 + 8, b * 128 : b * 128 + 128]
    return s


def sum_everywhere(net, own, first, second, total):
    w = lax.axis_index("wide")
    n = lax.axis_index("narrow")

    def rows(i):
        return pl.ds(pl.multiple_of(i * 8, 8), 8)

    copies = []
    for p in NARROW_ALL:
        target = moved(**p)
        copies.append(net.put(own.at[rows(target[1])], first.at[n], target))
    first[n] = own[rows(n), :]
    for copy in copies:
        copy.wait_recv()
    s = first[0]
    for i in range(1, NARROW):
        s = s + first[i]
    second[w] = s
    copies = [net.put(second.at[w], second.at[w], moved(**p)) for p in WIDE_ALL]
    for copy in copies:
        copy.wait_recv()
    s = second[0]
    for i in range(1, WIDE):
        s = s + second[i]
    total[rows(n), :] = s
    copies = [net.put(total.at[rows(n)], total.at[rows(n)], moved(**p)) for p in NARROW_ALL]
    for copy in copies:
        copy.wait_recv()


def attention_backward(
    d_attn_own, ffn_part, g_up, down_sums, normed, hidden_own, own, kept, cid
):
    table_rows = D // NARROW
    pair_rows = 2 * TOK
    head_part = D // NARROW
    units = FF // NARROW
    strip = 256
    scale = HEAD_DIM ** (-0.5)
    scratch = (
        [pltpu.VMEM(r.shape, r.dtype) for r in kept]
        + [
            pltpu.VMEM((GROUP, D), BF),
            pltpu.VMEM((GROUP, head_part), F32),
            pltpu.VMEM((GROUP, head_part), F32),
            pltpu.VMEM((GROUP, 3 * head_part), BF),
            pltpu.VMEM((D, 4 * head_part), BF),
        ]
        + pairs_scratch(TOK, D)[1:]
        + reduce_scratch(TOK, D)
        + first_scratch(4 * head_part)
        + second_scratch(4 * head_part)
        + first_scratch(units)
        + second_scratch(units)
        + [pltpu.VMEM(down_sums.shape, BF)]
        + second_scratch(units)
        + [
            pltpu.VMEM((GROUP, table_rows), BF),
            pltpu.VMEM((GROUP, RH), BF),
            pltpu.VMEM((table_rows, RH), BF),
            pltpu.VMEM((WIDE, ROWS, RH), BF),
            pltpu.VMEM((ROWS, RH), BF),
            pltpu.VMEM((table_rows, RH), BF),
            pltpu.VMEM((TOK, RH), BF),
            pltpu.VMEM((1, D), F32),
        ]
        + [pltpu.VMEM(r.shape, r.dtype) for r in own]
        + [
            pltpu.VMEM((ROWS, 4 * D + 2 * FF), BF),
            pltpu.VMEM((TOK, D), BF),
            pltpu.VMEM((NARROW, 8, 128), F32),
            pltpu.VMEM((WIDE, 8, 128), F32),
            pltpu.VMEM((VECTOR_ROWS, 128), F32),
            pltpu.VMEM((8, 128), F32),
        ]
    )

    def body(net, ins, outs, scr):
        d_attn_own, ffn_part, g_up, down_sums, normed, hidden_own = ins[:6]
        input_grad, result_out, block_out, table, vector_out, norm_out = outs
        wv, tv, mv, qv, kv, vv, pv, av = scr[:8]
        big, dk, dv, dproj, ga = scr[8:13]
        pairs, narrow = [big, *scr[13:18]], scr[18:24]
        wide_a, wide_up, wide_down = scr[24:32], scr[32:40], scr[40:45]
        columns, hidden, part, landed, shard, mine = scr[45:51]
        own_hidden, d_gain, held = scr[51], scr[52], scr[53:59]
        block, result, first, second, summed, norm = scr[59:65]
        n = lax.axis_index("narrow")
        x, z, y, c = here()
        first_load = net.keep(down_sums, wide_down[0])
        loads = [net.keep(a, b) for a, b in zip(ins[12:], scr[:8])]
        own_loads = [net.keep(a, b) for a, b in zip(ins[6:12], held)]
        own_loads.append(net.keep(hidden_own, own_hidden))
        loads.append(net.keep(normed.at[:, lanes(n * table_rows, table_rows)], columns))
        greet(NARROW_ALL + WIDE_ALL)
        sums = Pairs(net, None, pairs)
        quarter = [(i * head_part, head_part, i * D) for i in range(4)]

        def router():
            yield from gather_small(net, hidden_own, hidden)
            w = lax.axis_index("wide")
            part[...] = lax.dot_general(
                columns[...], hidden[...], CONTRACT_ROWS, preferred_element_type=F32
            ).astype(BF)
            copies = []
            for p in WIDE_ALL:
                target = moved(**p)
                rows = part.at[span(target[0] * ROWS, ROWS)]
                copies.append(net.put(rows, landed.at[w], target))
            kept = net.keep(part.at[span(w * ROWS, ROWS)], landed.at[w])
            yield
            kept.wait()
            for copy in copies:
                copy.wait_recv()
            s = landed[0].astype(F32)
            for i in range(1, WIDE):
                s = s + landed[i].astype(F32)
            shard[...] = s.astype(BF)
            spot = mine.at[span(w * ROWS, ROWS)]
            copies = [net.put(shard, spot, moved(**p)) for p in WIDE_ALL]
            kept = net.keep(shard, spot)
            yield
            kept.wait()
            for copy in copies:
                copy.wait_recv()
            yield from gather_small(net, mine, table)

        moves = dict(
            gather=gather_narrow(net, d_attn_own, big),
            down=second_then_narrow(
                net, wide_down[0], block, wide_down[1:], [(0, units, 4 * D + FF)]
            ),
            up=wide_then_narrow(net, g_up, block, wide_up, [(0, units, 4 * D)]),
            mixed=wide_then_narrow(net, ga, block, wide_a, quarter),
            feed=reduce_narrow(net, ffn_part, narrow),
            gates=router(),
            total=sums.steps(),
        )

        def wait_loads():
            first_load.wait()
            for load in loads:
                load.wait()
            dk[...] = jnp.zeros_like(dk)
            dv[...] = jnp.zeros_like(dv)

        def one_pair(dy):
            r = span(wrap(y + dy) * pair_rows, pair_rows)
            mask = branch_mask(mv[r, :], PICK_ATTN)
            back = jnp.dot(big[r, :], wv[:, 3 * head_part :], preferred_element_type=F32)
            back = (back * mask).astype(BF)
            for h in range(2):
                at = pl.ds(h * HEAD_DIM, HEAD_DIM)
                d_out = back[:, h * HEAD_DIM : (h + 1) * HEAD_DIM]
                d_probs = lax.dot_general(
                    d_out, vv[:, at], CONTRACT_COLS, preferred_element_type=F32
                )
                probs_low = pv[r, pl.ds(h * GROUP, GROUP)]
                probs = probs_low.astype(F32)
                weighted = probs * d_probs
                centre = jnp.sum(weighted, axis=-1, keepdims=True)
                ds = (weighted - probs * centre).astype(BF)
                dq = jnp.dot(ds, kv[:, at], preferred_element_type=F32) * scale
                dproj[r, at] = turn(dq, tv[0, r, :], -tv[1, r, :]).astype(BF)
                dk[:, at] += lax.dot_general(
                    ds, qv[r, at], CONTRACT_ROWS, preferred_element_type=F32
                )
                dv[:, at] += lax.dot_general(
                    probs_low, d_out, CONTRACT_ROWS, preferred_element_type=F32
                )

        refill = []

        def turn_back():
            refill.append(net.keep(normed, pv))

            @pl.loop(0, SIDE)
            def _(i):
                r = span(i * pair_rows, pair_rows)
                cosine, sine = tv[0, r, :], -tv[1, r, :]
                for h in range(2):
                    at = pl.ds(h * HEAD_DIM, HEAD_DIM)
                    to = pl.ds(head_part + h * HEAD_DIM, HEAD_DIM)
                    dproj[r, to] = turn(dk[r, at] * scale, cosine, sine).astype(BF)
                dproj[r, pl.ds(2 * head_part, head_part)] = dv[r, :].astype(BF)

        def gradient(left, right, start, width):
            @pl.loop(0, D // strip)
            def _(i):
                ga[span(i * strip, strip), pl.ds(start, width)] = lax.dot_general(
                    left[:, lanes(i * strip, strip)],
                    right[...],
                    CONTRACT_ROWS,
                    preferred_element_type=F32,
                ).astype(BF)

        def mixed_gradient():
            refill[0].wait()
            gradient(pv, dproj, 0, 3 * head_part)

        def norm_back(dy):
            r = span(wrap(y + dy) * pair_rows, pair_rows)
            back = lax.dot_general(
                dproj[r, :], wv[:, : 3 * head_part], CONTRACT_COLS, preferred_element_type=F32
            )
            sums.store(dy, back)
            sums.cross(dy)

        stores = []

        def first_norm_back():
            for load in own_loads:
                load.wait()
            tokens, after, gains, router_in = held[:4]
            total = sums.scr[5]
            d_normed = total[...] + lax.dot_general(
                own_hidden[...], router_in[...], CONTRACT_COLS, preferred_element_type=F32
            )
            hat, inverse = normal(tokens[...].astype(F32))
            d_gain[...] = jnp.sum(d_normed * hat, axis=0, keepdims=True)
            total[...] = after[...] + normal_back(hat, inverse, d_normed * gains[0:1, :])
            stores.append(net.keep(total, input_grad))

        works = dict(
            LB=first_norm_back,
            LD=wait_loads,
            RT=turn_back,
            GO=functools.partial(gradient, big, av, 3 * head_part, head_part),
            GQ=mixed_gradient,
        )
        for dy in PAIR_ORDER:
            works[f"P{dy}"] = functools.partial(one_pair, dy)
            works[f"N{dy}"] = functools.partial(norm_back, dy)
        follow(BACKWARD_PLAN, works, moves)
        stores.append(net.keep(block, block_out))
        vector = held[5]
        for i in range(GAIN_ROWS // 2):
            vector[i : i + 1, :] = d_gain[:, i * 128 : (i + 1) * 128]
        vector[VECTOR_ROWS - SQUARE_ROWS :, :] = squares_of(block, ROWS, 2048) + squares_of(
            shard, ROWS, RH
        )
        gate = mv[span(n * TOK, TOK), GATE_FFN : GATE_FFN + 1]
        result[...] = (held[4][...] + gate * narrow[5][...]).astype(BF)
        stores.append(net.keep(result, result_out))
        sum_everywhere(net, vector, first, second, summed)
        stores.append(net.keep(summed, vector_out))
        s = summed[...]
        small = s[:SMALL_ROWS]
        sum_all = jnp.sum(small * small) + jnp.sum(s[VECTOR_ROWS - SQUARE_ROWS :])
        norm[...] = jnp.sqrt(jnp.full((8, 128), sum_all, F32))
        stores.append(net.keep(norm, norm_out))
        for store in stores:
            store.wait()

    return comm_call(
        body,
        [d_attn_own, ffn_part, g_up, down_sums, normed, hidden_own] + list(own) + list(kept),
        [
            jax.ShapeDtypeStruct((TOK, D), F32),
            jax.ShapeDtypeStruct((TOK, D), BF),
            jax.ShapeDtypeStruct((ROWS, 4 * D + 2 * FF), BF),
            jax.ShapeDtypeStruct((D, RH), BF),
            jax.ShapeDtypeStruct((VECTOR_ROWS, 128), F32),
            jax.ShapeDtypeStruct((8, 128), F32),
        ],
        scratch,
        cid,
        GATHER_COPIES
        + 2 * REDUCE_COPIES
        + 2 * FIRST_COPIES
        + 3 * SECOND_COPIES
        + 6 * 7
        + 2 * (15 + GATHER_SMALL_COPIES)
        + 7 + 15 + 7,
        17 + 1 + 1 + 5 + REDUCE_LOCALS + 2 * FIRST_LOCALS + 6 + 4,
        "attention_backward",
    )


def adamw_step(master, moment_one, moment_two, grad, norm, tile):
    one_scale = 0.02 / (1.0 - 0.9**STEP)
    two_scale = 1.0 / (1.0 - 0.95**STEP)

    def kernel(w, m, v, g, n, new_w, new_m, new_v, *copy):
        clip = jnp.minimum(1.0, CLIP_NORM / n[0:1, 0:1])
        gradient = g[...].astype(F32) * clip
        one = 0.9 * m[...] + 0.1 * gradient
        two = 0.95 * v[...] + 0.05 * (gradient * gradient)
        new_m[...] = one
        new_v[...] = two
        scaled = jnp.maximum(two * two_scale, 1e-30)
        root = scaled * lax.rsqrt(scaled) + 1e-08
        guess = pl.reciprocal(root, approx=True)
        guess = guess * (2.0 - root * guess)
        updated = w[...] * (1.0 - 0.02 * 0.1) - (one * one_scale) * (guess * (2.0 - root * guess))
        new_w[...] = updated
        for ref in copy:
            ref[...] = updated.astype(BF)

    rows, cols = master.shape
    across = cols // tile[1]
    part = pl.BlockSpec(tile, lambda i: (i // across, i % across))
    shape = jax.ShapeDtypeStruct(master.shape, F32)
    low = jax.ShapeDtypeStruct(master.shape, BF)
    outs = [shape, shape, shape] + ([low] if rows == ROWS else [])
    return pl.pallas_call(
        kernel,
        grid=(rows * cols // (tile[0] * tile[1]),),
        out_shape=outs,
        in_specs=[part] * 4 + [pl.BlockSpec((8, 128), lambda i: (0, 0))],
        out_specs=[part] * len(outs),
        compiler_params=pltpu.CompilerParams(vmem_limit_bytes=60 * 2**20),
        name="adamw_step",
    )(master, moment_one, moment_two, grad, norm)


def adamw(weight, moment_one, moment_two, gradient, step_rate):
    moment_one = 0.9 * moment_one + 0.1 * gradient
    moment_two = 0.95 * moment_two + 0.05 * gradient * gradient
    first_hat = moment_one / (1.0 - 0.9**STEP)
    second_hat = moment_two / (1.0 - 0.95**STEP)
    updated = weight - step_rate * (first_hat / (jnp.sqrt(second_hat) + 1e-08) + 0.1 * weight)
    return (updated, moment_one, moment_two)


def cut(rows, start, width, pieces):
    part = rows[:, start : start + width].reshape(rows.shape[0], pieces, width // pieces)
    return part.transpose(1, 0, 2)


def on_device(
    tokens,
    lengths,
    picks,
    cotangent,
    block_master,
    block_first,
    block_second,
    gains,
    gains_first,
    gains_second,
    router_in,
    router_in_first,
    router_in_second,
    router_out,
    router_out_first,
    router_out_second,
):
    low = block_master.astype(BF)
    sources = [
        jnp.concatenate([cut(low, i * D, D, NARROW) for i in range(4)], axis=2),
        cut(low, 4 * D, FF, NARROW)[:, :, : FF // NARROW - LATER_UNITS],
        cut(low, 4 * D, FF, NARROW)[:, :, FF // NARROW - LATER_UNITS :],
        cut(low, 4 * D + FF, FF, NARROW),
    ]
    first_length = jnp.broadcast_to(lengths[:, 0:1], (8, 128))
    half_dim = HEAD_DIM // 2
    angle_steps = 10000.0 ** (-np.arange(half_dim, dtype=np.float32) / half_dim)
    frequency = jnp.asarray(np.tile(angle_steps.astype(np.float32), (8, 2)))
    router_out_low = jnp.pad(router_out, ((0, 0), (0, 128 - 2 * LEVELS))).astype(BF)
    f = attention_forward(
        tokens,
        picks,
        first_length,
        frequency,
        gains,
        router_in,
        router_out_low,
        sources,
        cotangent,
        1,
    )

    ffn_part, grad_up, down_sums, d_after, d_attn, d_hidden, d_gain_two, d_router = feed_forward(
        f["second"],
        f["g"],
        f["slab_up"],
        f["stage_up"],
        f["slab_down"],
        f["d_act"],
        f["marks"],
        [f["after"], f["attn_sum"], f["gate"], gains, f["slopes"], f["logit_slopes"], f["hidden"]],
        2,
    )
    levels = jnp.arange(LEVELS, dtype=jnp.int32)
    counts_local = [
        jnp.sum((picks[:, b : b + 1] == levels[None, :]).astype(F32), axis=0) for b in range(2)
    ]
    before = jnp.zeros((D,), F32)
    rest = jnp.zeros(((VECTOR_ROWS - SMALL_ROWS) * 128 - 2 * LEVELS,), F32)
    vector = jnp.concatenate(
        [before, d_gain_two[0], d_router[:, : 2 * LEVELS].ravel(), *counts_local, rest]
    ).reshape(VECTOR_ROWS, 128)
    d_inputs, result, block_low, router_in_grad, vector, norm = attention_backward(
        d_attn,
        ffn_part,
        grad_up,
        down_sums,
        f["normed"],
        d_hidden,
        [tokens, d_after, gains, f["router_low"], f["after"], vector],
        [f[k] for k in ("slab_a", "turns", "marks", "q", "k", "v", "p", "a")],
        3,
    )
    gain_grad = vector[:GAIN_ROWS].reshape(2, D)
    router_out_grad = vector[GAIN_ROWS:SMALL_ROWS].reshape(RH, 2 * LEVELS)
    counts = vector[SMALL_ROWS, : 2 * LEVELS].reshape(2, LEVELS)
    grad_norm = norm[0, 0]
    clip_factor = jnp.minimum(1.0, CLIP_NORM / grad_norm)
    new_block, new_block_first, new_block_second, block_copy = adamw_step(
        block_master, block_first, block_second, block_low, norm, (ROWS, 8192)
    )
    new_gains, new_gains_first, new_gains_second = adamw(
        gains, gains_first, gains_second, gain_grad * clip_factor, 0.6
    )
    new_router_in, new_router_in_first, new_router_in_second = adamw_step(
        router_in, router_in_first, router_in_second, router_in_grad, norm, (512, RH)
    )
    new_router_out, new_router_out_first, new_router_out_second = adamw(
        router_out, router_out_first, router_out_second, router_out_grad * clip_factor, 0.02
    )
    return (
        result,
        d_inputs,
        counts,
        grad_norm,
        new_block,
        new_block_first,
        new_block_second,
        block_copy,
        new_gains,
        new_gains_first,
        new_gains_second,
        new_router_in,
        new_router_in_first,
        new_router_in_second,
        new_router_out,
        new_router_out_first,
        new_router_out_second,
    )


def solution(mesh):
    both = P(("wide", "narrow"), None)
    return jax.shard_map(
        on_device,
        mesh=mesh,
        in_specs=(both, P("wide", None)) + (both,) * 5 + (P(),) * 9,
        out_specs=(both, both, P(), P()) + (both,) * 4 + (P(),) * 9,
        check_vma=False,
    )
```

```python
import functools

import jax
import jax.numpy as jnp
import numpy as np
from jax import lax
from jax.experimental import pallas as pl
from jax.experimental.pallas import tpu as pltpu
from jax.sharding import PartitionSpec as P

D = 2048
HEADS = 16
HEAD_DIM = 128
FF = 8192
RH = 256
LEVELS = 4
STEP = 10
TOK = 128
GROUP = 1024
SIDE = 4
WIDE = 16
NARROW = 8
ROWS = 16

VECTOR_ROWS = 64
GAIN_ROWS = 2 * D // 128
SMALL_ROWS = GAIN_ROWS + RH * 2 * LEVELS // 128
SQUARE_ROWS = 8

NORM_EPS = 1e-05
CLIP_NORM = 1.0
CONTRACT_COLS = (((1,), (1,)), ((), ()))
CONTRACT_ROWS = (((0,), (0,)), ((), ()))
MESH = pl.DeviceIdType.MESH
BF = jnp.bfloat16
F32 = jnp.float32


(
    CA, DA, DOWN, DS, FEED, FIRST, GATES, GATHER, GD, GE, GG, GM, GO, GQ, GU, GX, HID, L1, LB,
    LD, LN, MIXED, MO, MORE, N0, N1, N2, N3, OUT, P0, P1, P2, P3, Q, RF, RT, SA, SD, SL, SQ, SU,
    T0, T1, T2, T3, TB, TOTAL, U0, U1, U2, U3, UP, V0, V1, V2, V3, WA, WD, WU, Y0, Y1, Y2, Y3,
) = range(63)
ATTEND = (T0, T1, T2, T3)
EARLY = (V0, V1, V2, V3)
UNITS = (U0, U1, U2, U3)
OUTPUT = (Y0, Y1, Y2, Y3)
NORM = (N0, N1, N2, N3)
PAIR = (P0, P1, P2, P3)


FORWARD_PLAN = (
    CA, SA, L1, SU, RF, GM, SD, GM, SA, WA, GM, GX, WA, SU, GX, WA, GM, GM, WA, GX, WA, SD, GG,
    SL, WA, WU, GX, WD, GX, GM, GX, WU, WA, TB, GG, Q, WD, GM, GG, T2, T1, WD, TOTAL, T3, T0,
    TOTAL, WD, TOTAL, WD, GX, GG, SL, GG, WD, WU, TOTAL, WU, WU, WD, GG, DA, WU, GG, TOTAL,
    TOTAL, LN, WU, TOTAL, WU, GG,
)
FEED_PLAN = (
    GATHER, WU, WU, GATHER, WU, LD, GATHER, WU, WU, V0, WU, GATHER, V1, WU, V3, U1, GATHER, U3,
    N1, N3, GATHER, V2, U2, TOTAL, TOTAL, N2, U0, GE, TOTAL, DS, Y2, MORE, GD, FIRST, N0,
    GATHER, TOTAL, GU, FIRST, TOTAL, MORE, TOTAL, TOTAL, LB, HID, Y3, Y1, Y0, HID, FIRST, FIRST,
    MORE, HID,
)
BACKWARD_PLAN = (
    GATHER, UP, LD, GATES, UP, GATHER, GATHER, DOWN, FEED, P0, FEED, GATHER, P3, GATHER, P1,
    FEED, GATHER, DOWN, GATES, UP, P2, DOWN, GATHER, GO, MO, FEED, UP, GATES, RT, N2, GATES, N1,
    MO, GQ, UP, MIXED, GATES, TOTAL, MO, TOTAL, MIXED, DOWN, N3, N0, TOTAL, MO, GATES, TOTAL,
    FEED, MIXED, GATES, FEED, MIXED, TOTAL, GATES, MO, MIXED, TOTAL, GATES, GATES, MO, DOWN,
    TOTAL, MO, LB, UP, OUT, SQ, MIXED, UP,
)


def here():
    w = lax.axis_index("wide")
    n = lax.axis_index("narrow")
    return lax.div(w, SIDE), lax.rem(w, SIDE), lax.div(n, 2), lax.rem(n, 2)


def wrap(i):
    return lax.rem(i + 2 * SIDE, SIDE)


def moved(dx=0, dz=0, dy=0, dc=0):
    x, z, y, c = here()
    return (wrap(x + dx) * SIDE + wrap(z + dz), wrap(y + dy) * 2 + lax.rem(c + dc, 2))


NEAR_Y = [dict(dy=1), dict(dy=-1), dict(dc=1)]
NARROW_ALL = [dict(dy=a, dc=b) for a in range(SIDE) for b in range(2) if a or b]
NEAR_XZ = [dict(dx=1), dict(dx=-1), dict(dz=1), dict(dz=-1)]
LINES_XZ = [dict(dx=a) for a in (1, 2, 3)] + [dict(dz=a) for a in (1, 2, 3)]
WIDE_ALL = [dict(dx=a, dz=b) for a in range(SIDE) for b in range(SIDE) if a or b]


def greet(partners):
    barrier = pltpu.get_barrier_semaphore()
    for p in partners:
        pl.semaphore_signal(barrier, inc=1, device_id=moved(**p), device_id_type=MESH)
    pl.semaphore_wait(barrier, len(partners))


def span(start, size):
    if not isinstance(start, int):
        start = pl.multiple_of(start, ROWS)
    return pl.ds(start, size)


def lanes(start, size):
    if not isinstance(start, int):
        start = pl.multiple_of(start, 128)
    return pl.ds(start, size)


def step(*parts):
    for part in parts:
        next(part, None)


class Net:
    def __init__(self, send, recv, local):
        self.send, self.recv, self.local = send, recv, local
        self.used, self.used_local = 0, 0
        self.sent = []

    def put(self, src, dst, target):
        i = self.used
        self.used += 1
        copy = pltpu.make_async_remote_copy(
            src_ref=src,
            dst_ref=dst,
            send_sem=self.send.at[i],
            recv_sem=self.recv.at[i],
            device_id=target,
            device_id_type=MESH,
        )
        copy.start()
        self.sent.append(copy)
        return copy

    def keep(self, src, dst):
        i = self.used_local
        self.used_local += 1
        copy = pltpu.make_async_copy(src, dst, self.local.at[i])
        copy.start()
        return copy

    def sent_by(self, *copies):
        for copy in copies:
            copy.wait_send()
        done = [id(copy) for copy in copies]
        self.sent = [copy for copy in self.sent if id(copy) not in done]

    def finish(self):
        for copy in self.sent:
            copy.wait_send()


def take_turns(*parts):
    live = list(parts)
    while live:
        still = []
        for part in live:
            try:
                next(part)
                still.append(part)
            except StopIteration:
                pass
        live = still


def follow(plan, works, moves):
    for name in plan:
        if name in works:
            works[name]()
        else:
            next(moves[name], None)
    take_turns(*moves.values())


def comm_call(body, ins, outs, scratch, cid, copies, locals_, name, vmem=63, cost=None):
    n_in, n_out, n_scr = len(ins), len(outs), len(scratch)

    def kernel(*refs):
        in_refs = refs[:n_in]
        out_refs = refs[n_in : n_in + n_out]
        scr = refs[n_in + n_out : n_in + n_out + n_scr]
        send, recv, local = refs[n_in + n_out + n_scr :]
        net = Net(send, recv, local)
        body(net, in_refs, out_refs, scr)
        net.finish()
        assert net.used <= copies and net.used_local <= locals_, (net.used, net.used_local)

    return pl.pallas_call(
        kernel,
        out_shape=outs,
        in_specs=[pl.BlockSpec(memory_space=pl.ANY)] * n_in,
        out_specs=[pl.BlockSpec(memory_space=pl.ANY)] * n_out,
        scratch_shapes=list(scratch)
        + [
            pltpu.SemaphoreType.DMA((copies,)),
            pltpu.SemaphoreType.DMA((copies,)),
            pltpu.SemaphoreType.DMA((max(locals_, 1),)),
        ],
        compiler_params=pltpu.CompilerParams(
            collective_id=cid, has_side_effects=True, vmem_limit_bytes=vmem * 2**20
        ),
        name=name,
        cost_estimate=cost,
    )(*ins)


def gather_narrow(net, own, out):
    x, z, y, c = here()
    rows = own.shape[0]
    half = rows // 2

    def block(dy, lo=0, size=rows):
        return out.at[span((wrap(y + dy) * 2 + c) * rows + lo, size)]

    first, last = own.at[pl.ds(0, half)], own.at[pl.ds(half, half)]
    up = net.put(first, block(0, 0, half), moved(dy=1))
    down = net.put(last, block(0, half, half), moved(dy=-1))
    up_late = net.put(last, block(0, half, half), moved(dy=1))
    down_late = net.put(first, block(0, 0, half), moved(dy=-1))
    across = [net.put(own, block(0), moved(dc=1))]
    mine = net.keep(own, block(0))
    yield
    mine.wait()
    across[0].wait_recv()
    yield
    up.wait_recv()
    on = net.put(block(-1, 0, half), block(-1, 0, half), moved(dy=1))
    down.wait_recv()
    back = net.put(block(1, half, half), block(1, half, half), moved(dy=-1))
    yield
    up_late.wait_recv()
    across.append(net.put(block(-1), block(-1), moved(dc=1)))
    down_late.wait_recv()
    across.append(net.put(block(1), block(1), moved(dc=1)))
    across[1].wait_recv()
    across[2].wait_recv()
    yield
    on.wait_recv()
    across.append(net.put(block(2, 0, half), block(2, 0, half), moved(dc=1)))
    back.wait_recv()
    across.append(net.put(block(2, half, half), block(2, half, half), moved(dc=1)))
    yield
    across[3].wait_recv()
    across[4].wait_recv()
    yield
    net.sent_by(up, down, up_late, down_late, on, back, *across)


GATHER_COPIES = 12


def gather_small(net, own, out):
    c = here()[3]
    y = here()[2]
    rows = own.shape[0]

    def block(dy):
        return out.at[span((wrap(y + dy) * 2 + c) * rows, rows)]

    along = [net.put(own, block(0), moved(dy=d)) for d in (2, 1, 3)]
    across = [net.put(own, block(0), moved(dc=1))]
    mine = net.keep(own, block(0))
    yield
    for copy, d in zip(along, (2, 1, 3)):
        copy.wait_recv()
        across.append(net.put(block(-d), block(-d), moved(dc=1)))
    yield
    mine.wait()
    for copy in across:
        copy.wait_recv()


GATHER_SMALL_COPIES = 7


def gather_call(own, cid, name):
    rows, cols = own.shape

    def body(net, ins, outs, scr):
        greet(NEAR_Y)
        take_turns(gather_narrow(net, ins[0], outs[0]))

    return comm_call(
        body,
        [own],
        [jax.ShapeDtypeStruct((NARROW * rows, cols), own.dtype)],
        [],
        cid,
        GATHER_COPIES,
        1,
        name,
    )[0]


def reduce_scratch(rows, cols):
    return [
        pltpu.VMEM((SIDE, rows, cols), BF),
        pltpu.VMEM((SIDE, rows, cols), BF),
        pltpu.VMEM((2, rows // 2, cols), BF),
        pltpu.VMEM((2, rows, cols), BF),
        pltpu.VMEM((3, rows, cols), BF),
        pltpu.VMEM((rows, cols), F32),
    ]


REDUCE_COPIES = 10
REDUCE_LOCALS = 5


def reduce_narrow(net, part, scr):
    own, other, through, landed, ready, total = scr
    x, z, y, c = here()
    rows, cols = total.shape
    half = rows // 2

    def block(dy, core):
        return part.at[span((wrap(y + dy) * 2 + core) * rows, rows)]

    order = (2, 1, 3, 0)
    local, cross = {}, {}
    for dy in order:
        cross[dy] = net.put(block(dy, 1 - c), other.at[dy], moved(dc=1))
        local[dy] = net.keep(block(dy, c), own.at[dy])

    def pair(dy, lo, size):
        s = span(lo, size)
        return own[dy, s, :].astype(F32) + other[dy, s, :].astype(F32)

    yield
    local[2].wait()
    cross[2].wait_recv()
    ready[0] = pair(2, 0, rows).astype(BF)
    first, last = span(0, half), span(half, half)
    via_up = net.put(ready.at[0, first], through.at[0], moved(dy=1))
    via_down = net.put(ready.at[0, last], through.at[1], moved(dy=-1))
    yield
    local[1].wait()
    cross[1].wait_recv()
    ready[1, last, :] = pair(1, half, half).astype(BF)
    up_late = net.put(ready.at[1, last], landed.at[0, last], moved(dy=1))
    local[3].wait()
    cross[3].wait_recv()
    ready[2, first, :] = pair(3, 0, half).astype(BF)
    down_first = net.put(ready.at[2, first], landed.at[1, first], moved(dy=-1))
    yield
    via_up.wait_recv()
    ready[1, first, :] = (pair(1, 0, half) + through[0].astype(F32)).astype(BF)
    up_first = net.put(ready.at[1, first], landed.at[0, first], moved(dy=1))
    via_down.wait_recv()
    ready[2, last, :] = (pair(3, half, half) + through[1].astype(F32)).astype(BF)
    down_late = net.put(ready.at[2, last], landed.at[1, last], moved(dy=-1))
    yield
    local[0].wait()
    cross[0].wait_recv()
    total[...] = pair(0, 0, rows)
    yield
    for copy in (up_late, down_first, up_first, down_late):
        copy.wait_recv()
    total[...] += landed[0].astype(F32) + landed[1].astype(F32)


def pairs_scratch(rows, cols):
    return [
        pltpu.VMEM((SIDE * 2 * rows, cols), BF),
        pltpu.VMEM((SIDE, rows, cols), BF),
        pltpu.VMEM((2, rows // 2, cols), BF),
        pltpu.VMEM((2, rows, cols), BF),
        pltpu.VMEM((3, rows, cols), BF),
        pltpu.VMEM((rows, cols), F32),
    ]


PAIR_ORDER = (2, 1, 3, 0)


class Pairs:
    def __init__(self, net, out, scr, far_first=True):
        self.net, self.out, self.scr, self.far_first = net, out, scr, far_first
        self.crossed = {}

    def store(self, dy, value):
        rows = value.shape[0]
        self.scr[0][pl.ds(dy * rows, rows), :] = value.astype(BF)

    def cross(self, dy):
        parts, other = self.scr[:2]
        c = here()[3]
        rows = other.shape[1]
        self.crossed[dy] = self.net.put(
            parts.at[span((2 * dy + 1 - c) * rows, rows)], other.at[dy], moved(dc=1)
        )

    def steps(self):
        net = self.net
        parts, other, through, landed, ready, total = self.scr
        c = here()[3]
        rows = total.shape[0]
        half = rows // 2
        first, last = pl.ds(0, half), pl.ds(half, half)

        def pair(dy, lo, size):
            mine = parts[span((2 * dy + c) * rows + lo, size), :].astype(F32)
            return mine + other[dy, pl.ds(lo, size), :].astype(F32)

        def far():
            self.crossed[2].wait_recv()
            ready[0] = pair(2, 0, rows).astype(BF)
            via_up = net.put(ready.at[0, first], through.at[0], moved(dy=1))
            via_down = net.put(ready.at[0, last], through.at[1], moved(dy=-1))
            return via_up, via_down

        if self.far_first:
            via_up, via_down = far()
            yield
        self.crossed[1].wait_recv()
        ready[1, last, :] = pair(1, half, half).astype(BF)
        up_late = net.put(ready.at[1, last], landed.at[0, last], moved(dy=1))
        yield
        self.crossed[3].wait_recv()
        ready[2, first, :] = pair(3, 0, half).astype(BF)
        down_first = net.put(ready.at[2, first], landed.at[1, first], moved(dy=-1))
        yield
        if not self.far_first:
            via_up, via_down = far()
            yield
        via_up.wait_recv()
        ready[1, first, :] = (pair(1, 0, half) + through[0].astype(F32)).astype(BF)
        up_first = net.put(ready.at[1, first], landed.at[0, first], moved(dy=1))
        via_down.wait_recv()
        ready[2, last, :] = (pair(3, half, half) + through[1].astype(F32)).astype(BF)
        down_late = net.put(ready.at[2, last], landed.at[1, last], moved(dy=-1))
        yield
        self.crossed[0].wait_recv()
        total[...] = pair(0, 0, rows)
        yield
        for copy in (up_late, down_first, up_first, down_late):
            copy.wait_recv()
        total[...] += landed[0].astype(F32) + landed[1].astype(F32)
        if self.out is not None:
            done = net.keep(total, self.out)
            yield
            done.wait()


def spread_narrow(net, low, slab, pieces):
    w = lax.axis_index("wide")
    n = lax.axis_index("narrow")
    base = n * ROWS if slab.shape[0] == TOK else w * TOK + n * ROWS
    mine, copies = [], []
    for start, stride, width, to in pieces:
        spot = slab.at[span(base, ROWS), pl.ds(to, width)]
        for p in NARROW_ALL:
            target = moved(**p)
            columns = lanes(start + target[1] * stride, width)
            copies.append(net.put(low.at[:, columns], spot, target))
        mine.append(net.keep(low.at[:, lanes(start + n * stride, width)], spot))
    yield
    for copy in mine:
        copy.wait()
    for copy in copies:
        copy.wait_recv()


SPREAD_COPIES = 7


def gather_wide(net, slab, lead, stage=None):
    x, z, y, c = here()
    rows = TOK // 2
    half = rows // 2
    low = 0 if lead == "x" else rows

    def block(a, b, lo=0, size=rows):
        px, pz = (a, b) if lead == "x" else (b, a)
        return slab.at[span((wrap(x + px) * SIDE + wrap(z + pz)) * TOK + low + lo, size)]

    def lead_to(d):
        return moved(dx=d) if lead == "x" else moved(dz=d)

    def then_to(d):
        return moved(dz=d) if lead == "x" else moved(dx=d)

    def both(src, to, dst=None):
        dst = src if dst is None else dst
        return net.put(src, dst, to(1)), net.put(src, dst, to(-1))

    mine = block(0, 0) if stage is None else stage.at[pl.ds(low, rows)]
    fore, aft = both(mine, lead_to, block(0, 0))
    second = {0: both(mine, then_to, block(0, 0))}
    yield
    fore.wait_recv()
    on = net.put(block(-1, 0, 0, half), block(-1, 0, 0, half), lead_to(1))
    second[-1] = both(block(-1, 0), then_to)
    aft.wait_recv()
    back = net.put(block(1, 0, half, half), block(1, 0, half, half), lead_to(-1))
    second[1] = both(block(1, 0), then_to)
    yield
    last = []

    def relay(a):
        f, b = second[a]
        f.wait_recv()
        last.append(net.put(block(a, -1, 0, half), block(a, -1, 0, half), then_to(1)))
        b.wait_recv()
        last.append(net.put(block(a, 1, half, half), block(a, 1, half, half), then_to(-1)))

    kept = None if stage is None else net.keep(mine, block(0, 0))
    relay(0)
    yield
    on.wait_recv()
    back.wait_recv()
    second[2] = both(block(2, 0), then_to)
    yield
    relay(-1)
    relay(1)
    yield
    relay(2)
    yield
    if kept is not None:
        kept.wait()
    for copy in last:
        copy.wait_recv()


WIDE_COPIES = 20


def mean_of(values):
    return jnp.sum(values, axis=-1, keepdims=True) * (1.0 / D)


def normal(values):
    centered = values - mean_of(values)
    inverse = lax.rsqrt(mean_of(centered * centered) + NORM_EPS)
    return centered * inverse, inverse


def normal_back(hat, inverse, d_hat):
    return inverse * (d_hat - mean_of(d_hat) - hat * mean_of(d_hat * hat))


def turn(values, cosine, sine):
    return values * cosine + pltpu.roll(values, HEAD_DIM // 2, 1) * sine


def allowed_keys(first_row, rows, first_length):
    query = first_row + lax.broadcasted_iota(jnp.int32, (rows, 1), 0)
    key = lax.broadcasted_iota(jnp.int32, (rows, GROUP), 1)
    start = jnp.where(query >= first_length, first_length, 0)
    return (key <= query) & (key >= start)


PICK_ATTN, PICK_FFN, GATE_FFN = 0, 32, 64
LATER_UNITS = 512


def branch_mask(marks, lane):
    n = lax.axis_index("narrow").astype(F32)
    return (n < 2.0 * (marks[:, lane : lane + 1] + 1.0)).astype(F32)


def half_turns(first_length, frequency, tv):
    rows = 64
    half = GROUP // 2
    left = lax.broadcasted_iota(jnp.int32, (rows, 128), 1) < HEAD_DIM // 2
    row = lax.broadcasted_iota(jnp.int32, (rows, 128), 0)

    @pl.loop(0, half // rows)
    def _(i):
        token = row + i * rows + jnp.where(left, 0, half)
        position = token - jnp.where(token >= first_length, first_length, 0)
        angles = position.astype(F32) * frequency
        cosine, sine = jnp.cos(angles), jnp.sin(angles)
        cosine_other = pltpu.roll(cosine, HEAD_DIM // 2, 1)
        sine_other = pltpu.roll(sine, HEAD_DIM // 2, 1)
        low, high = span(i * rows, rows), span(half + i * rows, rows)
        tv[0, low, :] = jnp.where(left, cosine, cosine_other)
        tv[0, high, :] = jnp.where(left, cosine_other, cosine)
        tv[1, low, :] = jnp.where(left, -sine, sine_other)
        tv[1, high, :] = jnp.where(left, -sine_other, sine)


GELU_SCALE = (2.0 / 3.141592653589793) ** 0.5
GELU_CUBE = 0.044715


def route(normed, first_layer, second_layer, picks):
    before = jnp.dot(normed, first_layer, preferred_element_type=F32)
    square = before * before
    bent = jnp.tanh(GELU_SCALE * before * (1.0 + GELU_CUBE * square))
    hidden = 0.5 * before * (1.0 + bent)
    slope = 0.5 * (1.0 + bent) + 0.5 * before * (1.0 - bent * bent) * GELU_SCALE * (
        1.0 + 3.0 * GELU_CUBE * square
    )
    logits = jnp.dot(hidden.astype(BF), second_layer, preferred_element_type=F32)
    lane = lax.broadcasted_iota(jnp.int32, logits.shape, 1)
    gates, logit_slopes, slopes = [], [], []
    for branch in range(2):
        start = branch * LEVELS
        inside = (lane >= start) & (lane < start + LEVELS)
        shown = jnp.where(inside, logits, -1e30)
        expo = jnp.exp(shown - jnp.max(shown, axis=-1, keepdims=True))
        expo = jnp.where(inside, expo, 0.0)
        probs = expo / jnp.sum(expo, axis=-1, keepdims=True)
        chosen = jnp.where(lane.astype(F32) == picks[branch] + float(start), 1.0, 0.0)
        gate = float(LEVELS) * jnp.sum(probs * chosen, axis=-1, keepdims=True)
        logit_slope = gate * (chosen - probs)
        gates.append(gate)
        logit_slopes.append(logit_slope)
        slopes.append(
            slope
            * lax.dot_general(
                logit_slope.astype(BF), second_layer, CONTRACT_COLS, preferred_element_type=F32
            )
        )
    return hidden, gates, logit_slopes, slopes


def attention_forward(
    tokens, picks, lengths, frequency, gains, router_in, router_out, master, upstream, cid
):
    pair_rows = 2 * TOK
    head_part = D // NARROW
    units = FF // NARROW
    low = jax.ShapeDtypeStruct((GROUP, head_part), BF)
    results = dict(
        attn_sum=jax.ShapeDtypeStruct((TOK, D), F32),
        q=low,
        k=low,
        v=low,
        p=jax.ShapeDtypeStruct((GROUP, 2 * GROUP), BF),
        a=low,
        g=jax.ShapeDtypeStruct((GROUP, D), BF),
        slab_a=jax.ShapeDtypeStruct((D, 4 * head_part), BF),
        slab_up=jax.ShapeDtypeStruct((D, units - LATER_UNITS), BF),
        stage_up=jax.ShapeDtypeStruct((TOK, LATER_UNITS), BF),
        slab_down=jax.ShapeDtypeStruct((D, units), BF),
        normed=jax.ShapeDtypeStruct((GROUP, D), BF),
        marks=jax.ShapeDtypeStruct((GROUP, 128), F32),
        after=jax.ShapeDtypeStruct((TOK, D), F32),
        second=jax.ShapeDtypeStruct((TOK, D), BF),
        d_act=jax.ShapeDtypeStruct((GROUP, units), F32),
        turns=jax.ShapeDtypeStruct((2, GROUP, HEAD_DIM), F32),
        router_low=jax.ShapeDtypeStruct((D, RH), BF),
        hidden=jax.ShapeDtypeStruct((TOK, RH), F32),
        gate=jax.ShapeDtypeStruct((TOK, 128), F32),
        logit_slopes=jax.ShapeDtypeStruct((2, TOK, 128), F32),
        slopes=jax.ShapeDtypeStruct((2, TOK, RH), F32),
    )
    held = tuple(k for k in results if k not in ("attn_sum", "slab_up", "stage_up"))
    own_inputs = (tokens, picks, lengths, frequency, gains, router_in, router_out)

    def body(net, ins, outs, scr):
        out = dict(zip(results, outs))
        to = dict(zip(held, scr))
        scr = scr[len(held) :]
        xv, wv, tv, mv = to["normed"], to["slab_a"], to["turns"], to["marks"]
        qv, kv, vv, pv, av = (to[k] for k in "qkvpa")
        held_in, scr = scr[:7], scr[7:]
        own_tokens, own_picks, lv, fv, own_gains, rv, ov = held_in
        stage_up, stage_down, normed_own, marks_own, full, low = scr[:6]
        pairs = scr[6:]
        master, upstream = ins[7:]
        x, z, y, c = here()
        master_load = net.keep(master, full)
        loads = [net.keep(a, b) for a, b in zip(ins[:7], held_in)]
        greet(NARROW_ALL + NEAR_XZ)
        sums = Pairs(net, out["attn_sum"], pairs)
        stores = []

        def store(*names):
            stores.extend([net.keep(to[name], out[name]) for name in names])

        moves = {
            SA: spread_narrow(
                net, low, wv, [(i * D, head_part, head_part, i * head_part) for i in range(4)]
            ),
            SU: spread_narrow(net, low, stage_up, [(4 * D, units, units - LATER_UNITS, 0)]),
            SL: spread_narrow(
                net,
                low,
                out["stage_up"],
                [(4 * D + units - LATER_UNITS, units, LATER_UNITS, 0)],
            ),
            SD: spread_narrow(net, low, stage_down, [(4 * D + FF, units, units, 0)]),
            GX: gather_narrow(net, normed_own, xv),
            GM: gather_narrow(net, marks_own, mv),
            GG: gather_narrow(net, upstream, to["g"]),
            WA: side_by_side(*[gather_wide(net, wv, k) for k in "xz"]),
            WU: side_by_side(*[gather_wide(net, out["slab_up"], k, stage_up) for k in "xz"]),
            WD: side_by_side(*[gather_wide(net, to["slab_down"], k, stage_down) for k in "xz"]),
            TOTAL: sums.steps(),
        }

        def cast():
            master_load.wait()

            @pl.loop(0, low.shape[1] // 2048)
            def _(i):
                columns = lanes(i * 2048, 2048)
                low[:, columns] = full[:, columns].astype(BF)

        def first_norm():
            for load in loads:
                load.wait()
            hat, _ = normal(own_tokens[...].astype(F32))
            normed_own[...] = (hat * own_gains[0:1, :]).astype(BF)

        def route_own():
            to["router_low"][...] = rv[...].astype(BF)
            row = lax.broadcasted_iota(jnp.int32, (TOK, TOK), 0)
            lane = lax.broadcasted_iota(jnp.int32, (TOK, TOK), 1)
            level = [
                jnp.sum(
                    jnp.where(row == lane, own_picks[b : b + 1, :].astype(F32), 0.0),
                    axis=-1,
                    keepdims=True,
                )
                for b in range(2)
            ]
            hidden, gates, logit_slopes, slopes = route(
                normed_own[...], to["router_low"][...], ov[...], level
            )
            to["hidden"][...] = hidden
            to["gate"][...] = jnp.broadcast_to(gates[0], (TOK, 128))
            for branch in range(2):
                to["logit_slopes"][branch] = logit_slopes[branch]
                to["slopes"][branch] = slopes[branch]
            other = jnp.where(lane < GATE_FFN, level[1], gates[1])
            marks_own[...] = jnp.where(lane < PICK_FFN, level[0], other)
            store("router_low", "hidden", "gate", "logit_slopes", "slopes")

        def tables():
            half_turns(lv[0:1, 0:1], fv[0:1, :], tv)
            store("turns")

        def down_back():
            store("g", "slab_down")

            @pl.loop(0, SIDE)
            def _(i):
                r = span(i * pair_rows, pair_rows)
                to["d_act"][r, :] = jnp.dot(
                    to["g"][r, :], to["slab_down"][...], preferred_element_type=F32
                )

            store("d_act")

        def project():
            store("normed", "slab_a")

            @pl.loop(0, SIDE)
            def _(i):
                r = span(i * pair_rows, pair_rows)
                proj = jnp.dot(xv[r, :], wv[:, : 3 * head_part], preferred_element_type=F32)
                cosine, sine = tv[0, r, :], tv[1, r, :]
                for h in range(2):
                    at = pl.ds(h * HEAD_DIM, HEAD_DIM)
                    a = h * HEAD_DIM
                    qv[r, at] = turn(proj[:, a : a + HEAD_DIM], cosine, sine).astype(BF)
                    a += head_part
                    kv[r, at] = turn(proj[:, a : a + HEAD_DIM], cosine, sine).astype(BF)
                vv[r, :] = proj[:, 2 * head_part :].astype(BF)

            store("q", "k", "v")

        def attend(dy):
            first = wrap(y + dy) * pair_rows
            r = span(first, pair_rows)
            allowed = allowed_keys(first, pair_rows, lv[0:1, 0:1])
            heads = []
            for h in range(2):
                at = pl.ds(h * HEAD_DIM, HEAD_DIM)
                scores = lax.dot_general(
                    qv[r, at], kv[:, at], CONTRACT_COLS, preferred_element_type=F32
                )
                scores = jnp.where(allowed, scores * HEAD_DIM ** (-0.5), -1e30)
                expo = jnp.exp(scores - jnp.max(scores, axis=-1, keepdims=True))
                probs = expo * (1.0 / jnp.sum(expo, axis=-1, keepdims=True))
                low = probs.astype(BF)
                pv[r, pl.ds(h * GROUP, GROUP)] = low
                heads.append(jnp.dot(low, vv[:, at], preferred_element_type=F32))
            mask = branch_mask(mv[r, :], PICK_ATTN)
            av[r, :] = (jnp.concatenate(heads, axis=1) * mask).astype(BF)
            back = lax.dot_general(
                av[r, :], wv[:, 3 * head_part :], CONTRACT_COLS, preferred_element_type=F32
            )
            sums.store(dy, back)
            sums.cross(dy)

        def second_norm():
            values = own_tokens[...].astype(F32) + to["gate"][:, :1] * sums.scr[5][...]
            to["after"][...] = values
            to["second"][...] = (normal(values)[0] * own_gains[1:2, :]).astype(BF)
            store("after", "second")

        works = {
            CA: cast,
            L1: first_norm,
            RF: route_own,
            TB: tables,
            Q: project,
            LN: second_norm,
            DA: down_back,
        }
        for dy in PAIR_ORDER:
            works[ATTEND[dy]] = functools.partial(attend, dy)
        follow(FORWARD_PLAN, works, moves)
        store("p", "a", "marks")
        for done in stores:
            done.wait()

    got = comm_call(
        body,
        list(own_inputs) + [master, upstream],
        list(results.values()),
        [pltpu.VMEM(results[k].shape, results[k].dtype) for k in held]
        + [pltpu.VMEM(r.shape, r.dtype) for r in own_inputs]
        + [
            pltpu.VMEM((TOK, units - LATER_UNITS), BF),
            pltpu.VMEM((TOK, units), BF),
            pltpu.VMEM((TOK, D), BF),
            pltpu.VMEM((TOK, 128), F32),
            pltpu.VMEM(master.shape, F32),
            pltpu.VMEM(master.shape, BF),
        ]
        + pairs_scratch(TOK, D),
        cid,
        REDUCE_COPIES + 6 * WIDE_COPIES + 3 * GATHER_COPIES + 7 * SPREAD_COPIES,
        8 + 7 + 3 + 4 + 1 + len(held),
        "attention_forward",
    )
    return dict(zip(results, got))


def first_scratch(cols):
    part, half = TOK // 2, TOK // 4
    return [
        pltpu.VMEM((2, 2, SIDE, half, cols), BF),
        pltpu.VMEM((2, 2, SIDE, part, cols), BF),
        pltpu.VMEM((2, 2, SIDE, half, cols), BF),
        pltpu.VMEM((2, SIDE, part, cols), BF),
    ]


def second_scratch(cols):
    part, half = TOK // 2, TOK // 4
    return [
        pltpu.VMEM((2, 2, half, cols), BF),
        pltpu.VMEM((2, 2, part, cols), BF),
        pltpu.VMEM((2, 2, half, cols), BF),
        pltpu.VMEM((TOK, cols), BF),
    ]


FIRST_COPIES = 12
SECOND_COPIES = 12
FIRST_LOCALS = 6


def lead_moves(lead):
    def lead_to(d):
        return moved(dx=d) if lead == "x" else moved(dz=d)

    def then_to(d):
        return moved(dz=d) if lead == "x" else moved(dx=d)

    return lead_to, then_to


def reduce_first(net, grad, scr, lead):
    via, landed, ready, sums = scr
    x, z, y, c = here()
    part, half = TOK // 2, TOK // 4
    k = 0 if lead == "x" else 1
    low = k * part
    blocks = grad.reshape(SIDE, SIDE, TOK, grad.shape[1])
    first, last = pl.ds(0, half), pl.ds(half, half)
    lead_to, _ = lead_moves(lead)

    def line(d, lo, size):
        rows = pl.ds(low + lo, size)
        if lead == "x":
            return (wrap(x + d), slice(None), rows, slice(None))
        return (slice(None), wrap(z + d), rows, slice(None))

    via_up = net.put(blocks.at[line(2, 0, half)], via.at[k, 0], lead_to(1))
    via_down = net.put(blocks.at[line(2, half, half)], via.at[k, 1], lead_to(-1))
    up_late = net.put(blocks.at[line(1, half, half)], landed.at[k, 0, :, last], lead_to(1))
    down_first = net.put(blocks.at[line(3, 0, half)], landed.at[k, 1, :, first], lead_to(-1))
    loads = [
        net.keep(blocks.at[line(1, 0, half)], ready.at[k, 0]),
        net.keep(blocks.at[line(3, half, half)], ready.at[k, 1]),
        net.keep(blocks.at[line(0, 0, part)], sums.at[k]),
    ]
    yield
    for load in loads:
        load.wait()
    via_up.wait_recv()

    @pl.loop(0, SIDE)
    def _(i):
        ready[k, 0, i] = (ready[k, 0, i].astype(F32) + via[k, 0, i].astype(F32)).astype(BF)

    up_first = net.put(ready.at[k, 0], landed.at[k, 0, :, first], lead_to(1))
    via_down.wait_recv()

    @pl.loop(0, SIDE)
    def _(i):
        ready[k, 1, i] = (ready[k, 1, i].astype(F32) + via[k, 1, i].astype(F32)).astype(BF)

    down_late = net.put(ready.at[k, 1], landed.at[k, 1, :, last], lead_to(-1))
    yield
    for copy in (up_late, down_first, up_first, down_late):
        copy.wait_recv()

    @pl.loop(0, SIDE)
    def _(i):
        both = landed[k, 0, i].astype(F32) + landed[k, 1, i].astype(F32)
        sums[k, i] = (sums[k, i].astype(F32) + both).astype(BF)


def reduce_second(net, sums, scr, lead):
    via, landed, ready, total = scr
    x, z, y, c = here()
    part, half = TOK // 2, TOK // 4
    k = 0 if lead == "x" else 1
    first, last = pl.ds(0, half), pl.ds(half, half)
    _, then_to = lead_moves(lead)
    me = z if lead == "x" else x

    def block(d, rows):
        return sums.at[k, wrap(me + d), rows]

    via_up = net.put(block(2, first), via.at[k, 0], then_to(1))
    via_down = net.put(block(2, last), via.at[k, 1], then_to(-1))
    up_late = net.put(block(1, last), landed.at[k, 0, last], then_to(1))
    down_first = net.put(block(3, first), landed.at[k, 1, first], then_to(-1))
    yield
    via_up.wait_recv()
    ready[k, 0] = (block(1, first)[...].astype(F32) + via[k, 0].astype(F32)).astype(BF)
    up_first = net.put(ready.at[k, 0], landed.at[k, 0, first], then_to(1))
    via_down.wait_recv()
    ready[k, 1] = (block(3, last)[...].astype(F32) + via[k, 1].astype(F32)).astype(BF)
    down_late = net.put(ready.at[k, 1], landed.at[k, 1, last], then_to(-1))
    yield
    for copy in (up_late, down_first, up_first, down_late):
        copy.wait_recv()
    both = landed[k, 0].astype(F32) + landed[k, 1].astype(F32)
    total[pl.ds(k * part, part), :] = (sums[k, me].astype(F32) + both).astype(BF)


def side_by_side(*parts):
    while True:
        if StopIteration in [next(part, StopIteration) for part in parts]:
            break
        yield


def return_narrow(net, total, out, pieces):
    n = lax.axis_index("narrow")
    copies, mine = [], []
    for start, width, to in pieces:
        spot = out.at[:, lanes(to + n * width, width)]
        columns = pl.ds(start, width)
        for p in NARROW_ALL:
            target = moved(**p)
            copies.append(net.put(total.at[span(target[1] * ROWS, ROWS), columns], spot, target))
        mine.append(net.keep(total.at[span(n * ROWS, ROWS), columns], spot))
    yield
    for copy in mine:
        copy.wait()
    for copy in copies:
        copy.wait_recv()


def second_then_narrow(net, sums, out, scr, pieces):
    yield from side_by_side(*[reduce_second(net, sums, scr, lead) for lead in "xz"])
    yield from return_narrow(net, scr[3], out, pieces)


def wide_then_narrow(net, grad, out, scr, pieces):
    yield from side_by_side(*[reduce_first(net, grad, scr[:4], lead) for lead in "xz"])
    yield from second_then_narrow(net, scr[3], out, scr[4:], pieces)


def feed_forward(normed_own, upstream, w_up, stage_up, w_down, d_act, marks, own, cid):
    pair_rows = 2 * TOK
    units = FF // NARROW
    strip = 256

    def body(net, ins, outs, scr):
        own, upstream, up_in, stage_in, down_in, da_in, marks = ins[:7]
        kept_up = up_in.shape[1]
        rest = pl.ds(kept_up, units - kept_up)
        ffn_part, g_up, down_sums, after_out, attn_out, hidden_out, vector_out = outs
        xv, dv, w_up, w_down, mv, act, du, da, gu, yv = scr[:10]
        gated, dots, dots_in = scr[16:19]
        held, d_attn, d_hidden, vector = scr[19:26], *scr[26:29]
        gds, firsts = scr[29:31], (scr[31:35], scr[35:39])
        stage = scr[39]
        n = lax.axis_index("narrow")
        x, z, y, c = here()
        loads = [
            net.keep(a, b)
            for a, b in (
                (stage_in, stage),
                (marks, mv),
                (up_in, w_up.at[:, pl.ds(0, kept_up)]),
                (da_in, da),
                (upstream, dv),
                (down_in, w_down),
            )
        ]
        own_loads = [net.keep(a, b) for a, b in zip(ins[7:], held)]
        greet(NARROW_ALL + NEAR_XZ)
        loads.pop(0).wait()
        sums = Pairs(net, None, scr[10:16], far_first=False)
        stores, dot_copies = [], []

        def gradient(left, right, to):
            @pl.loop(0, D // strip)
            def _(i):
                at = lanes(i * strip, strip)
                to[span(i * strip, strip), :] = lax.dot_general(
                    left[:, at], right[...], CONTRACT_ROWS, preferred_element_type=F32
                ).astype(BF)

        def wait_loads():
            for load in loads:
                load.wait()

        def half_gradient(i):
            columns = pl.ds(i * units // 2, units // 2)
            gradient(dv, gated.at[:, columns], gds[i])

        def units_of(dy, later):
            r = span(wrap(y + dy) * pair_rows, pair_rows)
            columns = rest if later else pl.ds(0, kept_up)
            up = jnp.dot(xv[r, :], w_up[:, columns], preferred_element_type=F32)
            positive = jnp.maximum(up, 0.0)
            masked = positive * branch_mask(mv[r, :], PICK_FFN)
            gate = mv[r, GATE_FFN : GATE_FFN + 1]
            active = positive * masked
            act[r, columns] = active.astype(BF)
            gated[r, columns] = (active * gate).astype(BF)
            back = da[r, columns]
            du[r, columns] = (back * (2.0 * gate * masked)).astype(BF)
            dot = lax.dot_general(
                jnp.ones((8, up.shape[1]), BF),
                (back * active).astype(BF),
                CONTRACT_COLS,
                preferred_element_type=F32,
            )
            for core in range(2):
                spot = wrap(y + dy) * 2 + core
                part = dot[:, core * TOK : (core + 1) * TOK]
                dots[spot] = dots[spot] + part if later else part

        def norm_back(dy):
            r = span(wrap(y + dy) * pair_rows, pair_rows)
            back = lax.dot_general(
                du[r, :], w_up[...], CONTRACT_COLS, preferred_element_type=F32
            )
            sums.store(dy, back)
            sums.cross(dy)

        def send_dots():
            for p in NARROW_ALL:
                target = moved(**p)
                dot_copies.append(net.put(dots.at[target[1]], dots_in.at[n], target))
            dots_in[n] = dots[n]

        def up_gradient():
            gradient(xv, du, gu)
            stores.append(net.keep(gu, g_up))

        def output(dy):
            r = span(wrap(y + dy) * pair_rows, pair_rows)
            yv[r, :] = lax.dot_general(
                act[r, :], w_down[...], CONTRACT_COLS, preferred_element_type=F32
            ).astype(BF)
            stores.append(net.keep(yv.at[r], ffn_part.at[r]))

        def second_norm_back():
            for load in own_loads:
                load.wait()
            for copy in dot_copies:
                copy.wait_recv()
            s = dots_in[0]
            for i in range(1, NARROW):
                s = s + dots_in[i]
            row = lax.broadcasted_iota(jnp.int32, (TOK, TOK), 0)
            lane = lax.broadcasted_iota(jnp.int32, (TOK, TOK), 1)
            ffn = jnp.sum(jnp.where(row == lane, s[0:1, :], 0.0), axis=-1, keepdims=True)
            after, attn, gate, gains, slopes, logit_slopes, hidden = held
            total = sums.scr[5]
            hat, inverse = normal(after[...])
            d_gain = jnp.sum(total[...] * hat, axis=0, keepdims=True)
            back = normal_back(hat, inverse, total[...] * gains[1:2, :])
            back = back + dv[span(n * TOK, TOK), :].astype(F32)
            total[...] = back
            d_attn[...] = (back * gate[:, :1]).astype(BF)
            attn_gate = jnp.sum(back * attn[...], axis=-1, keepdims=True)
            d_hidden[...] = (attn_gate * slopes[0] + ffn * slopes[1]).astype(BF)
            d_logits = attn_gate * logit_slopes[0] + ffn * logit_slopes[1]
            d_router = lax.dot_general(
                d_logits.astype(BF),
                hidden[...].astype(BF),
                CONTRACT_ROWS,
                preferred_element_type=F32,
            )
            vector[...] = jnp.zeros_like(vector)
            for i in range(GAIN_ROWS // 2):
                at = GAIN_ROWS // 2 + i
                vector[at : at + 1, :] = d_gain[:, i * 128 : (i + 1) * 128]
            for i in range(RH // 128):
                at = GAIN_ROWS + i * 2 * LEVELS
                vector[at : at + 2 * LEVELS, :] = d_router[: 2 * LEVELS, i * 128 : (i + 1) * 128]
            own_marks = mv[span(n * TOK, TOK), :]
            levels = lane.astype(F32)
            picked = jnp.where(levels == own_marks[:, PICK_ATTN : PICK_ATTN + 1], 1.0, 0.0)
            other = own_marks[:, PICK_FFN : PICK_FFN + 1] + float(LEVELS)
            picked = picked + jnp.where(levels == other, 1.0, 0.0)
            vector[SMALL_ROWS : SMALL_ROWS + 1, :] = jnp.sum(picked, axis=0, keepdims=True)
            pairs = zip(
                (total, d_attn, vector),
                (after_out, attn_out, vector_out),
            )
            stores.extend([net.keep(a, b) for a, b in pairs])

        works = {
            LD: wait_loads,
            GD: functools.partial(half_gradient, 0),
            GE: functools.partial(half_gradient, 1),
            GU: up_gradient,
            DS: send_dots,
            LB: second_norm_back,
        }
        for dy in PAIR_ORDER:
            works[EARLY[dy]] = functools.partial(units_of, dy, False)
            works[UNITS[dy]] = functools.partial(units_of, dy, True)
            works[OUTPUT[dy]] = functools.partial(output, dy)
            works[NORM[dy]] = functools.partial(norm_back, dy)
        moves = {
            GATHER: gather_narrow(net, own, xv),
            TOTAL: sums.steps(),
            FIRST: side_by_side(*[reduce_first(net, gds[0], firsts[0], lead) for lead in "xz"]),
            MORE: side_by_side(*[reduce_first(net, gds[1], firsts[1], lead) for lead in "xz"]),
            HID: gather_small(net, d_hidden, hidden_out),
            WU: side_by_side(*[gather_wide(net, w_up.at[:, rest], k, stage) for k in "xz"]),
        }
        follow(FEED_PLAN, works, moves)
        for i in range(2):
            columns = pl.ds(i * units // 2, units // 2)
            stores.append(net.keep(firsts[i][3], down_sums.at[:, :, :, columns]))
        for store in stores:
            store.wait()

    wide = pltpu.VMEM((GROUP, D), BF)
    tall = pltpu.VMEM((D, units), BF)
    square = pltpu.VMEM((GROUP, units), BF)
    return comm_call(
        body,
        [normed_own, upstream, w_up, stage_up, w_down, d_act, marks] + list(own),
        [
            jax.ShapeDtypeStruct((GROUP, D), BF),
            jax.ShapeDtypeStruct((D, units), BF),
            jax.ShapeDtypeStruct((2, SIDE, TOK // 2, units), BF),
            jax.ShapeDtypeStruct((TOK, D), F32),
            jax.ShapeDtypeStruct((TOK, D), BF),
            jax.ShapeDtypeStruct((GROUP, RH), BF),
            jax.ShapeDtypeStruct((VECTOR_ROWS, 128), F32),
        ],
        [wide, wide, tall, tall, pltpu.VMEM(marks.shape, F32), square, square]
        + [pltpu.VMEM((GROUP, units), F32), tall, wide]
        + pairs_scratch(TOK, D)
        + [square]
        + [pltpu.VMEM((NARROW, 8, TOK), F32)] * 2
        + [pltpu.VMEM(r.shape, r.dtype) for r in own]
        + [
            pltpu.VMEM((TOK, D), BF),
            pltpu.VMEM((TOK, RH), BF),
            pltpu.VMEM((VECTOR_ROWS, 128), F32),
        ]
        + [pltpu.VMEM((D, units // 2), BF)] * 2
        + first_scratch(units // 2) * 2
        + [pltpu.VMEM(stage_up.shape, BF)],
        cid,
        GATHER_COPIES + REDUCE_COPIES + 7 + 2 * FIRST_COPIES + 2 * WIDE_COPIES + GATHER_SMALL_COPIES,
        14 + 1 + 1 + 12 + 2 * FIRST_LOCALS + 2,
        "feed_forward",
    )


def squares_of(ref, rows, cols):
    s = jnp.zeros((SQUARE_ROWS, 128), F32)
    for i in range(ref.shape[0] // rows):
        for j in range(ref.shape[1] // cols):
            piece = ref[i * rows : (i + 1) * rows, j * cols : (j + 1) * cols].astype(F32)
            piece = piece * piece
            for a in range(rows // SQUARE_ROWS):
                for b in range(cols // 128):
                    s = s + piece[a * 8 : a * 8 + 8, b * 128 : b * 128 + 128]
    return s


def sum_everywhere(net, own, first, second, total):
    w = lax.axis_index("wide")
    n = lax.axis_index("narrow")

    def rows(i):
        return pl.ds(pl.multiple_of(i * 8, 8), 8)

    copies = []
    for p in NARROW_ALL:
        target = moved(**p)
        copies.append(net.put(own.at[rows(target[1])], first.at[n], target))
    first[n] = own[rows(n), :]
    for copy in copies:
        copy.wait_recv()
    s = first[0]
    for i in range(1, NARROW):
        s = s + first[i]
    second[w] = s
    copies = [net.put(second.at[w], second.at[w], moved(**p)) for p in WIDE_ALL]
    for copy in copies:
        copy.wait_recv()
    s = second[0]
    for i in range(1, WIDE):
        s = s + second[i]
    total[rows(n), :] = s
    copies = [net.put(total.at[rows(n)], total.at[rows(n)], moved(**p)) for p in NARROW_ALL]
    for copy in copies:
        copy.wait_recv()


def attention_backward(
    d_attn_own, ffn_part, g_up, down_sums, normed, hidden_in, own, kept, cid
):
    table_rows = D // NARROW
    pair_rows = 2 * TOK
    head_part = D // NARROW
    units = FF // NARROW
    strip = 256
    scale = HEAD_DIM ** (-0.5)
    scratch = (
        [pltpu.VMEM(r.shape, r.dtype) for r in kept]
        + [
            pltpu.VMEM((GROUP, D), BF),
            pltpu.VMEM((GROUP, head_part), F32),
            pltpu.VMEM((GROUP, head_part), F32),
            pltpu.VMEM((GROUP, 3 * head_part), BF),
            pltpu.VMEM((D, 3 * head_part), BF),
        ]
        + pairs_scratch(TOK, D)[1:]
        + reduce_scratch(TOK, D)
        + first_scratch(3 * head_part)
        + second_scratch(3 * head_part)
        + first_scratch(units)
        + second_scratch(units)
        + [pltpu.VMEM(down_sums.shape, BF)]
        + second_scratch(units)
        + [
            pltpu.VMEM((GROUP, table_rows), BF),
            pltpu.VMEM((GROUP, RH), BF),
            pltpu.VMEM((table_rows, RH), BF),
            pltpu.VMEM((WIDE, ROWS, RH), BF),
            pltpu.VMEM((ROWS, RH), BF),
            pltpu.VMEM((table_rows, RH), BF),
            pltpu.VMEM((1, D), F32),
        ]
        + [pltpu.VMEM(r.shape, r.dtype) for r in own]
        + [
            pltpu.VMEM((ROWS, 4 * D + 2 * FF), BF),
            pltpu.VMEM((TOK, D), BF),
            pltpu.VMEM((NARROW, 8, 128), F32),
            pltpu.VMEM((WIDE, 8, 128), F32),
            pltpu.VMEM((VECTOR_ROWS, 128), F32),
            pltpu.VMEM((8, 128), F32),
            pltpu.VMEM((D, head_part), BF),
        ]
        + first_scratch(head_part)
        + second_scratch(head_part)
    )

    def body(net, ins, outs, scr):
        d_attn_own, ffn_part, g_up, down_sums, normed, hidden_in = ins[:6]
        input_grad, result_out, block_out, table, vector_out, norm_out = outs
        wv, tv, mv, qv, kv, vv, pv, av = scr[:8]
        big, dk, dv, dproj, ga = scr[8:13]
        pairs, narrow = [big, *scr[13:18]], scr[18:24]
        wide_a, wide_up, wide_down = scr[24:32], scr[32:40], scr[40:45]
        columns, hidden, part, landed, shard, mine = scr[45:51]
        d_gain, held = scr[51], scr[52:58]
        block, result, first, second, summed, norm = scr[58:64]
        go, wide_o = scr[64], scr[65:73]
        n = lax.axis_index("narrow")
        x, z, y, c = here()
        first_load = net.keep(down_sums, wide_down[0])
        loads = [net.keep(a, b) for a, b in zip(ins[12:], scr[:8])]
        own_loads = [net.keep(a, b) for a, b in zip(ins[6:12], held)]
        loads.append(net.keep(hidden_in, hidden))
        loads.append(net.keep(normed.at[:, lanes(n * table_rows, table_rows)], columns))
        greet(NARROW_ALL + WIDE_ALL)
        sums = Pairs(net, None, pairs)
        thirds = [(i * head_part, head_part, i * D) for i in range(3)]

        def router():
            w = lax.axis_index("wide")
            part[...] = lax.dot_general(
                columns[...], hidden[...], CONTRACT_ROWS, preferred_element_type=F32
            ).astype(BF)
            copies = []
            for p in WIDE_ALL:
                target = moved(**p)
                rows = part.at[span(target[0] * ROWS, ROWS)]
                copies.append(net.put(rows, landed.at[w], target))
            kept = net.keep(part.at[span(w * ROWS, ROWS)], landed.at[w])
            yield
            kept.wait()
            for copy in copies:
                copy.wait_recv()
            s = landed[0].astype(F32)
            for i in range(1, WIDE):
                s = s + landed[i].astype(F32)
            shard[...] = s.astype(BF)
            spot = mine.at[span(w * ROWS, ROWS)]
            copies = [net.put(shard, spot, moved(**p)) for p in WIDE_ALL]
            kept = net.keep(shard, spot)
            yield
            kept.wait()
            for copy in copies:
                copy.wait_recv()
            yield from gather_narrow(net, mine, table)

        moves = {
            GATHER: gather_narrow(net, d_attn_own, big),
            DOWN: second_then_narrow(
                net, wide_down[0], block, wide_down[1:], [(0, units, 4 * D + FF)]
            ),
            UP: wide_then_narrow(net, g_up, block, wide_up, [(0, units, 4 * D)]),
            MIXED: wide_then_narrow(net, ga, block, wide_a, thirds),
            MO: wide_then_narrow(net, go, block, wide_o, [(0, head_part, 3 * D)]),
            FEED: reduce_narrow(net, ffn_part, narrow),
            GATES: router(),
            TOTAL: sums.steps(),
        }

        def wait_loads():
            first_load.wait()
            for load in loads:
                load.wait()
            dk[...] = jnp.zeros_like(dk)
            dv[...] = jnp.zeros_like(dv)

        def one_pair(dy):
            r = span(wrap(y + dy) * pair_rows, pair_rows)
            mask = branch_mask(mv[r, :], PICK_ATTN)
            back = jnp.dot(big[r, :], wv[:, 3 * head_part :], preferred_element_type=F32)
            back = (back * mask).astype(BF)
            for h in range(2):
                at = pl.ds(h * HEAD_DIM, HEAD_DIM)
                d_out = back[:, h * HEAD_DIM : (h + 1) * HEAD_DIM]
                d_probs = lax.dot_general(
                    d_out, vv[:, at], CONTRACT_COLS, preferred_element_type=F32
                )
                probs_low = pv[r, pl.ds(h * GROUP, GROUP)]
                probs = probs_low.astype(F32)
                weighted = probs * d_probs
                centre = jnp.sum(weighted, axis=-1, keepdims=True)
                ds = (weighted - probs * centre).astype(BF)
                dq = jnp.dot(ds, kv[:, at], preferred_element_type=F32) * scale
                dproj[r, at] = turn(dq, tv[0, r, :], -tv[1, r, :]).astype(BF)
                dk[:, at] += lax.dot_general(
                    ds, qv[r, at], CONTRACT_ROWS, preferred_element_type=F32
                )
                dv[:, at] += lax.dot_general(
                    probs_low, d_out, CONTRACT_ROWS, preferred_element_type=F32
                )

        refill = []

        def turn_back():
            refill.append(net.keep(normed, pv))

            @pl.loop(0, SIDE)
            def _(i):
                r = span(i * pair_rows, pair_rows)
                cosine, sine = tv[0, r, :], -tv[1, r, :]
                for h in range(2):
                    at = pl.ds(h * HEAD_DIM, HEAD_DIM)
                    to = pl.ds(head_part + h * HEAD_DIM, HEAD_DIM)
                    dproj[r, to] = turn(dk[r, at] * scale, cosine, sine).astype(BF)
                dproj[r, pl.ds(2 * head_part, head_part)] = dv[r, :].astype(BF)

        def gradient(left, right, to):
            @pl.loop(0, D // strip)
            def _(i):
                to[span(i * strip, strip), :] = lax.dot_general(
                    left[:, lanes(i * strip, strip)],
                    right[...],
                    CONTRACT_ROWS,
                    preferred_element_type=F32,
                ).astype(BF)

        def mixed_gradient():
            refill[0].wait()
            gradient(pv, dproj, ga)

        def norm_back(dy):
            r = span(wrap(y + dy) * pair_rows, pair_rows)
            back = lax.dot_general(
                dproj[r, :], wv[:, : 3 * head_part], CONTRACT_COLS, preferred_element_type=F32
            )
            sums.store(dy, back)
            sums.cross(dy)

        stores = []

        own_there = []

        def wait_own():
            if not own_there:
                own_there.append(True)
                for load in own_loads:
                    load.wait()

        def output():
            wait_own()
            gate = mv[span(n * TOK, TOK), GATE_FFN : GATE_FFN + 1]
            result[...] = (held[4][...] + gate * narrow[5][...]).astype(BF)
            stores.append(net.keep(result, result_out))

        squares = []

        def late_squares():
            squares.append(squares_of(block.at[:, pl.ds(3 * D, D + 2 * FF)], ROWS, 2048))

        def first_norm_back():
            wait_own()
            tokens, after, gains, router_in = held[:4]
            total = sums.scr[5]
            d_normed = total[...] + lax.dot_general(
                hidden[span(n * TOK, TOK), :],
                router_in[...],
                CONTRACT_COLS,
                preferred_element_type=F32,
            )
            hat, inverse = normal(tokens[...].astype(F32))
            d_gain[...] = jnp.sum(d_normed * hat, axis=0, keepdims=True)
            total[...] = after[...] + normal_back(hat, inverse, d_normed * gains[0:1, :])
            stores.append(net.keep(total, input_grad))

        works = {
            LB: first_norm_back,
            OUT: output,
            SQ: late_squares,
            LD: wait_loads,
            RT: turn_back,
            GO: functools.partial(gradient, big, av, go),
            GQ: mixed_gradient,
        }
        for dy in PAIR_ORDER:
            works[PAIR[dy]] = functools.partial(one_pair, dy)
            works[NORM[dy]] = functools.partial(norm_back, dy)
        follow(BACKWARD_PLAN, works, moves)
        stores.append(net.keep(block, block_out))
        vector = held[5]
        for i in range(GAIN_ROWS // 2):
            vector[i : i + 1, :] = d_gain[:, i * 128 : (i + 1) * 128]
        others = squares_of(block.at[:, pl.ds(0, 3 * D)], ROWS, 2048)
        others = others + squares_of(shard, ROWS, RH)
        vector[VECTOR_ROWS - SQUARE_ROWS :, :] = squares[0] + others
        sum_everywhere(net, vector, first, second, summed)
        stores.append(net.keep(summed, vector_out))
        s = summed[...]
        small = s[:SMALL_ROWS]
        sum_all = jnp.sum(small * small) + jnp.sum(s[VECTOR_ROWS - SQUARE_ROWS :])
        norm[...] = jnp.sqrt(jnp.full((8, 128), sum_all, F32))
        stores.append(net.keep(norm, norm_out))
        for store in stores:
            store.wait()

    return comm_call(
        body,
        [d_attn_own, ffn_part, g_up, down_sums, normed, hidden_in] + list(own) + list(kept),
        [
            jax.ShapeDtypeStruct((TOK, D), F32),
            jax.ShapeDtypeStruct((TOK, D), BF),
            jax.ShapeDtypeStruct((ROWS, 4 * D + 2 * FF), BF),
            jax.ShapeDtypeStruct((D, RH), BF),
            jax.ShapeDtypeStruct((VECTOR_ROWS, 128), F32),
            jax.ShapeDtypeStruct((8, 128), F32),
        ],
        scratch,
        cid,
        GATHER_COPIES
        + 2 * REDUCE_COPIES
        + 3 * FIRST_COPIES
        + 4 * SECOND_COPIES
        + 6 * 7
        + 2 * 15
        + GATHER_COPIES
        + 7 + 15 + 7,
        17 + 1 + 1 + 5 + REDUCE_LOCALS + 3 * FIRST_LOCALS + 6 + 4,
        "attention_backward",
    )


def adamw(weight, moment_one, moment_two, gradient, step_rate):
    one = 0.9 * moment_one + 0.1 * gradient
    two = 0.95 * moment_two + 0.05 * (gradient * gradient)
    scaled = jnp.maximum(two * (1.0 / (1.0 - 0.95**STEP)), 1e-30)
    root = scaled * lax.rsqrt(scaled) + 1e-08
    guess = pltpu.reciprocal(root, approx=True)
    guess = guess * (2.0 - root * guess)
    guess = guess * (2.0 - root * guess)
    rate = step_rate / (1.0 - 0.9**STEP)
    updated = weight * (1.0 - step_rate * 0.1) - (one * rate) * guess
    return updated, one, two


def clip_of(norm):
    return jnp.minimum(1.0, CLIP_NORM / norm[0:1, 0:1])


def all_steps(block, layer, gains, second_layer, vector, norm):
    block_parts, layer_parts = 3, 2
    n_loads = 4 * (block_parts + layer_parts)

    def kernel(*refs):
        block_in, layer_in = refs[0:4], refs[4:8]
        gains_in, second_in, vec, n = refs[8:11], refs[11:14], refs[14], refs[15]
        block_out, layer_out = refs[16:20], refs[20:23]
        gains_out, second_out, counts_out, norm_out = refs[23:26], refs[26:29], refs[29], refs[30]
        held_block, held_layer, new_block, new_layer = (
            refs[31:35],
            refs[35:39],
            refs[39:43],
            refs[43:46],
        )
        gain_grad, second_grad, loaded, stored = refs[46:50]
        clip = clip_of(n)

        def start(pairs, part, sems, at):
            copies = []
            for i, (a, b) in enumerate(pairs):
                copies.append(pltpu.make_async_copy(a.at[part], b.at[part], sems.at[at + i]))
                copies[-1].start()
            return copies

        parts = []
        for i in range(block_parts):
            cols = block_in[0].shape[1] // block_parts
            parts.append((True, (slice(None), pl.ds(i * cols, cols))))
        for i in range(layer_parts):
            rows = layer_in[0].shape[0] // layer_parts
            parts.append((False, (pl.ds(i * rows, rows), slice(None))))
        loads, stores = [], []
        for i, (is_block, part) in enumerate(parts):
            pairs = zip(block_in, held_block) if is_block else zip(layer_in, held_layer)
            loads.append(start(pairs, part, loaded, 4 * i))

        for i in range(GAIN_ROWS):
            row, at = i // (GAIN_ROWS // 2), i % (GAIN_ROWS // 2) * 128
            gain_grad[row : row + 1, at : at + 128] = vec[i : i + 1, :]
        for i in range(RH // 128):
            at = GAIN_ROWS + i * 2 * LEVELS
            second_grad[:, i * 128 : (i + 1) * 128] = vec[at : at + 2 * LEVELS, :]
        for held, grad, new, rate in (
            (gains_in, gain_grad, gains_out, 0.6),
            (second_in, second_grad, second_out, 0.02),
        ):
            results = adamw(*[r[...] for r in held], grad[...] * clip, rate)
            for ref, value in zip(new, results):
                ref[...] = value
        row = vec[SMALL_ROWS : SMALL_ROWS + 1, :]
        counts_out[0:1, :] = row[:, :LEVELS]
        counts_out[1:2, :] = pltpu.roll(row, 128 - LEVELS, 1)[:, :LEVELS]
        norm_out[...] = n[0:1, 0:1]

        for i, (is_block, part) in enumerate(parts):
            for copy in loads[i]:
                copy.wait()
            held, new = (held_block, new_block) if is_block else (held_layer, new_layer)
            gradient = held[3][part].astype(F32) * clip
            results = adamw(*[r[part] for r in held[:3]], gradient, 0.02)
            for ref, value in zip(new, results):
                ref[part] = value
            if is_block:
                new[3][part] = results[0].astype(BF)
            pairs = zip(new, block_out if is_block else layer_out)
            stores += start(pairs, part, stored, 4 * i)
        for copy in stores:
            copy.wait()

    def like(x, dtype=F32):
        return jax.ShapeDtypeStruct(x.shape, dtype)

    def room(x, dtype=F32):
        return pltpu.VMEM(x.shape, dtype)

    far, near = pl.BlockSpec(memory_space=pl.ANY), pl.BlockSpec(memory_space=pltpu.VMEM)
    b, r, g, o = block[0], layer[0], gains[0], second_layer[0]
    return pl.pallas_call(
        kernel,
        out_shape=[like(b)] * 3
        + [like(b, BF)]
        + [like(r)] * 3
        + [like(g)] * 3
        + [like(o)] * 3
        + [jax.ShapeDtypeStruct((2, LEVELS), F32), jax.ShapeDtypeStruct((1, 1), F32)],
        in_specs=[far] * 8 + [near] * 8,
        out_specs=[far] * 7 + [near] * 8,
        scratch_shapes=[room(b)] * 3
        + [room(b, BF)]
        + [room(r)] * 3
        + [room(r, BF)]
        + [room(b)] * 3
        + [room(b, BF)]
        + [room(r)] * 3
        + [room(g), room(o)]
        + [pltpu.SemaphoreType.DMA((n_loads,)), pltpu.SemaphoreType.DMA((n_loads,))],
        compiler_params=pltpu.CompilerParams(vmem_limit_bytes=60 * 2**20),
        name="all_steps",
    )(*block, *layer, *gains, *second_layer, vector, norm)


def on_device(
    tokens,
    lengths,
    picks,
    cotangent,
    block_master,
    block_first,
    block_second,
    gains,
    gains_first,
    gains_second,
    router_in,
    router_in_first,
    router_in_second,
    router_out,
    router_out_first,
    router_out_second,
):
    half_dim = HEAD_DIM // 2
    angle_steps = 10000.0 ** (-np.arange(half_dim, dtype=np.float32) / half_dim)
    frequency = jnp.asarray(np.tile(angle_steps.astype(np.float32), (8, 2)))
    f = attention_forward(
        tokens,
        picks.T,
        lengths,
        frequency,
        gains,
        router_in,
        jnp.pad(router_out, ((0, 0), (0, 128 - 2 * LEVELS))).astype(BF),
        block_master,
        cotangent,
        1,
    )

    ffn_part, grad_up, down_sums, d_after, d_attn, d_hidden, vector = feed_forward(
        f["second"],
        f["g"],
        f["slab_up"],
        f["stage_up"],
        f["slab_down"],
        f["d_act"],
        f["marks"],
        [f["after"], f["attn_sum"], f["gate"], gains, f["slopes"], f["logit_slopes"], f["hidden"]],
        2,
    )
    d_inputs, result, block_low, router_in_grad, vector, norm = attention_backward(
        d_attn,
        ffn_part,
        grad_up,
        down_sums,
        f["normed"],
        d_hidden,
        [tokens, d_after, gains, f["router_low"], f["after"], vector],
        [f[k] for k in ("slab_a", "turns", "marks", "q", "k", "v", "p", "a")],
        3,
    )
    (
        new_block,
        new_block_first,
        new_block_second,
        block_copy,
        new_router_in,
        new_router_in_first,
        new_router_in_second,
        new_gains,
        new_gains_first,
        new_gains_second,
        new_router_out,
        new_router_out_first,
        new_router_out_second,
        counts,
        grad_norm,
    ) = all_steps(
        (block_master, block_first, block_second, block_low),
        (router_in, router_in_first, router_in_second, router_in_grad),
        (gains, gains_first, gains_second),
        (router_out.T, router_out_first.T, router_out_second.T),
        vector,
        norm,
    )
    return (
        result,
        d_inputs,
        counts,
        grad_norm.reshape(()),
        new_block,
        new_block_first,
        new_block_second,
        block_copy,
        new_gains,
        new_gains_first,
        new_gains_second,
        new_router_in,
        new_router_in_first,
        new_router_in_second,
        new_router_out.T,
        new_router_out_first.T,
        new_router_out_second.T,
    )


def solution(mesh):
    both = P(("wide", "narrow"), None)
    return jax.shard_map(
        on_device,
        mesh=mesh,
        in_specs=(both, P("wide", None)) + (both,) * 5 + (P(),) * 9,
        out_specs=(both, both, P(), P()) + (both,) * 4 + (P(),) * 9,
        check_vma=False,
    )
```

```python
import functools

import jax
import jax.numpy as jnp
import numpy as np
from jax import lax
from jax.experimental import pallas as pl
from jax.experimental.pallas import tpu as pltpu
from jax.sharding import PartitionSpec as P

D = 2048
HEADS = 16
HEAD_DIM = 128
FF = 8192
RH = 256
LEVELS = 4
STEP = 10
TOK = 128
GROUP = 1024
SIDE = 4
WIDE = 16
NARROW = 8
ROWS = 16

VECTOR_ROWS = 64
GAIN_ROWS = 2 * D // 128
SMALL_ROWS = GAIN_ROWS + RH * 2 * LEVELS // 128
SQUARE_ROWS = 8

NORM_EPS = 1e-05
CLIP_NORM = 1.0
CONTRACT_COLS = (((1,), (1,)), ((), ()))
CONTRACT_ROWS = (((0,), (0,)), ((), ()))
MESH = pl.DeviceIdType.MESH
BF = jnp.bfloat16
F32 = jnp.float32


(
    CA, DA, DOWN, DS, EX, FEED, FIRST, GATES, GATHER, GD, GE, GG, GM, GO, GQ, GU, GX, HID, L1,
    LB, LD, LN, MIXED, MO, MORE, N0, N1, N2, N3, OUT, P0, P1, P2, P3, Q, RF, RT, SA, SD, SL, SQ,
    SU, T0, T1, T2, T3, TB, TOTAL, U0, U1, U2, U3, UP, V0, V1, V2, V3, WA, WD, WU, Y0, Y1, Y2,
    Y3,
) = range(64)
ATTEND = (T0, T1, T2, T3)
EARLY = (V0, V1, V2, V3)
UNITS = (U0, U1, U2, U3)
OUTPUT = (Y0, Y1, Y2, Y3)
NORM = (N0, N1, N2, N3)
PAIR = (P0, P1, P2, P3)


FORWARD_PLAN = (
    CA, SA, L1, TB, GX, SA, GX, WA, RF, GM, WA, WA, GX, GX, SU, WA, SD, WA, GX, GG, GM, WA, SD,
    GG, WD, SU, GX, SL, GM, WU, EX, WA, Q, WD, T1, GG, WU, T2, WD, TOTAL, T0, WD, T3, TOTAL, WD,
    TOTAL, GG, TOTAL, WD, WU, TOTAL, GG, GG, WU, WD, DA, WU, GG, TOTAL, WU, LN, WU, GX, SL,
    TOTAL, GG, WU,
)
FEED_PLAN = (
    GATHER, WU, WU, GATHER, WU, LD, GATHER, WU, WU, V0, WU, GATHER, V1, WU, V3, U1, GATHER, U3,
    N1, N3, GATHER, V2, U2, TOTAL, TOTAL, N2, U0, GE, TOTAL, DS, Y2, MORE, GD, FIRST, N0,
    GATHER, TOTAL, GU, FIRST, TOTAL, MORE, TOTAL, TOTAL, LB, HID, Y3, Y1, Y0, HID, FIRST, FIRST,
    MORE, HID,
)
BACKWARD_PLAN = (
    GATHER, UP, LD, GATES, UP, GATHER, GATHER, DOWN, FEED, P0, FEED, GATHER, P3, GATHER, P1,
    FEED, GATHER, DOWN, GATES, UP, P2, DOWN, GATHER, GO, MO, FEED, UP, GATES, RT, N2, GATES, N1,
    MO, GQ, UP, MIXED, GATES, TOTAL, MO, TOTAL, MIXED, DOWN, N3, N0, TOTAL, MO, GATES, TOTAL,
    FEED, MIXED, GATES, FEED, MIXED, TOTAL, GATES, MO, MIXED, TOTAL, GATES, GATES, MO, DOWN,
    TOTAL, MO, LB, UP, OUT, SQ, MIXED, UP,
)


def here():
    w = lax.axis_index("wide")
    n = lax.axis_index("narrow")
    return lax.div(w, SIDE), lax.rem(w, SIDE), lax.div(n, 2), lax.rem(n, 2)


def wrap(i):
    return lax.rem(i + 2 * SIDE, SIDE)


def moved(dx=0, dz=0, dy=0, dc=0):
    x, z, y, c = here()
    return (wrap(x + dx) * SIDE + wrap(z + dz), wrap(y + dy) * 2 + lax.rem(c + dc, 2))


NEAR_Y = [dict(dy=1), dict(dy=-1), dict(dc=1)]
NARROW_ALL = [dict(dy=a, dc=b) for a in range(SIDE) for b in range(2) if a or b]
NEAR_XZ = [dict(dx=1), dict(dx=-1), dict(dz=1), dict(dz=-1)]
LINES_XZ = [dict(dx=a) for a in (1, 2, 3)] + [dict(dz=a) for a in (1, 2, 3)]
WIDE_ALL = [dict(dx=a, dz=b) for a in range(SIDE) for b in range(SIDE) if a or b]


def greet(partners):
    barrier = pltpu.get_barrier_semaphore()
    for p in partners:
        pl.semaphore_signal(barrier, inc=1, device_id=moved(**p), device_id_type=MESH)
    pl.semaphore_wait(barrier, len(partners))


def span(start, size):
    if not isinstance(start, int):
        start = pl.multiple_of(start, ROWS)
    return pl.ds(start, size)


def lanes(start, size):
    if not isinstance(start, int):
        start = pl.multiple_of(start, 128)
    return pl.ds(start, size)


def step(*parts):
    for part in parts:
        next(part, None)


class Net:
    def __init__(self, send, recv, local):
        self.send, self.recv, self.local = send, recv, local
        self.used, self.used_local = 0, 0
        self.sent = []

    def put(self, src, dst, target):
        i = self.used
        self.used += 1
        copy = pltpu.make_async_remote_copy(
            src_ref=src,
            dst_ref=dst,
            send_sem=self.send.at[i],
            recv_sem=self.recv.at[i],
            device_id=target,
            device_id_type=MESH,
        )
        copy.start()
        self.sent.append(copy)
        return copy

    def keep(self, src, dst):
        i = self.used_local
        self.used_local += 1
        copy = pltpu.make_async_copy(src, dst, self.local.at[i])
        copy.start()
        return copy

    def sent_by(self, *copies):
        for copy in copies:
            copy.wait_send()
        done = [id(copy) for copy in copies]
        self.sent = [copy for copy in self.sent if id(copy) not in done]

    def finish(self):
        for copy in self.sent:
            copy.wait_send()


def take_turns(*parts):
    live = list(parts)
    while live:
        still = []
        for part in live:
            try:
                next(part)
                still.append(part)
            except StopIteration:
                pass
        live = still


def follow(plan, works, moves):
    for name in plan:
        if name in works:
            works[name]()
        else:
            next(moves[name], None)
    take_turns(*moves.values())


def comm_call(body, ins, outs, scratch, cid, copies, locals_, name, vmem=63, cost=None):
    n_in, n_out, n_scr = len(ins), len(outs), len(scratch)

    def kernel(*refs):
        in_refs = refs[:n_in]
        out_refs = refs[n_in : n_in + n_out]
        scr = refs[n_in + n_out : n_in + n_out + n_scr]
        send, recv, local = refs[n_in + n_out + n_scr :]
        net = Net(send, recv, local)
        body(net, in_refs, out_refs, scr)
        net.finish()
        assert net.used <= copies and net.used_local <= locals_, (net.used, net.used_local)

    return pl.pallas_call(
        kernel,
        out_shape=outs,
        in_specs=[pl.BlockSpec(memory_space=pl.ANY)] * n_in,
        out_specs=[pl.BlockSpec(memory_space=pl.ANY)] * n_out,
        scratch_shapes=list(scratch)
        + [
            pltpu.SemaphoreType.DMA((copies,)),
            pltpu.SemaphoreType.DMA((copies,)),
            pltpu.SemaphoreType.DMA((max(locals_, 1),)),
        ],
        compiler_params=pltpu.CompilerParams(
            collective_id=cid, has_side_effects=True, vmem_limit_bytes=vmem * 2**20
        ),
        name=name,
        cost_estimate=cost,
    )(*ins)


def gather_narrow(net, own, out):
    x, z, y, c = here()
    rows = own.shape[0]
    half = rows // 2

    def block(dy, lo=0, size=rows):
        return out.at[span((wrap(y + dy) * 2 + c) * rows + lo, size)]

    first, last = own.at[pl.ds(0, half)], own.at[pl.ds(half, half)]
    up = net.put(first, block(0, 0, half), moved(dy=1))
    down = net.put(last, block(0, half, half), moved(dy=-1))
    up_late = net.put(last, block(0, half, half), moved(dy=1))
    down_late = net.put(first, block(0, 0, half), moved(dy=-1))
    across = [net.put(own, block(0), moved(dc=1))]
    mine = net.keep(own, block(0))
    yield
    mine.wait()
    across[0].wait_recv()
    yield
    up.wait_recv()
    on = net.put(block(-1, 0, half), block(-1, 0, half), moved(dy=1))
    down.wait_recv()
    back = net.put(block(1, half, half), block(1, half, half), moved(dy=-1))
    yield
    up_late.wait_recv()
    across.append(net.put(block(-1), block(-1), moved(dc=1)))
    down_late.wait_recv()
    across.append(net.put(block(1), block(1), moved(dc=1)))
    across[1].wait_recv()
    across[2].wait_recv()
    yield
    on.wait_recv()
    across.append(net.put(block(2, 0, half), block(2, 0, half), moved(dc=1)))
    back.wait_recv()
    across.append(net.put(block(2, half, half), block(2, half, half), moved(dc=1)))
    yield
    across[3].wait_recv()
    across[4].wait_recv()
    yield
    net.sent_by(up, down, up_late, down_late, on, back, *across)


GATHER_COPIES = 12


def gather_small(net, own, out):
    c = here()[3]
    y = here()[2]
    rows = own.shape[0]

    def block(dy):
        return out.at[span((wrap(y + dy) * 2 + c) * rows, rows)]

    along = [net.put(own, block(0), moved(dy=d)) for d in (2, 1, 3)]
    across = [net.put(own, block(0), moved(dc=1))]
    mine = net.keep(own, block(0))
    yield
    for copy, d in zip(along, (2, 1, 3)):
        copy.wait_recv()
        across.append(net.put(block(-d), block(-d), moved(dc=1)))
    yield
    mine.wait()
    for copy in across:
        copy.wait_recv()


GATHER_SMALL_COPIES = 7


def gather_call(own, cid, name):
    rows, cols = own.shape

    def body(net, ins, outs, scr):
        greet(NEAR_Y)
        take_turns(gather_narrow(net, ins[0], outs[0]))

    return comm_call(
        body,
        [own],
        [jax.ShapeDtypeStruct((NARROW * rows, cols), own.dtype)],
        [],
        cid,
        GATHER_COPIES,
        1,
        name,
    )[0]


def reduce_scratch(rows, cols):
    return [
        pltpu.VMEM((SIDE, rows, cols), BF),
        pltpu.VMEM((SIDE, rows, cols), BF),
        pltpu.VMEM((2, rows // 2, cols), BF),
        pltpu.VMEM((2, rows, cols), BF),
        pltpu.VMEM((3, rows, cols), BF),
        pltpu.VMEM((rows, cols), F32),
    ]


REDUCE_COPIES = 10
REDUCE_LOCALS = 5


def reduce_narrow(net, part, scr):
    own, other, through, landed, ready, total = scr
    x, z, y, c = here()
    rows, cols = total.shape
    half = rows // 2

    def block(dy, core):
        return part.at[span((wrap(y + dy) * 2 + core) * rows, rows)]

    order = (2, 1, 3, 0)
    local, cross = {}, {}
    for dy in order:
        cross[dy] = net.put(block(dy, 1 - c), other.at[dy], moved(dc=1))
        local[dy] = net.keep(block(dy, c), own.at[dy])

    def pair(dy, lo, size):
        s = span(lo, size)
        return own[dy, s, :].astype(F32) + other[dy, s, :].astype(F32)

    yield
    local[2].wait()
    cross[2].wait_recv()
    ready[0] = pair(2, 0, rows).astype(BF)
    first, last = span(0, half), span(half, half)
    via_up = net.put(ready.at[0, first], through.at[0], moved(dy=1))
    via_down = net.put(ready.at[0, last], through.at[1], moved(dy=-1))
    yield
    local[1].wait()
    cross[1].wait_recv()
    ready[1, last, :] = pair(1, half, half).astype(BF)
    up_late = net.put(ready.at[1, last], landed.at[0, last], moved(dy=1))
    local[3].wait()
    cross[3].wait_recv()
    ready[2, first, :] = pair(3, 0, half).astype(BF)
    down_first = net.put(ready.at[2, first], landed.at[1, first], moved(dy=-1))
    yield
    via_up.wait_recv()
    ready[1, first, :] = (pair(1, 0, half) + through[0].astype(F32)).astype(BF)
    up_first = net.put(ready.at[1, first], landed.at[0, first], moved(dy=1))
    via_down.wait_recv()
    ready[2, last, :] = (pair(3, half, half) + through[1].astype(F32)).astype(BF)
    down_late = net.put(ready.at[2, last], landed.at[1, last], moved(dy=-1))
    yield
    local[0].wait()
    cross[0].wait_recv()
    total[...] = pair(0, 0, rows)
    yield
    for copy in (up_late, down_first, up_first, down_late):
        copy.wait_recv()
    total[...] += landed[0].astype(F32) + landed[1].astype(F32)


def pairs_scratch(rows, cols):
    return [
        pltpu.VMEM((SIDE * 2 * rows, cols), BF),
        pltpu.VMEM((SIDE, rows, cols), BF),
        pltpu.VMEM((2, rows // 2, cols), BF),
        pltpu.VMEM((2, rows, cols), BF),
        pltpu.VMEM((3, rows, cols), BF),
        pltpu.VMEM((rows, cols), F32),
    ]


PAIR_ORDER = (2, 1, 3, 0)


class Pairs:
    def __init__(self, net, out, scr, far_first=True):
        self.net, self.out, self.scr, self.far_first = net, out, scr, far_first
        self.crossed = {}

    def store(self, dy, value):
        rows = value.shape[0]
        self.scr[0][pl.ds(dy * rows, rows), :] = value.astype(BF)

    def cross(self, dy):
        parts, other = self.scr[:2]
        c = here()[3]
        rows = other.shape[1]
        self.crossed[dy] = self.net.put(
            parts.at[span((2 * dy + 1 - c) * rows, rows)], other.at[dy], moved(dc=1)
        )

    def steps(self):
        net = self.net
        parts, other, through, landed, ready, total = self.scr
        c = here()[3]
        rows = total.shape[0]
        half = rows // 2
        first, last = pl.ds(0, half), pl.ds(half, half)

        def pair(dy, lo, size):
            mine = parts[span((2 * dy + c) * rows + lo, size), :].astype(F32)
            return mine + other[dy, pl.ds(lo, size), :].astype(F32)

        def far():
            self.crossed[2].wait_recv()
            ready[0] = pair(2, 0, rows).astype(BF)
            via_up = net.put(ready.at[0, first], through.at[0], moved(dy=1))
            via_down = net.put(ready.at[0, last], through.at[1], moved(dy=-1))
            return via_up, via_down

        if self.far_first:
            via_up, via_down = far()
            yield
        self.crossed[1].wait_recv()
        ready[1, last, :] = pair(1, half, half).astype(BF)
        up_late = net.put(ready.at[1, last], landed.at[0, last], moved(dy=1))
        yield
        self.crossed[3].wait_recv()
        ready[2, first, :] = pair(3, 0, half).astype(BF)
        down_first = net.put(ready.at[2, first], landed.at[1, first], moved(dy=-1))
        yield
        if not self.far_first:
            via_up, via_down = far()
            yield
        via_up.wait_recv()
        ready[1, first, :] = (pair(1, 0, half) + through[0].astype(F32)).astype(BF)
        up_first = net.put(ready.at[1, first], landed.at[0, first], moved(dy=1))
        via_down.wait_recv()
        ready[2, last, :] = (pair(3, half, half) + through[1].astype(F32)).astype(BF)
        down_late = net.put(ready.at[2, last], landed.at[1, last], moved(dy=-1))
        yield
        self.crossed[0].wait_recv()
        total[...] = pair(0, 0, rows)
        yield
        for copy in (up_late, down_first, up_first, down_late):
            copy.wait_recv()
        total[...] += landed[0].astype(F32) + landed[1].astype(F32)
        if self.out is not None:
            done = net.keep(total, self.out)
            yield
            done.wait()


def spread_narrow(net, low, slab, pieces):
    w = lax.axis_index("wide")
    n = lax.axis_index("narrow")
    base = n * ROWS if slab.shape[0] == TOK else w * TOK + n * ROWS
    mine, copies = [], []
    for start, stride, width, to in pieces:
        spot = slab.at[span(base, ROWS), pl.ds(to, width)]
        for p in NARROW_ALL:
            target = moved(**p)
            columns = lanes(start + target[1] * stride, width)
            copies.append(net.put(low.at[:, columns], spot, target))
        mine.append(net.keep(low.at[:, lanes(start + n * stride, width)], spot))
    yield
    for copy in mine:
        copy.wait()
    for copy in copies:
        copy.wait_recv()


SPREAD_COPIES = 7


def gather_wide(net, slab, lead, stage=None):
    x, z, y, c = here()
    rows = TOK // 2
    half = rows // 2
    low = 0 if lead == "x" else rows

    def block(a, b, lo=0, size=rows):
        px, pz = (a, b) if lead == "x" else (b, a)
        return slab.at[span((wrap(x + px) * SIDE + wrap(z + pz)) * TOK + low + lo, size)]

    def lead_to(d):
        return moved(dx=d) if lead == "x" else moved(dz=d)

    def then_to(d):
        return moved(dz=d) if lead == "x" else moved(dx=d)

    def both(src, to, dst=None):
        dst = src if dst is None else dst
        return net.put(src, dst, to(1)), net.put(src, dst, to(-1))

    mine = block(0, 0) if stage is None else stage.at[pl.ds(low, rows)]
    fore, aft = both(mine, lead_to, block(0, 0))
    second = {0: both(mine, then_to, block(0, 0))}
    yield
    fore.wait_recv()
    on = net.put(block(-1, 0, 0, half), block(-1, 0, 0, half), lead_to(1))
    second[-1] = both(block(-1, 0), then_to)
    aft.wait_recv()
    back = net.put(block(1, 0, half, half), block(1, 0, half, half), lead_to(-1))
    second[1] = both(block(1, 0), then_to)
    yield
    last = []

    def relay(a):
        f, b = second[a]
        f.wait_recv()
        last.append(net.put(block(a, -1, 0, half), block(a, -1, 0, half), then_to(1)))
        b.wait_recv()
        last.append(net.put(block(a, 1, half, half), block(a, 1, half, half), then_to(-1)))

    kept = None if stage is None else net.keep(mine, block(0, 0))
    relay(0)
    yield
    on.wait_recv()
    back.wait_recv()
    second[2] = both(block(2, 0), then_to)
    yield
    relay(-1)
    relay(1)
    yield
    relay(2)
    yield
    if kept is not None:
        kept.wait()
    for copy in last:
        copy.wait_recv()


WIDE_COPIES = 20


def mean_of(values):
    return jnp.sum(values, axis=-1, keepdims=True) * (1.0 / D)


def normal(values):
    centered = values - mean_of(values)
    inverse = lax.rsqrt(mean_of(centered * centered) + NORM_EPS)
    return centered * inverse, inverse


def normal_back(hat, inverse, d_hat):
    return inverse * (d_hat - mean_of(d_hat) - hat * mean_of(d_hat * hat))


def turn(values, cosine, sine):
    return values * cosine + pltpu.roll(values, HEAD_DIM // 2, 1) * sine


def allowed_keys(first_row, rows, first_length):
    query = first_row + lax.broadcasted_iota(jnp.int32, (rows, 1), 0)
    key = lax.broadcasted_iota(jnp.int32, (rows, GROUP), 1)
    start = jnp.where(query >= first_length, first_length, 0)
    return (key <= query) & (key >= start)


PICK_ATTN, PICK_FFN, GATE_FFN = 0, 32, 64
LATER_UNITS = 512


def branch_mask(marks, lane):
    n = lax.axis_index("narrow").astype(F32)
    return (n < 2.0 * (marks[:, lane : lane + 1] + 1.0)).astype(F32)


def half_turns(first_length, frequency, tv):
    rows = 64
    half = GROUP // 2
    left = lax.broadcasted_iota(jnp.int32, (rows, 128), 1) < HEAD_DIM // 2
    row = lax.broadcasted_iota(jnp.int32, (rows, 128), 0)

    @pl.loop(0, half // rows)
    def _(i):
        token = row + i * rows + jnp.where(left, 0, half)
        position = token - jnp.where(token >= first_length, first_length, 0)
        angles = position.astype(F32) * frequency
        cosine, sine = jnp.cos(angles), jnp.sin(angles)
        cosine_other = pltpu.roll(cosine, HEAD_DIM // 2, 1)
        sine_other = pltpu.roll(sine, HEAD_DIM // 2, 1)
        low, high = span(i * rows, rows), span(half + i * rows, rows)
        tv[0, low, :] = jnp.where(left, cosine, cosine_other)
        tv[0, high, :] = jnp.where(left, cosine_other, cosine)
        tv[1, low, :] = jnp.where(left, -sine, sine_other)
        tv[1, high, :] = jnp.where(left, -sine_other, sine)


GELU_SCALE = (2.0 / 3.141592653589793) ** 0.5
GELU_CUBE = 0.044715


def route(normed, first_layer, second_layer, picks):
    before = jnp.dot(normed, first_layer, preferred_element_type=F32)
    square = before * before
    bent = jnp.tanh(GELU_SCALE * before * (1.0 + GELU_CUBE * square))
    hidden = 0.5 * before * (1.0 + bent)
    slope = 0.5 * (1.0 + bent) + 0.5 * before * (1.0 - bent * bent) * GELU_SCALE * (
        1.0 + 3.0 * GELU_CUBE * square
    )
    logits = jnp.dot(hidden.astype(BF), second_layer, preferred_element_type=F32)
    lane = lax.broadcasted_iota(jnp.int32, logits.shape, 1)
    gates, logit_slopes, slopes = [], [], []
    for branch in range(2):
        start = branch * LEVELS
        inside = (lane >= start) & (lane < start + LEVELS)
        shown = jnp.where(inside, logits, -1e30)
        expo = jnp.exp(shown - jnp.max(shown, axis=-1, keepdims=True))
        expo = jnp.where(inside, expo, 0.0)
        probs = expo / jnp.sum(expo, axis=-1, keepdims=True)
        chosen = jnp.where(lane.astype(F32) == picks[branch] + float(start), 1.0, 0.0)
        gate = float(LEVELS) * jnp.sum(probs * chosen, axis=-1, keepdims=True)
        logit_slope = gate * (chosen - probs)
        gates.append(gate)
        logit_slopes.append(logit_slope)
        slopes.append(
            slope
            * lax.dot_general(
                logit_slope.astype(BF), second_layer, CONTRACT_COLS, preferred_element_type=F32
            )
        )
    return hidden, gates, logit_slopes, slopes


def attention_forward(
    tokens, picks, lengths, frequency, gains, router_in, router_out, master, upstream, cid
):
    pair_rows = 2 * TOK
    head_part = D // NARROW
    units = FF // NARROW
    low = jax.ShapeDtypeStruct((GROUP, head_part), BF)
    results = dict(
        attn_sum=jax.ShapeDtypeStruct((TOK, D), F32),
        q=low,
        k=low,
        v=low,
        p=jax.ShapeDtypeStruct((GROUP, 2 * GROUP), BF),
        a=low,
        g=jax.ShapeDtypeStruct((GROUP, D), BF),
        slab_a=jax.ShapeDtypeStruct((D, 4 * head_part), BF),
        slab_up=jax.ShapeDtypeStruct((D, units - LATER_UNITS), BF),
        stage_up=jax.ShapeDtypeStruct((TOK, LATER_UNITS), BF),
        slab_down=jax.ShapeDtypeStruct((D, units), BF),
        normed=jax.ShapeDtypeStruct((GROUP, D), BF),
        marks=jax.ShapeDtypeStruct((GROUP, 128), F32),
        after=jax.ShapeDtypeStruct((TOK, D), F32),
        second=jax.ShapeDtypeStruct((TOK, D), BF),
        d_act=jax.ShapeDtypeStruct((GROUP, units), F32),
        turns=jax.ShapeDtypeStruct((2, GROUP, HEAD_DIM), F32),
        router_low=jax.ShapeDtypeStruct((D, RH), BF),
        hidden=jax.ShapeDtypeStruct((TOK, RH), F32),
        gate=jax.ShapeDtypeStruct((TOK, 128), F32),
        logit_slopes=jax.ShapeDtypeStruct((2, TOK, 128), F32),
        slopes=jax.ShapeDtypeStruct((2, TOK, RH), F32),
    )
    held = tuple(k for k in results if k not in ("attn_sum", "slab_up", "stage_up"))
    own_inputs = (tokens, picks, lengths, frequency, gains, router_in, router_out)

    def body(net, ins, outs, scr):
        out = dict(zip(results, outs))
        to = dict(zip(held, scr))
        scr = scr[len(held) :]
        xv, wv, tv, mv = to["normed"], to["slab_a"], to["turns"], to["marks"]
        qv, kv, vv, pv, av = (to[k] for k in "qkvpa")
        held_in, scr = scr[:7], scr[7:]
        own_tokens, own_picks, lv, fv, own_gains, rv, ov = held_in
        stage_up, stage_down, normed_own, marks_own, full, low, mark_rows = scr[:7]
        pairs = scr[7:]
        master, upstream = ins[7:]
        x, z, y, c = here()
        master_load = net.keep(master, full)
        loads = [net.keep(a, b) for a, b in zip(ins[:7], held_in)]
        greet(NARROW_ALL + NEAR_XZ)
        sums = Pairs(net, out["attn_sum"], pairs)
        stores = []

        def store(*names):
            stores.extend([net.keep(to[name], out[name]) for name in names])

        moves = {
            SA: spread_narrow(
                net, low, wv, [(i * D, head_part, head_part, i * head_part) for i in range(4)]
            ),
            SU: spread_narrow(net, low, stage_up, [(4 * D, units, units - LATER_UNITS, 0)]),
            SL: spread_narrow(
                net,
                low,
                out["stage_up"],
                [(4 * D + units - LATER_UNITS, units, LATER_UNITS, 0)],
            ),
            SD: spread_narrow(net, low, stage_down, [(4 * D + FF, units, units, 0)]),
            GX: gather_narrow(net, normed_own, xv),
            GM: gather_small(net, marks_own, mark_rows),
            GG: gather_narrow(net, upstream, to["g"]),
            WA: side_by_side(*[gather_wide(net, wv, k) for k in "xz"]),
            WU: side_by_side(*[gather_wide(net, out["slab_up"], k, stage_up) for k in "xz"]),
            WD: side_by_side(*[gather_wide(net, to["slab_down"], k, stage_down) for k in "xz"]),
            TOTAL: sums.steps(),
        }

        def cast():
            master_load.wait()

            @pl.loop(0, low.shape[1] // 2048)
            def _(i):
                columns = lanes(i * 2048, 2048)
                low[:, columns] = full[:, columns].astype(BF)

        def first_norm():
            for load in loads:
                load.wait()
            hat, _ = normal(own_tokens[...].astype(F32))
            normed_own[...] = (hat * own_gains[0:1, :]).astype(BF)

        def route_own():
            to["router_low"][...] = rv[...].astype(BF)
            row = lax.broadcasted_iota(jnp.int32, (TOK, TOK), 0)
            lane = lax.broadcasted_iota(jnp.int32, (TOK, TOK), 1)
            level = [
                jnp.sum(
                    jnp.where(row == lane, own_picks[b : b + 1, :].astype(F32), 0.0),
                    axis=-1,
                    keepdims=True,
                )
                for b in range(2)
            ]
            hidden, gates, logit_slopes, slopes = route(
                normed_own[...], to["router_low"][...], ov[...], level
            )
            to["hidden"][...] = hidden
            to["gate"][...] = jnp.broadcast_to(gates[0], (TOK, 128))
            for branch in range(2):
                to["logit_slopes"][branch] = logit_slopes[branch]
                to["slopes"][branch] = slopes[branch]
            marks_own[...] = jnp.zeros_like(marks_own)
            for b in range(2):
                marks_own[b : b + 1, :] = own_picks[b : b + 1, :].astype(F32)
            marks_own[2:3, :] = jnp.sum(
                jnp.where(row == lane, gates[1], 0.0), axis=0, keepdims=True
            )
            store("router_low", "hidden", "gate", "logit_slopes", "slopes")

        def expand():
            row = lax.broadcasted_iota(jnp.int32, (TOK, TOK), 0)
            lane = lax.broadcasted_iota(jnp.int32, (TOK, TOK), 1)

            @pl.loop(0, NARROW)
            def _(i):
                rows = mark_rows[span(i * ROWS, ROWS), :]
                marks = [
                    jnp.sum(jnp.where(row == lane, rows[b : b + 1, :], 0.0), axis=1, keepdims=True)
                    for b in range(3)
                ]
                other = jnp.where(lane < GATE_FFN, marks[1], marks[2])
                mv[span(i * TOK, TOK), :] = jnp.where(lane < PICK_FFN, marks[0], other)

            store("marks")

        def tables():
            half_turns(lv[0:1, 0:1], fv[0:1, :], tv)
            store("turns")

        def down_back():
            store("g", "slab_down")

            @pl.loop(0, SIDE)
            def _(i):
                r = span(i * pair_rows, pair_rows)
                to["d_act"][r, :] = jnp.dot(
                    to["g"][r, :], to["slab_down"][...], preferred_element_type=F32
                )

            store("d_act")

        def project():
            store("normed", "slab_a")

            @pl.loop(0, SIDE)
            def _(i):
                r = span(i * pair_rows, pair_rows)
                proj = jnp.dot(xv[r, :], wv[:, : 3 * head_part], preferred_element_type=F32)
                cosine, sine = tv[0, r, :], tv[1, r, :]
                for h in range(2):
                    at = pl.ds(h * HEAD_DIM, HEAD_DIM)
                    a = h * HEAD_DIM
                    qv[r, at] = turn(proj[:, a : a + HEAD_DIM], cosine, sine).astype(BF)
                    a += head_part
                    kv[r, at] = turn(proj[:, a : a + HEAD_DIM], cosine, sine).astype(BF)
                vv[r, :] = proj[:, 2 * head_part :].astype(BF)

            store("q", "k", "v")

        def attend(dy):
            first = wrap(y + dy) * pair_rows
            r = span(first, pair_rows)
            allowed = allowed_keys(first, pair_rows, lv[0:1, 0:1])
            heads = []
            for h in range(2):
                at = pl.ds(h * HEAD_DIM, HEAD_DIM)
                scores = lax.dot_general(
                    qv[r, at], kv[:, at], CONTRACT_COLS, preferred_element_type=F32
                )
                scores = jnp.where(allowed, scores * HEAD_DIM ** (-0.5), -1e30)
                expo = jnp.exp(scores - jnp.max(scores, axis=-1, keepdims=True))
                probs = expo * (1.0 / jnp.sum(expo, axis=-1, keepdims=True))
                low = probs.astype(BF)
                pv[r, pl.ds(h * GROUP, GROUP)] = low
                heads.append(jnp.dot(low, vv[:, at], preferred_element_type=F32))
            mask = branch_mask(mv[r, :], PICK_ATTN)
            av[r, :] = (jnp.concatenate(heads, axis=1) * mask).astype(BF)
            back = lax.dot_general(
                av[r, :], wv[:, 3 * head_part :], CONTRACT_COLS, preferred_element_type=F32
            )
            sums.store(dy, back)
            sums.cross(dy)
            stores.append(net.keep(pv.at[r], out["p"].at[r]))
            stores.append(net.keep(av.at[r], out["a"].at[r]))

        def second_norm():
            values = own_tokens[...].astype(F32) + to["gate"][:, :1] * sums.scr[5][...]
            to["after"][...] = values
            to["second"][...] = (normal(values)[0] * own_gains[1:2, :]).astype(BF)
            store("after", "second")

        works = {
            CA: cast,
            L1: first_norm,
            RF: route_own,
            EX: expand,
            TB: tables,
            Q: project,
            LN: second_norm,
            DA: down_back,
        }
        for dy in PAIR_ORDER:
            works[ATTEND[dy]] = functools.partial(attend, dy)
        follow(FORWARD_PLAN, works, moves)
        for done in stores:
            done.wait()

    got = comm_call(
        body,
        list(own_inputs) + [master, upstream],
        list(results.values()),
        [pltpu.VMEM(results[k].shape, results[k].dtype) for k in held]
        + [pltpu.VMEM(r.shape, r.dtype) for r in own_inputs]
        + [
            pltpu.VMEM((TOK, units - LATER_UNITS), BF),
            pltpu.VMEM((TOK, units), BF),
            pltpu.VMEM((TOK, D), BF),
            pltpu.VMEM((ROWS, 128), F32),
            pltpu.VMEM(master.shape, F32),
            pltpu.VMEM(master.shape, BF),
            pltpu.VMEM((NARROW * ROWS, 128), F32),
        ]
        + pairs_scratch(TOK, D),
        cid,
        REDUCE_COPIES + 6 * WIDE_COPIES + 3 * GATHER_COPIES + 7 * SPREAD_COPIES,
        8 + 7 + 3 + 4 + 1 + 8 + len(held),
        "attention_forward",
    )
    return dict(zip(results, got))


def first_scratch(cols):
    part, half = TOK // 2, TOK // 4
    return [
        pltpu.VMEM((2, 2, SIDE, half, cols), BF),
        pltpu.VMEM((2, 2, SIDE, part, cols), BF),
        pltpu.VMEM((2, 2, SIDE, half, cols), BF),
        pltpu.VMEM((2, SIDE, part, cols), BF),
    ]


def second_scratch(cols):
    part, half = TOK // 2, TOK // 4
    return [
        pltpu.VMEM((2, 2, half, cols), BF),
        pltpu.VMEM((2, 2, part, cols), BF),
        pltpu.VMEM((2, 2, half, cols), BF),
        pltpu.VMEM((TOK, cols), BF),
    ]


FIRST_COPIES = 12
SECOND_COPIES = 12
FIRST_LOCALS = 6


def lead_moves(lead):
    def lead_to(d):
        return moved(dx=d) if lead == "x" else moved(dz=d)

    def then_to(d):
        return moved(dz=d) if lead == "x" else moved(dx=d)

    return lead_to, then_to


def reduce_first(net, grad, scr, lead):
    via, landed, ready, sums = scr
    x, z, y, c = here()
    part, half = TOK // 2, TOK // 4
    k = 0 if lead == "x" else 1
    low = k * part
    blocks = grad.reshape(SIDE, SIDE, TOK, grad.shape[1])
    first, last = pl.ds(0, half), pl.ds(half, half)
    lead_to, _ = lead_moves(lead)

    def line(d, lo, size):
        rows = pl.ds(low + lo, size)
        if lead == "x":
            return (wrap(x + d), slice(None), rows, slice(None))
        return (slice(None), wrap(z + d), rows, slice(None))

    via_up = net.put(blocks.at[line(2, 0, half)], via.at[k, 0], lead_to(1))
    via_down = net.put(blocks.at[line(2, half, half)], via.at[k, 1], lead_to(-1))
    up_late = net.put(blocks.at[line(1, half, half)], landed.at[k, 0, :, last], lead_to(1))
    down_first = net.put(blocks.at[line(3, 0, half)], landed.at[k, 1, :, first], lead_to(-1))
    loads = [
        net.keep(blocks.at[line(1, 0, half)], ready.at[k, 0]),
        net.keep(blocks.at[line(3, half, half)], ready.at[k, 1]),
        net.keep(blocks.at[line(0, 0, part)], sums.at[k]),
    ]
    yield
    for load in loads:
        load.wait()
    via_up.wait_recv()

    @pl.loop(0, SIDE)
    def _(i):
        ready[k, 0, i] = (ready[k, 0, i].astype(F32) + via[k, 0, i].astype(F32)).astype(BF)

    up_first = net.put(ready.at[k, 0], landed.at[k, 0, :, first], lead_to(1))
    via_down.wait_recv()

    @pl.loop(0, SIDE)
    def _(i):
        ready[k, 1, i] = (ready[k, 1, i].astype(F32) + via[k, 1, i].astype(F32)).astype(BF)

    down_late = net.put(ready.at[k, 1], landed.at[k, 1, :, last], lead_to(-1))
    yield
    for copy in (up_late, down_first, up_first, down_late):
        copy.wait_recv()

    @pl.loop(0, SIDE)
    def _(i):
        both = landed[k, 0, i].astype(F32) + landed[k, 1, i].astype(F32)
        sums[k, i] = (sums[k, i].astype(F32) + both).astype(BF)


def reduce_second(net, sums, scr, lead):
    via, landed, ready, total = scr
    x, z, y, c = here()
    part, half = TOK // 2, TOK // 4
    k = 0 if lead == "x" else 1
    first, last = pl.ds(0, half), pl.ds(half, half)
    _, then_to = lead_moves(lead)
    me = z if lead == "x" else x

    def block(d, rows):
        return sums.at[k, wrap(me + d), rows]

    via_up = net.put(block(2, first), via.at[k, 0], then_to(1))
    via_down = net.put(block(2, last), via.at[k, 1], then_to(-1))
    up_late = net.put(block(1, last), landed.at[k, 0, last], then_to(1))
    down_first = net.put(block(3, first), landed.at[k, 1, first], then_to(-1))
    yield
    via_up.wait_recv()
    ready[k, 0] = (block(1, first)[...].astype(F32) + via[k, 0].astype(F32)).astype(BF)
    up_first = net.put(ready.at[k, 0], landed.at[k, 0, first], then_to(1))
    via_down.wait_recv()
    ready[k, 1] = (block(3, last)[...].astype(F32) + via[k, 1].astype(F32)).astype(BF)
    down_late = net.put(ready.at[k, 1], landed.at[k, 1, last], then_to(-1))
    yield
    for copy in (up_late, down_first, up_first, down_late):
        copy.wait_recv()
    both = landed[k, 0].astype(F32) + landed[k, 1].astype(F32)
    total[pl.ds(k * part, part), :] = (sums[k, me].astype(F32) + both).astype(BF)


def side_by_side(*parts):
    while True:
        if StopIteration in [next(part, StopIteration) for part in parts]:
            break
        yield


def return_narrow(net, total, out, pieces):
    n = lax.axis_index("narrow")
    copies, mine = [], []
    for start, width, to in pieces:
        spot = out.at[:, lanes(to + n * width, width)]
        columns = pl.ds(start, width)
        for p in NARROW_ALL:
            target = moved(**p)
            copies.append(net.put(total.at[span(target[1] * ROWS, ROWS), columns], spot, target))
        mine.append(net.keep(total.at[span(n * ROWS, ROWS), columns], spot))
    yield
    for copy in mine:
        copy.wait()
    for copy in copies:
        copy.wait_recv()


def second_then_narrow(net, sums, out, scr, pieces):
    yield from side_by_side(*[reduce_second(net, sums, scr, lead) for lead in "xz"])
    yield from return_narrow(net, scr[3], out, pieces)


def wide_then_narrow(net, grad, out, scr, pieces):
    yield from side_by_side(*[reduce_first(net, grad, scr[:4], lead) for lead in "xz"])
    yield from second_then_narrow(net, scr[3], out, scr[4:], pieces)


def feed_forward(normed_own, upstream, w_up, stage_up, w_down, d_act, marks, own, cid):
    pair_rows = 2 * TOK
    units = FF // NARROW
    strip = 256

    def body(net, ins, outs, scr):
        own, upstream, up_in, stage_in, down_in, da_in, marks = ins[:7]
        kept_up = up_in.shape[1]
        rest = pl.ds(kept_up, units - kept_up)
        ffn_part, g_up, down_sums, after_out, attn_out, hidden_out, vector_out = outs
        xv, dv, w_up, w_down, mv, act, du, da, gu, yv = scr[:10]
        gated, dots, dots_in = scr[16:19]
        held, d_attn, d_hidden, vector = scr[19:26], *scr[26:29]
        gds, firsts = scr[29:31], (scr[31:35], scr[35:39])
        stage = scr[39]
        n = lax.axis_index("narrow")
        x, z, y, c = here()
        loads = [
            net.keep(a, b)
            for a, b in (
                (stage_in, stage),
                (marks, mv),
                (up_in, w_up.at[:, pl.ds(0, kept_up)]),
                (da_in, da),
                (upstream, dv),
                (down_in, w_down),
            )
        ]
        own_loads = [net.keep(a, b) for a, b in zip(ins[7:], held)]
        greet(NARROW_ALL + NEAR_XZ)
        loads.pop(0).wait()
        sums = Pairs(net, None, scr[10:16], far_first=False)
        stores, dot_copies = [], []

        def gradient(left, right, to):
            @pl.loop(0, D // strip)
            def _(i):
                at = lanes(i * strip, strip)
                to[span(i * strip, strip), :] = lax.dot_general(
                    left[:, at], right[...], CONTRACT_ROWS, preferred_element_type=F32
                ).astype(BF)

        def wait_loads():
            for load in loads:
                load.wait()

        def half_gradient(i):
            columns = pl.ds(i * units // 2, units // 2)
            gradient(dv, gated.at[:, columns], gds[i])

        def units_of(dy, later):
            r = span(wrap(y + dy) * pair_rows, pair_rows)
            columns = rest if later else pl.ds(0, kept_up)
            up = jnp.dot(xv[r, :], w_up[:, columns], preferred_element_type=F32)
            positive = jnp.maximum(up, 0.0)
            masked = positive * branch_mask(mv[r, :], PICK_FFN)
            gate = mv[r, GATE_FFN : GATE_FFN + 1]
            active = positive * masked
            act[r, columns] = active.astype(BF)
            gated[r, columns] = (active * gate).astype(BF)
            back = da[r, columns]
            du[r, columns] = (back * (2.0 * gate * masked)).astype(BF)
            dot = lax.dot_general(
                jnp.ones((8, up.shape[1]), BF),
                (back * active).astype(BF),
                CONTRACT_COLS,
                preferred_element_type=F32,
            )
            for core in range(2):
                spot = wrap(y + dy) * 2 + core
                part = dot[:, core * TOK : (core + 1) * TOK]
                dots[spot] = dots[spot] + part if later else part

        def norm_back(dy):
            r = span(wrap(y + dy) * pair_rows, pair_rows)
            back = lax.dot_general(
                du[r, :], w_up[...], CONTRACT_COLS, preferred_element_type=F32
            )
            sums.store(dy, back)
            sums.cross(dy)

        def send_dots():
            for p in NARROW_ALL:
                target = moved(**p)
                dot_copies.append(net.put(dots.at[target[1]], dots_in.at[n], target))
            dots_in[n] = dots[n]

        def up_gradient():
            gradient(xv, du, gu)
            stores.append(net.keep(gu, g_up))

        def output(dy):
            r = span(wrap(y + dy) * pair_rows, pair_rows)
            yv[r, :] = lax.dot_general(
                act[r, :], w_down[...], CONTRACT_COLS, preferred_element_type=F32
            ).astype(BF)
            stores.append(net.keep(yv.at[r], ffn_part.at[r]))

        def second_norm_back():
            for load in own_loads:
                load.wait()
            for copy in dot_copies:
                copy.wait_recv()
            s = dots_in[0]
            for i in range(1, NARROW):
                s = s + dots_in[i]
            row = lax.broadcasted_iota(jnp.int32, (TOK, TOK), 0)
            lane = lax.broadcasted_iota(jnp.int32, (TOK, TOK), 1)
            ffn = jnp.sum(jnp.where(row == lane, s[0:1, :], 0.0), axis=-1, keepdims=True)
            after, attn, gate, gains, slopes, logit_slopes, hidden = held
            total = sums.scr[5]
            hat, inverse = normal(after[...])
            d_gain = jnp.sum(total[...] * hat, axis=0, keepdims=True)
            back = normal_back(hat, inverse, total[...] * gains[1:2, :])
            back = back + dv[span(n * TOK, TOK), :].astype(F32)
            total[...] = back
            d_attn[...] = (back * gate[:, :1]).astype(BF)
            attn_gate = jnp.sum(back * attn[...], axis=-1, keepdims=True)
            d_hidden[...] = (attn_gate * slopes[0] + ffn * slopes[1]).astype(BF)
            d_logits = attn_gate * logit_slopes[0] + ffn * logit_slopes[1]
            d_router = lax.dot_general(
                d_logits.astype(BF),
                hidden[...].astype(BF),
                CONTRACT_ROWS,
                preferred_element_type=F32,
            )
            vector[...] = jnp.zeros_like(vector)
            for i in range(GAIN_ROWS // 2):
                at = GAIN_ROWS // 2 + i
                vector[at : at + 1, :] = d_gain[:, i * 128 : (i + 1) * 128]
            for i in range(RH // 128):
                at = GAIN_ROWS + i * 2 * LEVELS
                vector[at : at + 2 * LEVELS, :] = d_router[: 2 * LEVELS, i * 128 : (i + 1) * 128]
            own_marks = mv[span(n * TOK, TOK), :]
            levels = lane.astype(F32)
            picked = jnp.where(levels == own_marks[:, PICK_ATTN : PICK_ATTN + 1], 1.0, 0.0)
            other = own_marks[:, PICK_FFN : PICK_FFN + 1] + float(LEVELS)
            picked = picked + jnp.where(levels == other, 1.0, 0.0)
            vector[SMALL_ROWS : SMALL_ROWS + 1, :] = jnp.sum(picked, axis=0, keepdims=True)
            pairs = zip(
                (total, d_attn, vector),
                (after_out, attn_out, vector_out),
            )
            stores.extend([net.keep(a, b) for a, b in pairs])

        works = {
            LD: wait_loads,
            GD: functools.partial(half_gradient, 0),
            GE: functools.partial(half_gradient, 1),
            GU: up_gradient,
            DS: send_dots,
            LB: second_norm_back,
        }
        for dy in PAIR_ORDER:
            works[EARLY[dy]] = functools.partial(units_of, dy, False)
            works[UNITS[dy]] = functools.partial(units_of, dy, True)
            works[OUTPUT[dy]] = functools.partial(output, dy)
            works[NORM[dy]] = functools.partial(norm_back, dy)
        moves = {
            GATHER: gather_narrow(net, own, xv),
            TOTAL: sums.steps(),
            FIRST: side_by_side(*[reduce_first(net, gds[0], firsts[0], lead) for lead in "xz"]),
            MORE: side_by_side(*[reduce_first(net, gds[1], firsts[1], lead) for lead in "xz"]),
            HID: gather_small(net, d_hidden, hidden_out),
            WU: side_by_side(*[gather_wide(net, w_up.at[:, rest], k, stage) for k in "xz"]),
        }
        follow(FEED_PLAN, works, moves)
        for i in range(2):
            columns = pl.ds(i * units // 2, units // 2)
            stores.append(net.keep(firsts[i][3], down_sums.at[:, :, :, columns]))
        for store in stores:
            store.wait()

    wide = pltpu.VMEM((GROUP, D), BF)
    tall = pltpu.VMEM((D, units), BF)
    square = pltpu.VMEM((GROUP, units), BF)
    return comm_call(
        body,
        [normed_own, upstream, w_up, stage_up, w_down, d_act, marks] + list(own),
        [
            jax.ShapeDtypeStruct((GROUP, D), BF),
            jax.ShapeDtypeStruct((D, units), BF),
            jax.ShapeDtypeStruct((2, SIDE, TOK // 2, units), BF),
            jax.ShapeDtypeStruct((TOK, D), F32),
            jax.ShapeDtypeStruct((TOK, D), BF),
            jax.ShapeDtypeStruct((GROUP, RH), BF),
            jax.ShapeDtypeStruct((VECTOR_ROWS, 128), F32),
        ],
        [wide, wide, tall, tall, pltpu.VMEM(marks.shape, F32), square, square]
        + [pltpu.VMEM((GROUP, units), F32), tall, wide]
        + pairs_scratch(TOK, D)
        + [square]
        + [pltpu.VMEM((NARROW, 8, TOK), F32)] * 2
        + [pltpu.VMEM(r.shape, r.dtype) for r in own]
        + [
            pltpu.VMEM((TOK, D), BF),
            pltpu.VMEM((TOK, RH), BF),
            pltpu.VMEM((VECTOR_ROWS, 128), F32),
        ]
        + [pltpu.VMEM((D, units // 2), BF)] * 2
        + first_scratch(units // 2) * 2
        + [pltpu.VMEM(stage_up.shape, BF)],
        cid,
        GATHER_COPIES + REDUCE_COPIES + 7 + 2 * FIRST_COPIES + 2 * WIDE_COPIES + GATHER_SMALL_COPIES,
        14 + 1 + 1 + 12 + 2 * FIRST_LOCALS + 2,
        "feed_forward",
    )


def squares_of(ref, rows, cols):
    s = jnp.zeros((SQUARE_ROWS, 128), F32)
    for i in range(ref.shape[0] // rows):
        for j in range(ref.shape[1] // cols):
            piece = ref[i * rows : (i + 1) * rows, j * cols : (j + 1) * cols].astype(F32)
            piece = piece * piece
            for a in range(rows // SQUARE_ROWS):
                for b in range(cols // 128):
                    s = s + piece[a * 8 : a * 8 + 8, b * 128 : b * 128 + 128]
    return s


def sum_everywhere(net, own, first, second, total):
    w = lax.axis_index("wide")
    n = lax.axis_index("narrow")

    def rows(i):
        return pl.ds(pl.multiple_of(i * 8, 8), 8)

    copies = []
    for p in NARROW_ALL:
        target = moved(**p)
        copies.append(net.put(own.at[rows(target[1])], first.at[n], target))
    first[n] = own[rows(n), :]
    for copy in copies:
        copy.wait_recv()
    s = first[0]
    for i in range(1, NARROW):
        s = s + first[i]
    second[w] = s
    copies = [net.put(second.at[w], second.at[w], moved(**p)) for p in WIDE_ALL]
    for copy in copies:
        copy.wait_recv()
    s = second[0]
    for i in range(1, WIDE):
        s = s + second[i]
    total[rows(n), :] = s
    copies = [net.put(total.at[rows(n)], total.at[rows(n)], moved(**p)) for p in NARROW_ALL]
    for copy in copies:
        copy.wait_recv()


def attention_backward(
    d_attn_own, ffn_part, g_up, down_sums, normed, hidden_in, own, kept, cid
):
    table_rows = D // NARROW
    pair_rows = 2 * TOK
    head_part = D // NARROW
    units = FF // NARROW
    strip = 256
    scale = HEAD_DIM ** (-0.5)
    scratch = (
        [pltpu.VMEM(r.shape, r.dtype) for r in kept]
        + [
            pltpu.VMEM((GROUP, D), BF),
            pltpu.VMEM((GROUP, head_part), F32),
            pltpu.VMEM((GROUP, head_part), F32),
            pltpu.VMEM((GROUP, 3 * head_part), BF),
            pltpu.VMEM((D, 3 * head_part), BF),
        ]
        + pairs_scratch(TOK, D)[1:]
        + reduce_scratch(TOK, D)
        + first_scratch(3 * head_part)
        + second_scratch(3 * head_part)
        + first_scratch(units)
        + second_scratch(units)
        + [pltpu.VMEM(down_sums.shape, BF)]
        + second_scratch(units)
        + [
            pltpu.VMEM((GROUP, table_rows), BF),
            pltpu.VMEM((GROUP, RH), BF),
            pltpu.VMEM((table_rows, RH), BF),
            pltpu.VMEM((WIDE, ROWS, RH), BF),
            pltpu.VMEM((ROWS, RH), BF),
            pltpu.VMEM((table_rows, RH), BF),
            pltpu.VMEM((1, D), F32),
        ]
        + [pltpu.VMEM(r.shape, r.dtype) for r in own]
        + [
            pltpu.VMEM((ROWS, 4 * D + 2 * FF), BF),
            pltpu.VMEM((TOK, D), BF),
            pltpu.VMEM((NARROW, 8, 128), F32),
            pltpu.VMEM((WIDE, 8, 128), F32),
            pltpu.VMEM((VECTOR_ROWS, 128), F32),
            pltpu.VMEM((8, 128), F32),
            pltpu.VMEM((D, head_part), BF),
        ]
        + first_scratch(head_part)
        + second_scratch(head_part)
    )

    def body(net, ins, outs, scr):
        d_attn_own, ffn_part, g_up, down_sums, normed, hidden_in = ins[:6]
        input_grad, result_out, block_out, table, vector_out, norm_out = outs
        wv, tv, mv, qv, kv, vv, pv, av = scr[:8]
        big, dk, dv, dproj, ga = scr[8:13]
        pairs, narrow = [big, *scr[13:18]], scr[18:24]
        wide_a, wide_up, wide_down = scr[24:32], scr[32:40], scr[40:45]
        columns, hidden, part, landed, shard, mine = scr[45:51]
        d_gain, held = scr[51], scr[52:58]
        block, result, first, second, summed, norm = scr[58:64]
        go, wide_o = scr[64], scr[65:73]
        n = lax.axis_index("narrow")
        x, z, y, c = here()
        first_load = net.keep(down_sums, wide_down[0])
        loads = [net.keep(a, b) for a, b in zip(ins[12:], scr[:8])]
        own_loads = [net.keep(a, b) for a, b in zip(ins[6:12], held)]
        loads.append(net.keep(hidden_in, hidden))
        loads.append(net.keep(normed.at[:, lanes(n * table_rows, table_rows)], columns))
        greet(NARROW_ALL + WIDE_ALL)
        sums = Pairs(net, None, pairs)
        thirds = [(i * head_part, head_part, i * D) for i in range(3)]

        def router():
            w = lax.axis_index("wide")
            part[...] = lax.dot_general(
                columns[...], hidden[...], CONTRACT_ROWS, preferred_element_type=F32
            ).astype(BF)
            copies = []
            for p in WIDE_ALL:
                target = moved(**p)
                rows = part.at[span(target[0] * ROWS, ROWS)]
                copies.append(net.put(rows, landed.at[w], target))
            kept = net.keep(part.at[span(w * ROWS, ROWS)], landed.at[w])
            yield
            kept.wait()
            for copy in copies:
                copy.wait_recv()
            s = landed[0].astype(F32)
            for i in range(1, WIDE):
                s = s + landed[i].astype(F32)
            shard[...] = s.astype(BF)
            spot = mine.at[span(w * ROWS, ROWS)]
            copies = [net.put(shard, spot, moved(**p)) for p in WIDE_ALL]
            kept = net.keep(shard, spot)
            yield
            kept.wait()
            for copy in copies:
                copy.wait_recv()
            yield from gather_narrow(net, mine, table)

        moves = {
            GATHER: gather_narrow(net, d_attn_own, big),
            DOWN: second_then_narrow(
                net, wide_down[0], block, wide_down[1:], [(0, units, 4 * D + FF)]
            ),
            UP: wide_then_narrow(net, g_up, block, wide_up, [(0, units, 4 * D)]),
            MIXED: wide_then_narrow(net, ga, block, wide_a, thirds),
            MO: wide_then_narrow(net, go, block, wide_o, [(0, head_part, 3 * D)]),
            FEED: reduce_narrow(net, ffn_part, narrow),
            GATES: router(),
            TOTAL: sums.steps(),
        }

        def wait_loads():
            first_load.wait()
            for load in loads:
                load.wait()
            dk[...] = jnp.zeros_like(dk)
            dv[...] = jnp.zeros_like(dv)

        def one_pair(dy):
            r = span(wrap(y + dy) * pair_rows, pair_rows)
            mask = branch_mask(mv[r, :], PICK_ATTN)
            back = jnp.dot(big[r, :], wv[:, 3 * head_part :], preferred_element_type=F32)
            back = (back * mask).astype(BF)
            for h in range(2):
                at = pl.ds(h * HEAD_DIM, HEAD_DIM)
                d_out = back[:, h * HEAD_DIM : (h + 1) * HEAD_DIM]
                d_probs = lax.dot_general(
                    d_out, vv[:, at], CONTRACT_COLS, preferred_element_type=F32
                )
                probs_low = pv[r, pl.ds(h * GROUP, GROUP)]
                probs = probs_low.astype(F32)
                weighted = probs * d_probs
                centre = jnp.sum(weighted, axis=-1, keepdims=True)
                ds = (weighted - probs * centre).astype(BF)
                dq = jnp.dot(ds, kv[:, at], preferred_element_type=F32) * scale
                dproj[r, at] = turn(dq, tv[0, r, :], -tv[1, r, :]).astype(BF)
                dk[:, at] += lax.dot_general(
                    ds, qv[r, at], CONTRACT_ROWS, preferred_element_type=F32
                )
                dv[:, at] += lax.dot_general(
                    probs_low, d_out, CONTRACT_ROWS, preferred_element_type=F32
                )

        refill = []

        def turn_back():
            refill.append(net.keep(normed, pv))

            @pl.loop(0, SIDE)
            def _(i):
                r = span(i * pair_rows, pair_rows)
                cosine, sine = tv[0, r, :], -tv[1, r, :]
                for h in range(2):
                    at = pl.ds(h * HEAD_DIM, HEAD_DIM)
                    to = pl.ds(head_part + h * HEAD_DIM, HEAD_DIM)
                    dproj[r, to] = turn(dk[r, at] * scale, cosine, sine).astype(BF)
                dproj[r, pl.ds(2 * head_part, head_part)] = dv[r, :].astype(BF)

        def gradient(left, right, to):
            @pl.loop(0, D // strip)
            def _(i):
                to[span(i * strip, strip), :] = lax.dot_general(
                    left[:, lanes(i * strip, strip)],
                    right[...],
                    CONTRACT_ROWS,
                    preferred_element_type=F32,
                ).astype(BF)

        def mixed_gradient():
            refill[0].wait()
            gradient(pv, dproj, ga)

        def norm_back(dy):
            r = span(wrap(y + dy) * pair_rows, pair_rows)
            back = lax.dot_general(
                dproj[r, :], wv[:, : 3 * head_part], CONTRACT_COLS, preferred_element_type=F32
            )
            sums.store(dy, back)
            sums.cross(dy)

        stores = []

        own_there = []

        def wait_own():
            if not own_there:
                own_there.append(True)
                for load in own_loads:
                    load.wait()

        def output():
            wait_own()
            gate = mv[span(n * TOK, TOK), GATE_FFN : GATE_FFN + 1]
            result[...] = (held[4][...] + gate * narrow[5][...]).astype(BF)
            stores.append(net.keep(result, result_out))

        squares = []

        def late_squares():
            squares.append(squares_of(block.at[:, pl.ds(3 * D, D + 2 * FF)], ROWS, 2048))

        def first_norm_back():
            wait_own()
            tokens, after, gains, router_in = held[:4]
            total = sums.scr[5]
            d_normed = total[...] + lax.dot_general(
                hidden[span(n * TOK, TOK), :],
                router_in[...],
                CONTRACT_COLS,
                preferred_element_type=F32,
            )
            hat, inverse = normal(tokens[...].astype(F32))
            d_gain[...] = jnp.sum(d_normed * hat, axis=0, keepdims=True)
            total[...] = after[...] + normal_back(hat, inverse, d_normed * gains[0:1, :])
            stores.append(net.keep(total, input_grad))

        works = {
            LB: first_norm_back,
            OUT: output,
            SQ: late_squares,
            LD: wait_loads,
            RT: turn_back,
            GO: functools.partial(gradient, big, av, go),
            GQ: mixed_gradient,
        }
        for dy in PAIR_ORDER:
            works[PAIR[dy]] = functools.partial(one_pair, dy)
            works[NORM[dy]] = functools.partial(norm_back, dy)
        follow(BACKWARD_PLAN, works, moves)
        stores.append(net.keep(block, block_out))
        vector = held[5]
        for i in range(GAIN_ROWS // 2):
            vector[i : i + 1, :] = d_gain[:, i * 128 : (i + 1) * 128]
        others = squares_of(block.at[:, pl.ds(0, 3 * D)], ROWS, 2048)
        others = others + squares_of(shard, ROWS, RH)
        vector[VECTOR_ROWS - SQUARE_ROWS :, :] = squares[0] + others
        sum_everywhere(net, vector, first, second, summed)
        stores.append(net.keep(summed, vector_out))
        s = summed[...]
        small = s[:SMALL_ROWS]
        sum_all = jnp.sum(small * small) + jnp.sum(s[VECTOR_ROWS - SQUARE_ROWS :])
        norm[...] = jnp.sqrt(jnp.full((8, 128), sum_all, F32))
        stores.append(net.keep(norm, norm_out))
        for store in stores:
            store.wait()

    return comm_call(
        body,
        [d_attn_own, ffn_part, g_up, down_sums, normed, hidden_in] + list(own) + list(kept),
        [
            jax.ShapeDtypeStruct((TOK, D), F32),
            jax.ShapeDtypeStruct((TOK, D), BF),
            jax.ShapeDtypeStruct((ROWS, 4 * D + 2 * FF), BF),
            jax.ShapeDtypeStruct((D, RH), BF),
            jax.ShapeDtypeStruct((VECTOR_ROWS, 128), F32),
            jax.ShapeDtypeStruct((8, 128), F32),
        ],
        scratch,
        cid,
        GATHER_COPIES
        + 2 * REDUCE_COPIES
        + 3 * FIRST_COPIES
        + 4 * SECOND_COPIES
        + 6 * 7
        + 2 * 15
        + GATHER_COPIES
        + 7 + 15 + 7,
        17 + 1 + 1 + 5 + REDUCE_LOCALS + 3 * FIRST_LOCALS + 6 + 4,
        "attention_backward",
    )


def adamw(weight, moment_one, moment_two, gradient, step_rate):
    one = 0.9 * moment_one + 0.1 * gradient
    two = 0.95 * moment_two + 0.05 * (gradient * gradient)
    scaled = jnp.maximum(two * (1.0 / (1.0 - 0.95**STEP)), 1e-30)
    root = scaled * lax.rsqrt(scaled) + 1e-08
    guess = pltpu.reciprocal(root, approx=True)
    guess = guess * (2.0 - root * guess)
    guess = guess * (2.0 - root * guess)
    rate = step_rate / (1.0 - 0.9**STEP)
    updated = weight * (1.0 - step_rate * 0.1) - (one * rate) * guess
    return updated, one, two


def clip_of(norm):
    return jnp.minimum(1.0, CLIP_NORM / norm[0:1, 0:1])


def all_steps(block, layer, gains, second_layer, vector, norm):
    block_parts, layer_parts = 3, 2
    n_loads = 4 * (block_parts + layer_parts)

    def kernel(*refs):
        block_in, layer_in = refs[0:4], refs[4:8]
        gains_in, second_in, vec, n = refs[8:11], refs[11:14], refs[14], refs[15]
        block_out, layer_out = refs[16:20], refs[20:23]
        gains_out, second_out, counts_out, norm_out = refs[23:26], refs[26:29], refs[29], refs[30]
        held_block, held_layer, new_block, new_layer = (
            refs[31:35],
            refs[35:39],
            refs[39:43],
            refs[43:46],
        )
        gain_grad, second_grad, loaded, stored = refs[46:50]
        clip = clip_of(n)

        def start(pairs, part, sems, at):
            copies = []
            for i, (a, b) in enumerate(pairs):
                copies.append(pltpu.make_async_copy(a.at[part], b.at[part], sems.at[at + i]))
                copies[-1].start()
            return copies

        parts = []
        for i in range(block_parts):
            cols = block_in[0].shape[1] // block_parts
            parts.append((True, (slice(None), pl.ds(i * cols, cols))))
        for i in range(layer_parts):
            rows = layer_in[0].shape[0] // layer_parts
            parts.append((False, (pl.ds(i * rows, rows), slice(None))))
        loads, stores = [], []
        for i, (is_block, part) in enumerate(parts):
            pairs = zip(block_in, held_block) if is_block else zip(layer_in, held_layer)
            loads.append(start(pairs, part, loaded, 4 * i))

        for i in range(GAIN_ROWS):
            row, at = i // (GAIN_ROWS // 2), i % (GAIN_ROWS // 2) * 128
            gain_grad[row : row + 1, at : at + 128] = vec[i : i + 1, :]
        for i in range(RH // 128):
            at = GAIN_ROWS + i * 2 * LEVELS
            second_grad[:, i * 128 : (i + 1) * 128] = vec[at : at + 2 * LEVELS, :]
        for held, grad, new, rate in (
            (gains_in, gain_grad, gains_out, 0.6),
            (second_in, second_grad, second_out, 0.02),
        ):
            results = adamw(*[r[...] for r in held], grad[...] * clip, rate)
            for ref, value in zip(new, results):
                ref[...] = value
        row = vec[SMALL_ROWS : SMALL_ROWS + 1, :]
        counts_out[0:1, :] = row[:, :LEVELS]
        counts_out[1:2, :] = pltpu.roll(row, 128 - LEVELS, 1)[:, :LEVELS]
        norm_out[...] = n[0:1, 0:1]

        for i, (is_block, part) in enumerate(parts):
            for copy in loads[i]:
                copy.wait()
            held, new = (held_block, new_block) if is_block else (held_layer, new_layer)
            gradient = held[3][part].astype(F32) * clip
            results = adamw(*[r[part] for r in held[:3]], gradient, 0.02)
            for ref, value in zip(new, results):
                ref[part] = value
            if is_block:
                new[3][part] = results[0].astype(BF)
            pairs = zip(new, block_out if is_block else layer_out)
            stores += start(pairs, part, stored, 4 * i)
        for copy in stores:
            copy.wait()

    def like(x, dtype=F32):
        return jax.ShapeDtypeStruct(x.shape, dtype)

    def room(x, dtype=F32):
        return pltpu.VMEM(x.shape, dtype)

    far, near = pl.BlockSpec(memory_space=pl.ANY), pl.BlockSpec(memory_space=pltpu.VMEM)
    b, r, g, o = block[0], layer[0], gains[0], second_layer[0]
    return pl.pallas_call(
        kernel,
        out_shape=[like(b)] * 3
        + [like(b, BF)]
        + [like(r)] * 3
        + [like(g)] * 3
        + [like(o)] * 3
        + [jax.ShapeDtypeStruct((2, LEVELS), F32), jax.ShapeDtypeStruct((1, 1), F32)],
        in_specs=[far] * 8 + [near] * 8,
        out_specs=[far] * 7 + [near] * 8,
        scratch_shapes=[room(b)] * 3
        + [room(b, BF)]
        + [room(r)] * 3
        + [room(r, BF)]
        + [room(b)] * 3
        + [room(b, BF)]
        + [room(r)] * 3
        + [room(g), room(o)]
        + [pltpu.SemaphoreType.DMA((n_loads,)), pltpu.SemaphoreType.DMA((n_loads,))],
        compiler_params=pltpu.CompilerParams(vmem_limit_bytes=60 * 2**20),
        name="all_steps",
    )(*block, *layer, *gains, *second_layer, vector, norm)


def on_device(
    tokens,
    lengths,
    picks,
    cotangent,
    block_master,
    block_first,
    block_second,
    gains,
    gains_first,
    gains_second,
    router_in,
    router_in_first,
    router_in_second,
    router_out,
    router_out_first,
    router_out_second,
):
    half_dim = HEAD_DIM // 2
    angle_steps = 10000.0 ** (-np.arange(half_dim, dtype=np.float32) / half_dim)
    frequency = jnp.asarray(np.tile(angle_steps.astype(np.float32), (8, 2)))
    f = attention_forward(
        tokens,
        picks.T,
        lengths,
        frequency,
        gains,
        router_in,
        jnp.pad(router_out, ((0, 0), (0, 128 - 2 * LEVELS))).astype(BF),
        block_master,
        cotangent,
        1,
    )

    ffn_part, grad_up, down_sums, d_after, d_attn, d_hidden, vector = feed_forward(
        f["second"],
        f["g"],
        f["slab_up"],
        f["stage_up"],
        f["slab_down"],
        f["d_act"],
        f["marks"],
        [f["after"], f["attn_sum"], f["gate"], gains, f["slopes"], f["logit_slopes"], f["hidden"]],
        2,
    )
    d_inputs, result, block_low, router_in_grad, vector, norm = attention_backward(
        d_attn,
        ffn_part,
        grad_up,
        down_sums,
        f["normed"],
        d_hidden,
        [tokens, d_after, gains, f["router_low"], f["after"], vector],
        [f[k] for k in ("slab_a", "turns", "marks", "q", "k", "v", "p", "a")],
        3,
    )
    (
        new_block,
        new_block_first,
        new_block_second,
        block_copy,
        new_router_in,
        new_router_in_first,
        new_router_in_second,
        new_gains,
        new_gains_first,
        new_gains_second,
        new_router_out,
        new_router_out_first,
        new_router_out_second,
        counts,
        grad_norm,
    ) = all_steps(
        (block_master, block_first, block_second, block_low),
        (router_in, router_in_first, router_in_second, router_in_grad),
        (gains, gains_first, gains_second),
        (router_out.T, router_out_first.T, router_out_second.T),
        vector,
        norm,
    )
    return (
        result,
        d_inputs,
        counts,
        grad_norm.reshape(()),
        new_block,
        new_block_first,
        new_block_second,
        block_copy,
        new_gains,
        new_gains_first,
        new_gains_second,
        new_router_in,
        new_router_in_first,
        new_router_in_second,
        new_router_out.T,
        new_router_out_first.T,
        new_router_out_second.T,
    )


def solution(mesh):
    both = P(("wide", "narrow"), None)
    return jax.shard_map(
        on_device,
        mesh=mesh,
        in_specs=(both, P("wide", None)) + (both,) * 5 + (P(),) * 9,
        out_specs=(both, both, P(), P()) + (both,) * 4 + (P(),) * 9,
        check_vma=False,
    )
```

```python
import functools

import jax
import jax.numpy as jnp
import numpy as np
from jax import lax
from jax.experimental import pallas as pl
from jax.experimental.pallas import tpu as pltpu
from jax.sharding import PartitionSpec as P

D = 2048
HEAD_DIM = 128
FF = 8192
RH = 256
LEVELS = 4
STEP = 10
TOK = 128
GROUP = 1024
SIDE = 4
WIDE = 16
NARROW = 8
ROWS = 16

VECTOR_ROWS = 64
GAIN_ROWS = 2 * D // 128
SMALL_ROWS = GAIN_ROWS + RH * 2 * LEVELS // 128
SQUARE_ROWS = 8

NORM_EPS = 1e-05
CLIP_NORM = 1.0
CONTRACT_COLS = (((1,), (1,)), ((), ()))
CONTRACT_ROWS = (((0,), (0,)), ((), ()))
MESH = pl.DeviceIdType.MESH
BF = jnp.bfloat16
F32 = jnp.float32


(
    CA, DA, DOWN, DS, EX, FEED, FIRST, GATES, GATHER, GD, GE, GG, GM, GO, GQ, GU, GX, HID, L1,
    LB, LD, LN, LV, MIXED, MO, MORE, N0, N1, N2, N3, OUT, P0, P1, P2, P3, Q, RF, RT, SA, SD, SL,
    SQ, SU, T0, T1, T2, T3, TB, TOTAL, U0, U1, U2, U3, UP, V0, V1, V2, V3, WA, WD, WU, Y0, Y1,
    Y2, Y3,
) = range(65)
ATTEND = (T0, T1, T2, T3)
EARLY = (V0, V1, V2, V3)
UNITS = (U0, U1, U2, U3)
OUTPUT = (Y0, Y1, Y2, Y3)
NORM = (N0, N1, N2, N3)
PAIR = (P0, P1, P2, P3)


FORWARD_PLAN = (
    CA, SA, L1, TB, GX, SA, GX, WA, RF, GM, WA, WA, GX, GX, SU, WA, SD, WA, GX, GG, GM, WA, SD,
    GG, WD, SU, GX, SL, GM, WU, EX, WA, Q, WD, T1, GG, WU, T2, WD, TOTAL, T0, WD, T3, TOTAL, WD,
    TOTAL, GG, TOTAL, WD, WU, TOTAL, GG, GG, WU, WD, DA, WU, GG, TOTAL, WU, LN, WU, GX, SL,
    TOTAL, GG, WU,
)
FEED_PLAN = (
    GATHER, WU, WU, GATHER, WU, LD, GATHER, WU, WU, V0, WU, GATHER, V1, WU, V3, U1, GATHER, U3,
    N1, N3, GATHER, V2, U2, TOTAL, TOTAL, N2, U0, GE, TOTAL, DS, Y2, MORE, GD, FIRST, N0,
    GATHER, TOTAL, GU, FIRST, TOTAL, MORE, TOTAL, TOTAL, LB, HID, LV, Y3, Y1, Y0, HID, FIRST,
    FIRST, MORE, HID,
)
BACKWARD_PLAN = (
    GATHER, UP, LD, GATES, UP, GATHER, GATHER, DOWN, FEED, P0, FEED, GATHER, P3, GATHER, P1,
    FEED, GATHER, DOWN, GATES, UP, P2, DOWN, GATHER, GO, MO, FEED, UP, GATES, RT, N2, GATES, N1,
    MO, GQ, UP, MIXED, GATES, TOTAL, MO, TOTAL, MIXED, DOWN, N3, N0, TOTAL, MO, GATES, TOTAL,
    FEED, MIXED, GATES, FEED, MIXED, TOTAL, GATES, MO, MIXED, TOTAL, GATES, GATES, MO, DOWN,
    TOTAL, MO, LB, UP, OUT, SQ, MIXED, UP,
)


def here():
    w = lax.axis_index("wide")
    n = lax.axis_index("narrow")
    return lax.div(w, SIDE), lax.rem(w, SIDE), lax.div(n, 2), lax.rem(n, 2)


def wrap(i):
    return lax.rem(i + 2 * SIDE, SIDE)


def moved(dx=0, dz=0, dy=0, dc=0):
    x, z, y, c = here()
    return (wrap(x + dx) * SIDE + wrap(z + dz), wrap(y + dy) * 2 + lax.rem(c + dc, 2))


NEAR_Y = [dict(dy=1), dict(dy=-1), dict(dc=1)]
NARROW_ALL = [dict(dy=a, dc=b) for a in range(SIDE) for b in range(2) if a or b]
NEAR_XZ = [dict(dx=1), dict(dx=-1), dict(dz=1), dict(dz=-1)]
WIDE_ALL = [dict(dx=a, dz=b) for a in range(SIDE) for b in range(SIDE) if a or b]


def greet(partners):
    barrier = pltpu.get_barrier_semaphore()
    for p in partners:
        pl.semaphore_signal(barrier, inc=1, device_id=moved(**p), device_id_type=MESH)
    pl.semaphore_wait(barrier, len(partners))


def span(start, size):
    if not isinstance(start, int):
        start = pl.multiple_of(start, ROWS)
    return pl.ds(start, size)


def lanes(start, size):
    if not isinstance(start, int):
        start = pl.multiple_of(start, 128)
    return pl.ds(start, size)


def step(*parts):
    for part in parts:
        next(part, None)


class Net:
    def __init__(self, send, recv, local):
        self.send, self.recv, self.local = send, recv, local
        self.used, self.used_local = 0, 0
        self.sent = []

    def put(self, src, dst, target):
        i = self.used
        self.used += 1
        copy = pltpu.make_async_remote_copy(
            src_ref=src,
            dst_ref=dst,
            send_sem=self.send.at[i],
            recv_sem=self.recv.at[i],
            device_id=target,
            device_id_type=MESH,
        )
        copy.start()
        self.sent.append(copy)
        return copy

    def keep(self, src, dst):
        i = self.used_local
        self.used_local += 1
        copy = pltpu.make_async_copy(src, dst, self.local.at[i])
        copy.start()
        return copy

    def sent_by(self, *copies):
        for copy in copies:
            copy.wait_send()
        done = [id(copy) for copy in copies]
        self.sent = [copy for copy in self.sent if id(copy) not in done]

    def finish(self):
        for copy in self.sent:
            copy.wait_send()


def take_turns(*parts):
    live = list(parts)
    while live:
        still = []
        for part in live:
            try:
                next(part)
                still.append(part)
            except StopIteration:
                pass
        live = still


def follow(plan, works, moves):
    for name in plan:
        if name in works:
            works[name]()
        else:
            next(moves[name], None)
    take_turns(*moves.values())


def comm_call(body, ins, outs, scratch, cid, copies, locals_, name, vmem=63, cost=None):
    n_in, n_out, n_scr = len(ins), len(outs), len(scratch)

    def kernel(*refs):
        in_refs = refs[:n_in]
        out_refs = refs[n_in : n_in + n_out]
        scr = refs[n_in + n_out : n_in + n_out + n_scr]
        send, recv, local = refs[n_in + n_out + n_scr :]
        net = Net(send, recv, local)
        body(net, in_refs, out_refs, scr)
        net.finish()
        assert net.used <= copies and net.used_local <= locals_, (net.used, net.used_local)

    return pl.pallas_call(
        kernel,
        out_shape=outs,
        in_specs=[pl.BlockSpec(memory_space=pl.ANY)] * n_in,
        out_specs=[pl.BlockSpec(memory_space=pl.ANY)] * n_out,
        scratch_shapes=list(scratch)
        + [
            pltpu.SemaphoreType.DMA((copies,)),
            pltpu.SemaphoreType.DMA((copies,)),
            pltpu.SemaphoreType.DMA((max(locals_, 1),)),
        ],
        compiler_params=pltpu.CompilerParams(
            collective_id=cid, has_side_effects=True, vmem_limit_bytes=vmem * 2**20
        ),
        name=name,
        cost_estimate=cost,
    )(*ins)


def gather_narrow(net, own, out):
    x, z, y, c = here()
    rows = own.shape[0]
    half = rows // 2

    def block(dy, lo=0, size=rows):
        return out.at[span((wrap(y + dy) * 2 + c) * rows + lo, size)]

    first, last = own.at[pl.ds(0, half)], own.at[pl.ds(half, half)]
    up = net.put(first, block(0, 0, half), moved(dy=1))
    down = net.put(last, block(0, half, half), moved(dy=-1))
    up_late = net.put(last, block(0, half, half), moved(dy=1))
    down_late = net.put(first, block(0, 0, half), moved(dy=-1))
    across = [net.put(own, block(0), moved(dc=1))]
    mine = net.keep(own, block(0))
    yield
    mine.wait()
    across[0].wait_recv()
    yield
    up.wait_recv()
    on = net.put(block(-1, 0, half), block(-1, 0, half), moved(dy=1))
    down.wait_recv()
    back = net.put(block(1, half, half), block(1, half, half), moved(dy=-1))
    yield
    up_late.wait_recv()
    across.append(net.put(block(-1), block(-1), moved(dc=1)))
    down_late.wait_recv()
    across.append(net.put(block(1), block(1), moved(dc=1)))
    across[1].wait_recv()
    across[2].wait_recv()
    yield
    on.wait_recv()
    across.append(net.put(block(2, 0, half), block(2, 0, half), moved(dc=1)))
    back.wait_recv()
    across.append(net.put(block(2, half, half), block(2, half, half), moved(dc=1)))
    yield
    across[3].wait_recv()
    across[4].wait_recv()
    yield
    net.sent_by(up, down, up_late, down_late, on, back, *across)


GATHER_COPIES = 12


def gather_small(net, own, out):
    c = here()[3]
    y = here()[2]
    rows = own.shape[0]

    def block(dy):
        return out.at[span((wrap(y + dy) * 2 + c) * rows, rows)]

    along = [net.put(own, block(0), moved(dy=d)) for d in (2, 1, 3)]
    across = [net.put(own, block(0), moved(dc=1))]
    mine = net.keep(own, block(0))
    yield
    for copy, d in zip(along, (2, 1, 3)):
        copy.wait_recv()
        across.append(net.put(block(-d), block(-d), moved(dc=1)))
    yield
    mine.wait()
    for copy in across:
        copy.wait_recv()


GATHER_SMALL_COPIES = 7


def reduce_scratch(rows, cols):
    return [
        pltpu.VMEM((SIDE, rows, cols), BF),
        pltpu.VMEM((SIDE, rows, cols), BF),
        pltpu.VMEM((2, rows // 2, cols), BF),
        pltpu.VMEM((2, rows, cols), BF),
        pltpu.VMEM((3, rows, cols), BF),
        pltpu.VMEM((rows, cols), F32),
    ]


REDUCE_COPIES = 10
REDUCE_LOCALS = 5


def reduce_narrow(net, part, scr):
    own, other, through, landed, ready, total = scr
    x, z, y, c = here()
    rows, cols = total.shape
    half = rows // 2

    def block(dy, core):
        return part.at[span((wrap(y + dy) * 2 + core) * rows, rows)]

    order = (2, 1, 3, 0)
    local, cross = {}, {}
    for dy in order:
        cross[dy] = net.put(block(dy, 1 - c), other.at[dy], moved(dc=1))
        local[dy] = net.keep(block(dy, c), own.at[dy])

    def pair(dy, lo, size):
        s = span(lo, size)
        return own[dy, s, :].astype(F32) + other[dy, s, :].astype(F32)

    yield
    local[2].wait()
    cross[2].wait_recv()
    ready[0] = pair(2, 0, rows).astype(BF)
    first, last = span(0, half), span(half, half)
    via_up = net.put(ready.at[0, first], through.at[0], moved(dy=1))
    via_down = net.put(ready.at[0, last], through.at[1], moved(dy=-1))
    yield
    local[1].wait()
    cross[1].wait_recv()
    ready[1, last, :] = pair(1, half, half).astype(BF)
    up_late = net.put(ready.at[1, last], landed.at[0, last], moved(dy=1))
    local[3].wait()
    cross[3].wait_recv()
    ready[2, first, :] = pair(3, 0, half).astype(BF)
    down_first = net.put(ready.at[2, first], landed.at[1, first], moved(dy=-1))
    yield
    via_up.wait_recv()
    ready[1, first, :] = (pair(1, 0, half) + through[0].astype(F32)).astype(BF)
    up_first = net.put(ready.at[1, first], landed.at[0, first], moved(dy=1))
    via_down.wait_recv()
    ready[2, last, :] = (pair(3, half, half) + through[1].astype(F32)).astype(BF)
    down_late = net.put(ready.at[2, last], landed.at[1, last], moved(dy=-1))
    yield
    local[0].wait()
    cross[0].wait_recv()
    total[...] = pair(0, 0, rows)
    yield
    for copy in (up_late, down_first, up_first, down_late):
        copy.wait_recv()
    total[...] += landed[0].astype(F32) + landed[1].astype(F32)


def pairs_scratch(rows, cols):
    return [
        pltpu.VMEM((SIDE * 2 * rows, cols), BF),
        pltpu.VMEM((SIDE, rows, cols), BF),
        pltpu.VMEM((2, rows // 2, cols), BF),
        pltpu.VMEM((2, rows, cols), BF),
        pltpu.VMEM((3, rows, cols), BF),
        pltpu.VMEM((rows, cols), F32),
    ]


PAIR_ORDER = (2, 1, 3, 0)


class Pairs:
    def __init__(self, net, out, scr, far_first=True):
        self.net, self.out, self.scr, self.far_first = net, out, scr, far_first
        self.crossed = {}

    def store(self, dy, value):
        rows = value.shape[0]
        self.scr[0][pl.ds(dy * rows, rows), :] = value.astype(BF)

    def cross(self, dy):
        parts, other = self.scr[:2]
        c = here()[3]
        rows = other.shape[1]
        self.crossed[dy] = self.net.put(
            parts.at[span((2 * dy + 1 - c) * rows, rows)], other.at[dy], moved(dc=1)
        )

    def steps(self):
        net = self.net
        parts, other, through, landed, ready, total = self.scr
        c = here()[3]
        rows = total.shape[0]
        half = rows // 2
        first, last = pl.ds(0, half), pl.ds(half, half)

        def pair(dy, lo, size):
            mine = parts[span((2 * dy + c) * rows + lo, size), :].astype(F32)
            return mine + other[dy, pl.ds(lo, size), :].astype(F32)

        def far():
            self.crossed[2].wait_recv()
            ready[0] = pair(2, 0, rows).astype(BF)
            via_up = net.put(ready.at[0, first], through.at[0], moved(dy=1))
            via_down = net.put(ready.at[0, last], through.at[1], moved(dy=-1))
            return via_up, via_down

        if self.far_first:
            via_up, via_down = far()
            yield
        self.crossed[1].wait_recv()
        ready[1, last, :] = pair(1, half, half).astype(BF)
        up_late = net.put(ready.at[1, last], landed.at[0, last], moved(dy=1))
        yield
        self.crossed[3].wait_recv()
        ready[2, first, :] = pair(3, 0, half).astype(BF)
        down_first = net.put(ready.at[2, first], landed.at[1, first], moved(dy=-1))
        yield
        if not self.far_first:
            via_up, via_down = far()
            yield
        via_up.wait_recv()
        ready[1, first, :] = (pair(1, 0, half) + through[0].astype(F32)).astype(BF)
        up_first = net.put(ready.at[1, first], landed.at[0, first], moved(dy=1))
        via_down.wait_recv()
        ready[2, last, :] = (pair(3, half, half) + through[1].astype(F32)).astype(BF)
        down_late = net.put(ready.at[2, last], landed.at[1, last], moved(dy=-1))
        yield
        self.crossed[0].wait_recv()
        total[...] = pair(0, 0, rows)
        yield
        for copy in (up_late, down_first, up_first, down_late):
            copy.wait_recv()
        total[...] += landed[0].astype(F32) + landed[1].astype(F32)
        if self.out is not None:
            done = net.keep(total, self.out)
            yield
            done.wait()


def spread_narrow(net, low, slab, pieces):
    w = lax.axis_index("wide")
    n = lax.axis_index("narrow")
    base = n * ROWS if slab.shape[0] == TOK else w * TOK + n * ROWS
    mine, copies = [], []
    for start, stride, width, to in pieces:
        spot = slab.at[span(base, ROWS), pl.ds(to, width)]
        for p in NARROW_ALL:
            target = moved(**p)
            columns = lanes(start + target[1] * stride, width)
            copies.append(net.put(low.at[:, columns], spot, target))
        mine.append(net.keep(low.at[:, lanes(start + n * stride, width)], spot))
    yield
    for copy in mine:
        copy.wait()
    for copy in copies:
        copy.wait_recv()


SPREAD_COPIES = 7


def gather_wide(net, slab, lead, stage=None):
    x, z, y, c = here()
    rows = TOK // 2
    half = rows // 2
    low = 0 if lead == "x" else rows

    def block(a, b, lo=0, size=rows):
        px, pz = (a, b) if lead == "x" else (b, a)
        return slab.at[span((wrap(x + px) * SIDE + wrap(z + pz)) * TOK + low + lo, size)]

    def lead_to(d):
        return moved(dx=d) if lead == "x" else moved(dz=d)

    def then_to(d):
        return moved(dz=d) if lead == "x" else moved(dx=d)

    def both(src, to, dst=None):
        dst = src if dst is None else dst
        return net.put(src, dst, to(1)), net.put(src, dst, to(-1))

    mine = block(0, 0) if stage is None else stage.at[pl.ds(low, rows)]
    fore, aft = both(mine, lead_to, block(0, 0))
    second = {0: both(mine, then_to, block(0, 0))}
    yield
    fore.wait_recv()
    on = net.put(block(-1, 0, 0, half), block(-1, 0, 0, half), lead_to(1))
    second[-1] = both(block(-1, 0), then_to)
    aft.wait_recv()
    back = net.put(block(1, 0, half, half), block(1, 0, half, half), lead_to(-1))
    second[1] = both(block(1, 0), then_to)
    yield
    last = []

    def relay(a):
        f, b = second[a]
        f.wait_recv()
        last.append(net.put(block(a, -1, 0, half), block(a, -1, 0, half), then_to(1)))
        b.wait_recv()
        last.append(net.put(block(a, 1, half, half), block(a, 1, half, half), then_to(-1)))

    kept = None if stage is None else net.keep(mine, block(0, 0))
    relay(0)
    yield
    on.wait_recv()
    back.wait_recv()
    second[2] = both(block(2, 0), then_to)
    yield
    relay(-1)
    relay(1)
    yield
    relay(2)
    yield
    if kept is not None:
        kept.wait()
    for copy in last:
        copy.wait_recv()


WIDE_COPIES = 20


def mean_of(values):
    return jnp.sum(values, axis=-1, keepdims=True) * (1.0 / D)


def normal(values):
    centered = values - mean_of(values)
    inverse = lax.rsqrt(mean_of(centered * centered) + NORM_EPS)
    return centered * inverse, inverse


def normal_back(hat, inverse, d_hat):
    return inverse * (d_hat - mean_of(d_hat) - hat * mean_of(d_hat * hat))


def turn(values, cosine, sine):
    return values * cosine + pltpu.roll(values, HEAD_DIM // 2, 1) * sine


def allowed_keys(first_row, rows, first_length):
    query = first_row + lax.broadcasted_iota(jnp.int32, (rows, 1), 0)
    key = lax.broadcasted_iota(jnp.int32, (rows, GROUP), 1)
    start = jnp.where(query >= first_length, first_length, 0)
    return (key <= query) & (key >= start)


PICK_ATTN, PICK_FFN, GATE_FFN = 0, 32, 64
LATER_UNITS = 512


def branch_mask(marks, lane):
    n = lax.axis_index("narrow").astype(F32)
    return (n < 2.0 * (marks[:, lane : lane + 1] + 1.0)).astype(F32)


def half_turns(first_length, frequency, tv):
    rows = 64
    half = GROUP // 2
    left = lax.broadcasted_iota(jnp.int32, (rows, 128), 1) < HEAD_DIM // 2
    row = lax.broadcasted_iota(jnp.int32, (rows, 128), 0)

    @pl.loop(0, half // rows)
    def _(i):
        token = row + i * rows + jnp.where(left, 0, half)
        position = token - jnp.where(token >= first_length, first_length, 0)
        angles = position.astype(F32) * frequency
        cosine, sine = jnp.cos(angles), jnp.sin(angles)
        cosine_other = pltpu.roll(cosine, HEAD_DIM // 2, 1)
        sine_other = pltpu.roll(sine, HEAD_DIM // 2, 1)
        low, high = span(i * rows, rows), span(half + i * rows, rows)
        tv[0, low, :] = jnp.where(left, cosine, cosine_other)
        tv[0, high, :] = jnp.where(left, cosine_other, cosine)
        tv[1, low, :] = jnp.where(left, -sine, sine_other)
        tv[1, high, :] = jnp.where(left, -sine_other, sine)


GELU_SCALE = (2.0 / 3.141592653589793) ** 0.5
GELU_CUBE = 0.044715


def route(normed, first_layer, second_layer, picks):
    before = jnp.dot(normed, first_layer, preferred_element_type=F32)
    square = before * before
    bent = jnp.tanh(GELU_SCALE * before * (1.0 + GELU_CUBE * square))
    hidden = 0.5 * before * (1.0 + bent)
    slope = 0.5 * (1.0 + bent) + 0.5 * before * (1.0 - bent * bent) * GELU_SCALE * (
        1.0 + 3.0 * GELU_CUBE * square
    )
    logits = jnp.dot(hidden.astype(BF), second_layer, preferred_element_type=F32)
    lane = lax.broadcasted_iota(jnp.int32, logits.shape, 1)
    gates, logit_slopes, slopes = [], [], []
    for branch in range(2):
        start = branch * LEVELS
        inside = (lane >= start) & (lane < start + LEVELS)
        shown = jnp.where(inside, logits, -1e30)
        expo = jnp.exp(shown - jnp.max(shown, axis=-1, keepdims=True))
        expo = jnp.where(inside, expo, 0.0)
        probs = expo / jnp.sum(expo, axis=-1, keepdims=True)
        chosen = jnp.where(lane.astype(F32) == picks[branch] + float(start), 1.0, 0.0)
        gate = float(LEVELS) * jnp.sum(probs * chosen, axis=-1, keepdims=True)
        logit_slope = gate * (chosen - probs)
        gates.append(gate)
        logit_slopes.append(logit_slope)
        slopes.append(
            slope
            * lax.dot_general(
                logit_slope.astype(BF), second_layer, CONTRACT_COLS, preferred_element_type=F32
            )
        )
    return hidden, gates, logit_slopes, slopes


def attention_forward(
    tokens, picks, lengths, frequency, gains, router_in, router_out, master, upstream, cid
):
    pair_rows = 2 * TOK
    head_part = D // NARROW
    units = FF // NARROW
    low = jax.ShapeDtypeStruct((GROUP, head_part), BF)
    results = dict(
        attn_sum=jax.ShapeDtypeStruct((TOK, D), F32),
        q=low,
        k=low,
        v=low,
        p=jax.ShapeDtypeStruct((GROUP, 2 * GROUP), BF),
        a=low,
        g=jax.ShapeDtypeStruct((GROUP, D), BF),
        slab_a=jax.ShapeDtypeStruct((D, 4 * head_part), BF),
        slab_up=jax.ShapeDtypeStruct((D, units - LATER_UNITS), BF),
        stage_up=jax.ShapeDtypeStruct((TOK, LATER_UNITS), BF),
        slab_down=jax.ShapeDtypeStruct((D, units), BF),
        normed=jax.ShapeDtypeStruct((GROUP, D), BF),
        marks=jax.ShapeDtypeStruct((GROUP, 128), F32),
        after=jax.ShapeDtypeStruct((TOK, D), F32),
        second=jax.ShapeDtypeStruct((TOK, D), BF),
        d_act=jax.ShapeDtypeStruct((GROUP, units), F32),
        turns=jax.ShapeDtypeStruct((2, GROUP, HEAD_DIM), F32),
        router_low=jax.ShapeDtypeStruct((D, RH), BF),
        hidden=jax.ShapeDtypeStruct((TOK, RH), F32),
        gate=jax.ShapeDtypeStruct((TOK, 128), F32),
        logit_slopes=jax.ShapeDtypeStruct((2, TOK, 128), F32),
        slopes=jax.ShapeDtypeStruct((2, TOK, RH), F32),
    )
    held = tuple(k for k in results if k not in ("attn_sum", "slab_up", "stage_up"))
    own_inputs = (tokens, picks, lengths, frequency, gains, router_in, router_out)

    def body(net, ins, outs, scr):
        out = dict(zip(results, outs))
        to = dict(zip(held, scr))
        scr = scr[len(held) :]
        xv, wv, tv, mv = to["normed"], to["slab_a"], to["turns"], to["marks"]
        qv, kv, vv, pv, av = (to[k] for k in "qkvpa")
        held_in, scr = scr[:7], scr[7:]
        own_tokens, own_picks, lv, fv, own_gains, rv, ov = held_in
        stage_up, stage_down, normed_own, marks_own, full, low, mark_rows = scr[:7]
        pairs = scr[7:]
        master, upstream = ins[7:]
        x, z, y, c = here()
        master_load = net.keep(master, full)
        loads = [net.keep(a, b) for a, b in zip(ins[:7], held_in)]
        greet(NARROW_ALL + NEAR_XZ)
        sums = Pairs(net, out["attn_sum"], pairs)
        stores = []

        def store(*names):
            stores.extend([net.keep(to[name], out[name]) for name in names])

        moves = {
            SA: spread_narrow(
                net, low, wv, [(i * D, head_part, head_part, i * head_part) for i in range(4)]
            ),
            SU: spread_narrow(net, low, stage_up, [(4 * D, units, units - LATER_UNITS, 0)]),
            SL: spread_narrow(
                net,
                low,
                out["stage_up"],
                [(4 * D + units - LATER_UNITS, units, LATER_UNITS, 0)],
            ),
            SD: spread_narrow(net, low, stage_down, [(4 * D + FF, units, units, 0)]),
            GX: gather_narrow(net, normed_own, xv),
            GM: gather_small(net, marks_own, mark_rows),
            GG: gather_narrow(net, upstream, to["g"]),
            WA: side_by_side(*[gather_wide(net, wv, k) for k in "xz"]),
            WU: side_by_side(*[gather_wide(net, out["slab_up"], k, stage_up) for k in "xz"]),
            WD: side_by_side(*[gather_wide(net, to["slab_down"], k, stage_down) for k in "xz"]),
            TOTAL: sums.steps(),
        }

        def cast():
            master_load.wait()

            @pl.loop(0, low.shape[1] // 2048)
            def _(i):
                columns = lanes(i * 2048, 2048)
                low[:, columns] = full[:, columns].astype(BF)

        def first_norm():
            for load in loads:
                load.wait()
            hat, _ = normal(own_tokens[...].astype(F32))
            normed_own[...] = (hat * own_gains[0:1, :]).astype(BF)

        def route_own():
            to["router_low"][...] = rv[...].astype(BF)
            row = lax.broadcasted_iota(jnp.int32, (TOK, TOK), 0)
            lane = lax.broadcasted_iota(jnp.int32, (TOK, TOK), 1)
            level = [
                jnp.sum(
                    jnp.where(row == lane, own_picks[b : b + 1, :].astype(F32), 0.0),
                    axis=-1,
                    keepdims=True,
                )
                for b in range(2)
            ]
            hidden, gates, logit_slopes, slopes = route(
                normed_own[...], to["router_low"][...], ov[...], level
            )
            to["hidden"][...] = hidden
            to["gate"][...] = jnp.broadcast_to(gates[0], (TOK, 128))
            for branch in range(2):
                to["logit_slopes"][branch] = logit_slopes[branch]
                to["slopes"][branch] = slopes[branch]
            marks_own[...] = jnp.zeros_like(marks_own)
            for b in range(2):
                marks_own[b : b + 1, :] = own_picks[b : b + 1, :].astype(F32)
            marks_own[2:3, :] = jnp.sum(
                jnp.where(row == lane, gates[1], 0.0), axis=0, keepdims=True
            )
            store("router_low", "hidden", "gate", "logit_slopes", "slopes")

        def expand():
            row = lax.broadcasted_iota(jnp.int32, (TOK, TOK), 0)
            lane = lax.broadcasted_iota(jnp.int32, (TOK, TOK), 1)

            @pl.loop(0, NARROW)
            def _(i):
                rows = mark_rows[span(i * ROWS, ROWS), :]
                marks = [
                    jnp.sum(jnp.where(row == lane, rows[b : b + 1, :], 0.0), axis=1, keepdims=True)
                    for b in range(3)
                ]
                other = jnp.where(lane < GATE_FFN, marks[1], marks[2])
                mv[span(i * TOK, TOK), :] = jnp.where(lane < PICK_FFN, marks[0], other)

            store("marks")

        def tables():
            half_turns(lv[0:1, 0:1], fv[0:1, :], tv)
            store("turns")

        def down_back():
            store("g", "slab_down")

            @pl.loop(0, SIDE)
            def _(i):
                r = span(i * pair_rows, pair_rows)
                to["d_act"][r, :] = jnp.dot(
                    to["g"][r, :], to["slab_down"][...], preferred_element_type=F32
                )

            store("d_act")

        def project():
            store("normed", "slab_a")

            @pl.loop(0, SIDE)
            def _(i):
                r = span(i * pair_rows, pair_rows)
                proj = jnp.dot(xv[r, :], wv[:, : 3 * head_part], preferred_element_type=F32)
                cosine, sine = tv[0, r, :], tv[1, r, :]
                for h in range(2):
                    at = pl.ds(h * HEAD_DIM, HEAD_DIM)
                    a = h * HEAD_DIM
                    qv[r, at] = turn(proj[:, a : a + HEAD_DIM], cosine, sine).astype(BF)
                    a += head_part
                    kv[r, at] = turn(proj[:, a : a + HEAD_DIM], cosine, sine).astype(BF)
                vv[r, :] = proj[:, 2 * head_part :].astype(BF)

            store("q", "k", "v")

        def attend(dy):
            first = wrap(y + dy) * pair_rows
            r = span(first, pair_rows)
            allowed = allowed_keys(first, pair_rows, lv[0:1, 0:1])
            heads = []
            for h in range(2):
                at = pl.ds(h * HEAD_DIM, HEAD_DIM)
                scores = lax.dot_general(
                    qv[r, at], kv[:, at], CONTRACT_COLS, preferred_element_type=F32
                )
                scores = jnp.where(allowed, scores * HEAD_DIM ** (-0.5), -1e30)
                expo = jnp.exp(scores - jnp.max(scores, axis=-1, keepdims=True))
                probs = expo * (1.0 / jnp.sum(expo, axis=-1, keepdims=True))
                low = probs.astype(BF)
                pv[r, pl.ds(h * GROUP, GROUP)] = low
                heads.append(jnp.dot(low, vv[:, at], preferred_element_type=F32))
            mask = branch_mask(mv[r, :], PICK_ATTN)
            av[r, :] = (jnp.concatenate(heads, axis=1) * mask).astype(BF)
            back = lax.dot_general(
                av[r, :], wv[:, 3 * head_part :], CONTRACT_COLS, preferred_element_type=F32
            )
            sums.store(dy, back)
            sums.cross(dy)
            stores.append(net.keep(pv.at[r], out["p"].at[r]))
            stores.append(net.keep(av.at[r], out["a"].at[r]))

        def second_norm():
            values = own_tokens[...].astype(F32) + to["gate"][:, :1] * sums.scr[5][...]
            to["after"][...] = values
            to["second"][...] = (normal(values)[0] * own_gains[1:2, :]).astype(BF)
            store("after", "second")

        works = {
            CA: cast,
            L1: first_norm,
            RF: route_own,
            EX: expand,
            TB: tables,
            Q: project,
            LN: second_norm,
            DA: down_back,
        }
        for dy in PAIR_ORDER:
            works[ATTEND[dy]] = functools.partial(attend, dy)
        follow(FORWARD_PLAN, works, moves)
        for done in stores:
            done.wait()

    got = comm_call(
        body,
        list(own_inputs) + [master, upstream],
        list(results.values()),
        [pltpu.VMEM(results[k].shape, results[k].dtype) for k in held]
        + [pltpu.VMEM(r.shape, r.dtype) for r in own_inputs]
        + [
            pltpu.VMEM((TOK, units - LATER_UNITS), BF),
            pltpu.VMEM((TOK, units), BF),
            pltpu.VMEM((TOK, D), BF),
            pltpu.VMEM((ROWS, 128), F32),
            pltpu.VMEM(master.shape, F32),
            pltpu.VMEM(master.shape, BF),
            pltpu.VMEM((NARROW * ROWS, 128), F32),
        ]
        + pairs_scratch(TOK, D),
        cid,
        REDUCE_COPIES + 6 * WIDE_COPIES + 3 * GATHER_COPIES + 7 * SPREAD_COPIES,
        8 + 7 + 3 + 4 + 1 + 8 + len(held),
        "attention_forward",
    )
    return dict(zip(results, got))


def first_scratch(cols):
    part, half = TOK // 2, TOK // 4
    return [
        pltpu.VMEM((2, 2, SIDE, half, cols), BF),
        pltpu.VMEM((2, 2, SIDE, part, cols), BF),
        pltpu.VMEM((2, 2, SIDE, half, cols), BF),
        pltpu.VMEM((2, SIDE, part, cols), BF),
    ]


def second_scratch(cols):
    part, half = TOK // 2, TOK // 4
    return [
        pltpu.VMEM((2, 2, half, cols), BF),
        pltpu.VMEM((2, 2, part, cols), BF),
        pltpu.VMEM((2, 2, half, cols), BF),
        pltpu.VMEM((TOK, cols), BF),
    ]


FIRST_COPIES = 12
SECOND_COPIES = 12
FIRST_LOCALS = 6


def lead_moves(lead):
    def lead_to(d):
        return moved(dx=d) if lead == "x" else moved(dz=d)

    def then_to(d):
        return moved(dz=d) if lead == "x" else moved(dx=d)

    return lead_to, then_to


def reduce_first(net, grad, scr, lead):
    via, landed, ready, sums = scr
    x, z, y, c = here()
    part, half = TOK // 2, TOK // 4
    k = 0 if lead == "x" else 1
    low = k * part
    blocks = grad.reshape(SIDE, SIDE, TOK, grad.shape[1])
    first, last = pl.ds(0, half), pl.ds(half, half)
    lead_to, _ = lead_moves(lead)

    def line(d, lo, size):
        rows = pl.ds(low + lo, size)
        if lead == "x":
            return (wrap(x + d), slice(None), rows, slice(None))
        return (slice(None), wrap(z + d), rows, slice(None))

    via_up = net.put(blocks.at[line(2, 0, half)], via.at[k, 0], lead_to(1))
    via_down = net.put(blocks.at[line(2, half, half)], via.at[k, 1], lead_to(-1))
    up_late = net.put(blocks.at[line(1, half, half)], landed.at[k, 0, :, last], lead_to(1))
    down_first = net.put(blocks.at[line(3, 0, half)], landed.at[k, 1, :, first], lead_to(-1))
    loads = [
        net.keep(blocks.at[line(1, 0, half)], ready.at[k, 0]),
        net.keep(blocks.at[line(3, half, half)], ready.at[k, 1]),
        net.keep(blocks.at[line(0, 0, part)], sums.at[k]),
    ]
    yield
    for load in loads:
        load.wait()
    via_up.wait_recv()

    @pl.loop(0, SIDE)
    def _(i):
        ready[k, 0, i] = (ready[k, 0, i].astype(F32) + via[k, 0, i].astype(F32)).astype(BF)

    up_first = net.put(ready.at[k, 0], landed.at[k, 0, :, first], lead_to(1))
    via_down.wait_recv()

    @pl.loop(0, SIDE)
    def _(i):
        ready[k, 1, i] = (ready[k, 1, i].astype(F32) + via[k, 1, i].astype(F32)).astype(BF)

    down_late = net.put(ready.at[k, 1], landed.at[k, 1, :, last], lead_to(-1))
    yield
    for copy in (up_late, down_first, up_first, down_late):
        copy.wait_recv()

    @pl.loop(0, SIDE)
    def _(i):
        both = landed[k, 0, i].astype(F32) + landed[k, 1, i].astype(F32)
        sums[k, i] = (sums[k, i].astype(F32) + both).astype(BF)


def reduce_second(net, sums, scr, lead):
    via, landed, ready, total = scr
    x, z, y, c = here()
    part, half = TOK // 2, TOK // 4
    k = 0 if lead == "x" else 1
    first, last = pl.ds(0, half), pl.ds(half, half)
    _, then_to = lead_moves(lead)
    me = z if lead == "x" else x

    def block(d, rows):
        return sums.at[k, wrap(me + d), rows]

    via_up = net.put(block(2, first), via.at[k, 0], then_to(1))
    via_down = net.put(block(2, last), via.at[k, 1], then_to(-1))
    up_late = net.put(block(1, last), landed.at[k, 0, last], then_to(1))
    down_first = net.put(block(3, first), landed.at[k, 1, first], then_to(-1))
    yield
    via_up.wait_recv()
    ready[k, 0] = (block(1, first)[...].astype(F32) + via[k, 0].astype(F32)).astype(BF)
    up_first = net.put(ready.at[k, 0], landed.at[k, 0, first], then_to(1))
    via_down.wait_recv()
    ready[k, 1] = (block(3, last)[...].astype(F32) + via[k, 1].astype(F32)).astype(BF)
    down_late = net.put(ready.at[k, 1], landed.at[k, 1, last], then_to(-1))
    yield
    for copy in (up_late, down_first, up_first, down_late):
        copy.wait_recv()
    both = landed[k, 0].astype(F32) + landed[k, 1].astype(F32)
    total[pl.ds(k * part, part), :] = (sums[k, me].astype(F32) + both).astype(BF)


def side_by_side(*parts):
    while True:
        if StopIteration in [next(part, StopIteration) for part in parts]:
            break
        yield


def return_narrow(net, total, out, pieces):
    n = lax.axis_index("narrow")
    copies, mine = [], []
    for start, width, to in pieces:
        spot = out.at[:, lanes(to + n * width, width)]
        columns = pl.ds(start, width)
        for p in NARROW_ALL:
            target = moved(**p)
            copies.append(net.put(total.at[span(target[1] * ROWS, ROWS), columns], spot, target))
        mine.append(net.keep(total.at[span(n * ROWS, ROWS), columns], spot))
    yield
    for copy in mine:
        copy.wait()
    for copy in copies:
        copy.wait_recv()


def second_then_narrow(net, sums, out, scr, pieces):
    yield from side_by_side(*[reduce_second(net, sums, scr, lead) for lead in "xz"])
    yield from return_narrow(net, scr[3], out, pieces)


def wide_then_narrow(net, grad, out, scr, pieces):
    yield from side_by_side(*[reduce_first(net, grad, scr[:4], lead) for lead in "xz"])
    yield from second_then_narrow(net, scr[3], out, scr[4:], pieces)


def feed_forward(normed_own, upstream, w_up, stage_up, w_down, d_act, marks, own, cid):
    pair_rows = 2 * TOK
    units = FF // NARROW
    strip = 256

    def body(net, ins, outs, scr):
        own, upstream, up_in, stage_in, down_in, da_in, marks = ins[:7]
        kept_up = up_in.shape[1]
        rest = pl.ds(kept_up, units - kept_up)
        ffn_part, g_up, down_sums, after_out, attn_out, hidden_out, vector_out = outs
        xv, dv, w_up, w_down, mv, act, du, da, gu, yv = scr[:10]
        gated, dots, dots_in = scr[16:19]
        held, d_attn, d_hidden, vector = scr[19:26], *scr[26:29]
        gds, firsts = scr[29:31], (scr[31:35], scr[35:39])
        stage = scr[39]
        n = lax.axis_index("narrow")
        x, z, y, c = here()
        loads = [
            net.keep(a, b)
            for a, b in (
                (stage_in, stage),
                (marks, mv),
                (up_in, w_up.at[:, pl.ds(0, kept_up)]),
                (da_in, da),
                (upstream, dv),
                (down_in, w_down),
            )
        ]
        own_loads = [net.keep(a, b) for a, b in zip(ins[7:], held)]
        greet(NARROW_ALL + NEAR_XZ)
        loads.pop(0).wait()
        sums = Pairs(net, None, scr[10:16], far_first=False)
        stores, dot_copies, gate_grads = [], [], []

        def gradient(left, right, to):
            @pl.loop(0, D // strip)
            def _(i):
                at = lanes(i * strip, strip)
                to[span(i * strip, strip), :] = lax.dot_general(
                    left[:, at], right[...], CONTRACT_ROWS, preferred_element_type=F32
                ).astype(BF)

        def wait_loads():
            for load in loads:
                load.wait()

        def half_gradient(i):
            columns = pl.ds(i * units // 2, units // 2)
            gradient(dv, gated.at[:, columns], gds[i])

        def units_of(dy, later):
            r = span(wrap(y + dy) * pair_rows, pair_rows)
            columns = rest if later else pl.ds(0, kept_up)
            up = jnp.dot(xv[r, :], w_up[:, columns], preferred_element_type=F32)
            positive = jnp.maximum(up, 0.0)
            masked = positive * branch_mask(mv[r, :], PICK_FFN)
            gate = mv[r, GATE_FFN : GATE_FFN + 1]
            active = positive * masked
            act[r, columns] = active.astype(BF)
            gated[r, columns] = (active * gate).astype(BF)
            back = da[r, columns]
            du[r, columns] = (back * (2.0 * gate * masked)).astype(BF)
            dot = lax.dot_general(
                jnp.ones((8, up.shape[1]), BF),
                (back * active).astype(BF),
                CONTRACT_COLS,
                preferred_element_type=F32,
            )
            for core in range(2):
                spot = wrap(y + dy) * 2 + core
                part = dot[:, core * TOK : (core + 1) * TOK]
                dots[spot] = dots[spot] + part if later else part

        def norm_back(dy):
            r = span(wrap(y + dy) * pair_rows, pair_rows)
            back = lax.dot_general(
                du[r, :], w_up[...], CONTRACT_COLS, preferred_element_type=F32
            )
            sums.store(dy, back)
            sums.cross(dy)

        def send_dots():
            for p in NARROW_ALL:
                target = moved(**p)
                dot_copies.append(net.put(dots.at[target[1]], dots_in.at[n], target))
            dots_in[n] = dots[n]

        def up_gradient():
            gradient(xv, du, gu)
            stores.append(net.keep(gu, g_up))

        def output(dy):
            r = span(wrap(y + dy) * pair_rows, pair_rows)
            yv[r, :] = lax.dot_general(
                act[r, :], w_down[...], CONTRACT_COLS, preferred_element_type=F32
            ).astype(BF)
            stores.append(net.keep(yv.at[r], ffn_part.at[r]))

        def second_norm_back():
            for load in own_loads:
                load.wait()
            for copy in dot_copies:
                copy.wait_recv()
            s = dots_in[0]
            for i in range(1, NARROW):
                s = s + dots_in[i]
            row = lax.broadcasted_iota(jnp.int32, (TOK, TOK), 0)
            lane = lax.broadcasted_iota(jnp.int32, (TOK, TOK), 1)
            ffn = jnp.sum(jnp.where(row == lane, s[0:1, :], 0.0), axis=-1, keepdims=True)
            after, attn, gate, gains, slopes = held[:5]
            total = sums.scr[5]
            hat, inverse = normal(after[...])
            back = normal_back(hat, inverse, total[...] * gains[1:2, :])
            back = back + dv[span(n * TOK, TOK), :].astype(F32)
            d_attn[...] = (back * gate[:, :1]).astype(BF)
            attn_gate = jnp.sum(back * attn[...], axis=-1, keepdims=True)
            d_hidden[...] = (attn_gate * slopes[0] + ffn * slopes[1]).astype(BF)
            attn[...] = back
            stores.extend([net.keep(attn, after_out), net.keep(d_attn, attn_out)])
            gate_grads.extend([attn_gate, ffn])

        def fill_vector():
            after, _, _, _, _, logit_slopes, hidden = held
            hat, _ = normal(after[...])
            d_gain = jnp.sum(sums.scr[5][...] * hat, axis=0, keepdims=True)
            d_logits = gate_grads[0] * logit_slopes[0] + gate_grads[1] * logit_slopes[1]
            d_router = lax.dot_general(
                d_logits.astype(BF),
                hidden[...].astype(BF),
                CONTRACT_ROWS,
                preferred_element_type=F32,
            )
            vector[...] = jnp.zeros_like(vector)
            for i in range(GAIN_ROWS // 2):
                at = GAIN_ROWS // 2 + i
                vector[at : at + 1, :] = d_gain[:, i * 128 : (i + 1) * 128]
            for i in range(RH // 128):
                at = GAIN_ROWS + i * 2 * LEVELS
                vector[at : at + 2 * LEVELS, :] = d_router[: 2 * LEVELS, i * 128 : (i + 1) * 128]
            own_marks = mv[span(n * TOK, TOK), :]
            levels = lax.broadcasted_iota(jnp.int32, (TOK, 128), 1).astype(F32)
            picked = jnp.where(levels == own_marks[:, PICK_ATTN : PICK_ATTN + 1], 1.0, 0.0)
            other = own_marks[:, PICK_FFN : PICK_FFN + 1] + float(LEVELS)
            picked = picked + jnp.where(levels == other, 1.0, 0.0)
            vector[SMALL_ROWS : SMALL_ROWS + 1, :] = jnp.sum(picked, axis=0, keepdims=True)
            stores.append(net.keep(vector, vector_out))

        works = {
            LD: wait_loads,
            GD: functools.partial(half_gradient, 0),
            GE: functools.partial(half_gradient, 1),
            GU: up_gradient,
            DS: send_dots,
            LB: second_norm_back,
            LV: fill_vector,
        }
        for dy in PAIR_ORDER:
            works[EARLY[dy]] = functools.partial(units_of, dy, False)
            works[UNITS[dy]] = functools.partial(units_of, dy, True)
            works[OUTPUT[dy]] = functools.partial(output, dy)
            works[NORM[dy]] = functools.partial(norm_back, dy)
        moves = {
            GATHER: gather_narrow(net, own, xv),
            TOTAL: sums.steps(),
            FIRST: side_by_side(*[reduce_first(net, gds[0], firsts[0], lead) for lead in "xz"]),
            MORE: side_by_side(*[reduce_first(net, gds[1], firsts[1], lead) for lead in "xz"]),
            HID: gather_small(net, d_hidden, hidden_out),
            WU: side_by_side(*[gather_wide(net, w_up.at[:, rest], k, stage) for k in "xz"]),
        }
        follow(FEED_PLAN, works, moves)
        for i in range(2):
            columns = pl.ds(i * units // 2, units // 2)
            stores.append(net.keep(firsts[i][3], down_sums.at[:, :, :, columns]))
        for store in stores:
            store.wait()

    wide = pltpu.VMEM((GROUP, D), BF)
    tall = pltpu.VMEM((D, units), BF)
    square = pltpu.VMEM((GROUP, units), BF)
    return comm_call(
        body,
        [normed_own, upstream, w_up, stage_up, w_down, d_act, marks] + list(own),
        [
            jax.ShapeDtypeStruct((GROUP, D), BF),
            jax.ShapeDtypeStruct((D, units), BF),
            jax.ShapeDtypeStruct((2, SIDE, TOK // 2, units), BF),
            jax.ShapeDtypeStruct((TOK, D), F32),
            jax.ShapeDtypeStruct((TOK, D), BF),
            jax.ShapeDtypeStruct((GROUP, RH), BF),
            jax.ShapeDtypeStruct((VECTOR_ROWS, 128), F32),
        ],
        [wide, wide, tall, tall, pltpu.VMEM(marks.shape, F32), square, square]
        + [pltpu.VMEM((GROUP, units), F32), tall, wide]
        + pairs_scratch(TOK, D)
        + [square]
        + [pltpu.VMEM((NARROW, 8, TOK), F32)] * 2
        + [pltpu.VMEM(r.shape, r.dtype) for r in own]
        + [
            pltpu.VMEM((TOK, D), BF),
            pltpu.VMEM((TOK, RH), BF),
            pltpu.VMEM((VECTOR_ROWS, 128), F32),
        ]
        + [pltpu.VMEM((D, units // 2), BF)] * 2
        + first_scratch(units // 2) * 2
        + [pltpu.VMEM(stage_up.shape, BF)],
        cid,
        GATHER_COPIES + REDUCE_COPIES + 7 + 2 * FIRST_COPIES + 2 * WIDE_COPIES + GATHER_SMALL_COPIES,
        14 + 1 + 1 + 12 + 2 * FIRST_LOCALS + 2,
        "feed_forward",
    )


def squares_of(ref, rows, cols):
    s = jnp.zeros((SQUARE_ROWS, 128), F32)
    for i in range(ref.shape[0] // rows):
        for j in range(ref.shape[1] // cols):
            piece = ref[i * rows : (i + 1) * rows, j * cols : (j + 1) * cols].astype(F32)
            piece = piece * piece
            for a in range(rows // SQUARE_ROWS):
                for b in range(cols // 128):
                    s = s + piece[a * 8 : a * 8 + 8, b * 128 : b * 128 + 128]
    return s


def sum_everywhere(net, own, first, second, total):
    w = lax.axis_index("wide")
    n = lax.axis_index("narrow")

    def rows(i):
        return pl.ds(pl.multiple_of(i * 8, 8), 8)

    copies = []
    for p in NARROW_ALL:
        target = moved(**p)
        copies.append(net.put(own.at[rows(target[1])], first.at[n], target))
    first[n] = own[rows(n), :]
    for copy in copies:
        copy.wait_recv()
    s = first[0]
    for i in range(1, NARROW):
        s = s + first[i]
    second[w] = s
    copies = [net.put(second.at[w], second.at[w], moved(**p)) for p in WIDE_ALL]
    for copy in copies:
        copy.wait_recv()
    s = second[0]
    for i in range(1, WIDE):
        s = s + second[i]
    total[rows(n), :] = s
    copies = [net.put(total.at[rows(n)], total.at[rows(n)], moved(**p)) for p in NARROW_ALL]
    for copy in copies:
        copy.wait_recv()


def attention_backward(
    d_attn_own, ffn_part, g_up, down_sums, normed, hidden_in, own, kept, cid
):
    table_rows = D // NARROW
    pair_rows = 2 * TOK
    head_part = D // NARROW
    units = FF // NARROW
    strip = 256
    scale = HEAD_DIM ** (-0.5)
    scratch = (
        [pltpu.VMEM(r.shape, r.dtype) for r in kept]
        + [
            pltpu.VMEM((GROUP, D), BF),
            pltpu.VMEM((GROUP, head_part), F32),
            pltpu.VMEM((GROUP, head_part), F32),
            pltpu.VMEM((GROUP, 3 * head_part), BF),
            pltpu.VMEM((D, 3 * head_part), BF),
        ]
        + pairs_scratch(TOK, D)[1:]
        + reduce_scratch(TOK, D)
        + first_scratch(3 * head_part)
        + second_scratch(3 * head_part)
        + first_scratch(units)
        + second_scratch(units)
        + [pltpu.VMEM(down_sums.shape, BF)]
        + second_scratch(units)
        + [
            pltpu.VMEM((GROUP, table_rows), BF),
            pltpu.VMEM((GROUP, RH), BF),
            pltpu.VMEM((table_rows, RH), BF),
            pltpu.VMEM((WIDE, ROWS, RH), BF),
            pltpu.VMEM((ROWS, RH), BF),
            pltpu.VMEM((table_rows, RH), BF),
            pltpu.VMEM((1, D), F32),
        ]
        + [pltpu.VMEM(r.shape, r.dtype) for r in own]
        + [
            pltpu.VMEM((ROWS, 4 * D + 2 * FF), BF),
            pltpu.VMEM((TOK, D), BF),
            pltpu.VMEM((NARROW, 8, 128), F32),
            pltpu.VMEM((WIDE, 8, 128), F32),
            pltpu.VMEM((VECTOR_ROWS, 128), F32),
            pltpu.VMEM((8, 128), F32),
            pltpu.VMEM((D, head_part), BF),
        ]
        + first_scratch(head_part)
        + second_scratch(head_part)
    )

    def body(net, ins, outs, scr):
        d_attn_own, ffn_part, g_up, down_sums, normed, hidden_in = ins[:6]
        input_grad, result_out, block_out, table, vector_out, norm_out = outs
        wv, tv, mv, qv, kv, vv, pv, av = scr[:8]
        big, dk, dv, dproj, ga = scr[8:13]
        pairs, narrow = [big, *scr[13:18]], scr[18:24]
        wide_a, wide_up, wide_down = scr[24:32], scr[32:40], scr[40:45]
        columns, hidden, part, landed, shard, mine = scr[45:51]
        d_gain, held = scr[51], scr[52:58]
        block, result, first, second, summed, norm = scr[58:64]
        go, wide_o = scr[64], scr[65:73]
        n = lax.axis_index("narrow")
        x, z, y, c = here()
        first_load = net.keep(down_sums, wide_down[0])
        loads = [net.keep(a, b) for a, b in zip(ins[12:], scr[:8])]
        own_loads = [net.keep(a, b) for a, b in zip(ins[6:12], held)]
        loads.append(net.keep(hidden_in, hidden))
        loads.append(net.keep(normed.at[:, lanes(n * table_rows, table_rows)], columns))
        greet(NARROW_ALL + WIDE_ALL)
        sums = Pairs(net, None, pairs)
        thirds = [(i * head_part, head_part, i * D) for i in range(3)]

        def router():
            w = lax.axis_index("wide")
            part[...] = lax.dot_general(
                columns[...], hidden[...], CONTRACT_ROWS, preferred_element_type=F32
            ).astype(BF)
            copies = []
            for p in WIDE_ALL:
                target = moved(**p)
                rows = part.at[span(target[0] * ROWS, ROWS)]
                copies.append(net.put(rows, landed.at[w], target))
            kept = net.keep(part.at[span(w * ROWS, ROWS)], landed.at[w])
            yield
            kept.wait()
            for copy in copies:
                copy.wait_recv()
            s = landed[0].astype(F32)
            for i in range(1, WIDE):
                s = s + landed[i].astype(F32)
            shard[...] = s.astype(BF)
            spot = mine.at[span(w * ROWS, ROWS)]
            copies = [net.put(shard, spot, moved(**p)) for p in WIDE_ALL]
            kept = net.keep(shard, spot)
            yield
            kept.wait()
            for copy in copies:
                copy.wait_recv()
            yield from gather_narrow(net, mine, table)

        moves = {
            GATHER: gather_narrow(net, d_attn_own, big),
            DOWN: second_then_narrow(
                net, wide_down[0], block, wide_down[1:], [(0, units, 4 * D + FF)]
            ),
            UP: wide_then_narrow(net, g_up, block, wide_up, [(0, units, 4 * D)]),
            MIXED: wide_then_narrow(net, ga, block, wide_a, thirds),
            MO: wide_then_narrow(net, go, block, wide_o, [(0, head_part, 3 * D)]),
            FEED: reduce_narrow(net, ffn_part, narrow),
            GATES: router(),
            TOTAL: sums.steps(),
        }

        def wait_loads():
            first_load.wait()
            for load in loads:
                load.wait()
            dk[...] = jnp.zeros_like(dk)
            dv[...] = jnp.zeros_like(dv)

        def one_pair(dy):
            r = span(wrap(y + dy) * pair_rows, pair_rows)
            mask = branch_mask(mv[r, :], PICK_ATTN)
            back = jnp.dot(big[r, :], wv[:, 3 * head_part :], preferred_element_type=F32)
            back = (back * mask).astype(BF)
            for h in range(2):
                at = pl.ds(h * HEAD_DIM, HEAD_DIM)
                d_out = back[:, h * HEAD_DIM : (h + 1) * HEAD_DIM]
                d_probs = lax.dot_general(
                    d_out, vv[:, at], CONTRACT_COLS, preferred_element_type=F32
                )
                probs_low = pv[r, pl.ds(h * GROUP, GROUP)]
                probs = probs_low.astype(F32)
                weighted = probs * d_probs
                centre = jnp.sum(weighted, axis=-1, keepdims=True)
                ds = (weighted - probs * centre).astype(BF)
                dq = jnp.dot(ds, kv[:, at], preferred_element_type=F32) * scale
                dproj[r, at] = turn(dq, tv[0, r, :], -tv[1, r, :]).astype(BF)
                dk[:, at] += lax.dot_general(
                    ds, qv[r, at], CONTRACT_ROWS, preferred_element_type=F32
                )
                dv[:, at] += lax.dot_general(
                    probs_low, d_out, CONTRACT_ROWS, preferred_element_type=F32
                )

        refill = []

        def turn_back():
            refill.append(net.keep(normed, pv))

            @pl.loop(0, SIDE)
            def _(i):
                r = span(i * pair_rows, pair_rows)
                cosine, sine = tv[0, r, :], -tv[1, r, :]
                for h in range(2):
                    at = pl.ds(h * HEAD_DIM, HEAD_DIM)
                    to = pl.ds(head_part + h * HEAD_DIM, HEAD_DIM)
                    dproj[r, to] = turn(dk[r, at] * scale, cosine, sine).astype(BF)
                dproj[r, pl.ds(2 * head_part, head_part)] = dv[r, :].astype(BF)

        def gradient(left, right, to):
            @pl.loop(0, D // strip)
            def _(i):
                to[span(i * strip, strip), :] = lax.dot_general(
                    left[:, lanes(i * strip, strip)],
                    right[...],
                    CONTRACT_ROWS,
                    preferred_element_type=F32,
                ).astype(BF)

        def mixed_gradient():
            refill[0].wait()
            gradient(pv, dproj, ga)

        def norm_back(dy):
            r = span(wrap(y + dy) * pair_rows, pair_rows)
            back = lax.dot_general(
                dproj[r, :], wv[:, : 3 * head_part], CONTRACT_COLS, preferred_element_type=F32
            )
            sums.store(dy, back)
            sums.cross(dy)

        stores = []

        own_there = []

        def wait_own():
            if not own_there:
                own_there.append(True)
                for load in own_loads:
                    load.wait()

        def output():
            wait_own()
            gate = mv[span(n * TOK, TOK), GATE_FFN : GATE_FFN + 1]
            result[...] = (held[4][...] + gate * narrow[5][...]).astype(BF)
            stores.append(net.keep(result, result_out))

        squares = []

        def late_squares():
            squares.append(squares_of(block.at[:, pl.ds(3 * D, D + 2 * FF)], ROWS, 2048))

        def first_norm_back():
            wait_own()
            tokens, after, gains, router_in = held[:4]
            total = sums.scr[5]
            d_normed = total[...] + lax.dot_general(
                hidden[span(n * TOK, TOK), :],
                router_in[...],
                CONTRACT_COLS,
                preferred_element_type=F32,
            )
            hat, inverse = normal(tokens[...].astype(F32))
            d_gain[...] = jnp.sum(d_normed * hat, axis=0, keepdims=True)
            total[...] = after[...] + normal_back(hat, inverse, d_normed * gains[0:1, :])
            stores.append(net.keep(total, input_grad))

        works = {
            LB: first_norm_back,
            OUT: output,
            SQ: late_squares,
            LD: wait_loads,
            RT: turn_back,
            GO: functools.partial(gradient, big, av, go),
            GQ: mixed_gradient,
        }
        for dy in PAIR_ORDER:
            works[PAIR[dy]] = functools.partial(one_pair, dy)
            works[NORM[dy]] = functools.partial(norm_back, dy)
        follow(BACKWARD_PLAN, works, moves)
        stores.append(net.keep(block, block_out))
        vector = held[5]
        for i in range(GAIN_ROWS // 2):
            vector[i : i + 1, :] = d_gain[:, i * 128 : (i + 1) * 128]
        others = squares_of(block.at[:, pl.ds(0, 3 * D)], ROWS, 2048)
        others = others + squares_of(shard, ROWS, RH)
        vector[VECTOR_ROWS - SQUARE_ROWS :, :] = squares[0] + others
        sum_everywhere(net, vector, first, second, summed)
        stores.append(net.keep(summed, vector_out))
        s = summed[...]
        small = s[:SMALL_ROWS]
        sum_all = jnp.sum(small * small) + jnp.sum(s[VECTOR_ROWS - SQUARE_ROWS :])
        norm[...] = jnp.sqrt(jnp.full((8, 128), sum_all, F32))
        stores.append(net.keep(norm, norm_out))
        for store in stores:
            store.wait()

    return comm_call(
        body,
        [d_attn_own, ffn_part, g_up, down_sums, normed, hidden_in] + list(own) + list(kept),
        [
            jax.ShapeDtypeStruct((TOK, D), F32),
            jax.ShapeDtypeStruct((TOK, D), BF),
            jax.ShapeDtypeStruct((ROWS, 4 * D + 2 * FF), BF),
            jax.ShapeDtypeStruct((D, RH), BF),
            jax.ShapeDtypeStruct((VECTOR_ROWS, 128), F32),
            jax.ShapeDtypeStruct((8, 128), F32),
        ],
        scratch,
        cid,
        GATHER_COPIES
        + 2 * REDUCE_COPIES
        + 3 * FIRST_COPIES
        + 4 * SECOND_COPIES
        + 6 * 7
        + 2 * 15
        + GATHER_COPIES
        + 7 + 15 + 7,
        17 + 1 + 1 + 5 + REDUCE_LOCALS + 3 * FIRST_LOCALS + 6 + 4,
        "attention_backward",
    )


def adamw(weight, moment_one, moment_two, gradient, step_rate):
    one = 0.9 * moment_one + 0.1 * gradient
    two = 0.95 * moment_two + 0.05 * (gradient * gradient)
    scaled = jnp.maximum(two * (1.0 / (1.0 - 0.95**STEP)), 1e-30)
    root = scaled * lax.rsqrt(scaled) + 1e-08
    guess = pltpu.reciprocal(root, approx=True)
    guess = guess * (2.0 - root * guess)
    guess = guess * (2.0 - root * guess)
    rate = step_rate / (1.0 - 0.9**STEP)
    updated = weight * (1.0 - step_rate * 0.1) - (one * rate) * guess
    return updated, one, two


def clip_of(norm):
    return jnp.minimum(1.0, CLIP_NORM / norm[0:1, 0:1])


def all_steps(block, layer, gains, second_layer, vector, norm):
    block_parts, layer_parts = 3, 2
    n_loads = 4 * (block_parts + layer_parts)

    def kernel(*refs):
        block_in, layer_in = refs[0:4], refs[4:8]
        gains_in, second_in, vec, n = refs[8:11], refs[11:14], refs[14], refs[15]
        block_out, layer_out = refs[16:20], refs[20:23]
        gains_out, second_out, counts_out, norm_out = refs[23:26], refs[26:29], refs[29], refs[30]
        held_block, held_layer, new_block, new_layer = (
            refs[31:35],
            refs[35:39],
            refs[39:43],
            refs[43:46],
        )
        gain_grad, second_grad, loaded, stored = refs[46:50]
        clip = clip_of(n)

        def start(pairs, part, sems, at):
            copies = []
            for i, (a, b) in enumerate(pairs):
                copies.append(pltpu.make_async_copy(a.at[part], b.at[part], sems.at[at + i]))
                copies[-1].start()
            return copies

        parts = []
        for i in range(block_parts):
            cols = block_in[0].shape[1] // block_parts
            parts.append((True, (slice(None), pl.ds(i * cols, cols))))
        for i in range(layer_parts):
            rows = layer_in[0].shape[0] // layer_parts
            parts.append((False, (pl.ds(i * rows, rows), slice(None))))
        loads, stores = [], []
        for i, (is_block, part) in enumerate(parts):
            pairs = zip(block_in, held_block) if is_block else zip(layer_in, held_layer)
            loads.append(start(pairs, part, loaded, 4 * i))

        for i in range(GAIN_ROWS):
            row, at = i // (GAIN_ROWS // 2), i % (GAIN_ROWS // 2) * 128
            gain_grad[row : row + 1, at : at + 128] = vec[i : i + 1, :]
        for i in range(RH // 128):
            at = GAIN_ROWS + i * 2 * LEVELS
            second_grad[:, i * 128 : (i + 1) * 128] = vec[at : at + 2 * LEVELS, :]
        for held, grad, new, rate in (
            (gains_in, gain_grad, gains_out, 0.6),
            (second_in, second_grad, second_out, 0.02),
        ):
            results = adamw(*[r[...] for r in held], grad[...] * clip, rate)
            for ref, value in zip(new, results):
                ref[...] = value
        row = vec[SMALL_ROWS : SMALL_ROWS + 1, :]
        counts_out[0:1, :] = row[:, :LEVELS]
        counts_out[1:2, :] = pltpu.roll(row, 128 - LEVELS, 1)[:, :LEVELS]
        norm_out[...] = n[0:1, 0:1]

        for i, (is_block, part) in enumerate(parts):
            for copy in loads[i]:
                copy.wait()
            held, new = (held_block, new_block) if is_block else (held_layer, new_layer)
            gradient = held[3][part].astype(F32) * clip
            results = adamw(*[r[part] for r in held[:3]], gradient, 0.02)
            for ref, value in zip(new, results):
                ref[part] = value
            if is_block:
                new[3][part] = results[0].astype(BF)
            pairs = zip(new, block_out if is_block else layer_out)
            stores += start(pairs, part, stored, 4 * i)
        for copy in stores:
            copy.wait()

    def like(x, dtype=F32):
        return jax.ShapeDtypeStruct(x.shape, dtype)

    def room(x, dtype=F32):
        return pltpu.VMEM(x.shape, dtype)

    far, near = pl.BlockSpec(memory_space=pl.ANY), pl.BlockSpec(memory_space=pltpu.VMEM)
    b, r, g, o = block[0], layer[0], gains[0], second_layer[0]
    return pl.pallas_call(
        kernel,
        out_shape=[like(b)] * 3
        + [like(b, BF)]
        + [like(r)] * 3
        + [like(g)] * 3
        + [like(o)] * 3
        + [jax.ShapeDtypeStruct((2, LEVELS), F32), jax.ShapeDtypeStruct((1, 1), F32)],
        in_specs=[far] * 8 + [near] * 8,
        out_specs=[far] * 7 + [near] * 8,
        scratch_shapes=[room(b)] * 3
        + [room(b, BF)]
        + [room(r)] * 3
        + [room(r, BF)]
        + [room(b)] * 3
        + [room(b, BF)]
        + [room(r)] * 3
        + [room(g), room(o)]
        + [pltpu.SemaphoreType.DMA((n_loads,)), pltpu.SemaphoreType.DMA((n_loads,))],
        compiler_params=pltpu.CompilerParams(vmem_limit_bytes=60 * 2**20),
        name="all_steps",
    )(*block, *layer, *gains, *second_layer, vector, norm)


def on_device(
    tokens,
    lengths,
    picks,
    cotangent,
    block_master,
    block_first,
    block_second,
    gains,
    gains_first,
    gains_second,
    router_in,
    router_in_first,
    router_in_second,
    router_out,
    router_out_first,
    router_out_second,
):
    half_dim = HEAD_DIM // 2
    angle_steps = 10000.0 ** (-np.arange(half_dim, dtype=np.float32) / half_dim)
    frequency = jnp.asarray(np.tile(angle_steps.astype(np.float32), (8, 2)))
    f = attention_forward(
        tokens,
        picks.T,
        lengths,
        frequency,
        gains,
        router_in,
        jnp.pad(router_out, ((0, 0), (0, 128 - 2 * LEVELS))).astype(BF),
        block_master,
        cotangent,
        1,
    )

    ffn_part, grad_up, down_sums, d_after, d_attn, d_hidden, vector = feed_forward(
        f["second"],
        f["g"],
        f["slab_up"],
        f["stage_up"],
        f["slab_down"],
        f["d_act"],
        f["marks"],
        [f["after"], f["attn_sum"], f["gate"], gains, f["slopes"], f["logit_slopes"], f["hidden"]],
        2,
    )
    d_inputs, result, block_low, router_in_grad, vector, norm = attention_backward(
        d_attn,
        ffn_part,
        grad_up,
        down_sums,
        f["normed"],
        d_hidden,
        [tokens, d_after, gains, f["router_low"], f["after"], vector],
        [f[k] for k in ("slab_a", "turns", "marks", "q", "k", "v", "p", "a")],
        3,
    )
    (
        new_block,
        new_block_first,
        new_block_second,
        block_copy,
        new_router_in,
        new_router_in_first,
        new_router_in_second,
        new_gains,
        new_gains_first,
        new_gains_second,
        new_router_out,
        new_router_out_first,
        new_router_out_second,
        counts,
        grad_norm,
    ) = all_steps(
        (block_master, block_first, block_second, block_low),
        (router_in, router_in_first, router_in_second, router_in_grad),
        (gains, gains_first, gains_second),
        (router_out.T, router_out_first.T, router_out_second.T),
        vector,
        norm,
    )
    return (
        result,
        d_inputs,
        counts,
        grad_norm.reshape(()),
        new_block,
        new_block_first,
        new_block_second,
        block_copy,
        new_gains,
        new_gains_first,
        new_gains_second,
        new_router_in,
        new_router_in_first,
        new_router_in_second,
        new_router_out.T,
        new_router_out_first.T,
        new_router_out_second.T,
    )


def solution(mesh):
    both = P(("wide", "narrow"), None)
    return jax.shard_map(
        on_device,
        mesh=mesh,
        in_specs=(both, P("wide", None)) + (both,) * 5 + (P(),) * 9,
        out_specs=(both, both, P(), P()) + (both,) * 4 + (P(),) * 9,
        check_vma=False,
    )
```
